128 devices in a mesh: lat: 8 (over x, core), lon: 16 (over y, z).
Axes of the slice: x: 4, y: 4, z: 4, core: 2. Of those that a mesh axis runs over, the one named last changes fastest.
Arguments:
- spectrum: float32 [36, 2, 256, 4096], P(None, None, 'lat', 'lon'), may hold values from 0.05 to 2
- speed_factor: float32 [256, 4096], P('lat', 'lon'), may hold values from 0.3 to 1
- land_sea_mask: int32 [256, 4096], P('lat', 'lon'), may hold values 0 or 1
- courant: float32 [2], replicated, may hold values from 0.25 to 0.65
- depth_kernel: float32 [64, 72], replicated, may hold values from -0.75 to 0.75
- send_rows: int32 [128, 128, 128], P(('lat', 'lon')), may hold values from -1 to 8191, as said below
- recv_rows: int32 [128, 128, 128], P(('lat', 'lon')), may hold values from -1 to 4095, as said below
Outputs:
- propagated: float32 [36, 2, 256, 4096], P(None, None, 'lat', 'lon')
- stokes_tiles: float32 [64, 524288], P(None, ('lat', 'lon'))
The draws below stay inside these ranges and needn't reach their ends.
Inputs may be any that keep to these rules, and one draw needn't show every extreme that they name: Slots 0 to n - 1 of send_rows[s, o] hold the listed local cells (repeats allowed) and the rest -1, with n at most 128; in every draw some owner receives a full list of 128 from every source. recv_rows[o, s, k] is -1 exactly where send_rows[s, o, k] is -1.
All inputs are finite; a program needn't handle non-finite values. No bound on the sum of `land_sea_mask` on one device may be relied on, other than what follows from the above.
Results may differ from the reference program's by a relative error of at most 0.002.
Values may be sent and summed in bfloat16 or wider, within the bound.
No kernel may reach another device: no remote copies, remote signals or barrier semaphores. Data moves between devices by JAX's collectives and lax.ppermute only.
A program may use at most 64 MiB of HBM per device.

```python
import math
import jax
import jax.numpy as jnp
from jax import lax

DIRS = 36
FREQ = 2
DEPTHS = 32
RY = 32
CX = 256
CAP = 128
OUT_DEV = 4096
NY = 256
NX = 4096
N_LAT = 8
N_LON = 16
DEVICES = 128


def route_counts(key):
    key_load, key_raw, key_owner = jax.random.split(key, 3)
    dest_load = jax.random.randint(key_load, (DEVICES,), 1, 5)
    raw_counts = jax.random.randint(key_raw, (DEVICES, DEVICES), 0, CAP + 1)
    counts = jnp.minimum(CAP, raw_counts * dest_load[None, :] // 2)
    full_owner = jax.random.randint(key_owner, (), 0, DEVICES)
    owner_ids = jnp.arange(DEVICES, dtype=jnp.int32)[None, :]
    return jnp.where(owner_ids == full_owner, CAP, counts)


def draw_send_rows(key, part):
    counts = route_counts(key)
    key = jax.random.fold_in(key, 11)
    cell_index = jax.random.randint(key, (DEVICES, DEVICES, CAP), 0, RY * CX)
    slot_index = jnp.arange(CAP, dtype=jnp.int32)[None, None, :]
    return jnp.where(slot_index < counts[:, :, None], cell_index, -1).astype(jnp.int32)


def draw_recv_rows(key, part):
    counts = route_counts(key)
    key = jax.random.fold_in(key, 12)
    row_index = jax.random.randint(key, (DEVICES, DEVICES, CAP), 0, OUT_DEV)
    slot_index = jnp.arange(CAP, dtype=jnp.int32)[None, None, :]
    return jnp.where(slot_index < counts.T[:, :, None], row_index, -1).astype(jnp.int32)


def place_ends(entries, own_key, low, largest):
    index_at = [jax.random.randint(jax.random.fold_in(own_key, axis), (), 0, length) for axis, length in enumerate(entries.shape)]
    widest = entries.shape.index(max(entries.shape))
    neighbour = index_at[:widest] + [(index_at[widest] + 1) % entries.shape[widest]] + index_at[widest + 1:]
    return entries.at[tuple(index_at)].set(low).at[tuple(neighbour)].set(largest)


def levels(stream_key, shape, shards, low, top_value):
    factor_of = 1.0
    for dim, parts in shards:
        heights = jax.random.uniform(jax.random.fold_in(jax.random.fold_in(stream_key, 6), dim), (parts,), jnp.float32, low / len(shards), top_value / len(shards))
        factor_of = factor_of * jnp.repeat(jnp.exp(heights), shape[dim] // parts).reshape((-1,) + (1,) * (len(shape) - 1 - dim))
    return factor_of


def normal_values(key, dims, width, limit, kind=jnp.bfloat16):
    array = width * jax.random.normal(key, dims, jnp.float32)
    return jnp.clip(array, min=-limit, max=limit).astype(kind)


def setup_inputs(seed: int = 0) -> dict:
    seeds = jax.random.split(jax.random.key(seed), 8)
    spectrum = jnp.clip(jnp.exp(math.log(2.0) - 3.6888794 * jax.random.uniform(seeds[0], (DIRS, FREQ, NY, NX), jnp.float32) ** levels(seeds[0], (DIRS, FREQ, NY, NX), ((2, 8), (3, 16)), -0.2, 0.2)), 0.05, 2.0)
    speed_factor = jnp.clip(jnp.exp(math.log(1.0) - 1.2039728 * jax.random.uniform(seeds[1], (NY, NX), jnp.float32) ** levels(seeds[1], (NY, NX), ((0, 8), (1, 16)), -0.2, 0.2)), 0.3, 1.0)
    land_sea_mask = place_ends((jax.random.randint(seeds[2], (NY, NX), 0, 4) < 3).astype(jnp.int32), jax.random.fold_in(seeds[2], 1), 0, 1)
    courant = jnp.clip(jnp.exp(jax.random.uniform(seeds[3], (FREQ,), jnp.float32, math.log(0.25), math.log(0.65))), 0.25, 0.65)
    depth_kernel = normal_values(seeds[4], (2 * DEPTHS, DIRS * FREQ), (DIRS * FREQ) ** -0.5, 0.75, jnp.float32)
    send_rows = draw_send_rows(jax.random.fold_in(seeds[7], 71), 0)
    recv_rows = draw_recv_rows(jax.random.fold_in(seeds[7], 71), 0)
    return {"spectrum": spectrum, "speed_factor": speed_factor, "land_sea_mask": land_sea_mask, "courant": courant, "depth_kernel": depth_kernel, "send_rows": send_rows, "recv_rows": recv_rows}


def shift_dirs(planes_in):
    return jnp.roll(planes_in, (DIRS // 2) * FREQ, axis=0)


def margins(source):
    lon_wide = jnp.concatenate([source[:, :, -1:], source, source[:, :, :1]], axis=2)
    south_rim = jnp.zeros_like(lon_wide[:, :1, :])
    north_rim = shift_dirs(lon_wide[:, -1:, ::-1])
    return jnp.concatenate([south_rim, lon_wide, north_rim], axis=1)


def divergence(extended, courant_x, courant_y):
    centre = extended[:, 1:-1, 1:-1]
    east_plus = jnp.maximum(courant_x, 0.0)[:, None, None]
    east_minus = jnp.minimum(courant_x, 0.0)[:, None, None]
    north_plus = jnp.maximum(courant_y, 0.0)[:, None, None]
    north_minus = jnp.minimum(courant_y, 0.0)[:, None, None]
    flux_east = east_plus * (centre - extended[:, 1:-1, :-2]) + east_minus * (extended[:, 1:-1, 2:] - centre)
    flux_north = north_plus * (centre - extended[:, :-2, 1:-1]) + north_minus * (extended[:, 2:, 1:-1] - centre)
    return flux_east, flux_north


def reference(spectrum, speed_factor, land_sea_mask, courant, depth_kernel, send_rows, recv_rows):
    planes = spectrum.reshape(DIRS * FREQ, NY, NX)
    sea_mask = land_sea_mask.astype(jnp.float32)
    moving = speed_factor * sea_mask
    heading = (jnp.arange(DIRS, dtype=jnp.float32) + 0.5) * (2.0 * math.pi / DIRS)
    courant_x = (jnp.cos(heading)[:, None] * courant[None, :]).reshape(-1)
    courant_y = (jnp.sin(heading)[:, None] * courant[None, :]).reshape(-1)
    for substep in range(2):
        extended = margins(moving * planes)
        flux_east, flux_north = divergence(extended, courant_x, courant_y)
        planes = sea_mask * ((planes - flux_east) - flux_north)
    profiles = jnp.dot(depth_kernel, planes.reshape(DIRS * FREQ, NY * NX), precision=lax.Precision.HIGHEST, preferred_element_type=jnp.float32).astype(jnp.bfloat16)
    blocks = profiles.reshape(2 * DEPTHS, N_LAT, RY, N_LON, CX).transpose(0, 1, 3, 2, 4).reshape(2 * DEPTHS, DEVICES, RY * CX)
    sources = jnp.arange(DEVICES, dtype=jnp.int32)[:, None]

    def place_owner(lists):
        cell_lists, row_lists = lists
        cell_index = jnp.maximum(cell_lists, 0).astype(jnp.int32)
        values = blocks[:, sources, cell_index]
        target = jnp.where(row_lists < 0, OUT_DEV, row_lists).astype(jnp.int32)
        empty = jnp.zeros((2 * DEPTHS, OUT_DEV), jnp.float32)
        return empty.at[:, target.reshape(-1)].add(values.reshape(2 * DEPTHS, -1).astype(jnp.float32), mode="drop")

    tile_sums = lax.map(place_owner, (jnp.swapaxes(send_rows, 0, 1), recv_rows))
    stokes_tiles = jnp.swapaxes(tile_sums, 0, 1).reshape(2 * DEPTHS, DEVICES * OUT_DEV)
    return planes.reshape(DIRS, FREQ, NY, NX), stokes_tiles
```

```python
import functools
import math

import jax
import jax.numpy as jnp
import numpy as np
from jax import lax
from jax.experimental import pallas as pl
from jax.experimental.pallas import tpu as pltpu
from jax.sharding import PartitionSpec as P

DIRS = 36
FREQ = 2
PLANES = DIRS * FREQ
HALF = PLANES // 2
QUAD = PLANES // 4
OUT_DEV = 4096
N_ACC = 4
VMEM_LIMIT = 48 * 1024 * 1024


def chain_perms(n_lat, n_lon):
    top = n_lat - 1

    def flat(j, i):
        return j * n_lon + i % n_lon

    def build(step, fold):
        first, second = [], []
        for j in range(n_lat):
            for i in range(n_lon):
                start = (i + (top - j) * step) % n_lon
                partner = fold(start) % n_lon
                rising = start <= partner
                up = (flat(j, i), flat(j + 1, i + step)) if j < top else (flat(j, i), flat(j, partner))
                down = (flat(j, i), flat(j - 1, i - step)) if j > 0 else None
                if j == top and start == partner:
                    up = None
                a, b = (up, down) if rising else (down, up)
                first += [a] if a else []
                second += [b] if b else []
        return first, second

    return (
        build(0, lambda i: n_lon - 1 - i),
        build(1, lambda i: n_lon - 2 - i),
        build(-1, lambda i: n_lon - i),
    )


def rising_flags(n_lat, n_lon):
    j, i = lax.axis_index("lat"), lax.axis_index("lon")
    left = n_lat - 1 - j
    row = i <= n_lon - 1 - i
    start = lax.rem(i + left, n_lon)
    partner = lax.rem(2 * n_lon - 2 - start, n_lon)
    start_l = lax.rem(i - left + n_lon, n_lon)
    partner_l = lax.rem(n_lon - start_l, n_lon)
    return row, start <= partner, start_l <= partner_l, j == n_lat - 1, start == partner, start_l == partner_l


def pack_kernel(n_lat, n_lon, x_ref, speed_ref, mask_ref, a_ref, b_ref, c_ref, d_ref, xa_ref, xb_ref, ya_ref, yb_ref,
                mov_ref, sea_ref, up_ref, down_ref):
    height, breadth = speed_ref.shape
    row_asc, right_asc, left_asc, _, _, _ = rising_flags(n_lat, n_lon)
    sea = mask_ref[...].astype(jnp.float32)
    moving = speed_ref[...] * sea
    mov_ref[...] = moving
    sea_ref[...] = sea
    for k in range(2):
        for q in range(HALF):
            up_ref[k, q : q + 1, :] = x_ref[q, height - 1 - k : height - k, :]
            down_ref[k, q : q + 1, :] = x_ref[HALF + q, k : k + 1, :]
        up_ref[k, HALF : HALF + 1, :] = moving[height - 1 - k : height - k, :]
        down_ref[k, HALF : HALF + 1, :] = moving[k : k + 1, :]
        up_ref[k, HALF + 1 : HALF + 2, :] = sea[height - 1 - k : height - k, :]
        down_ref[k, HALF + 1 : HALF + 2, :] = sea[k : k + 1, :]
        up_ref[k, HALF + 2 :, :] = jnp.zeros((2, breadth), jnp.float32)
        down_ref[k, HALF + 2 :, :] = jnp.zeros((2, breadth), jnp.float32)

    @pl.when(row_asc)
    def _():
        a_ref[...] = up_ref[...]
        b_ref[...] = down_ref[...]

    @pl.when(jnp.logical_not(row_asc))
    def _():
        a_ref[...] = down_ref[...]
        b_ref[...] = up_ref[...]

    lane = lax.broadcasted_iota(jnp.int32, (height, 128), 1)
    east = jnp.zeros((height, 128), jnp.float32)
    west = jnp.zeros((height, 128), jnp.float32)
    for q in range(HALF + 2):
        mine = lane // 2 == q
        if q < HALF:
            p_e = q if q < QUAD else q + HALF
            p_w = q + QUAD
            edge_e, edge_w = x_ref[p_e, :, breadth - 128 :], x_ref[p_w, :, :128]
        else:
            field = moving if q == HALF else sea
            edge_e, edge_w = field[:, breadth - 128 :], field[:, :128]
        east = jnp.where(mine, pltpu.roll(edge_e, (2 * q + 2) % 128, axis=1), east)
        west = jnp.where(mine, pltpu.roll(edge_w, 2 * q, axis=1), west)
    c_ref[...] = east
    d_ref[...] = west
    up_right, up_left = east[height - 8 :], west[height - 8 :]
    down_right, down_left = east[:8], west[:8]
    xa_ref[...] = jnp.where(right_asc, up_right, down_left)
    xb_ref[...] = jnp.where(right_asc, down_left, up_right)
    ya_ref[...] = jnp.where(left_asc, up_left, down_right)
    yb_ref[...] = jnp.where(left_asc, down_right, up_left)


def wave_kernel(n_lat, n_lon, slots, courant_ref, cos_ref, sin_ref, cells_ref, x_ref, mov_ref, sea_ref, kernel_ref,
                a_ref, b_ref, c_ref, d_ref, xa_ref, xb_ref, ya_ref, yb_ref, own_c_ref, own_d_ref,
                lanes_ref, subs_ref, out_ref, picked_ref,
                south0, south1, north0, north1, west0, west1, east0, east1, halves, table, owner_rows, wide_kernel):
    height, breadth = mov_ref.shape
    row_asc, right_asc, left_asc, at_top, right_self, left_self = rising_flags(n_lat, n_lon)
    c0, c1 = courant_ref[0], courant_ref[1]

    xa, xb, ya, yb = xa_ref[...], xb_ref[...], ya_ref[...], yb_ref[...]
    sw = jnp.where(right_asc, xa, xb)[7:8]
    se = jnp.where(left_asc, ya, yb)[7:8]
    ne_in = jnp.where(right_asc, xb, xa)
    nw_in = jnp.where(left_asc, yb, ya)
    ne_fold = jnp.where(right_self, own_c_ref[height - 1 :, :], ne_in[7:8])
    nw_fold = jnp.where(left_self, own_d_ref[height - 1 :, :], nw_in[7:8])
    near_c, near_d = 2 * HALF + 1, 2 * HALF

    def with_moving(row, lane_of):
        return row * row[:, lane_of : lane_of + 1]

    sw = with_moving(sw, near_c)
    se = with_moving(se, near_d)
    ne = jnp.where(at_top, pltpu.roll(with_moving(ne_fold, near_c), HALF - 1, axis=1), with_moving(ne_in[0:1], near_d))
    nw = jnp.where(at_top, pltpu.roll(with_moving(nw_fold, near_d), HALF + 1, axis=1), with_moving(nw_in[0:1], near_c))

    lane = lax.broadcasted_iota(jnp.int32, (height, 128), 1)
    row = lax.broadcasted_iota(jnp.int32, (height, 128), 0)
    odd = lane % 2 == 1

    def columns(ref, near, far, southern, northern, cx, cy, sign, flux0, flux1):
        e0 = ref[...]
        mov = jnp.where(odd, e0[:, 2 * HALF + 1 : 2 * HALF + 2], e0[:, 2 * HALF : 2 * HALF + 1])
        sea = e0[:, 2 * HALF + 2 + near : 2 * HALF + 3 + near]
        f0 = mov * e0
        f_far = pltpu.roll(f0, 1 if near > far else 127, axis=1)
        f_south = jnp.where(row == 0, southern, pltpu.roll(f0, 1, axis=0))
        f_north = jnp.where(row == height - 1, northern, pltpu.roll(f0, height - 1, axis=0))
        div_x = cx * (f0 - f_far) if sign > 0 else cx * (f_far - f0)
        div_y = jnp.where(lane < HALF, cy * (f0 - f_south), cy * (f_north - f0))
        flux0[...] = f0
        flux1[...] = mov * (sea * ((e0 - div_x) - div_y))

    lanes = lanes_ref[...]
    lane_courant = jnp.where(lanes[4:5] > 0.5, c1, c0)
    columns(c_ref, 1, 0, sw, nw, lanes[0:1] * lane_courant, lanes[1:2] * lane_courant, 1, west0, west1)
    columns(d_ref, 0, 1, se, ne, lanes[2:3] * lane_courant, lanes[3:4] * lane_courant, -1, east0, east1)

    wide = lax.broadcasted_iota(jnp.int32, (HALF + 4, breadth), 1)
    plane = lax.broadcasted_iota(jnp.int32, (HALF + 4, 1), 0)
    plane_l = lax.broadcasted_iota(jnp.int32, (HALF + 4, 128), 0)
    lane_l = lax.broadcasted_iota(jnp.int32, (HALF + 4, 128), 1)
    subs = subs_ref[...]
    sub_courant = jnp.where(plane % 2 == 1, c1, c0)

    def to_sublanes(corner, lane_of):
        return jnp.sum(jnp.where(lane_l == lane_of, corner, 0.0), axis=1, keepdims=True)

    def rows(near, far, first_west, west_corner, east_corner, cx, cy, sign, flux0, flux1):
        mov, sea = near[HALF : HALF + 1], near[HALF + 1 : HALF + 2]
        f0 = mov * near
        f_far = far[HALF : HALF + 1] * far
        f_west = jnp.where(wide == 0, west_corner, pltpu.roll(f0, 1, axis=1))
        f_east = jnp.where(wide == breadth - 1, east_corner, pltpu.roll(f0, breadth - 1, axis=1))
        from_west = (plane < QUAD) if first_west else (plane >= QUAD)
        div_x = jnp.where(from_west, cx * (f0 - f_west), cx * (f_east - f0))
        div_y = cy * (f0 - f_far) if sign > 0 else cy * (f_far - f0)
        flux0[...] = f0
        flux1[...] = mov * (sea * ((near - div_x) - div_y))

    south = jnp.where(row_asc, a_ref[...], b_ref[...])
    north0[...] = jnp.where(row_asc, b_ref[0], a_ref[0])
    north1[...] = jnp.where(row_asc, b_ref[1], a_ref[1])

    @pl.when(at_top)
    def _():
        flip_i = lax.broadcasted_iota(jnp.int32, (breadth, breadth), 0)
        flip_j = lax.broadcasted_iota(jnp.int32, (breadth, breadth), 1)
        flip = (flip_i + flip_j == breadth - 1).astype(jnp.float32)
        for ref in (north0, north1):
            ref[...] = jnp.dot(ref[...], flip, precision=lax.Precision.HIGHEST, preferred_element_type=jnp.float32)

    sw_s = to_sublanes(sw, 2 * plane_l + 1)
    se_s = to_sublanes(se, 2 * plane_l - HALF)
    ne_s = to_sublanes(ne, 2 * plane_l + HALF)
    nw_s = to_sublanes(nw, 2 * plane_l + 1)
    rows(south[0], south[1], True, sw_s, se_s, subs[:, 0:1] * sub_courant, subs[:, 1:2] * sub_courant, 1, south0, south1)
    rows(north0[...], north1[...], False, nw_s, ne_s, subs[:, 2:3] * sub_courant, subs[:, 3:4] * sub_courant, -1,
         north0, north1)

    moving = mov_ref[...]
    sea_all = sea_ref[...]
    lane_edge = lax.broadcasted_iota(jnp.int32, (height, 128), 1)
    row_edge = lax.broadcasted_iota(jnp.int32, (8, breadth), 0)

    def quadrant(first, from_west, from_south, column0, column1, lane_first, row0, row1, row_first):
        def upstream(flux, column, line):
            if from_west:
                moved = pltpu.roll(flux, 1, axis=1)
                side = jnp.concatenate([jnp.where(lane_edge == 0, column, moved[:, :128]), moved[:, 128:]], axis=1)
            else:
                moved = pltpu.roll(flux, breadth - 1, axis=1)
                edge = jnp.where(lane_edge == 127, column, moved[:, breadth - 128 :])
                side = jnp.concatenate([moved[:, : breadth - 128], edge], axis=1)
            if from_south:
                moved = pltpu.roll(flux, 1, axis=0)
                below = jnp.concatenate([jnp.where(row_edge == 0, line, moved[:8]), moved[8:]], axis=0)
            else:
                moved = pltpu.roll(flux, height - 1, axis=0)
                edge = jnp.where(row_edge == 7, line, moved[height - 8 :])
                below = jnp.concatenate([moved[: height - 8], edge], axis=0)
            return side, below

        def step(t, carry):
            p = first + t
            courant = jnp.where(p % 2 == 1, c1, c0)
            cx = cos_ref[p] * courant
            cy = sin_ref[p] * courant
            place = lane_first + 2 * t
            turn = (128 - place) if from_west else (127 - place)
            energy = x_ref[p]
            for column_ref, row_ref in ((column0, row0), (column1, row1)):
                flux = moving * energy
                column = pltpu.roll(column_ref[...], turn, axis=1)
                side, below = upstream(flux, column, row_ref[pl.ds(row_first + t, 1), :])
                div_x = cx * (flux - side) if from_west else cx * (side - flux)
                div_y = cy * (flux - below) if from_south else cy * (below - flux)
                energy = sea_all * ((energy - div_x) - div_y)
            out_ref[p] = energy
            start = pl.ds(pl.multiple_of(p * height, height), height)
            for h in range(breadth // 128):
                halves[h, start, :] = energy[:, h * 128 : (h + 1) * 128]
            return carry

        lax.fori_loop(0, QUAD, step, 0)

    quadrant(0, True, True, west0, west1, 1, south0, south1, 0)
    quadrant(QUAD, False, True, east0, east1, 0, south0, south1, QUAD)
    quadrant(2 * QUAD, False, False, east0, east1, HALF, north0, north1, 0)
    quadrant(3 * QUAD, True, False, west0, west1, HALF + 1, north0, north1, QUAD)

    pad = jnp.zeros((8, 128), jnp.bfloat16)
    wide_kernel[...] = jnp.zeros((128, 128), jnp.float32)
    wide_kernel[:64, :PLANES] = kernel_ref[...]
    wide_kernel[64:, :PLANES] = kernel_ref[...]
    turned = wide_kernel[...].T[:PLANES]
    weight_high = turned.astype(jnp.bfloat16)
    weight_low = (turned - weight_high.astype(jnp.float32)).astype(jnp.bfloat16)
    weight = jnp.concatenate([weight_high, pad, weight_high, pad, weight_low, pad], axis=0)

    @pl.loop(0, height)
    def _(r):
        for h in range(breadth // 128):
            spectra = halves[h, pl.ds(r, PLANES, stride=height), :]
            high = spectra.astype(jnp.bfloat16)
            low = (spectra - high.astype(jnp.float32)).astype(jnp.bfloat16)
            stacked = jnp.concatenate([high, pad, low, pad, high, pad], axis=0)
            profile = lax.dot_general(stacked, weight, (((0,), (0,)), ((), ())), preferred_element_type=jnp.float32)
            start = pl.multiple_of(r * breadth + h * 128, 128)
            table[pl.ds(start, 128), :] = profile.astype(jnp.bfloat16).astype(jnp.float32)

    first_half = lax.broadcasted_iota(jnp.int32, (1, 128), 1) < 64

    @pl.loop(0, picked_ref.shape[0])
    def _(owner):
        for g in range(slots // 16):
            for j in range(8):
                one = cells_ref[owner * slots + g * 16 + j]
                two = cells_ref[owner * slots + g * 16 + 8 + j]
                line = jnp.where(first_half, table[pl.ds(one, 1), :], table[pl.ds(two, 1), :])
                owner_rows[g * 8 + j : g * 8 + j + 1, :] = line
        picked_ref[owner] = owner_rows[...].astype(jnp.bfloat16)


def add_kernel(slots, rows_ref, values_ref, out_ref, lines, *sums):
    n_acc = len(sums) // 2
    tile = out_ref.shape[1]
    block = 512
    for total in sums:

        @pl.loop(0, tile // block)
        def _(i):
            total[pl.ds(pl.multiple_of(i * block, block), block), :] = jnp.zeros((block, 128), jnp.float32)

    @pl.loop(0, values_ref.shape[0])
    def _(source):
        lines[...] = values_ref[source].astype(jnp.float32)
        for g in range(slots // 16):
            for j in range(8):
                one = rows_ref[source * slots + g * 16 + j]
                two = rows_ref[source * slots + g * 16 + 8 + j]
                line = lines[g * 8 + j : g * 8 + j + 1, :]
                left, right = sums[j % n_acc], sums[n_acc + j % n_acc]
                left[pl.ds(one, 1), :] = left[pl.ds(one, 1), :] + line
                right[pl.ds(two, 1), :] = right[pl.ds(two, 1), :] + line

    first_half = lax.broadcasted_iota(jnp.int32, (block, 128), 1) < 64

    @pl.loop(0, tile // block)
    def _(i):
        here = pl.ds(pl.multiple_of(i * block, block), block)
        left, right = sums[0][here, :], sums[n_acc][here, :]
        for q in range(1, n_acc):
            left = left + sums[q][here, :]
            right = right + sums[n_acc + q][here, :]
        both = jnp.where(first_half, left, right).T
        out_ref[:, here] = both[:64] + both[64:]


def constant_tables():
    heading = (np.arange(DIRS) + 0.5) * (2.0 * math.pi / DIRS)
    cos = np.repeat(np.cos(heading), FREQ)
    sin = np.repeat(np.sin(heading), FREQ)
    lanes = np.zeros((8, 128))
    q = np.arange(HALF)
    from_west = np.where(q < QUAD, q, q + HALF)
    from_east = q + QUAD
    for column in range(2):
        lanes[0, 2 * q + column] = cos[from_west]
        lanes[1, 2 * q + column] = sin[from_west]
        lanes[2, 2 * q + column] = cos[from_east]
        lanes[3, 2 * q + column] = sin[from_east]
        lanes[4, 2 * q + column] = q % 2
    subs = np.zeros((HALF + 4, 128))
    subs[:HALF, 0], subs[:HALF, 1] = cos[:HALF], sin[:HALF]
    subs[:HALF, 2], subs[:HALF, 3] = cos[HALF:], sin[HALF:]
    return [t.astype(np.float32) for t in (cos, sin, lanes, subs)]


def body(n_lat, n_lon, spectrum, speed_factor, land_sea_mask, courant, depth_kernel, send_rows, recv_rows):
    height, breadth = speed_factor.shape
    devices, slots = send_rows.shape[1:]
    x = spectrum.reshape(PLANES, height, breadth)
    f32 = jnp.float32
    vmem = pl.BlockSpec(memory_space=pltpu.VMEM)
    smem = pl.BlockSpec(memory_space=pltpu.SMEM)
    params = pltpu.CompilerParams(vmem_limit_bytes=VMEM_LIMIT)

    def shape(*dims, kind=f32):
        return jax.ShapeDtypeStruct(dims, kind)

    row_message = shape(2, HALF + 4, breadth)
    column_message = shape(height, 128)
    corner_message = shape(8, 128)
    a, b, c, d, xa, xb, ya, yb, moving, sea = pl.pallas_call(
        functools.partial(pack_kernel, n_lat, n_lon),
        out_shape=[row_message] * 2 + [column_message] * 2 + [corner_message] * 4 + [shape(height, breadth)] * 2,
        in_specs=[vmem] * 3,
        out_specs=[vmem] * 10,
        scratch_shapes=[pltpu.VMEM((2, HALF + 4, breadth), f32)] * 2,
        compiler_params=params,
        name="pack_halos",
    )(x, speed_factor, land_sea_mask)

    both = ("lat", "lon")
    row_perms, right_perms, left_perms = chain_perms(n_lat, n_lon)
    east = [(i, (i + 1) % n_lon) for i in range(n_lon)]
    west = [(j, i) for i, j in east]
    got = [lax.ppermute(m, both, perm) for m, perm in zip((a, b), row_perms)]
    got += [lax.ppermute(c, "lon", east), lax.ppermute(d, "lon", west)]
    got += [lax.ppermute(m, both, perm) for m, perm in zip((xa, xb, ya, yb), right_perms + left_perms)]

    cos, sin, lanes, subs = constant_tables()
    cells = jnp.maximum(send_rows, 0).reshape(-1)
    targets = jnp.where(recv_rows < 0, OUT_DEV, recv_rows).reshape(-1)
    propagated, picked = pl.pallas_call(
        functools.partial(wave_kernel, n_lat, n_lon, slots),
        out_shape=[shape(PLANES, height, breadth), shape(devices, slots // 2, 128, kind=jnp.bfloat16)],
        in_specs=[smem] * 4 + [vmem] * 16,
        out_specs=[vmem] * 2,
        scratch_shapes=[pltpu.VMEM((HALF + 4, breadth), f32)] * 4
        + [pltpu.VMEM((height, 128), f32)] * 4
        + [
            pltpu.VMEM((breadth // 128, PLANES * height, 128), f32),
            pltpu.VMEM((height * breadth, 128), f32),
            pltpu.VMEM((slots // 2, 128), f32),
            pltpu.VMEM((128, 128), f32),
        ],
        compiler_params=params,
        name="propagate_and_pick",
    )(courant, cos, sin, cells, x, moving, sea, depth_kernel, *got, c, d, lanes, subs)

    received = lax.all_to_all(picked, both, split_axis=0, concat_axis=0, tiled=True)

    stokes = pl.pallas_call(
        functools.partial(add_kernel, slots),
        out_shape=shape(depth_kernel.shape[0], OUT_DEV),
        in_specs=[smem, vmem],
        out_specs=vmem,
        scratch_shapes=[pltpu.VMEM((slots // 2, 128), f32)] + [pltpu.VMEM((OUT_DEV + 8, 128), f32)] * (2 * N_ACC),
        compiler_params=params,
        name="add_profiles",
    )(targets, received)
    return propagated.reshape(DIRS, FREQ, height, breadth), stokes


def solution(mesh):
    placed = (
        P(None, None, "lat", "lon"),
        P("lat", "lon"),
        P("lat", "lon"),
        P(),
        P(),
        P(("lat", "lon"), None, None),
        P(("lat", "lon"), None, None),
    )
    return jax.shard_map(
        functools.partial(body, mesh.shape["lat"], mesh.shape["lon"]),
        mesh=mesh,
        in_specs=placed,
        out_specs=(P(None, None, "lat", "lon"), P(None, ("lat", "lon"))),
        check_vma=False,
    )
```

```python
import functools
import math

import jax
import jax.numpy as jnp
import numpy as np
from jax import lax
from jax.experimental import pallas as pl
from jax.experimental.pallas import tpu as pltpu
from jax.sharding import PartitionSpec as P

DIRS = 36
FREQ = 2
PLANES = DIRS * FREQ
HALF = PLANES // 2
QUAD = PLANES // 4
OUT_DEV = 4096
N_ACC = 4
VMEM_LIMIT = 48 * 1024 * 1024


def exchange_pairs(n_lat, n_lon):
    def flat(j, i):
        return j * n_lon + i % n_lon

    row_first = [(j, j ^ 1) for j in range(n_lat)]
    row_second = []
    for i in range(n_lon):
        row_second += [(flat(0, i), flat(0, i)), (flat(n_lat - 1, i), flat(n_lat - 1, n_lon - 1 - i))]
        for j in range(1, n_lat - 1, 2):
            row_second += [(flat(j, i), flat(j + 1, i)), (flat(j + 1, i), flat(j, i))]
    column_first = [(i, i ^ 1) for i in range(n_lon)]
    column_second = [(i, (i + 1 if i % 2 else i - 1) % n_lon) for i in range(n_lon)]
    return row_first, row_second, column_first, column_second


def pack_kernel(x_ref, speed_ref, mask_ref, first_ref, second_ref, east_ref, west_ref, mov_ref, sea_ref, up_ref, down_ref):
    height, breadth = speed_ref.shape
    even = lax.axis_index("lat") % 2 == 0
    sea = mask_ref[...].astype(jnp.float32)
    moving = speed_ref[...] * sea
    mov_ref[...] = moving
    sea_ref[...] = sea
    for k in range(2):
        for q in range(HALF):
            up_ref[k, q : q + 1, :] = x_ref[q, height - 1 - k : height - k, :]
            down_ref[k, q : q + 1, :] = x_ref[HALF + q, k : k + 1, :]
        up_ref[k, HALF : HALF + 1, :] = moving[height - 1 - k : height - k, :]
        down_ref[k, HALF : HALF + 1, :] = moving[k : k + 1, :]
        up_ref[k, HALF + 1 : HALF + 2, :] = sea[height - 1 - k : height - k, :]
        down_ref[k, HALF + 1 : HALF + 2, :] = sea[k : k + 1, :]
        up_ref[k, HALF + 2 :, :] = jnp.zeros((2, breadth), jnp.float32)
        down_ref[k, HALF + 2 :, :] = jnp.zeros((2, breadth), jnp.float32)

    @pl.when(even)
    def _():
        first_ref[...] = up_ref[...]
        second_ref[...] = down_ref[...]

    @pl.when(jnp.logical_not(even))
    def _():
        first_ref[...] = down_ref[...]
        second_ref[...] = up_ref[...]

    lane = lax.broadcasted_iota(jnp.int32, (height, 128), 1)
    east = jnp.zeros((height, 128), jnp.float32)
    west = jnp.zeros((height, 128), jnp.float32)
    for q in range(HALF + 2):
        mine = lane // 2 == q
        if q < HALF:
            p_e = q if q < QUAD else q + HALF
            p_w = q + QUAD
            edge_e, edge_w = x_ref[p_e, :, breadth - 128 :], x_ref[p_w, :, :128]
        else:
            field = moving if q == HALF else sea
            edge_e, edge_w = field[:, breadth - 128 :], field[:, :128]
        east = jnp.where(mine, pltpu.roll(edge_e, (2 * q + 2) % 128, axis=1), east)
        west = jnp.where(mine, pltpu.roll(edge_w, 2 * q, axis=1), west)
    east_ref[...] = east
    west_ref[...] = west


def corner_kernel(n_lat, first_ref, second_ref, east_ref, west_ref, south_ref, north_ref, out_first, out_second):
    height = east_ref.shape[0]
    breadth = first_ref.shape[2]
    lat = lax.axis_index("lat")
    even = lat % 2 == 0

    @pl.when(even)
    def _():
        north_ref[...] = first_ref[...]
        south_ref[...] = second_ref[...]

    @pl.when(jnp.logical_not(even))
    def _():
        south_ref[...] = first_ref[...]
        north_ref[...] = second_ref[...]

    @pl.when(lat == 0)
    def _():
        south_ref[...] = jnp.zeros_like(south_ref)

    @pl.when(lat == n_lat - 1)
    def _():
        flip_i = lax.broadcasted_iota(jnp.int32, (breadth, breadth), 0)
        flip_j = lax.broadcasted_iota(jnp.int32, (breadth, breadth), 1)
        flip = (flip_i + flip_j == breadth - 1).astype(jnp.float32)
        for k in range(2):
            north_ref[k] = jnp.dot(
                north_ref[k], flip, precision=lax.Precision.HIGHEST, preferred_element_type=jnp.float32
            )

    plane = lax.broadcasted_iota(jnp.int32, (HALF + 4, 128), 0)
    lane = lax.broadcasted_iota(jnp.int32, (HALF + 4, 128), 1)
    south = south_ref[0] * south_ref[0, HALF : HALF + 1, :]
    north = north_ref[0] * north_ref[0, HALF : HALF + 1, :]

    def to_lanes(column, low, high, place):
        mine = (plane >= low) & (plane < high) & (lane == place)
        return jnp.where(mine, column, 0.0)

    east_edge = to_lanes(south[:, breadth - 1 :], 0, QUAD, 2 * plane + 1)
    east_edge += to_lanes(north[:, breadth - 1 :], QUAD, HALF, 2 * plane + 1)
    west_edge = to_lanes(south[:, :1], QUAD, HALF, 2 * plane - HALF)
    west_edge += to_lanes(north[:, :1], 0, QUAD, 2 * plane + HALF)
    east_edge = jnp.broadcast_to(jnp.sum(east_edge, axis=0, keepdims=True), (8, 128))
    west_edge = jnp.broadcast_to(jnp.sum(west_edge, axis=0, keepdims=True), (8, 128))
    even_lon = lax.axis_index("lon") % 2 == 0
    out_first[:height] = jnp.where(even_lon, east_ref[...], west_ref[...])
    out_second[:height] = jnp.where(even_lon, west_ref[...], east_ref[...])
    out_first[height:] = jnp.where(even_lon, east_edge, west_edge)
    out_second[height:] = jnp.where(even_lon, west_edge, east_edge)


def wave_kernel(slots, courant_ref, cos_ref, sin_ref, cells_ref, x_ref, mov_ref, sea_ref, kernel_ref,
                south_ref, north_ref, first_ref, second_ref, lanes_ref, subs_ref, out_ref, picked_ref,
                south0, south1, north0, north1, west0, west1, east0, east1, halves, table, owner_rows, wide_kernel,
                out_sems):
    height, breadth = mov_ref.shape
    c0, c1 = courant_ref[0], courant_ref[1]
    even_lon = lax.axis_index("lon") % 2 == 0
    from_west = jnp.where(even_lon, second_ref[...], first_ref[...])
    from_east = jnp.where(even_lon, first_ref[...], second_ref[...])
    corner_w, corner_e = from_west[height : height + 1], from_east[height : height + 1]

    lane = lax.broadcasted_iota(jnp.int32, (height, 128), 1)
    row = lax.broadcasted_iota(jnp.int32, (height, 128), 0)
    odd = lane % 2 == 1

    def columns(e0, near, far, corner, cx, cy, sign, flux0, flux1):
        mov = jnp.where(odd, e0[:, 2 * HALF + 1 : 2 * HALF + 2], e0[:, 2 * HALF : 2 * HALF + 1])
        sea = e0[:, 2 * HALF + 2 + near : 2 * HALF + 3 + near]
        f0 = mov * e0
        f_far = pltpu.roll(f0, 1 if near > far else 127, axis=1)
        f_south = jnp.where(row == 0, corner, pltpu.roll(f0, 1, axis=0))
        f_north = jnp.where(row == height - 1, corner, pltpu.roll(f0, height - 1, axis=0))
        div_x = cx * (f0 - f_far) if sign > 0 else cx * (f_far - f0)
        div_y = jnp.where(lane < HALF, cy * (f0 - f_south), cy * (f_north - f0))
        flux0[...] = f0
        flux1[...] = mov * (sea * ((e0 - div_x) - div_y))

    lanes = lanes_ref[...]
    lane_courant = jnp.where(lanes[4:5] > 0.5, c1, c0)
    columns(from_west[:height], 1, 0, corner_w, lanes[0:1] * lane_courant, lanes[1:2] * lane_courant, 1, west0, west1)
    columns(from_east[:height], 0, 1, corner_e, lanes[2:3] * lane_courant, lanes[3:4] * lane_courant, -1, east0, east1)

    wide = lax.broadcasted_iota(jnp.int32, (HALF + 4, breadth), 1)
    plane = lax.broadcasted_iota(jnp.int32, (HALF + 4, 1), 0)
    plane_l = lax.broadcasted_iota(jnp.int32, (HALF + 4, 128), 0)
    lane_l = lax.broadcasted_iota(jnp.int32, (HALF + 4, 128), 1)
    subs = subs_ref[...]
    sub_courant = jnp.where(plane % 2 == 1, c1, c0)

    def to_sublanes(corner, lane_of):
        return jnp.sum(jnp.where(lane_l == lane_of, corner, 0.0), axis=1, keepdims=True)

    def rows(near, far, first_west, west_corner, east_corner, cx, cy, sign, flux0, flux1):
        mov, sea = near[HALF : HALF + 1], near[HALF + 1 : HALF + 2]
        f0 = mov * near
        f_far = far[HALF : HALF + 1] * far
        f_west = jnp.where(wide == 0, west_corner, pltpu.roll(f0, 1, axis=1))
        f_east = jnp.where(wide == breadth - 1, east_corner, pltpu.roll(f0, breadth - 1, axis=1))
        from_west = (plane < QUAD) if first_west else (plane >= QUAD)
        div_x = jnp.where(from_west, cx * (f0 - f_west), cx * (f_east - f0))
        div_y = cy * (f0 - f_far) if sign > 0 else cy * (f_far - f0)
        flux0[...] = f0
        flux1[...] = mov * (sea * ((near - div_x) - div_y))

    sw = to_sublanes(corner_w, 2 * plane_l + 1)
    se = to_sublanes(corner_e, 2 * plane_l - HALF)
    ne = to_sublanes(corner_e, 2 * plane_l + HALF)
    nw = sw
    rows(south_ref[0], south_ref[1], True, sw, se, subs[:, 0:1] * sub_courant, subs[:, 1:2] * sub_courant, 1,
         south0, south1)
    rows(north_ref[0], north_ref[1], False, nw, ne, subs[:, 2:3] * sub_courant, subs[:, 3:4] * sub_courant, -1,
         north0, north1)

    moving = mov_ref[...]
    sea_all = sea_ref[...]
    lane_edge = lax.broadcasted_iota(jnp.int32, (height, 128), 1)
    row_edge = lax.broadcasted_iota(jnp.int32, (8, breadth), 0)

    def write_out(planes, h):
        target = out_ref.at[planes, pl.ds(h * 128, 128)]
        return pltpu.make_async_copy(halves.at[h, planes, :], target, out_sems.at[h])

    def quadrant(first, from_west, from_south, column0, column1, lane_first, row0, row1, row_first):
        def upstream(flux, column, line):
            if from_west:
                moved = pltpu.roll(flux, 1, axis=1)
                side = jnp.concatenate([jnp.where(lane_edge == 0, column, moved[:, :128]), moved[:, 128:]], axis=1)
            else:
                moved = pltpu.roll(flux, breadth - 1, axis=1)
                edge = jnp.where(lane_edge == 127, column, moved[:, breadth - 128 :])
                side = jnp.concatenate([moved[:, : breadth - 128], edge], axis=1)
            if from_south:
                moved = pltpu.roll(flux, 1, axis=0)
                below = jnp.concatenate([jnp.where(row_edge == 0, line, moved[:8]), moved[8:]], axis=0)
            else:
                moved = pltpu.roll(flux, height - 1, axis=0)
                edge = jnp.where(row_edge == 7, line, moved[height - 8 :])
                below = jnp.concatenate([moved[: height - 8], edge], axis=0)
            return side, below

        def step(t, carry):
            p = first + t
            courant = jnp.where(p % 2 == 1, c1, c0)
            cx = cos_ref[p] * courant
            cy = sin_ref[p] * courant
            place = lane_first + 2 * t
            turn = (128 - place) if from_west else (127 - place)
            energy = x_ref[p]
            for column_ref, row_ref in ((column0, row0), (column1, row1)):
                flux = moving * energy
                column = pltpu.roll(column_ref[...], turn, axis=1)
                side, below = upstream(flux, column, row_ref[pl.ds(row_first + t, 1), :])
                div_x = cx * (flux - side) if from_west else cx * (side - flux)
                div_y = cy * (flux - below) if from_south else cy * (below - flux)
                energy = sea_all * ((energy - div_x) - div_y)
            start = pl.ds(pl.multiple_of(p * height, height), height)
            for h in range(breadth // 128):
                halves[h, start, :] = energy[:, h * 128 : (h + 1) * 128]
            return carry

        lax.fori_loop(0, QUAD, step, 0, unroll=6)
        planes = pl.ds(first * height, QUAD * height)
        for h in range(breadth // 128):
            write_out(planes, h).start()

    quadrant(0, True, True, west0, west1, 1, south0, south1, 0)
    quadrant(QUAD, False, True, east0, east1, 0, south0, south1, QUAD)
    quadrant(2 * QUAD, False, False, east0, east1, HALF, north0, north1, 0)
    quadrant(3 * QUAD, True, False, west0, west1, HALF + 1, north0, north1, QUAD)

    pad = jnp.zeros((8, 128), jnp.bfloat16)
    wide_kernel[...] = jnp.zeros((128, 128), jnp.float32)
    wide_kernel[:64, :PLANES] = kernel_ref[...]
    wide_kernel[64:, :PLANES] = kernel_ref[...]
    turned = wide_kernel[...].T[:PLANES]
    weight_high = turned.astype(jnp.bfloat16)
    weight_low = (turned - weight_high.astype(jnp.float32)).astype(jnp.bfloat16)
    weight = jnp.concatenate([weight_high, pad, weight_high, pad, weight_low, pad], axis=0)

    group = 8

    @pl.loop(0, height // group)
    def _(r):
        blocks = []
        for k in range(group):
            for h in range(breadth // 128):
                spectra = halves[h, pl.ds(r * group + k, PLANES, stride=height), :]
                high = spectra.astype(jnp.bfloat16)
                low = (spectra - high.astype(jnp.float32)).astype(jnp.bfloat16)
                blocks.append(jnp.concatenate([high, pad, low, pad, high, pad], axis=0))
        stacked = jnp.concatenate(blocks, axis=1)
        profile = lax.dot_general(stacked, weight, (((0,), (0,)), ((), ())), preferred_element_type=jnp.float32)
        start = pl.multiple_of(r * group * breadth, 128)
        table[pl.ds(start, group * breadth), :] = profile

    first_half = lax.broadcasted_iota(jnp.int32, (1, 128), 1) < 64
    cell_count = height * breadth
    table[cell_count:, :] = jnp.zeros((8, 128), jnp.float32)
    owner_rows[...] = jnp.zeros_like(owner_rows)

    @pl.loop(0, picked_ref.shape[0])
    def _(owner):
        base = owner * slots
        for s in range(0, slots, 32):

            @pl.when(cells_ref[base + s] < cell_count)
            def _():
                for g in range(s, s + 32, 16):
                    for j in range(8):
                        one, two = cells_ref[base + g + j], cells_ref[base + g + 8 + j]
                        line = jnp.where(first_half, table[pl.ds(one, 1), :], table[pl.ds(two, 1), :])
                        owner_rows[g // 2 + j : g // 2 + j + 1, :] = line

        picked_ref[owner] = owner_rows[...].astype(jnp.bfloat16)

    whole = pl.ds(0, PLANES * height)
    for h in range(breadth // 128):
        write_out(whole, h).wait()


def add_kernel(slots, rows_ref, values_ref, out_ref, lines, *sums):
    n_acc = len(sums) // 2
    tile = out_ref.shape[1]
    block = 512
    for total in sums:

        @pl.loop(0, tile // block)
        def _(i):
            total[pl.ds(pl.multiple_of(i * block, block), block), :] = jnp.zeros((block, 128), jnp.float32)

    @pl.loop(0, values_ref.shape[0])
    def _(source):
        lines[...] = values_ref[source].astype(jnp.float32)
        for g in range(slots // 16):
            for j in range(8):
                one = rows_ref[source * slots + g * 16 + j]
                two = rows_ref[source * slots + g * 16 + 8 + j]
                line = lines[g * 8 + j : g * 8 + j + 1, :]
                left, right = sums[j % n_acc], sums[n_acc + j % n_acc]
                left[pl.ds(one, 1), :] = left[pl.ds(one, 1), :] + line
                right[pl.ds(two, 1), :] = right[pl.ds(two, 1), :] + line

    first_half = lax.broadcasted_iota(jnp.int32, (block, 128), 1) < 64

    @pl.loop(0, tile // block)
    def _(i):
        here = pl.ds(pl.multiple_of(i * block, block), block)
        left, right = sums[0][here, :], sums[n_acc][here, :]
        for q in range(1, n_acc):
            left = left + sums[q][here, :]
            right = right + sums[n_acc + q][here, :]
        both = jnp.where(first_half, left, right).T
        out_ref[:, here] = both[:64] + both[64:]


def constant_tables():
    heading = (np.arange(DIRS) + 0.5) * (2.0 * math.pi / DIRS)
    cos = np.repeat(np.cos(heading), FREQ)
    sin = np.repeat(np.sin(heading), FREQ)
    lanes = np.zeros((8, 128))
    q = np.arange(HALF)
    from_west = np.where(q < QUAD, q, q + HALF)
    from_east = q + QUAD
    for column in range(2):
        lanes[0, 2 * q + column] = cos[from_west]
        lanes[1, 2 * q + column] = sin[from_west]
        lanes[2, 2 * q + column] = cos[from_east]
        lanes[3, 2 * q + column] = sin[from_east]
        lanes[4, 2 * q + column] = q % 2
    subs = np.zeros((HALF + 4, 128))
    subs[:HALF, 0], subs[:HALF, 1] = cos[:HALF], sin[:HALF]
    subs[:HALF, 2], subs[:HALF, 3] = cos[HALF:], sin[HALF:]
    return [t.astype(np.float32) for t in (cos, sin, lanes, subs)]


def body(n_lat, n_lon, spectrum, speed_factor, land_sea_mask, courant, depth_kernel, send_rows, recv_rows):
    height, breadth = speed_factor.shape
    devices, slots = send_rows.shape[1:]
    x = spectrum.reshape(PLANES, height, breadth)
    f32 = jnp.float32
    vmem = pl.BlockSpec(memory_space=pltpu.VMEM)
    smem = pl.BlockSpec(memory_space=pltpu.SMEM)
    params = pltpu.CompilerParams(vmem_limit_bytes=VMEM_LIMIT)

    both = ("lat", "lon")

    def shape(*dims, kind=f32):
        return jax.ShapeDtypeStruct(dims, kind)

    row_message = shape(2, HALF + 4, breadth)
    columns = shape(height, 128)
    column_message = shape(height + 8, 128)
    row_first, row_second, column_first, column_second = exchange_pairs(n_lat, n_lon)
    first, second, east, west, moving, sea = pl.pallas_call(
        pack_kernel,
        out_shape=[row_message] * 2 + [columns] * 2 + [shape(height, breadth)] * 2,
        in_specs=[vmem] * 3,
        out_specs=[vmem] * 6,
        scratch_shapes=[pltpu.VMEM((2, HALF + 4, breadth), f32)] * 2,
        compiler_params=params,
        name="pack_halos",
    )(x, speed_factor, land_sea_mask)
    first = lax.ppermute(first, "lat", row_first)
    second = lax.ppermute(second, both, row_second)
    south, north, first, second = pl.pallas_call(
        functools.partial(corner_kernel, n_lat),
        out_shape=[row_message] * 2 + [column_message] * 2,
        in_specs=[vmem] * 4,
        out_specs=[vmem] * 4,
        compiler_params=params,
        name="add_corners",
    )(first, second, east, west)
    first = lax.ppermute(first, "lon", column_first)
    second = lax.ppermute(second, "lon", column_second)

    cos, sin, lanes, subs = constant_tables()
    cells = jnp.where(send_rows < 0, height * breadth, send_rows).reshape(-1)
    targets = jnp.where(recv_rows < 0, OUT_DEV, recv_rows).reshape(-1)
    propagated, picked = pl.pallas_call(
        functools.partial(wave_kernel, slots),
        out_shape=[shape(PLANES * height, breadth), shape(devices, slots // 2, 128, kind=jnp.bfloat16)],
        in_specs=[smem] * 4 + [vmem] * 10,
        out_specs=[pl.BlockSpec(memory_space=pl.ANY), vmem],
        scratch_shapes=[pltpu.VMEM((HALF + 4, breadth), f32)] * 4
        + [pltpu.VMEM((height, 128), f32)] * 4
        + [
            pltpu.VMEM((breadth // 128, PLANES * height, 128), f32),
            pltpu.VMEM((height * breadth + 8, 128), f32),
            pltpu.VMEM((slots // 2, 128), f32),
            pltpu.VMEM((128, 128), f32),
            pltpu.SemaphoreType.DMA((breadth // 128,)),
        ],
        compiler_params=params,
        name="propagate_and_pick",
    )(courant, cos, sin, cells, x, moving, sea, depth_kernel, south, north, first, second, lanes, subs)

    received = lax.all_to_all(picked, both, split_axis=0, concat_axis=0, tiled=True)

    stokes = pl.pallas_call(
        functools.partial(add_kernel, slots),
        out_shape=shape(depth_kernel.shape[0], OUT_DEV),
        in_specs=[smem, vmem],
        out_specs=vmem,
        scratch_shapes=[pltpu.VMEM((slots // 2, 128), f32)] + [pltpu.VMEM((OUT_DEV + 8, 128), f32)] * (2 * N_ACC),
        compiler_params=params,
        name="add_profiles",
    )(targets, received)
    return propagated.reshape(DIRS, FREQ, height, breadth), stokes


def solution(mesh):
    placed = (
        P(None, None, "lat", "lon"),
        P("lat", "lon"),
        P("lat", "lon"),
        P(),
        P(),
        P(("lat", "lon"), None, None),
        P(("lat", "lon"), None, None),
    )
    return jax.shard_map(
        functools.partial(body, mesh.shape["lat"], mesh.shape["lon"]),
        mesh=mesh,
        in_specs=placed,
        out_specs=(P(None, None, "lat", "lon"), P(None, ("lat", "lon"))),
        check_vma=False,
    )
```

```python
import functools
import math

import jax
import jax.numpy as jnp
import numpy as np
from jax import lax
from jax.experimental import pallas as pl
from jax.experimental.pallas import tpu as pltpu
from jax.sharding import PartitionSpec as P

DIRS = 36
FREQ = 2
PLANES = DIRS * FREQ
HALF = PLANES // 2
QUAD = PLANES // 4
OUT_DEV = 4096
N_ACC = 4
WINDOW = 1024
VMEM_LIMIT = 48 * 1024 * 1024


def exchange_pairs(n_lat, n_lon):
    def flat(j, i):
        return j * n_lon + i % n_lon

    row_first = [(j, j ^ 1) for j in range(n_lat)]
    row_second = []
    for i in range(n_lon):
        row_second += [(flat(0, i), flat(0, i)), (flat(n_lat - 1, i), flat(n_lat - 1, n_lon - 1 - i))]
        for j in range(1, n_lat - 1, 2):
            row_second += [(flat(j, i), flat(j + 1, i)), (flat(j + 1, i), flat(j, i))]
    column_first = [(i, i ^ 1) for i in range(n_lon)]
    column_second = [(i, (i + 1 if i % 2 else i - 1) % n_lon) for i in range(n_lon)]
    return row_first, row_second, column_first, column_second


def pack_kernel(x_hbm, speed_hbm, mask_hbm, first_ref, second_ref, east_ref, west_ref, mov_ref, sea_ref,
                up_ref, down_ref, top_rows, bottom_rows, east_edge, west_edge, speed_ref, mask_ref, sems):
    height, breadth = speed_ref.shape
    first_quad, mid_quads, last_quad = pl.ds(0, QUAD), pl.ds(QUAD, HALF), pl.ds(3 * QUAD, QUAD)
    last_lanes = pl.ds(breadth - 128, 128)
    copies = [
        pltpu.make_async_copy(source, target, sems.at[k])
        for k, (source, target) in enumerate((
            (speed_hbm, speed_ref),
            (mask_hbm, mask_ref),
            (x_hbm.at[pl.ds(0, HALF), pl.ds(height - 8, 8), :], top_rows),
            (x_hbm.at[pl.ds(HALF, HALF), pl.ds(0, 8), :], bottom_rows),
            (x_hbm.at[first_quad, :, last_lanes], east_edge.at[first_quad]),
            (x_hbm.at[last_quad, :, last_lanes], east_edge.at[pl.ds(QUAD, QUAD)]),
            (x_hbm.at[mid_quads, :, pl.ds(0, 128)], west_edge),
        ))
    ]
    for copy in copies:
        copy.start()
    even = lax.axis_index("lat") % 2 == 0
    for copy in copies[:4]:
        copy.wait()
    sea = mask_ref[...].astype(jnp.float32)
    moving = speed_ref[...] * sea
    mov_ref[...] = moving
    sea_ref[...] = sea
    for k in range(2):
        for q in range(HALF):
            up_ref[k, q : q + 1, :] = top_rows[q, 7 - k : 8 - k, :]
            down_ref[k, q : q + 1, :] = bottom_rows[q, k : k + 1, :]
        up_ref[k, HALF : HALF + 1, :] = moving[height - 1 - k : height - k, :]
        down_ref[k, HALF : HALF + 1, :] = moving[k : k + 1, :]
        up_ref[k, HALF + 1 : HALF + 2, :] = sea[height - 1 - k : height - k, :]
        down_ref[k, HALF + 1 : HALF + 2, :] = sea[k : k + 1, :]
        up_ref[k, HALF + 2 :, :] = jnp.zeros((2, breadth), jnp.float32)
        down_ref[k, HALF + 2 :, :] = jnp.zeros((2, breadth), jnp.float32)

    @pl.when(even)
    def _():
        first_ref[...] = up_ref[...]
        second_ref[...] = down_ref[...]

    @pl.when(jnp.logical_not(even))
    def _():
        first_ref[...] = down_ref[...]
        second_ref[...] = up_ref[...]

    for copy in copies[4:]:
        copy.wait()
    lane = lax.broadcasted_iota(jnp.int32, (height, 128), 1)
    east = jnp.zeros((height, 128), jnp.float32)
    west = jnp.zeros((height, 128), jnp.float32)
    for q in range(HALF + 2):
        mine = lane // 2 == q
        if q < HALF:
            edge_e, edge_w = east_edge[q], west_edge[q]
        else:
            field = moving if q == HALF else sea
            edge_e, edge_w = field[:, breadth - 128 :], field[:, :128]
        east = jnp.where(mine, pltpu.roll(edge_e, (2 * q + 2) % 128, axis=1), east)
        west = jnp.where(mine, pltpu.roll(edge_w, 2 * q, axis=1), west)
    east_ref[...] = east
    west_ref[...] = west


def corner_kernel(n_lat, first_ref, second_ref, east_ref, west_ref, south_ref, north_ref, out_first, out_second):
    height = east_ref.shape[0]
    breadth = first_ref.shape[2]
    lat = lax.axis_index("lat")
    even = lat % 2 == 0

    @pl.when(even)
    def _():
        north_ref[...] = first_ref[...]
        south_ref[...] = second_ref[...]

    @pl.when(jnp.logical_not(even))
    def _():
        south_ref[...] = first_ref[...]
        north_ref[...] = second_ref[...]

    @pl.when(lat == 0)
    def _():
        south_ref[...] = jnp.zeros_like(south_ref)

    @pl.when(lat == n_lat - 1)
    def _():
        flip_i = lax.broadcasted_iota(jnp.int32, (breadth, breadth), 0)
        flip_j = lax.broadcasted_iota(jnp.int32, (breadth, breadth), 1)
        flip = (flip_i + flip_j == breadth - 1).astype(jnp.float32)
        for k in range(2):
            north_ref[k] = jnp.dot(
                north_ref[k], flip, precision=lax.Precision.HIGHEST, preferred_element_type=jnp.float32
            )

    plane = lax.broadcasted_iota(jnp.int32, (HALF + 4, 128), 0)
    lane = lax.broadcasted_iota(jnp.int32, (HALF + 4, 128), 1)
    south = south_ref[0] * south_ref[0, HALF : HALF + 1, :]
    north = north_ref[0] * north_ref[0, HALF : HALF + 1, :]

    def to_lanes(column, low, high, place):
        mine = (plane >= low) & (plane < high) & (lane == place)
        return jnp.where(mine, column, 0.0)

    east_edge = to_lanes(south[:, breadth - 1 :], 0, QUAD, 2 * plane + 1)
    east_edge += to_lanes(north[:, breadth - 1 :], QUAD, HALF, 2 * plane + 1)
    west_edge = to_lanes(south[:, :1], QUAD, HALF, 2 * plane - HALF)
    west_edge += to_lanes(north[:, :1], 0, QUAD, 2 * plane + HALF)
    east_edge = jnp.broadcast_to(jnp.sum(east_edge, axis=0, keepdims=True), (8, 128))
    west_edge = jnp.broadcast_to(jnp.sum(west_edge, axis=0, keepdims=True), (8, 128))
    even_lon = lax.axis_index("lon") % 2 == 0
    out_first[:height] = jnp.where(even_lon, east_ref[...], west_ref[...])
    out_second[:height] = jnp.where(even_lon, west_ref[...], east_ref[...])
    out_first[height:] = jnp.where(even_lon, east_edge, west_edge)
    out_second[height:] = jnp.where(even_lon, west_edge, east_edge)


def for_windows(list_ref, window, sems, work):
    count = list_ref.shape[0] // WINDOW

    def fetch(i, w):
        source = list_ref.at[pl.ds(pl.multiple_of(i * WINDOW, WINDOW), WINDOW)]
        return pltpu.make_async_copy(source, window.at[pl.ds(w * WINDOW, WINDOW)], sems.at[w])

    for w in range(2):
        fetch(w, w).start()

    @pl.loop(0, count // 2)
    def _(t):
        for w in range(2):
            i = 2 * t + w
            fetch(i, w).wait()
            work(lambda k, start=w * WINDOW: window[start + k], i)

            @pl.when(i + 2 < count)
            def _():
                fetch(i + 2, w).start()


def wave_kernel( courant_ref, cos_ref, sin_ref, cells_ref, x_ref, mov_ref, sea_ref, kernel_ref,
                south_ref, north_ref, first_ref, second_ref, lanes_ref, subs_ref, out_ref, picked_ref,
                south0, south1, north0, north1, west0, west1, east0, east1, halves, table, lines, picks, wide_kernel,
                window, out_sems, window_sems, pick_sem):
    height, breadth = mov_ref.shape
    c0, c1 = courant_ref[0], courant_ref[1]
    even_lon = lax.axis_index("lon") % 2 == 0
    from_west = jnp.where(even_lon, second_ref[...], first_ref[...])
    from_east = jnp.where(even_lon, first_ref[...], second_ref[...])
    corner_w, corner_e = from_west[height : height + 1], from_east[height : height + 1]

    lane = lax.broadcasted_iota(jnp.int32, (height, 128), 1)
    row = lax.broadcasted_iota(jnp.int32, (height, 128), 0)
    odd = lane % 2 == 1

    def columns(e0, near, far, corner, cx, cy, sign, flux0, flux1):
        mov = jnp.where(odd, e0[:, 2 * HALF + 1 : 2 * HALF + 2], e0[:, 2 * HALF : 2 * HALF + 1])
        sea = e0[:, 2 * HALF + 2 + near : 2 * HALF + 3 + near]
        f0 = mov * e0
        f_far = pltpu.roll(f0, 1 if near > far else 127, axis=1)
        f_south = jnp.where(row == 0, corner, pltpu.roll(f0, 1, axis=0))
        f_north = jnp.where(row == height - 1, corner, pltpu.roll(f0, height - 1, axis=0))
        div_x = cx * (f0 - f_far) if sign > 0 else cx * (f_far - f0)
        div_y = jnp.where(lane < HALF, cy * (f0 - f_south), cy * (f_north - f0))
        flux0[...] = f0
        flux1[...] = mov * (sea * ((e0 - div_x) - div_y))

    lanes = lanes_ref[...]
    lane_courant = jnp.where(lanes[4:5] > 0.5, c1, c0)
    columns(from_west[:height], 1, 0, corner_w, lanes[0:1] * lane_courant, lanes[1:2] * lane_courant, 1, west0, west1)
    columns(from_east[:height], 0, 1, corner_e, lanes[2:3] * lane_courant, lanes[3:4] * lane_courant, -1, east0, east1)

    wide = lax.broadcasted_iota(jnp.int32, (HALF + 4, breadth), 1)
    plane = lax.broadcasted_iota(jnp.int32, (HALF + 4, 1), 0)
    plane_l = lax.broadcasted_iota(jnp.int32, (HALF + 4, 128), 0)
    lane_l = lax.broadcasted_iota(jnp.int32, (HALF + 4, 128), 1)
    subs = subs_ref[...]
    sub_courant = jnp.where(plane % 2 == 1, c1, c0)

    def to_sublanes(corner, lane_of):
        return jnp.sum(jnp.where(lane_l == lane_of, corner, 0.0), axis=1, keepdims=True)

    def rows(near, far, first_west, west_corner, east_corner, cx, cy, sign, flux0, flux1):
        mov, sea = near[HALF : HALF + 1], near[HALF + 1 : HALF + 2]
        f0 = mov * near
        f_far = far[HALF : HALF + 1] * far
        f_west = jnp.where(wide == 0, west_corner, pltpu.roll(f0, 1, axis=1))
        f_east = jnp.where(wide == breadth - 1, east_corner, pltpu.roll(f0, breadth - 1, axis=1))
        from_west = (plane < QUAD) if first_west else (plane >= QUAD)
        div_x = jnp.where(from_west, cx * (f0 - f_west), cx * (f_east - f0))
        div_y = cy * (f0 - f_far) if sign > 0 else cy * (f_far - f0)
        flux0[...] = f0
        flux1[...] = mov * (sea * ((near - div_x) - div_y))

    sw = to_sublanes(corner_w, 2 * plane_l + 1)
    se = to_sublanes(corner_e, 2 * plane_l - HALF)
    ne = to_sublanes(corner_e, 2 * plane_l + HALF)
    nw = sw
    rows(south_ref[0], south_ref[1], True, sw, se, subs[:, 0:1] * sub_courant, subs[:, 1:2] * sub_courant, 1,
         south0, south1)
    rows(north_ref[0], north_ref[1], False, nw, ne, subs[:, 2:3] * sub_courant, subs[:, 3:4] * sub_courant, -1,
         north0, north1)

    moving = mov_ref[...]
    sea_all = sea_ref[...]
    lane_edge = lax.broadcasted_iota(jnp.int32, (height, 128), 1)
    row_edge = lax.broadcasted_iota(jnp.int32, (8, breadth), 0)

    def write_out(planes, h):
        target = out_ref.at[planes, pl.ds(h * 128, 128)]
        return pltpu.make_async_copy(halves.at[h, planes, :], target, out_sems.at[h])

    def quadrant(first, from_west, from_south, column0, column1, lane_first, row0, row1, row_first):
        def upstream(flux, column, line):
            if from_west:
                moved = pltpu.roll(flux, 1, axis=1)
                side = jnp.concatenate([jnp.where(lane_edge == 0, column, moved[:, :128]), moved[:, 128:]], axis=1)
            else:
                moved = pltpu.roll(flux, breadth - 1, axis=1)
                edge = jnp.where(lane_edge == 127, column, moved[:, breadth - 128 :])
                side = jnp.concatenate([moved[:, : breadth - 128], edge], axis=1)
            if from_south:
                moved = pltpu.roll(flux, 1, axis=0)
                below = jnp.concatenate([jnp.where(row_edge == 0, line, moved[:8]), moved[8:]], axis=0)
            else:
                moved = pltpu.roll(flux, height - 1, axis=0)
                edge = jnp.where(row_edge == 7, line, moved[height - 8 :])
                below = jnp.concatenate([moved[: height - 8], edge], axis=0)
            return side, below

        def step(t, carry):
            p = first + t
            courant = jnp.where(p % 2 == 1, c1, c0)
            cx = cos_ref[p] * courant
            cy = sin_ref[p] * courant
            place = lane_first + 2 * t
            turn = (128 - place) if from_west else (127 - place)
            energy = x_ref[p]
            for column_ref, row_ref in ((column0, row0), (column1, row1)):
                flux = moving * energy
                column = pltpu.roll(column_ref[...], turn, axis=1)
                side, below = upstream(flux, column, row_ref[pl.ds(row_first + t, 1), :])
                div_x = cx * (flux - side) if from_west else cx * (side - flux)
                div_y = cy * (flux - below) if from_south else cy * (below - flux)
                energy = sea_all * ((energy - div_x) - div_y)
            start = pl.ds(pl.multiple_of(p * height, height), height)
            for h in range(breadth // 128):
                halves[h, start, :] = energy[:, h * 128 : (h + 1) * 128]
            return carry

        lax.fori_loop(0, QUAD, step, 0, unroll=6)
        planes = pl.ds(first * height, QUAD * height)
        for h in range(breadth // 128):
            write_out(planes, h).start()

    quadrant(0, True, True, west0, west1, 1, south0, south1, 0)
    quadrant(QUAD, False, True, east0, east1, 0, south0, south1, QUAD)
    quadrant(2 * QUAD, False, False, east0, east1, HALF, north0, north1, 0)
    quadrant(3 * QUAD, True, False, west0, west1, HALF + 1, north0, north1, QUAD)

    pad = jnp.zeros((8, 128), jnp.bfloat16)
    wide_kernel[...] = jnp.zeros((128, 128), jnp.float32)
    wide_kernel[:64, :PLANES] = kernel_ref[...]
    wide_kernel[64:, :PLANES] = kernel_ref[...]
    turned = wide_kernel[...].T[:PLANES]
    weight_high = turned.astype(jnp.bfloat16)
    weight_low = (turned - weight_high.astype(jnp.float32)).astype(jnp.bfloat16)
    weight = jnp.concatenate([weight_high, pad, weight_high, pad, weight_low, pad], axis=0)

    group = 8

    @pl.loop(0, height // group)
    def _(r):
        blocks = []
        for k in range(group):
            for h in range(breadth // 128):
                spectra = halves[h, pl.ds(r * group + k, PLANES, stride=height), :]
                high = spectra.astype(jnp.bfloat16)
                low = (spectra - high.astype(jnp.float32)).astype(jnp.bfloat16)
                blocks.append(jnp.concatenate([high, pad, low, pad, high, pad], axis=0))
        stacked = jnp.concatenate(blocks, axis=1)
        profile = lax.dot_general(stacked, weight, (((0,), (0,)), ((), ())), preferred_element_type=jnp.float32)
        start = pl.multiple_of(r * group * breadth, 128)
        table[pl.ds(start, group * breadth), :] = profile

    first_half = lax.broadcasted_iota(jnp.int32, (1, 128), 1) < 64
    half = WINDOW // 2

    def pick(cell, i):
        for g in range(WINDOW // 16):
            for j in range(8):
                one, two = cell(16 * g + j), cell(16 * g + 8 + j)
                line = jnp.where(first_half, table[pl.ds(one, 1), :], table[pl.ds(two, 1), :])
                lines[8 * g + j : 8 * g + j + 1, :] = line
        here = pl.ds(pl.multiple_of(i * half, half), half)
        picks[here, :] = lines[...].astype(jnp.bfloat16)
        pltpu.make_async_copy(picks.at[here, :], picked_ref.at[here, :], pick_sem).start()

    for_windows(cells_ref, window, window_sems, pick)
    pltpu.make_async_copy(picks, picked_ref, pick_sem).wait()
    whole = pl.ds(0, PLANES * height)
    for h in range(breadth // 128):
        write_out(whole, h).wait()


def add_kernel(rows_ref, values_ref, out_ref, values, lines, tile_sums, window, value_sems, window_sems, out_sem, *sums):
    n_acc = len(sums) // 2
    tile = out_ref.shape[1]
    block = 512
    half = WINDOW // 2

    def fetch(i):
        here = pl.ds(pl.multiple_of(i * half, half), half)
        return pltpu.make_async_copy(values_ref.at[here, :], values.at[here, :], value_sems.at[i])

    for i in range(value_sems.shape[0]):
        fetch(i).start()

    @pl.loop(0, tile // block)
    def _(i):
        for total in sums:
            total[pl.ds(pl.multiple_of(i * block, block), block), :] = jnp.zeros((block, 128), jnp.float32)

    def add(row, i):
        fetch(i).wait()
        lines[...] = values[pl.ds(pl.multiple_of(i * half, half), half), :].astype(jnp.float32)
        for g in range(WINDOW // 16):
            for j in range(8):
                one, two = row(16 * g + j), row(16 * g + 8 + j)
                line = lines[8 * g + j : 8 * g + j + 1, :]
                left, right = sums[j % n_acc], sums[n_acc + j % n_acc]
                left[pl.ds(one, 1), :] = left[pl.ds(one, 1), :] + line
                right[pl.ds(two, 1), :] = right[pl.ds(two, 1), :] + line

    for_windows(rows_ref, window, window_sems, add)
    first_half = lax.broadcasted_iota(jnp.int32, (block, 128), 1) < 64

    @pl.loop(0, tile // block)
    def _(i):
        here = pl.ds(pl.multiple_of(i * block, block), block)
        left, right = sums[0][here, :], sums[n_acc][here, :]
        for q in range(1, n_acc):
            left = left + sums[q][here, :]
            right = right + sums[n_acc + q][here, :]
        both = jnp.where(first_half, left, right).T
        tile_sums[:, here] = both[:64] + both[64:]
        pltpu.make_async_copy(tile_sums.at[:, here], out_ref.at[:, here], out_sem).start()

    pltpu.make_async_copy(tile_sums, out_ref, out_sem).wait()


def constant_tables():
    heading = (np.arange(DIRS) + 0.5) * (2.0 * math.pi / DIRS)
    cos = np.repeat(np.cos(heading), FREQ)
    sin = np.repeat(np.sin(heading), FREQ)
    lanes = np.zeros((8, 128))
    q = np.arange(HALF)
    from_west = np.where(q < QUAD, q, q + HALF)
    from_east = q + QUAD
    for column in range(2):
        lanes[0, 2 * q + column] = cos[from_west]
        lanes[1, 2 * q + column] = sin[from_west]
        lanes[2, 2 * q + column] = cos[from_east]
        lanes[3, 2 * q + column] = sin[from_east]
        lanes[4, 2 * q + column] = q % 2
    subs = np.zeros((HALF + 4, 128))
    subs[:HALF, 0], subs[:HALF, 1] = cos[:HALF], sin[:HALF]
    subs[:HALF, 2], subs[:HALF, 3] = cos[HALF:], sin[HALF:]
    return [t.astype(np.float32) for t in (cos, sin, lanes, subs)]


def body(n_lat, n_lon, spectrum, speed_factor, land_sea_mask, courant, depth_kernel, send_rows, recv_rows):
    height, breadth = speed_factor.shape
    devices, slots = send_rows.shape[1:]
    x = spectrum.reshape(PLANES, height, breadth)
    f32 = jnp.float32
    vmem = pl.BlockSpec(memory_space=pltpu.VMEM)
    smem = pl.BlockSpec(memory_space=pltpu.SMEM)
    hbm = pl.BlockSpec(memory_space=pltpu.HBM)
    params = pltpu.CompilerParams(vmem_limit_bytes=VMEM_LIMIT)

    both = ("lat", "lon")

    def shape(*dims, kind=f32):
        return jax.ShapeDtypeStruct(dims, kind)

    row_message = shape(2, HALF + 4, breadth)
    columns = shape(height, 128)
    column_message = shape(height + 8, 128)
    row_first, row_second, column_first, column_second = exchange_pairs(n_lat, n_lon)
    first, second, east, west, moving, sea = pl.pallas_call(
        pack_kernel,
        out_shape=[row_message] * 2 + [columns] * 2 + [shape(height, breadth)] * 2,
        in_specs=[hbm] * 3,
        out_specs=[vmem] * 6,
        scratch_shapes=[pltpu.VMEM((2, HALF + 4, breadth), f32)] * 2
        + [pltpu.VMEM((HALF, 8, breadth), f32)] * 2
        + [pltpu.VMEM((HALF, height, 128), f32)] * 2
        + [pltpu.VMEM((height, breadth), f32), pltpu.VMEM((height, breadth), jnp.int32), pltpu.SemaphoreType.DMA((7,))],
        compiler_params=params,
        name="pack_halos",
    )(x, speed_factor, land_sea_mask)
    first = lax.ppermute(first, "lat", row_first)
    second = lax.ppermute(second, both, row_second)
    south, north, first, second = pl.pallas_call(
        functools.partial(corner_kernel, n_lat),
        out_shape=[row_message] * 2 + [column_message] * 2,
        in_specs=[vmem] * 4,
        out_specs=[vmem] * 4,
        compiler_params=params,
        name="add_corners",
    )(first, second, east, west)
    first = lax.ppermute(first, "lon", column_first)
    second = lax.ppermute(second, "lon", column_second)

    cos, sin, lanes, subs = constant_tables()
    cells = jnp.maximum(send_rows, 0).reshape(-1)
    targets = jnp.where(recv_rows < 0, OUT_DEV, recv_rows).reshape(-1)
    propagated, picked = pl.pallas_call(
        wave_kernel,
        out_shape=[shape(PLANES * height, breadth), shape(devices * slots // 2, 128, kind=jnp.bfloat16)],
        in_specs=[smem] * 3 + [hbm] + [vmem] * 10,
        out_specs=[hbm] * 2,
        scratch_shapes=[pltpu.VMEM((HALF + 4, breadth), f32)] * 4
        + [pltpu.VMEM((height, 128), f32)] * 4
        + [
            pltpu.VMEM((breadth // 128, PLANES * height, 128), f32),
            pltpu.VMEM((height * breadth, 128), f32),
            pltpu.VMEM((WINDOW // 2, 128), f32),
            pltpu.VMEM((devices * slots // 2, 128), jnp.bfloat16),
            pltpu.VMEM((128, 128), f32),
            pltpu.SMEM((2 * WINDOW,), jnp.int32),
            pltpu.SemaphoreType.DMA((breadth // 128,)),
            pltpu.SemaphoreType.DMA((2,)),
            pltpu.SemaphoreType.DMA,
        ],
        compiler_params=params,
        name="propagate_and_pick",
    )(courant, cos, sin, cells, x, moving, sea, depth_kernel, south, north, first, second, lanes, subs)

    picked = picked.reshape(devices, slots // 2, 128)
    received = lax.all_to_all(picked, both, split_axis=0, concat_axis=0, tiled=True)

    slot_rows = devices * slots // 2
    components = depth_kernel.shape[0]
    stokes = pl.pallas_call(
        add_kernel,
        out_shape=shape(components, OUT_DEV),
        in_specs=[hbm] * 2,
        out_specs=hbm,
        scratch_shapes=[
            pltpu.VMEM((slot_rows, 128), jnp.bfloat16),
            pltpu.VMEM((WINDOW // 2, 128), f32),
            pltpu.VMEM((components, OUT_DEV), f32),
            pltpu.SMEM((2 * WINDOW,), jnp.int32),
            pltpu.SemaphoreType.DMA((slot_rows // (WINDOW // 2),)),
            pltpu.SemaphoreType.DMA((2,)),
            pltpu.SemaphoreType.DMA,
        ]
        + [pltpu.VMEM((OUT_DEV + 8, 128), f32)] * (2 * N_ACC),
        compiler_params=params,
        name="add_profiles",
    )(targets, received.reshape(slot_rows, 128))
    return propagated.reshape(DIRS, FREQ, height, breadth), stokes


def solution(mesh):
    placed = (
        P(None, None, "lat", "lon"),
        P("lat", "lon"),
        P("lat", "lon"),
        P(),
        P(),
        P(("lat", "lon"), None, None),
        P(("lat", "lon"), None, None),
    )
    return jax.shard_map(
        functools.partial(body, mesh.shape["lat"], mesh.shape["lon"]),
        mesh=mesh,
        in_specs=placed,
        out_specs=(P(None, None, "lat", "lon"), P(None, ("lat", "lon"))),
        check_vma=False,
    )
```

```python
import functools
import math

import jax
import jax.numpy as jnp
import numpy as np
from jax import lax
from jax.experimental import pallas as pl
from jax.experimental.pallas import tpu as pltpu
from jax.sharding import PartitionSpec as P

DIRS = 36
FREQ = 2
PLANES = DIRS * FREQ
HALF = PLANES // 2
QUAD = PLANES // 4
OUT_DEV = 4096
N_ACC = 4
WINDOW = 1024
VMEM_LIMIT = 32 * 1024 * 1024


def exchange_pairs(n_lat, n_lon):
    def flat(j, i):
        return j * n_lon + i % n_lon

    row_first = [(j, j ^ 1) for j in range(n_lat)]
    row_second = []
    for i in range(n_lon):
        row_second += [(flat(0, i), flat(0, i)), (flat(n_lat - 1, i), flat(n_lat - 1, n_lon - 1 - i))]
        for j in range(1, n_lat - 1, 2):
            row_second += [(flat(j, i), flat(j + 1, i)), (flat(j + 1, i), flat(j, i))]
    column_first = [(i, i ^ 1) for i in range(n_lon)]
    column_second = [(i, (i + 1 if i % 2 else i - 1) % n_lon) for i in range(n_lon)]
    return row_first, row_second, column_first, column_second


def pack_kernel(x_hbm, speed_hbm, mask_hbm, first_ref, second_ref, east_ref, west_ref, mov_ref, sea_ref,
                up_ref, down_ref, top_rows, bottom_rows, east_edge, west_edge, speed_ref, mask_ref, sems):
    height, breadth = speed_ref.shape
    first_quad, mid_quads, last_quad = pl.ds(0, QUAD), pl.ds(QUAD, HALF), pl.ds(3 * QUAD, QUAD)
    last_lanes = pl.ds(breadth - 128, 128)
    copies = [
        pltpu.make_async_copy(source, target, sems.at[k])
        for k, (source, target) in enumerate((
            (speed_hbm, speed_ref),
            (mask_hbm, mask_ref),
            (x_hbm.at[pl.ds(0, HALF), pl.ds(height - 8, 8), :], top_rows),
            (x_hbm.at[pl.ds(HALF, HALF), pl.ds(0, 8), :], bottom_rows),
            (x_hbm.at[first_quad, :, last_lanes], east_edge.at[first_quad]),
            (x_hbm.at[last_quad, :, last_lanes], east_edge.at[pl.ds(QUAD, QUAD)]),
            (x_hbm.at[mid_quads, :, pl.ds(0, 128)], west_edge),
        ))
    ]
    for copy in copies:
        copy.start()
    even = lax.axis_index("lat") % 2 == 0
    for copy in copies[:4]:
        copy.wait()
    sea = mask_ref[...].astype(jnp.float32)
    moving = speed_ref[...] * sea
    mov_ref[...] = moving
    sea_ref[...] = sea
    for k in range(2):
        for q in range(HALF):
            up_ref[k, q : q + 1, :] = top_rows[q, 7 - k : 8 - k, :]
            down_ref[k, q : q + 1, :] = bottom_rows[q, k : k + 1, :]
        up_ref[k, HALF : HALF + 1, :] = moving[height - 1 - k : height - k, :]
        down_ref[k, HALF : HALF + 1, :] = moving[k : k + 1, :]
        up_ref[k, HALF + 1 : HALF + 2, :] = sea[height - 1 - k : height - k, :]
        down_ref[k, HALF + 1 : HALF + 2, :] = sea[k : k + 1, :]
        up_ref[k, HALF + 2 :, :] = jnp.zeros((2, breadth), jnp.float32)
        down_ref[k, HALF + 2 :, :] = jnp.zeros((2, breadth), jnp.float32)

    @pl.when(even)
    def _():
        first_ref[...] = up_ref[...]
        second_ref[...] = down_ref[...]

    @pl.when(jnp.logical_not(even))
    def _():
        first_ref[...] = down_ref[...]
        second_ref[...] = up_ref[...]

    for copy in copies[4:]:
        copy.wait()
    lane = lax.broadcasted_iota(jnp.int32, (height, 128), 1)
    east = jnp.zeros((height, 128), jnp.float32)
    west = jnp.zeros((height, 128), jnp.float32)
    for q in range(HALF + 2):
        mine = lane // 2 == q
        if q < HALF:
            edge_e, edge_w = east_edge[q], west_edge[q]
        else:
            field = moving if q == HALF else sea
            edge_e, edge_w = field[:, breadth - 128 :], field[:, :128]
        east = jnp.where(mine, pltpu.roll(edge_e, (2 * q + 2) % 128, axis=1), east)
        west = jnp.where(mine, pltpu.roll(edge_w, 2 * q, axis=1), west)
    east_ref[...] = east
    west_ref[...] = west


def corner_kernel(n_lat, first_ref, second_ref, east_ref, west_ref, south_ref, north_ref, out_first, out_second):
    height = east_ref.shape[0]
    breadth = first_ref.shape[2]
    lat = lax.axis_index("lat")
    even = lat % 2 == 0

    @pl.when(even)
    def _():
        north_ref[...] = first_ref[...]
        south_ref[...] = second_ref[...]

    @pl.when(jnp.logical_not(even))
    def _():
        south_ref[...] = first_ref[...]
        north_ref[...] = second_ref[...]

    @pl.when(lat == 0)
    def _():
        south_ref[...] = jnp.zeros_like(south_ref)

    @pl.when(lat == n_lat - 1)
    def _():
        flip_i = lax.broadcasted_iota(jnp.int32, (breadth, breadth), 0)
        flip_j = lax.broadcasted_iota(jnp.int32, (breadth, breadth), 1)
        flip = (flip_i + flip_j == breadth - 1).astype(jnp.float32)
        for k in range(2):
            north_ref[k] = jnp.dot(
                north_ref[k], flip, precision=lax.Precision.HIGHEST, preferred_element_type=jnp.float32
            )

    plane = lax.broadcasted_iota(jnp.int32, (HALF + 4, 128), 0)
    lane = lax.broadcasted_iota(jnp.int32, (HALF + 4, 128), 1)
    south = south_ref[0] * south_ref[0, HALF : HALF + 1, :]
    north = north_ref[0] * north_ref[0, HALF : HALF + 1, :]

    def to_lanes(column, low, high, place):
        mine = (plane >= low) & (plane < high) & (lane == place)
        return jnp.where(mine, column, 0.0)

    east_edge = to_lanes(south[:, breadth - 1 :], 0, QUAD, 2 * plane + 1)
    east_edge += to_lanes(north[:, breadth - 1 :], QUAD, HALF, 2 * plane + 1)
    west_edge = to_lanes(south[:, :1], QUAD, HALF, 2 * plane - HALF)
    west_edge += to_lanes(north[:, :1], 0, QUAD, 2 * plane + HALF)
    east_edge = jnp.broadcast_to(jnp.sum(east_edge, axis=0, keepdims=True), (8, 128))
    west_edge = jnp.broadcast_to(jnp.sum(west_edge, axis=0, keepdims=True), (8, 128))
    even_lon = lax.axis_index("lon") % 2 == 0
    out_first[:height] = jnp.where(even_lon, east_ref[...], west_ref[...])
    out_second[:height] = jnp.where(even_lon, west_ref[...], east_ref[...])
    out_first[height:] = jnp.where(even_lon, east_edge, west_edge)
    out_second[height:] = jnp.where(even_lon, west_edge, east_edge)


def for_windows(list_ref, window, sems, work):
    count = list_ref.shape[0] // WINDOW

    def fetch(i, w):
        source = list_ref.at[pl.ds(pl.multiple_of(i * WINDOW, WINDOW), WINDOW)]
        return pltpu.make_async_copy(source, window.at[pl.ds(w * WINDOW, WINDOW)], sems.at[w])

    for w in range(2):
        fetch(w, w).start()

    @pl.loop(0, count // 2)
    def _(t):
        for w in range(2):
            i = 2 * t + w
            fetch(i, w).wait()
            work(lambda k, start=w * WINDOW: window[start + k], i)

            @pl.when(i + 2 < count)
            def _():
                fetch(i + 2, w).start()


def inside_kernel(courant_ref, cos_ref, sin_ref, x_ref, mov_ref, sea_ref, halves):
    height, breadth = mov_ref.shape
    c0, c1 = courant_ref[0], courant_ref[1]
    moving = mov_ref[...]
    sea = sea_ref[...]
    lane = lax.broadcasted_iota(jnp.int32, (height, 128), 1)
    row = lax.broadcasted_iota(jnp.int32, (8, breadth), 0)
    for h in range(breadth // 128):
        halves[h, PLANES * height :, :] = jnp.zeros((4 * height, 128), jnp.float32)

    def quadrant(first, from_west, from_south):
        def upstream(flux):
            if from_west:
                moved = pltpu.roll(flux, 1, axis=1)
                side = jnp.concatenate([jnp.where(lane == 0, 0.0, moved[:, :128]), moved[:, 128:]], axis=1)
            else:
                moved = pltpu.roll(flux, breadth - 1, axis=1)
                edge = jnp.where(lane == 127, 0.0, moved[:, breadth - 128 :])
                side = jnp.concatenate([moved[:, : breadth - 128], edge], axis=1)
            if from_south:
                moved = pltpu.roll(flux, 1, axis=0)
                below = jnp.concatenate([jnp.where(row == 0, 0.0, moved[:8]), moved[8:]], axis=0)
            else:
                moved = pltpu.roll(flux, height - 1, axis=0)
                below = jnp.concatenate([moved[: height - 8], jnp.where(row == 7, 0.0, moved[height - 8 :])], axis=0)
            return side, below

        def step(t, carry):
            p = first + t
            courant = jnp.where(p % 2 == 1, c1, c0)
            cx = cos_ref[p] * courant
            cy = sin_ref[p] * courant
            energy = x_ref[p]
            for _ in range(2):
                flux = moving * energy
                side, below = upstream(flux)
                div_x = cx * (flux - side) if from_west else cx * (side - flux)
                div_y = cy * (flux - below) if from_south else cy * (below - flux)
                energy = sea * ((energy - div_x) - div_y)
            start = pl.ds(pl.multiple_of(p * height, height), height)
            for h in range(breadth // 128):
                halves[h, start, :] = energy[:, h * 128 : (h + 1) * 128]
            return carry

        lax.fori_loop(0, QUAD, step, 0, unroll=6)

    quadrant(0, True, True)
    quadrant(QUAD, False, True)
    quadrant(2 * QUAD, False, False)
    quadrant(3 * QUAD, True, False)


def finish_kernel(courant_ref, cells_ref, mov_ref, sea_ref, kernel_ref, south_ref, north_ref, first_ref, second_ref,
                  lanes_ref, subs_ref, halves_in, out_ref, picked_ref, halves,
                  table, lines, picks, wide_kernel, window, out_sems, window_sems, pick_sem):
    height, breadth = mov_ref.shape
    c0, c1 = courant_ref[0], courant_ref[1]
    even_lon = lax.axis_index("lon") % 2 == 0
    from_west = jnp.where(even_lon, second_ref[...], first_ref[...])
    from_east = jnp.where(even_lon, first_ref[...], second_ref[...])
    corner_w, corner_e = from_west[height : height + 1], from_east[height : height + 1]

    lane = lax.broadcasted_iota(jnp.int32, (height, 128), 1)
    row = lax.broadcasted_iota(jnp.int32, (height, 128), 0)
    odd = lane % 2 == 1

    def columns(e0, near, far, corner, cx, cy, sign):
        mov = jnp.where(odd, e0[:, 2 * HALF + 1 : 2 * HALF + 2], e0[:, 2 * HALF : 2 * HALF + 1])
        sea = e0[:, 2 * HALF + 2 + near : 2 * HALF + 3 + near]
        f0 = mov * e0
        f_far = pltpu.roll(f0, 1 if near > far else 127, axis=1)
        f_south = jnp.where(row == 0, corner, pltpu.roll(f0, 1, axis=0))
        f_north = jnp.where(row == height - 1, corner, pltpu.roll(f0, height - 1, axis=0))
        div_x = cx * (f0 - f_far) if sign > 0 else cx * (f_far - f0)
        div_y = jnp.where(lane < HALF, cy * (f0 - f_south), cy * (f_north - f0))
        return f0, mov * (sea * ((e0 - div_x) - div_y))

    lanes = lanes_ref[...]
    lane_courant = jnp.where(lanes[4:5] > 0.5, c1, c0)
    cx_w, cy_w, cx_e, cy_e = (lanes[k : k + 1] * lane_courant for k in range(4))
    west_flux0, west_flux1 = columns(from_west[:height], 1, 0, corner_w, cx_w, cy_w, 1)
    east_flux0, east_flux1 = columns(from_east[:height], 0, 1, corner_e, cx_e, cy_e, -1)

    wide = lax.broadcasted_iota(jnp.int32, (HALF + 4, breadth), 1)
    plane = lax.broadcasted_iota(jnp.int32, (HALF + 4, 1), 0)
    plane_l = lax.broadcasted_iota(jnp.int32, (HALF + 4, 128), 0)
    lane_l = lax.broadcasted_iota(jnp.int32, (HALF + 4, 128), 1)
    subs = subs_ref[...]
    sub_courant = jnp.where(plane % 2 == 1, c1, c0)

    def to_sublanes(corner, lane_of):
        return jnp.sum(jnp.where(lane_l == lane_of, corner, 0.0), axis=1, keepdims=True)

    def rows(near, far, first_west, west_corner, east_corner, cx, cy, sign):
        mov, sea = near[HALF : HALF + 1], near[HALF + 1 : HALF + 2]
        f0 = mov * near
        f_far = far[HALF : HALF + 1] * far
        f_west = jnp.where(wide == 0, west_corner, pltpu.roll(f0, 1, axis=1))
        f_east = jnp.where(wide == breadth - 1, east_corner, pltpu.roll(f0, breadth - 1, axis=1))
        from_west = (plane < QUAD) if first_west else (plane >= QUAD)
        div_x = jnp.where(from_west, cx * (f0 - f_west), cx * (f_east - f0))
        div_y = cy * (f0 - f_far) if sign > 0 else cy * (f_far - f0)
        return f0, mov * (sea * ((near - div_x) - div_y))

    sw = to_sublanes(corner_w, 2 * plane_l + 1)
    se = to_sublanes(corner_e, 2 * plane_l - HALF)
    ne = to_sublanes(corner_e, 2 * plane_l + HALF)
    nw = sw
    cx_s, cy_s, cx_n, cy_n = (subs[:, k : k + 1] * sub_courant for k in range(4))
    south_flux0, south_flux1 = rows(south_ref[0], south_ref[1], True, sw, se, cx_s, cy_s, 1)
    north_flux0, north_flux1 = rows(north_ref[0], north_ref[1], False, nw, ne, cx_n, cy_n, -1)

    def add_rows(first, near, next_row, flux0, flux1, cx, cy, first_west):
        sea0, sea1 = sea_ref[near : near + 1, :], sea_ref[next_row : next_row + 1, :]
        change = sea0 * (cy * flux0)
        flux = mov_ref[near : near + 1, :] * change
        west_flux = jnp.where(wide == 0, 0.0, pltpu.roll(flux, 1, axis=1))
        east_flux = jnp.where(wide == breadth - 1, 0.0, pltpu.roll(flux, breadth - 1, axis=1))
        from_west = (plane < QUAD) if first_west else (plane >= QUAD)
        div_x = jnp.where(from_west, cx * (flux - west_flux), cx * (east_flux - flux))
        near_change = sea0 * (((change - div_x) - cy * flux) + cy * flux1)
        next_change = sea1 * (cy * flux)
        for at, delta in ((near, near_change), (next_row, next_change)):
            for h in range(breadth // 128):
                place = pl.ds(first * height + at, HALF + 4, stride=height)
                halves[h, place, :] = halves[h, place, :] + delta[:, h * 128 : (h + 1) * 128]

    def add_columns(half, near, next_column, flux0, flux1, cx, cy, from_west):
        sea0, sea1 = sea_ref[:, near : near + 1], sea_ref[:, next_column : next_column + 1]
        change = sea0 * (cx * flux0)
        flux = mov_ref[:, near : near + 1] * change
        south_flux = jnp.where(row == 0, 0.0, pltpu.roll(flux, 1, axis=0))
        north_flux = jnp.where(row == height - 1, 0.0, pltpu.roll(flux, height - 1, axis=0))
        div_y = jnp.where(lane < HALF, cy * (flux - south_flux), cy * (north_flux - flux))
        near_change = sea0 * (((change - cx * flux) - div_y) + cx * flux1)
        next_change = sea1 * (cx * flux)
        if from_west:
            both = jnp.where(odd, next_change, pltpu.roll(near_change, 127, axis=1))
        else:
            both = jnp.where(odd, pltpu.roll(near_change, 1, axis=1), next_change)
        edge = lane < 2 if from_west else lane >= 126
        for q in range(HALF):
            p = q + QUAD if not from_west else (q if q < QUAD else q + HALF)
            turned = pltpu.roll(both, ((128 if from_west else 126) - 2 * q) % 128, axis=1)
            place = pl.ds(p * height, height)
            halves[half, place, :] = halves[half, place, :] + jnp.where(edge, turned, 0.0)

    add_rows(0, 0, 1, south_flux0, south_flux1, cx_s, cy_s, True)
    add_rows(HALF, height - 1, height - 2, north_flux0, north_flux1, cx_n, -cy_n, False)
    add_columns(0, 0, 1, west_flux0, west_flux1, cx_w, cy_w, True)
    add_columns(breadth // 128 - 1, breadth - 1, breadth - 2, east_flux0, east_flux1, -cx_e, cy_e, False)
    whole = pl.ds(0, PLANES * height)
    writes = [
        pltpu.make_async_copy(halves.at[h, whole, :], out_ref.at[:, pl.ds(h * 128, 128)], out_sems.at[h])
        for h in range(breadth // 128)
    ]
    for write in writes:
        write.start()

    pad = jnp.zeros((8, 128), jnp.bfloat16)
    wide_kernel[...] = jnp.zeros((128, 128), jnp.float32)
    wide_kernel[:64, :PLANES] = kernel_ref[...]
    wide_kernel[64:, :PLANES] = kernel_ref[...]
    turned = wide_kernel[...].T[:PLANES]
    weight_high = turned.astype(jnp.bfloat16)
    weight_low = (turned - weight_high.astype(jnp.float32)).astype(jnp.bfloat16)
    weight = jnp.concatenate([weight_high, pad, weight_high, pad, weight_low, pad], axis=0)

    group = 8

    @pl.loop(0, height // group)
    def _(r):
        blocks = []
        for k in range(group):
            for h in range(breadth // 128):
                spectra = halves[h, pl.ds(r * group + k, PLANES, stride=height), :]
                high = spectra.astype(jnp.bfloat16)
                low = (spectra - high.astype(jnp.float32)).astype(jnp.bfloat16)
                blocks.append(jnp.concatenate([high, pad, low, pad, high, pad], axis=0))
        stacked = jnp.concatenate(blocks, axis=1)
        profile = lax.dot_general(stacked, weight, (((0,), (0,)), ((), ())), preferred_element_type=jnp.float32)
        start = pl.multiple_of(r * group * breadth, 128)
        table[pl.ds(start, group * breadth), :] = profile

    first_half = lax.broadcasted_iota(jnp.int32, (1, 128), 1) < 64
    half = WINDOW // 2

    def pick(cell, i):
        for g in range(WINDOW // 16):
            for j in range(8):
                one, two = cell(16 * g + j), cell(16 * g + 8 + j)
                line = jnp.where(first_half, table[pl.ds(one, 1), :], table[pl.ds(two, 1), :])
                lines[8 * g + j : 8 * g + j + 1, :] = line
        here = pl.ds(pl.multiple_of(i * half, half), half)
        picks[here, :] = lines[...].astype(jnp.bfloat16)
        pltpu.make_async_copy(picks.at[here, :], picked_ref.at[here, :], pick_sem).start()

    for_windows(cells_ref, window, window_sems, pick)
    pltpu.make_async_copy(picks, picked_ref, pick_sem).wait()
    for write in writes:
        write.wait()


def add_kernel(rows_ref, values_ref, out_ref, lines, tile_sums, window, window_sems, out_sem, *sums):
    n_acc = len(sums) // 2
    tile = out_ref.shape[1]
    block = 512
    half = WINDOW // 2

    @pl.loop(0, tile // block)
    def _(i):
        for total in sums:
            total[pl.ds(pl.multiple_of(i * block, block), block), :] = jnp.zeros((block, 128), jnp.float32)

    def add(row, i):
        lines[...] = values_ref[pl.ds(pl.multiple_of(i * half, half), half), :].astype(jnp.float32)
        for g in range(WINDOW // 16):
            for j in range(8):
                one, two = row(16 * g + j), row(16 * g + 8 + j)
                line = lines[8 * g + j : 8 * g + j + 1, :]
                left, right = sums[j % n_acc], sums[n_acc + j % n_acc]
                left[pl.ds(one, 1), :] = left[pl.ds(one, 1), :] + line
                right[pl.ds(two, 1), :] = right[pl.ds(two, 1), :] + line

    for_windows(rows_ref, window, window_sems, add)
    first_half = lax.broadcasted_iota(jnp.int32, (block, 128), 1) < 64

    @pl.loop(0, tile // block)
    def _(i):
        here = pl.ds(pl.multiple_of(i * block, block), block)
        left, right = sums[0][here, :], sums[n_acc][here, :]
        for q in range(1, n_acc):
            left = left + sums[q][here, :]
            right = right + sums[n_acc + q][here, :]
        both = jnp.where(first_half, left, right).T
        tile_sums[:, here] = both[:64] + both[64:]
        pltpu.make_async_copy(tile_sums.at[:, here], out_ref.at[:, here], out_sem).start()

    pltpu.make_async_copy(tile_sums, out_ref, out_sem).wait()


def constant_tables():
    heading = (np.arange(DIRS) + 0.5) * (2.0 * math.pi / DIRS)
    cos = np.repeat(np.cos(heading), FREQ)
    sin = np.repeat(np.sin(heading), FREQ)
    lanes = np.zeros((8, 128))
    q = np.arange(HALF)
    from_west = np.where(q < QUAD, q, q + HALF)
    from_east = q + QUAD
    for column in range(2):
        lanes[0, 2 * q + column] = cos[from_west]
        lanes[1, 2 * q + column] = sin[from_west]
        lanes[2, 2 * q + column] = cos[from_east]
        lanes[3, 2 * q + column] = sin[from_east]
        lanes[4, 2 * q + column] = q % 2
    subs = np.zeros((HALF + 4, 128))
    subs[:HALF, 0], subs[:HALF, 1] = cos[:HALF], sin[:HALF]
    subs[:HALF, 2], subs[:HALF, 3] = cos[HALF:], sin[HALF:]
    return [t.astype(np.float32) for t in (cos, sin, lanes, subs)]


def body(n_lat, n_lon, spectrum, speed_factor, land_sea_mask, courant, depth_kernel, send_rows, recv_rows):
    height, breadth = speed_factor.shape
    devices, slots = send_rows.shape[1:]
    x = spectrum.reshape(PLANES, height, breadth)
    f32 = jnp.float32
    vmem = pl.BlockSpec(memory_space=pltpu.VMEM)
    smem = pl.BlockSpec(memory_space=pltpu.SMEM)
    hbm = pl.BlockSpec(memory_space=pltpu.HBM)
    params = pltpu.CompilerParams(vmem_limit_bytes=VMEM_LIMIT)

    both = ("lat", "lon")

    def shape(*dims, kind=f32):
        return jax.ShapeDtypeStruct(dims, kind)

    cos, sin, lanes, subs = constant_tables()
    row_message = shape(2, HALF + 4, breadth)
    columns = shape(height, 128)
    column_message = shape(height + 8, 128)
    row_first, row_second, column_first, column_second = exchange_pairs(n_lat, n_lon)
    first, second, east, west, moving, sea = pl.pallas_call(
        pack_kernel,
        out_shape=[row_message] * 2 + [columns] * 2 + [shape(height, breadth)] * 2,
        in_specs=[hbm] * 3,
        out_specs=[vmem] * 6,
        scratch_shapes=[pltpu.VMEM((2, HALF + 4, breadth), f32)] * 2
        + [pltpu.VMEM((HALF, 8, breadth), f32)] * 2
        + [pltpu.VMEM((HALF, height, 128), f32)] * 2
        + [pltpu.VMEM((height, breadth), f32), pltpu.VMEM((height, breadth), jnp.int32), pltpu.SemaphoreType.DMA((7,))],
        compiler_params=params,
        name="pack_halos",
    )(*(pltpu.with_memory_space_constraint(v, pltpu.HBM) for v in (x, speed_factor, land_sea_mask)))
    second = lax.ppermute(second, both, row_second)
    first = lax.ppermute(first, "lat", row_first)
    halves = pl.pallas_call(
        inside_kernel,
        out_shape=pltpu.VMEM((breadth // 128, (PLANES + 4) * height, 128), f32),
        in_specs=[smem] * 3 + [vmem] * 3,
        out_specs=vmem,
        compiler_params=params,
        cost_estimate=pl.CostEstimate(flops=4_000_000_000, bytes_accessed=5_000_000, transcendentals=0),
        name="advance_inside",
    )(courant, cos, sin, x, moving, sea)
    south, north, first, second = pl.pallas_call(
        functools.partial(corner_kernel, n_lat),
        out_shape=[row_message] * 2 + [column_message] * 2,
        in_specs=[vmem] * 4,
        out_specs=[vmem] * 4,
        compiler_params=params,
        name="add_corners",
    )(first, second, east, west)
    second = lax.ppermute(second, "lon", column_second)
    first = lax.ppermute(first, "lon", column_first)

    cells = jnp.maximum(send_rows, 0).reshape(-1)
    targets = jnp.where(recv_rows < 0, OUT_DEV, recv_rows).reshape(-1)
    slot_rows = devices * slots // 2
    propagated, picked, _ = pl.pallas_call(
        finish_kernel,
        out_shape=[
            pltpu.HBM((PLANES * height, breadth), f32),
            pltpu.HBM((slot_rows, 128), jnp.bfloat16),
            pltpu.VMEM(halves.shape, f32),
        ],
        in_specs=[smem, hbm] + [vmem] * 10,
        out_specs=[hbm, hbm, vmem],
        input_output_aliases={11: 2},
        scratch_shapes=[
            pltpu.VMEM((height * breadth, 128), f32),
            pltpu.VMEM((WINDOW // 2, 128), f32),
            pltpu.VMEM((slot_rows, 128), jnp.bfloat16),
            pltpu.VMEM((128, 128), f32),
            pltpu.SMEM((2 * WINDOW,), jnp.int32),
            pltpu.SemaphoreType.DMA((breadth // 128,)),
            pltpu.SemaphoreType.DMA((2,)),
            pltpu.SemaphoreType.DMA,
        ],
        compiler_params=params,
        name="finish_and_pick",
    )(courant, cells, moving, sea, depth_kernel, south, north, first, second, lanes, subs, halves)

    picked = picked.reshape(devices, slots // 2, 128)
    received = lax.all_to_all(picked, both, split_axis=0, concat_axis=0, tiled=True)

    components = depth_kernel.shape[0]
    stokes = pl.pallas_call(
        add_kernel,
        out_shape=pltpu.HBM((components, OUT_DEV), f32),
        in_specs=[hbm, vmem],
        out_specs=hbm,
        scratch_shapes=[
            pltpu.VMEM((WINDOW // 2, 128), f32),
            pltpu.VMEM((components, OUT_DEV), f32),
            pltpu.SMEM((2 * WINDOW,), jnp.int32),
            pltpu.SemaphoreType.DMA((2,)),
            pltpu.SemaphoreType.DMA,
        ]
        + [pltpu.VMEM((OUT_DEV + 8, 128), f32)] * (2 * N_ACC),
        compiler_params=params,
        name="add_profiles",
    )(targets, received.reshape(slot_rows, 128))
    return propagated.reshape(DIRS, FREQ, height, breadth), stokes


def solution(mesh):
    placed = (
        P(None, None, "lat", "lon"),
        P("lat", "lon"),
        P("lat", "lon"),
        P(),
        P(),
        P(("lat", "lon"), None, None),
        P(("lat", "lon"), None, None),
    )
    return jax.shard_map(
        functools.partial(body, mesh.shape["lat"], mesh.shape["lon"]),
        mesh=mesh,
        in_specs=placed,
        out_specs=(P(None, None, "lat", "lon"), P(None, ("lat", "lon"))),
        check_vma=False,
    )
```

```python
import functools
import math

import jax
import jax.numpy as jnp
import numpy as np
from jax import lax
from jax.experimental import pallas as pl
from jax.experimental.pallas import tpu as pltpu
from jax.sharding import PartitionSpec as P

DIRS = 36
FREQ = 2
PLANES = DIRS * FREQ
HALF = PLANES // 2
QUAD = PLANES // 4
OUT_DEV = 4096
SPARE = 64
N_ACC = 4
WINDOW = 1024
VMEM_LIMIT = 16 * 1024 * 1024


def exchange_pairs(n_lat, n_lon):
    def flat(j, i):
        return j * n_lon + i % n_lon

    row_first = [(j, j ^ 1) for j in range(n_lat)]
    row_second = []
    for i in range(n_lon):
        row_second += [(flat(0, i), flat(0, i)), (flat(n_lat - 1, i), flat(n_lat - 1, n_lon - 1 - i))]
        for j in range(1, n_lat - 1, 2):
            row_second += [(flat(j, i), flat(j + 1, i)), (flat(j + 1, i), flat(j, i))]
    column_first = [(i, i ^ 1) for i in range(n_lon)]
    column_second = [(i, (i + 1 if i % 2 else i - 1) % n_lon) for i in range(n_lon)]
    return row_first, row_second, column_first, column_second


def pack_rows_kernel(x_hbm, speed_hbm, mask_hbm, first_ref, second_ref, mov_ref, sea_ref,
                     up_ref, down_ref, top_rows, bottom_rows, speed_ref, mask_ref, sems):
    height, breadth = speed_ref.shape
    copies = [
        pltpu.make_async_copy(source, target, sems.at[k])
        for k, (source, target) in enumerate((
            (speed_hbm, speed_ref),
            (mask_hbm, mask_ref),
            (x_hbm.at[pl.ds(0, HALF), pl.ds(height - 8, 8), :], top_rows),
            (x_hbm.at[pl.ds(HALF, HALF), pl.ds(0, 8), :], bottom_rows),
        ))
    ]
    for copy in copies:
        copy.start()
    even = lax.axis_index("lat") % 2 == 0
    for copy in copies:
        copy.wait()
    sea = mask_ref[...].astype(jnp.float32)
    moving = speed_ref[...] * sea
    mov_ref[...] = moving
    sea_ref[...] = sea
    for k in range(2):
        for q in range(HALF):
            up_ref[k, q : q + 1, :] = top_rows[q, 7 - k : 8 - k, :]
            down_ref[k, q : q + 1, :] = bottom_rows[q, k : k + 1, :]
        up_ref[k, HALF : HALF + 1, :] = moving[height - 1 - k : height - k, :]
        down_ref[k, HALF : HALF + 1, :] = moving[k : k + 1, :]
        up_ref[k, HALF + 1 : HALF + 2, :] = sea[height - 1 - k : height - k, :]
        down_ref[k, HALF + 1 : HALF + 2, :] = sea[k : k + 1, :]
        up_ref[k, HALF + 2 :, :] = jnp.zeros((2, breadth), jnp.float32)
        down_ref[k, HALF + 2 :, :] = jnp.zeros((2, breadth), jnp.float32)

    @pl.when(even)
    def _():
        first_ref[...] = up_ref[...]
        second_ref[...] = down_ref[...]

    @pl.when(jnp.logical_not(even))
    def _():
        first_ref[...] = down_ref[...]
        second_ref[...] = up_ref[...]


def pack_columns_kernel(x_ref, mov_ref, sea_ref, east_ref, west_ref):
    height, breadth = mov_ref.shape
    lane = lax.broadcasted_iota(jnp.int32, (height, 128), 1)
    east = jnp.zeros((height, 128), jnp.float32)
    west = jnp.zeros((height, 128), jnp.float32)
    for q in range(HALF + 2):
        mine = lane // 2 == q
        if q < HALF:
            p_e = q if q < QUAD else q + HALF
            edge_e, edge_w = x_ref[p_e, :, breadth - 128 :], x_ref[q + QUAD, :, :128]
        else:
            field = (mov_ref if q == HALF else sea_ref)[...]
            edge_e, edge_w = field[:, breadth - 128 :], field[:, :128]
        east = jnp.where(mine, pltpu.roll(edge_e, (2 * q + 2) % 128, axis=1), east)
        west = jnp.where(mine, pltpu.roll(edge_w, 2 * q, axis=1), west)
    east_ref[...] = east
    west_ref[...] = west


def corner_kernel(n_lat, first_ref, second_ref, east_ref, west_ref, south_ref, north_ref, out_first, out_second):
    height = east_ref.shape[0]
    breadth = first_ref.shape[2]
    lat = lax.axis_index("lat")
    even = lat % 2 == 0

    @pl.when(even)
    def _():
        north_ref[...] = first_ref[...]
        south_ref[...] = second_ref[...]

    @pl.when(jnp.logical_not(even))
    def _():
        south_ref[...] = first_ref[...]
        north_ref[...] = second_ref[...]

    @pl.when(lat == 0)
    def _():
        south_ref[...] = jnp.zeros_like(south_ref)

    @pl.when(lat == n_lat - 1)
    def _():
        flip_i = lax.broadcasted_iota(jnp.int32, (breadth, breadth), 0)
        flip_j = lax.broadcasted_iota(jnp.int32, (breadth, breadth), 1)
        flip = (flip_i + flip_j == breadth - 1).astype(jnp.float32)
        for k in range(2):
            north_ref[k] = jnp.dot(
                north_ref[k], flip, precision=lax.Precision.HIGHEST, preferred_element_type=jnp.float32
            )

    plane = lax.broadcasted_iota(jnp.int32, (HALF + 4, 128), 0)
    lane = lax.broadcasted_iota(jnp.int32, (HALF + 4, 128), 1)
    south = south_ref[0] * south_ref[0, HALF : HALF + 1, :]
    north = north_ref[0] * north_ref[0, HALF : HALF + 1, :]

    def to_lanes(column, low, high, place):
        mine = (plane >= low) & (plane < high) & (lane == place)
        return jnp.where(mine, column, 0.0)

    east_edge = to_lanes(south[:, breadth - 1 :], 0, QUAD, 2 * plane + 1)
    east_edge += to_lanes(north[:, breadth - 1 :], QUAD, HALF, 2 * plane + 1)
    west_edge = to_lanes(south[:, :1], QUAD, HALF, 2 * plane - HALF)
    west_edge += to_lanes(north[:, :1], 0, QUAD, 2 * plane + HALF)
    east_edge = jnp.broadcast_to(jnp.sum(east_edge, axis=0, keepdims=True), (8, 128))
    west_edge = jnp.broadcast_to(jnp.sum(west_edge, axis=0, keepdims=True), (8, 128))
    even_lon = lax.axis_index("lon") % 2 == 0
    out_first[:height] = jnp.where(even_lon, east_ref[...], west_ref[...])
    out_second[:height] = jnp.where(even_lon, west_ref[...], east_ref[...])
    out_first[height:] = jnp.where(even_lon, east_edge, west_edge)
    out_second[height:] = jnp.where(even_lon, west_edge, east_edge)


def for_windows(list_ref, window, sems, work):
    count = list_ref.shape[0] // WINDOW

    def fetch(i, w):
        source = list_ref.at[pl.ds(pl.multiple_of(i * WINDOW, WINDOW), WINDOW)]
        return pltpu.make_async_copy(source, window.at[pl.ds(w * WINDOW, WINDOW)], sems.at[w])

    for w in range(2):
        fetch(w, w).start()

    @pl.loop(0, count // 2)
    def _(t):
        for w in range(2):
            i = 2 * t + w
            fetch(i, w).wait()
            work(lambda k, start=w * WINDOW: window[start + k], i)

            @pl.when(i + 2 < count)
            def _():
                fetch(i + 2, w).start()


def inside_kernel(courant_ref, cos_ref, sin_ref, x_ref, mov_ref, sea_ref, halves):
    height, breadth = mov_ref.shape
    c0, c1 = courant_ref[0], courant_ref[1]
    moving = mov_ref[...]
    sea = sea_ref[...]
    lane = lax.broadcasted_iota(jnp.int32, (height, 128), 1)
    row = lax.broadcasted_iota(jnp.int32, (8, breadth), 0)
    for h in range(breadth // 128):
        halves[h, PLANES * height :, :] = jnp.zeros((4 * height, 128), jnp.float32)

    def quadrant(first, from_west, from_south):
        def upstream(flux):
            if from_west:
                moved = pltpu.roll(flux, 1, axis=1)
                side = jnp.concatenate([jnp.where(lane == 0, 0.0, moved[:, :128]), moved[:, 128:]], axis=1)
            else:
                moved = pltpu.roll(flux, breadth - 1, axis=1)
                edge = jnp.where(lane == 127, 0.0, moved[:, breadth - 128 :])
                side = jnp.concatenate([moved[:, : breadth - 128], edge], axis=1)
            if from_south:
                moved = pltpu.roll(flux, 1, axis=0)
                below = jnp.concatenate([jnp.where(row == 0, 0.0, moved[:8]), moved[8:]], axis=0)
            else:
                moved = pltpu.roll(flux, height - 1, axis=0)
                below = jnp.concatenate([moved[: height - 8], jnp.where(row == 7, 0.0, moved[height - 8 :])], axis=0)
            return side, below

        def step(t, carry):
            p = first + t
            courant = jnp.where(p % 2 == 1, c1, c0)
            cx = cos_ref[p] * courant
            cy = sin_ref[p] * courant
            energy = x_ref[p]
            for _ in range(2):
                flux = moving * energy
                side, below = upstream(flux)
                div_x = cx * (flux - side) if from_west else cx * (side - flux)
                div_y = cy * (flux - below) if from_south else cy * (below - flux)
                energy = sea * ((energy - div_x) - div_y)
            start = pl.ds(pl.multiple_of(p * height, height), height)
            for h in range(breadth // 128):
                halves[h, start, :] = energy[:, h * 128 : (h + 1) * 128]
            return carry

        lax.fori_loop(0, QUAD, step, 0, unroll=6)

    quadrant(0, True, True)
    quadrant(QUAD, False, True)
    quadrant(2 * QUAD, False, False)
    quadrant(3 * QUAD, True, False)


def finish_kernel(courant_ref, cells_ref, mov_ref, sea_ref, kernel_ref, south_ref, north_ref, first_ref, second_ref,
                  lanes_ref, subs_ref, halves_in, out_ref, picked_ref, halves,
                  table, lines, picks, wide_kernel, window, out_sems, window_sems, pick_sem):
    height, breadth = mov_ref.shape
    c0, c1 = courant_ref[0], courant_ref[1]
    even_lon = lax.axis_index("lon") % 2 == 0
    from_west = jnp.where(even_lon, second_ref[...], first_ref[...])
    from_east = jnp.where(even_lon, first_ref[...], second_ref[...])
    corner_w, corner_e = from_west[height : height + 1], from_east[height : height + 1]

    lane = lax.broadcasted_iota(jnp.int32, (height, 128), 1)
    row = lax.broadcasted_iota(jnp.int32, (height, 128), 0)
    odd = lane % 2 == 1

    def columns(e0, near, far, corner, cx, cy, sign):
        mov = jnp.where(odd, e0[:, 2 * HALF + 1 : 2 * HALF + 2], e0[:, 2 * HALF : 2 * HALF + 1])
        sea = e0[:, 2 * HALF + 2 + near : 2 * HALF + 3 + near]
        f0 = mov * e0
        f_far = pltpu.roll(f0, 1 if near > far else 127, axis=1)
        f_south = jnp.where(row == 0, corner, pltpu.roll(f0, 1, axis=0))
        f_north = jnp.where(row == height - 1, corner, pltpu.roll(f0, height - 1, axis=0))
        div_x = cx * (f0 - f_far) if sign > 0 else cx * (f_far - f0)
        div_y = jnp.where(lane < HALF, cy * (f0 - f_south), cy * (f_north - f0))
        return f0, mov * (sea * ((e0 - div_x) - div_y))

    lanes = lanes_ref[...]
    lane_courant = jnp.where(lanes[4:5] > 0.5, c1, c0)
    cx_w, cy_w, cx_e, cy_e = (lanes[k : k + 1] * lane_courant for k in range(4))
    west_flux0, west_flux1 = columns(from_west[:height], 1, 0, corner_w, cx_w, cy_w, 1)
    east_flux0, east_flux1 = columns(from_east[:height], 0, 1, corner_e, cx_e, cy_e, -1)

    wide = lax.broadcasted_iota(jnp.int32, (HALF + 4, breadth), 1)
    plane = lax.broadcasted_iota(jnp.int32, (HALF + 4, 1), 0)
    plane_l = lax.broadcasted_iota(jnp.int32, (HALF + 4, 128), 0)
    lane_l = lax.broadcasted_iota(jnp.int32, (HALF + 4, 128), 1)
    subs = subs_ref[...]
    sub_courant = jnp.where(plane % 2 == 1, c1, c0)

    def to_sublanes(corner, lane_of):
        return jnp.sum(jnp.where(lane_l == lane_of, corner, 0.0), axis=1, keepdims=True)

    def rows(near, far, first_west, west_corner, east_corner, cx, cy, sign):
        mov, sea = near[HALF : HALF + 1], near[HALF + 1 : HALF + 2]
        f0 = mov * near
        f_far = far[HALF : HALF + 1] * far
        f_west = jnp.where(wide == 0, west_corner, pltpu.roll(f0, 1, axis=1))
        f_east = jnp.where(wide == breadth - 1, east_corner, pltpu.roll(f0, breadth - 1, axis=1))
        from_west = (plane < QUAD) if first_west else (plane >= QUAD)
        div_x = jnp.where(from_west, cx * (f0 - f_west), cx * (f_east - f0))
        div_y = cy * (f0 - f_far) if sign > 0 else cy * (f_far - f0)
        return f0, mov * (sea * ((near - div_x) - div_y))

    sw = to_sublanes(corner_w, 2 * plane_l + 1)
    se = to_sublanes(corner_e, 2 * plane_l - HALF)
    ne = to_sublanes(corner_e, 2 * plane_l + HALF)
    nw = sw
    cx_s, cy_s, cx_n, cy_n = (subs[:, k : k + 1] * sub_courant for k in range(4))
    south_flux0, south_flux1 = rows(south_ref[0], south_ref[1], True, sw, se, cx_s, cy_s, 1)
    north_flux0, north_flux1 = rows(north_ref[0], north_ref[1], False, nw, ne, cx_n, cy_n, -1)

    def add_rows(first, near, next_row, flux0, flux1, cx, cy, first_west):
        sea0, sea1 = sea_ref[near : near + 1, :], sea_ref[next_row : next_row + 1, :]
        change = sea0 * (cy * flux0)
        flux = mov_ref[near : near + 1, :] * change
        west_flux = jnp.where(wide == 0, 0.0, pltpu.roll(flux, 1, axis=1))
        east_flux = jnp.where(wide == breadth - 1, 0.0, pltpu.roll(flux, breadth - 1, axis=1))
        from_west = (plane < QUAD) if first_west else (plane >= QUAD)
        div_x = jnp.where(from_west, cx * (flux - west_flux), cx * (east_flux - flux))
        near_change = sea0 * (((change - div_x) - cy * flux) + cy * flux1)
        next_change = sea1 * (cy * flux)
        for at, delta in ((near, near_change), (next_row, next_change)):
            for h in range(breadth // 128):
                place = pl.ds(first * height + at, HALF + 4, stride=height)
                halves[h, place, :] = halves[h, place, :] + delta[:, h * 128 : (h + 1) * 128]

    def add_columns(half, near, next_column, flux0, flux1, cx, cy, from_west):
        sea0, sea1 = sea_ref[:, near : near + 1], sea_ref[:, next_column : next_column + 1]
        change = sea0 * (cx * flux0)
        flux = mov_ref[:, near : near + 1] * change
        south_flux = jnp.where(row == 0, 0.0, pltpu.roll(flux, 1, axis=0))
        north_flux = jnp.where(row == height - 1, 0.0, pltpu.roll(flux, height - 1, axis=0))
        div_y = jnp.where(lane < HALF, cy * (flux - south_flux), cy * (north_flux - flux))
        near_change = sea0 * (((change - cx * flux) - div_y) + cx * flux1)
        next_change = sea1 * (cx * flux)
        if from_west:
            both = jnp.where(odd, next_change, pltpu.roll(near_change, 127, axis=1))
        else:
            both = jnp.where(odd, pltpu.roll(near_change, 1, axis=1), next_change)
        edge = lane < 2 if from_west else lane >= 126
        for q in range(HALF):
            p = q + QUAD if not from_west else (q if q < QUAD else q + HALF)
            turned = pltpu.roll(both, ((128 if from_west else 126) - 2 * q) % 128, axis=1)
            place = pl.ds(p * height, height)
            halves[half, place, :] = halves[half, place, :] + jnp.where(edge, turned, 0.0)

    add_rows(0, 0, 1, south_flux0, south_flux1, cx_s, cy_s, True)
    add_rows(HALF, height - 1, height - 2, north_flux0, north_flux1, cx_n, -cy_n, False)
    add_columns(0, 0, 1, west_flux0, west_flux1, cx_w, cy_w, True)
    add_columns(breadth // 128 - 1, breadth - 1, breadth - 2, east_flux0, east_flux1, -cx_e, cy_e, False)
    whole = pl.ds(0, PLANES * height)
    writes = [
        pltpu.make_async_copy(halves.at[h, whole, :], out_ref.at[:, pl.ds(h * 128, 128)], out_sems.at[h])
        for h in range(breadth // 128)
    ]
    for write in writes:
        write.start()

    pad = jnp.zeros((8, 128), jnp.bfloat16)
    wide_kernel[...] = jnp.zeros((128, 128), jnp.float32)
    wide_kernel[:64, :PLANES] = kernel_ref[...]
    wide_kernel[64:, :PLANES] = kernel_ref[...]
    turned = wide_kernel[...].T[:PLANES]
    weight_high = turned.astype(jnp.bfloat16)
    weight_low = (turned - weight_high.astype(jnp.float32)).astype(jnp.bfloat16)
    weight = jnp.concatenate([weight_high, pad, weight_high, pad, weight_low, pad], axis=0)

    group = 8

    @pl.loop(0, height // group)
    def _(r):
        blocks = []
        for k in range(group):
            for h in range(breadth // 128):
                spectra = halves[h, pl.ds(r * group + k, PLANES, stride=height), :]
                high = spectra.astype(jnp.bfloat16)
                low = (spectra - high.astype(jnp.float32)).astype(jnp.bfloat16)
                blocks.append(jnp.concatenate([high, pad, low, pad, high, pad], axis=0))
        stacked = jnp.concatenate(blocks, axis=1)
        profile = lax.dot_general(stacked, weight, (((0,), (0,)), ((), ())), preferred_element_type=jnp.float32)
        start = pl.multiple_of(r * group * breadth, 128)
        table[pl.ds(start, group * breadth), :] = profile

    first_half = lax.broadcasted_iota(jnp.int32, (1, 128), 1) < 64
    half = WINDOW // 2

    def pick(cell, i):
        for g in range(WINDOW // 16):
            for j in range(8):
                one, two = cell(16 * g + j), cell(16 * g + 8 + j)
                line = jnp.where(first_half, table[pl.ds(one, 1), :], table[pl.ds(two, 1), :])
                lines[8 * g + j : 8 * g + j + 1, :] = line
        here = pl.ds(pl.multiple_of(i * half, half), half)
        picks[here, :] = lines[...].astype(jnp.bfloat16)
        pltpu.make_async_copy(picks.at[here, :], picked_ref.at[here, :], pick_sem).start()

    for_windows(cells_ref, window, window_sems, pick)
    pltpu.make_async_copy(picks, picked_ref, pick_sem).wait()
    for write in writes:
        write.wait()


def clear_kernel(_, *sums):
    block = 520

    @pl.loop(0, sums[0].shape[0] // block)
    def _(i):
        for total in sums:
            total[pl.ds(pl.multiple_of(i * block, 8), block), :] = jnp.zeros((block, 128), jnp.float32)


def add_kernel(rows_ref, values_ref, *refs):
    n_acc = N_ACC
    out_ref, sums = refs[2 * n_acc], refs[2 * n_acc + 1 : 4 * n_acc + 1]
    lines, tile_sums, window, window_sems, out_sem = refs[4 * n_acc + 1 :]
    tile = out_ref.shape[1]
    block = 512
    half = WINDOW // 2

    def add(row, i):
        lines[...] = values_ref[pl.ds(pl.multiple_of(i * half, half), half), :].astype(jnp.float32)
        for g in range(WINDOW // 16):
            for j in range(8):
                one, two = row(16 * g + j), row(16 * g + 8 + j)
                line = lines[8 * g + j : 8 * g + j + 1, :]
                left, right = sums[j % n_acc], sums[n_acc + j % n_acc]
                left[pl.ds(one, 1), :] = left[pl.ds(one, 1), :] + line
                right[pl.ds(two, 1), :] = right[pl.ds(two, 1), :] + line

    for_windows(rows_ref, window, window_sems, add)
    first_half = lax.broadcasted_iota(jnp.int32, (block, 128), 1) < 64

    @pl.loop(0, tile // block)
    def _(i):
        here = pl.ds(pl.multiple_of(i * block, block), block)
        left, right = sums[0][here, :], sums[n_acc][here, :]
        for q in range(1, n_acc):
            left = left + sums[q][here, :]
            right = right + sums[n_acc + q][here, :]
        both = jnp.where(first_half, left, right).T
        tile_sums[:, here] = both[:64] + both[64:]
        pltpu.make_async_copy(tile_sums.at[:, here], out_ref.at[:, here], out_sem).start()

    pltpu.make_async_copy(tile_sums, out_ref, out_sem).wait()


def constant_tables():
    heading = (np.arange(DIRS) + 0.5) * (2.0 * math.pi / DIRS)
    cos = np.repeat(np.cos(heading), FREQ)
    sin = np.repeat(np.sin(heading), FREQ)
    lanes = np.zeros((8, 128))
    q = np.arange(HALF)
    from_west = np.where(q < QUAD, q, q + HALF)
    from_east = q + QUAD
    for column in range(2):
        lanes[0, 2 * q + column] = cos[from_west]
        lanes[1, 2 * q + column] = sin[from_west]
        lanes[2, 2 * q + column] = cos[from_east]
        lanes[3, 2 * q + column] = sin[from_east]
        lanes[4, 2 * q + column] = q % 2
    subs = np.zeros((HALF + 4, 128))
    subs[:HALF, 0], subs[:HALF, 1] = cos[:HALF], sin[:HALF]
    subs[:HALF, 2], subs[:HALF, 3] = cos[HALF:], sin[HALF:]
    return [t.astype(np.float32) for t in (cos, sin, lanes, subs)]


def body(n_lat, n_lon, spectrum, speed_factor, land_sea_mask, courant, depth_kernel, send_rows, recv_rows):
    height, breadth = speed_factor.shape
    devices, slots = send_rows.shape[1:]
    x = spectrum.reshape(PLANES, height, breadth)
    f32 = jnp.float32
    vmem = pl.BlockSpec(memory_space=pltpu.VMEM)
    smem = pl.BlockSpec(memory_space=pltpu.SMEM)
    hbm = pl.BlockSpec(memory_space=pltpu.HBM)
    params = pltpu.CompilerParams(vmem_limit_bytes=VMEM_LIMIT)

    both = ("lat", "lon")

    def shape(*dims, kind=f32):
        return jax.ShapeDtypeStruct(dims, kind)

    cos, sin, lanes, subs = constant_tables()
    row_message = shape(2, HALF + 4, breadth)
    columns = shape(height, 128)
    column_message = shape(height + 8, 128)
    row_first, row_second, column_first, column_second = exchange_pairs(n_lat, n_lon)
    first, second, moving, sea = pl.pallas_call(
        pack_rows_kernel,
        out_shape=[row_message] * 2 + [shape(height, breadth)] * 2,
        in_specs=[hbm] * 3,
        out_specs=[vmem] * 4,
        scratch_shapes=[pltpu.VMEM((2, HALF + 4, breadth), f32)] * 2
        + [pltpu.VMEM((HALF, 8, breadth), f32)] * 2
        + [pltpu.VMEM((height, breadth), f32), pltpu.VMEM((height, breadth), jnp.int32), pltpu.SemaphoreType.DMA((4,))],
        compiler_params=params,
        name="pack_rows",
    )(*(pltpu.with_memory_space_constraint(v, pltpu.HBM) for v in (x, speed_factor, land_sea_mask)))
    second = lax.ppermute(second, both, row_second)
    first = lax.ppermute(first, "lat", row_first)
    east, west = pl.pallas_call(
        pack_columns_kernel,
        out_shape=[columns] * 2,
        in_specs=[vmem] * 3,
        out_specs=[vmem] * 2,
        compiler_params=params,
        cost_estimate=pl.CostEstimate(flops=2_000_000_000, bytes_accessed=5_000_000, transcendentals=0),
        name="pack_columns",
    )(x, moving, sea)
    halves = pl.pallas_call(
        inside_kernel,
        out_shape=pltpu.VMEM((breadth // 128, (PLANES + 4) * height, 128), f32),
        in_specs=[smem] * 3 + [vmem] * 3,
        out_specs=vmem,
        compiler_params=params,
        cost_estimate=pl.CostEstimate(flops=4_000_000_000, bytes_accessed=5_000_000, transcendentals=0),
        name="advance_inside",
    )(courant, cos, sin, x, moving, sea)
    south, north, first, second = pl.pallas_call(
        functools.partial(corner_kernel, n_lat),
        out_shape=[row_message] * 2 + [column_message] * 2,
        in_specs=[vmem] * 4,
        out_specs=[vmem] * 4,
        compiler_params=params,
        name="add_corners",
    )(first, second, east, west)
    second = lax.ppermute(second, "lon", column_second)
    first = lax.ppermute(first, "lon", column_first)

    cells = jnp.maximum(send_rows, 0).reshape(-1)
    slot = jnp.arange(slots, dtype=jnp.int32)
    spare = OUT_DEV + (slot // 16 * 8 + slot % 8) % SPARE
    targets = jnp.where(recv_rows < 0, spare, recv_rows).reshape(-1)
    slot_rows = devices * slots // 2
    propagated, picked, _ = pl.pallas_call(
        finish_kernel,
        out_shape=[
            pltpu.HBM((PLANES * height, breadth), f32),
            pltpu.HBM((slot_rows, 128), jnp.bfloat16),
            pltpu.VMEM(halves.shape, f32),
        ],
        in_specs=[smem, hbm] + [vmem] * 10,
        out_specs=[hbm, hbm, vmem],
        input_output_aliases={11: 2},
        scratch_shapes=[
            pltpu.VMEM((height * breadth, 128), f32),
            pltpu.VMEM((WINDOW // 2, 128), f32),
            pltpu.VMEM((slot_rows, 128), jnp.bfloat16),
            pltpu.VMEM((128, 128), f32),
            pltpu.SMEM((2 * WINDOW,), jnp.int32),
            pltpu.SemaphoreType.DMA((breadth // 128,)),
            pltpu.SemaphoreType.DMA((2,)),
            pltpu.SemaphoreType.DMA,
        ],
        compiler_params=params,
        name="finish_and_pick",
    )(courant, cells, moving, sea, depth_kernel, south, north, first, second, lanes, subs, halves)

    picked = picked.reshape(devices, slots // 2, 128)
    received = lax.all_to_all(picked, both, split_axis=0, concat_axis=0, tiled=True)

    components = depth_kernel.shape[0]
    sums = [pltpu.VMEM((OUT_DEV + SPARE, 128), f32)] * (2 * N_ACC)
    cleared = pl.pallas_call(
        clear_kernel,
        out_shape=sums,
        in_specs=[hbm],
        out_specs=[vmem] * len(sums),
        compiler_params=params,
        cost_estimate=pl.CostEstimate(flops=2_000_000_000, bytes_accessed=17_000_000, transcendentals=0),
        name="clear_sums",
    )(pltpu.with_memory_space_constraint(picked, pltpu.HBM))
    stokes, *_ = pl.pallas_call(
        add_kernel,
        out_shape=[pltpu.HBM((components, OUT_DEV), f32)] + sums,
        in_specs=[hbm, vmem] + [vmem] * len(sums),
        out_specs=[hbm] + [vmem] * len(sums),
        input_output_aliases={2 + k: 1 + k for k in range(len(sums))},
        scratch_shapes=[
            pltpu.VMEM((WINDOW // 2, 128), f32),
            pltpu.VMEM((components, OUT_DEV), f32),
            pltpu.SMEM((2 * WINDOW,), jnp.int32),
            pltpu.SemaphoreType.DMA((2,)),
            pltpu.SemaphoreType.DMA,
        ],
        compiler_params=params,
        name="add_profiles",
    )(targets, received.reshape(slot_rows, 128), *cleared)
    return propagated.reshape(DIRS, FREQ, height, breadth), stokes


def solution(mesh):
    placed = (
        P(None, None, "lat", "lon"),
        P("lat", "lon"),
        P("lat", "lon"),
        P(),
        P(),
        P(("lat", "lon"), None, None),
        P(("lat", "lon"), None, None),
    )
    return jax.shard_map(
        functools.partial(body, mesh.shape["lat"], mesh.shape["lon"]),
        mesh=mesh,
        in_specs=placed,
        out_specs=(P(None, None, "lat", "lon"), P(None, ("lat", "lon"))),
        check_vma=False,
    )
```

```python
import functools
import math

import jax
import jax.numpy as jnp
import numpy as np
from jax import lax
from jax.experimental import pallas as pl
from jax.experimental.pallas import tpu as pltpu
from jax.sharding import PartitionSpec as P

DIRS = 36
FREQ = 2
PLANES = DIRS * FREQ
HALF = PLANES // 2
QUAD = PLANES // 4
OUT_DEV = 4096
SPARE = 64
N_ACC = 4
ROWS = HALF + 12
WINDOW = 1024
VMEM_LIMIT = 16 * 1024 * 1024
ADD_VMEM_LIMIT = 32 * 1024 * 1024


def exchange_pairs(n_lat, n_lon):
    def flat(j, i):
        return j * n_lon + i % n_lon

    row_first = [(j, j ^ 1) for j in range(n_lat)]
    row_second = []
    for i in range(n_lon):
        row_second += [(flat(0, i), flat(0, i)), (flat(n_lat - 1, i), flat(n_lat - 1, n_lon - 1 - i))]
        for j in range(1, n_lat - 1, 2):
            row_second += [(flat(j, i), flat(j + 1, i)), (flat(j + 1, i), flat(j, i))]
    column_first = [(i, i ^ 1) for i in range(n_lon)]
    column_second = [(i, (i + 1 if i % 2 else i - 1) % n_lon) for i in range(n_lon)]
    return row_first, row_second, column_first, column_second


def pack_rows_kernel(x_hbm, speed_hbm, mask_hbm, first_ref, second_ref, mov_ref, sea_ref,
                     up_ref, down_ref, top_rows, bottom_rows, speed_ref, mask_ref, sems):
    height, breadth = speed_ref.shape
    copies = [
        pltpu.make_async_copy(source, target, sems.at[k])
        for k, (source, target) in enumerate((
            (speed_hbm, speed_ref),
            (mask_hbm, mask_ref),
            (x_hbm.at[pl.ds(0, HALF), pl.ds(height - 8, 8), :], top_rows),
            (x_hbm.at[pl.ds(HALF, HALF), pl.ds(0, 8), :], bottom_rows),
        ))
    ]
    for copy in copies:
        copy.start()
    even = lax.axis_index("lat") % 2 == 0
    for copy in copies:
        copy.wait()
    sea = mask_ref[...].astype(jnp.float32)
    moving = speed_ref[...] * sea
    mov_ref[...] = moving
    sea_ref[...] = sea
    for k in range(2):
        for q in range(HALF):
            up_ref[k, q : q + 1, :] = top_rows[q, 7 - k : 8 - k, :]
            down_ref[k, q : q + 1, :] = bottom_rows[q, k : k + 1, :]
        up_ref[k, HALF : HALF + 1, :] = moving[height - 1 - k : height - k, :]
        down_ref[k, HALF : HALF + 1, :] = moving[k : k + 1, :]
        up_ref[k, HALF + 1 : HALF + 2, :] = sea[height - 1 - k : height - k, :]
        down_ref[k, HALF + 1 : HALF + 2, :] = sea[k : k + 1, :]
        up_ref[k, HALF + 2 :, :] = jnp.zeros((ROWS - HALF - 2, breadth), jnp.float32)
        down_ref[k, HALF + 2 :, :] = jnp.zeros((ROWS - HALF - 2, breadth), jnp.float32)

    @pl.when(even)
    def _():
        first_ref[...] = up_ref[...].astype(jnp.bfloat16)
        second_ref[...] = down_ref[...].astype(jnp.bfloat16)

    @pl.when(jnp.logical_not(even))
    def _():
        first_ref[...] = down_ref[...].astype(jnp.bfloat16)
        second_ref[...] = up_ref[...].astype(jnp.bfloat16)


def pack_columns_kernel(x_ref, mov_ref, sea_ref, east_ref, west_ref):
    height, breadth = mov_ref.shape
    lane = lax.broadcasted_iota(jnp.int32, (height, 128), 1)
    east = jnp.zeros((height, 128), jnp.float32)
    west = jnp.zeros((height, 128), jnp.float32)
    for q in range(HALF + 2):
        mine = lane // 2 == q
        if q < HALF:
            p_e = q if q < QUAD else q + HALF
            edge_e, edge_w = x_ref[p_e, :, breadth - 128 :], x_ref[q + QUAD, :, :128]
        else:
            field = (mov_ref if q == HALF else sea_ref)[...]
            edge_e, edge_w = field[:, breadth - 128 :], field[:, :128]
        east = jnp.where(mine, pltpu.roll(edge_e, (2 * q + 2) % 128, axis=1), east)
        west = jnp.where(mine, pltpu.roll(edge_w, 2 * q, axis=1), west)
    east_ref[...] = east
    west_ref[...] = west


def corner_kernel(n_lat, first_ref, second_ref, east_ref, west_ref, south_ref, north_ref, out_first, out_second):
    height = east_ref.shape[0]
    breadth = first_ref.shape[2]
    lat = lax.axis_index("lat")
    even = lat % 2 == 0

    used = HALF + 4

    @pl.when(even)
    def _():
        north_ref[...] = first_ref[...].astype(jnp.float32)[:, :used]
        south_ref[...] = second_ref[...].astype(jnp.float32)[:, :used]

    @pl.when(jnp.logical_not(even))
    def _():
        south_ref[...] = first_ref[...].astype(jnp.float32)[:, :used]
        north_ref[...] = second_ref[...].astype(jnp.float32)[:, :used]

    @pl.when(lat == 0)
    def _():
        south_ref[...] = jnp.zeros_like(south_ref)

    @pl.when(lat == n_lat - 1)
    def _():
        flip_i = lax.broadcasted_iota(jnp.int32, (breadth, breadth), 0)
        flip_j = lax.broadcasted_iota(jnp.int32, (breadth, breadth), 1)
        flip = (flip_i + flip_j == breadth - 1).astype(jnp.bfloat16)
        both = jnp.concatenate([second_ref[0], second_ref[1]], axis=0)
        flipped = jnp.dot(both, flip, preferred_element_type=jnp.float32)
        north_ref[0] = flipped[:used]
        north_ref[1] = flipped[ROWS : ROWS + used]

    plane = lax.broadcasted_iota(jnp.int32, (HALF + 4, 128), 0)
    lane = lax.broadcasted_iota(jnp.int32, (HALF + 4, 128), 1)
    south = south_ref[0] * south_ref[0, HALF : HALF + 1, :]
    north = north_ref[0] * north_ref[0, HALF : HALF + 1, :]

    def to_lanes(column, low, high, place):
        mine = (plane >= low) & (plane < high) & (lane == place)
        return jnp.where(mine, column, 0.0)

    east_edge = to_lanes(south[:, breadth - 1 :], 0, QUAD, 2 * plane + 1)
    east_edge += to_lanes(north[:, breadth - 1 :], QUAD, HALF, 2 * plane + 1)
    west_edge = to_lanes(south[:, :1], QUAD, HALF, 2 * plane - HALF)
    west_edge += to_lanes(north[:, :1], 0, QUAD, 2 * plane + HALF)
    east_edge = jnp.broadcast_to(jnp.sum(east_edge, axis=0, keepdims=True), (8, 128))
    west_edge = jnp.broadcast_to(jnp.sum(west_edge, axis=0, keepdims=True), (8, 128))
    even_lon = lax.axis_index("lon") % 2 == 0
    out_first[:height] = jnp.where(even_lon, east_ref[...], west_ref[...])
    out_second[:height] = jnp.where(even_lon, west_ref[...], east_ref[...])
    out_first[height:] = jnp.where(even_lon, east_edge, west_edge)
    out_second[height:] = jnp.where(even_lon, west_edge, east_edge)


def for_windows(list_ref, window, sems, work):
    count = list_ref.shape[0] // WINDOW

    def fetch(i, w):
        source = list_ref.at[pl.ds(pl.multiple_of(i * WINDOW, WINDOW), WINDOW)]
        return pltpu.make_async_copy(source, window.at[pl.ds(w * WINDOW, WINDOW)], sems.at[w])

    for w in range(2):
        fetch(w, w).start()

    @pl.loop(0, count // 2)
    def _(t):
        for w in range(2):
            i = 2 * t + w
            fetch(i, w).wait()
            work(lambda k, start=w * WINDOW: window[start + k], i)

            @pl.when(i + 2 < count)
            def _():
                fetch(i + 2, w).start()


def inside_kernel(courant_ref, cos_ref, sin_ref, x_ref, mov_ref, sea_ref, halves):
    height, breadth = mov_ref.shape
    c0, c1 = courant_ref[0], courant_ref[1]
    moving = mov_ref[...]
    sea = sea_ref[...]
    lane = lax.broadcasted_iota(jnp.int32, (height, 128), 1)
    row = lax.broadcasted_iota(jnp.int32, (8, breadth), 0)
    for h in range(breadth // 128):
        halves[h, PLANES * height :, :] = jnp.zeros((4 * height, 128), jnp.float32)

    def quadrant(first, from_west, from_south):
        def upstream(flux):
            if from_west:
                moved = pltpu.roll(flux, 1, axis=1)
                side = jnp.concatenate([jnp.where(lane == 0, 0.0, moved[:, :128]), moved[:, 128:]], axis=1)
            else:
                moved = pltpu.roll(flux, breadth - 1, axis=1)
                edge = jnp.where(lane == 127, 0.0, moved[:, breadth - 128 :])
                side = jnp.concatenate([moved[:, : breadth - 128], edge], axis=1)
            if from_south:
                moved = pltpu.roll(flux, 1, axis=0)
                below = jnp.concatenate([jnp.where(row == 0, 0.0, moved[:8]), moved[8:]], axis=0)
            else:
                moved = pltpu.roll(flux, height - 1, axis=0)
                below = jnp.concatenate([moved[: height - 8], jnp.where(row == 7, 0.0, moved[height - 8 :])], axis=0)
            return side, below

        def step(t, carry):
            p = first + t
            courant = jnp.where(p % 2 == 1, c1, c0)
            cx = cos_ref[p] * courant
            cy = sin_ref[p] * courant
            energy = x_ref[p]
            for _ in range(2):
                flux = moving * energy
                side, below = upstream(flux)
                div_x = cx * (flux - side) if from_west else cx * (side - flux)
                div_y = cy * (flux - below) if from_south else cy * (below - flux)
                energy = sea * ((energy - div_x) - div_y)
            start = pl.ds(pl.multiple_of(p * height, height), height)
            for h in range(breadth // 128):
                halves[h, start, :] = energy[:, h * 128 : (h + 1) * 128]
            return carry

        lax.fori_loop(0, QUAD, step, 0, unroll=6)

    quadrant(0, True, True)
    quadrant(QUAD, False, True)
    quadrant(2 * QUAD, False, False)
    quadrant(3 * QUAD, True, False)


def profile_rows(halves, weight, table, first_row, count, height, breadth):
    pad = jnp.zeros((8, 128), jnp.bfloat16)
    blocks = []
    for k in range(count):
        for h in range(breadth // 128):
            spectra = halves[h, pl.ds(first_row + k, PLANES, stride=height), :]
            high = spectra.astype(jnp.bfloat16)
            low = (spectra - high.astype(jnp.float32)).astype(jnp.bfloat16)
            blocks.append(jnp.concatenate([high, pad, low, pad, high, pad], axis=0))
    stacked = jnp.concatenate(blocks, axis=1)
    profile = lax.dot_general(stacked, weight, (((0,), (0,)), ((), ())), preferred_element_type=jnp.float32)
    start = first_row * breadth
    if not isinstance(start, int):
        start = pl.multiple_of(start, 128)
    table[pl.ds(start, count * breadth), :] = profile


def profile_kernel(halves, kernel_ref, table, weight_ref, edge_ref, wide_kernel):
    height, breadth = halves.shape[1] // (PLANES + 4), table.shape[0] // (halves.shape[1] // (PLANES + 4))
    pad = jnp.zeros((8, 128), jnp.bfloat16)
    wide_kernel[...] = jnp.zeros((128, 128), jnp.float32)
    wide_kernel[:64, :PLANES] = kernel_ref[...]
    wide_kernel[64:, :PLANES] = kernel_ref[...]
    turned = wide_kernel[...].T
    weight_high = turned[:PLANES].astype(jnp.bfloat16)
    weight_low = (turned[:PLANES] - weight_high.astype(jnp.float32)).astype(jnp.bfloat16)
    weight = jnp.concatenate([weight_high, pad, weight_high, pad, weight_low, pad], axis=0)
    weight_ref[...] = weight

    lane = lax.broadcasted_iota(jnp.int32, (128, 128), 0)
    plane = lax.broadcasted_iota(jnp.int32, (128, 128), 1)
    q = lane // 2
    used = lane < 2 * HALF
    for side, owner in ((0, jnp.where(q < QUAD, q, q + HALF)), (1, q + QUAD)):
        for k in range(2):
            chosen = used & (plane == owner) & (lane % 2 == (k if side == 0 else 1 - k))
            edge_ref[side, :, k * 128 : (k + 1) * 128] = jnp.dot(
                chosen.astype(jnp.float32), turned, precision=lax.Precision.HIGHEST, preferred_element_type=jnp.float32
            )
    group = 8

    @pl.loop(0, height // group)
    def _(r):
        profile_rows(halves, weight, table, r * group, group, height, breadth)


def finish_kernel(courant_ref, cells_ref, mov_ref, sea_ref, weight_ref, edge_ref, south_ref, north_ref, first_ref,
                  second_ref, lanes_ref, subs_ref, halves_in, table_in, out_ref, picked_ref, halves, table,
                  lines, picks, window, out_sems, window_sems, pick_sem):
    height, breadth = mov_ref.shape
    c0, c1 = courant_ref[0], courant_ref[1]
    even_lon = lax.axis_index("lon") % 2 == 0
    from_west = jnp.where(even_lon, second_ref[...], first_ref[...])
    from_east = jnp.where(even_lon, first_ref[...], second_ref[...])
    corner_w, corner_e = from_west[height : height + 1], from_east[height : height + 1]

    lane = lax.broadcasted_iota(jnp.int32, (height, 128), 1)
    row = lax.broadcasted_iota(jnp.int32, (height, 128), 0)
    odd = lane % 2 == 1

    def columns(e0, near, far, corner, cx, cy, sign):
        mov = jnp.where(odd, e0[:, 2 * HALF + 1 : 2 * HALF + 2], e0[:, 2 * HALF : 2 * HALF + 1])
        sea = e0[:, 2 * HALF + 2 + near : 2 * HALF + 3 + near]
        f0 = mov * e0
        f_far = pltpu.roll(f0, 1 if near > far else 127, axis=1)
        f_south = jnp.where(row == 0, corner, pltpu.roll(f0, 1, axis=0))
        f_north = jnp.where(row == height - 1, corner, pltpu.roll(f0, height - 1, axis=0))
        div_x = cx * (f0 - f_far) if sign > 0 else cx * (f_far - f0)
        div_y = jnp.where(lane < HALF, cy * (f0 - f_south), cy * (f_north - f0))
        return f0, mov * (sea * ((e0 - div_x) - div_y))

    lanes = lanes_ref[...]
    lane_courant = jnp.where(lanes[4:5] > 0.5, c1, c0)
    cx_w, cy_w, cx_e, cy_e = (lanes[k : k + 1] * lane_courant for k in range(4))
    west_flux0, west_flux1 = columns(from_west[:height], 1, 0, corner_w, cx_w, cy_w, 1)
    east_flux0, east_flux1 = columns(from_east[:height], 0, 1, corner_e, cx_e, cy_e, -1)

    wide = lax.broadcasted_iota(jnp.int32, (HALF + 4, breadth), 1)
    plane = lax.broadcasted_iota(jnp.int32, (HALF + 4, 1), 0)
    plane_l = lax.broadcasted_iota(jnp.int32, (HALF + 4, 128), 0)
    lane_l = lax.broadcasted_iota(jnp.int32, (HALF + 4, 128), 1)
    subs = subs_ref[...]
    sub_courant = jnp.where(plane % 2 == 1, c1, c0)

    def to_sublanes(corner, lane_of):
        return jnp.sum(jnp.where(lane_l == lane_of, corner, 0.0), axis=1, keepdims=True)

    def rows(near, far, first_west, west_corner, east_corner, cx, cy, sign):
        mov, sea = near[HALF : HALF + 1], near[HALF + 1 : HALF + 2]
        f0 = mov * near
        f_far = far[HALF : HALF + 1] * far
        f_west = jnp.where(wide == 0, west_corner, pltpu.roll(f0, 1, axis=1))
        f_east = jnp.where(wide == breadth - 1, east_corner, pltpu.roll(f0, breadth - 1, axis=1))
        from_west = (plane < QUAD) if first_west else (plane >= QUAD)
        div_x = jnp.where(from_west, cx * (f0 - f_west), cx * (f_east - f0))
        div_y = cy * (f0 - f_far) if sign > 0 else cy * (f_far - f0)
        return f0, mov * (sea * ((near - div_x) - div_y))

    sw = to_sublanes(corner_w, 2 * plane_l + 1)
    se = to_sublanes(corner_e, 2 * plane_l - HALF)
    ne = to_sublanes(corner_e, 2 * plane_l + HALF)
    nw = sw
    cx_s, cy_s, cx_n, cy_n = (subs[:, k : k + 1] * sub_courant for k in range(4))
    south_flux0, south_flux1 = rows(south_ref[0], south_ref[1], True, sw, se, cx_s, cy_s, 1)
    north_flux0, north_flux1 = rows(north_ref[0], north_ref[1], False, nw, ne, cx_n, cy_n, -1)

    def add_rows(first, near, next_row, flux0, flux1, cx, cy, first_west):
        sea0, sea1 = sea_ref[near : near + 1, :], sea_ref[next_row : next_row + 1, :]
        change = sea0 * (cy * flux0)
        flux = mov_ref[near : near + 1, :] * change
        west_flux = jnp.where(wide == 0, 0.0, pltpu.roll(flux, 1, axis=1))
        east_flux = jnp.where(wide == breadth - 1, 0.0, pltpu.roll(flux, breadth - 1, axis=1))
        from_west = (plane < QUAD) if first_west else (plane >= QUAD)
        div_x = jnp.where(from_west, cx * (flux - west_flux), cx * (east_flux - flux))
        near_change = sea0 * (((change - div_x) - cy * flux) + cy * flux1)
        next_change = sea1 * (cy * flux)
        for at, delta in ((near, near_change), (next_row, next_change)):
            for h in range(breadth // 128):
                place = pl.ds(first * height + at, HALF + 4, stride=height)
                halves[h, place, :] = halves[h, place, :] + delta[:, h * 128 : (h + 1) * 128]

    def add_columns(half, near, next_column, flux0, flux1, cx, cy, from_west):
        sea0, sea1 = sea_ref[:, near : near + 1], sea_ref[:, next_column : next_column + 1]
        change = sea0 * (cx * flux0)
        flux = mov_ref[:, near : near + 1] * change
        south_flux = jnp.where(row == 0, 0.0, pltpu.roll(flux, 1, axis=0))
        north_flux = jnp.where(row == height - 1, 0.0, pltpu.roll(flux, height - 1, axis=0))
        div_y = jnp.where(lane < HALF, cy * (flux - south_flux), cy * (north_flux - flux))
        near_change = sea0 * (((change - cx * flux) - div_y) + cx * flux1)
        next_change = sea1 * (cx * flux)
        if from_west:
            both = jnp.where(odd, next_change, pltpu.roll(near_change, 127, axis=1))
        else:
            both = jnp.where(odd, pltpu.roll(near_change, 1, axis=1), next_change)
        edge = lane < 2 if from_west else lane >= 126
        for q in range(HALF):
            p = q + QUAD if not from_west else (q if q < QUAD else q + HALF)
            turned = pltpu.roll(both, ((128 if from_west else 126) - 2 * q) % 128, axis=1)
            place = pl.ds(p * height, height)
            halves[half, place, :] = halves[half, place, :] + jnp.where(edge, turned, 0.0)
        return jnp.where(lane < 2 * HALF, both, 0.0)

    add_rows(0, 0, 1, south_flux0, south_flux1, cx_s, cy_s, True)
    add_rows(HALF, height - 1, height - 2, north_flux0, north_flux1, cx_n, -cy_n, False)
    change_w = add_columns(0, 0, 1, west_flux0, west_flux1, cx_w, cy_w, True)
    change_e = add_columns(breadth // 128 - 1, breadth - 1, breadth - 2, east_flux0, east_flux1, -cx_e, cy_e, False)
    whole = pl.ds(0, PLANES * height)
    writes = [
        pltpu.make_async_copy(halves.at[h, whole, :], out_ref.at[:, pl.ds(h * 128, 128)], out_sems.at[h])
        for h in range(breadth // 128)
    ]
    for write in writes:
        write.start()

    for change, columns_of, near, next_column in ((change_w, 0, 0, 1), (change_e, 1, breadth - 1, breadth - 2)):
        profile = jnp.dot(
            change, edge_ref[columns_of], precision=lax.Precision.HIGHEST, preferred_element_type=jnp.float32
        )
        for k, column in enumerate((near, next_column)):
            place = pl.ds(column, height, stride=breadth)
            table[place, :] = table[place, :] + profile[:, k * 128 : (k + 1) * 128]
    for first_row in (0, height - 2):
        profile_rows(halves, weight_ref[...], table, first_row, 2, height, breadth)

    first_half = lax.broadcasted_iota(jnp.int32, (1, 128), 1) < 64
    half = WINDOW // 2

    def pick(cell, i):
        for g in range(WINDOW // 16):
            for j in range(8):
                one, two = cell(16 * g + j), cell(16 * g + 8 + j)
                line = jnp.where(first_half, table[pl.ds(one, 1), :], table[pl.ds(two, 1), :])
                lines[8 * g + j : 8 * g + j + 1, :] = line
        here = pl.ds(pl.multiple_of(i * half, half), half)
        picks[here, :] = lines[...].astype(jnp.bfloat16)
        pltpu.make_async_copy(picks.at[here, :], picked_ref.at[here, :], pick_sem).start()

    for_windows(cells_ref, window, window_sems, pick)
    pltpu.make_async_copy(picks, picked_ref, pick_sem).wait()
    for write in writes:
        write.wait()


def add_kernel(rows_ref, values_ref, out_ref, lines, tile_sums, window, window_sems, out_sem, *sums):
    n_acc = len(sums) // 2
    tile = out_ref.shape[1]
    block = 512
    half = WINDOW // 2

    @pl.loop(0, tile // block)
    def _(i):
        for total in sums:
            total[pl.ds(pl.multiple_of(i * block, block), block), :] = jnp.zeros((block, 128), jnp.float32)

    def add(row, i):
        lines[...] = values_ref[pl.ds(pl.multiple_of(i * half, half), half), :].astype(jnp.float32)
        for g in range(WINDOW // 16):
            for j in range(8):
                one, two = row(16 * g + j), row(16 * g + 8 + j)
                line = lines[8 * g + j : 8 * g + j + 1, :]
                left, right = sums[j % n_acc], sums[n_acc + j % n_acc]
                left[pl.ds(one, 1), :] = left[pl.ds(one, 1), :] + line
                right[pl.ds(two, 1), :] = right[pl.ds(two, 1), :] + line

    for_windows(rows_ref, window, window_sems, add)
    first_half = lax.broadcasted_iota(jnp.int32, (block, 128), 1) < 64

    @pl.loop(0, tile // block)
    def _(i):
        here = pl.ds(pl.multiple_of(i * block, block), block)
        left, right = sums[0][here, :], sums[n_acc][here, :]
        for q in range(1, n_acc):
            left = left + sums[q][here, :]
            right = right + sums[n_acc + q][here, :]
        both = jnp.where(first_half, left, right).T
        tile_sums[:, here] = both[:64] + both[64:]
        pltpu.make_async_copy(tile_sums.at[:, here], out_ref.at[:, here], out_sem).start()

    pltpu.make_async_copy(tile_sums, out_ref, out_sem).wait()


def constant_tables():
    heading = (np.arange(DIRS) + 0.5) * (2.0 * math.pi / DIRS)
    cos = np.repeat(np.cos(heading), FREQ)
    sin = np.repeat(np.sin(heading), FREQ)
    lanes = np.zeros((8, 128))
    q = np.arange(HALF)
    from_west = np.where(q < QUAD, q, q + HALF)
    from_east = q + QUAD
    for column in range(2):
        lanes[0, 2 * q + column] = cos[from_west]
        lanes[1, 2 * q + column] = sin[from_west]
        lanes[2, 2 * q + column] = cos[from_east]
        lanes[3, 2 * q + column] = sin[from_east]
        lanes[4, 2 * q + column] = q % 2
    subs = np.zeros((HALF + 4, 128))
    subs[:HALF, 0], subs[:HALF, 1] = cos[:HALF], sin[:HALF]
    subs[:HALF, 2], subs[:HALF, 3] = cos[HALF:], sin[HALF:]
    return [t.astype(np.float32) for t in (cos, sin, lanes, subs)]


def body(n_lat, n_lon, spectrum, speed_factor, land_sea_mask, courant, depth_kernel, send_rows, recv_rows):
    height, breadth = speed_factor.shape
    devices, slots = send_rows.shape[1:]
    x = spectrum.reshape(PLANES, height, breadth)
    f32 = jnp.float32
    vmem = pl.BlockSpec(memory_space=pltpu.VMEM)
    smem = pl.BlockSpec(memory_space=pltpu.SMEM)
    hbm = pl.BlockSpec(memory_space=pltpu.HBM)
    params = pltpu.CompilerParams(vmem_limit_bytes=VMEM_LIMIT)

    both = ("lat", "lon")

    def shape(*dims, kind=f32):
        return jax.ShapeDtypeStruct(dims, kind)

    cos, sin, lanes, subs = constant_tables()
    row_message = shape(2, ROWS, breadth, kind=jnp.bfloat16)
    row_halo = shape(2, HALF + 4, breadth)
    columns = shape(height, 128)
    column_message = shape(height + 8, 128)
    row_first, row_second, column_first, column_second = exchange_pairs(n_lat, n_lon)
    first, second, moving, sea = pl.pallas_call(
        pack_rows_kernel,
        out_shape=[row_message] * 2 + [shape(height, breadth)] * 2,
        in_specs=[hbm] * 3,
        out_specs=[vmem] * 4,
        scratch_shapes=[pltpu.VMEM((2, ROWS, breadth), f32)] * 2
        + [pltpu.VMEM((HALF, 8, breadth), f32)] * 2
        + [pltpu.VMEM((height, breadth), f32), pltpu.VMEM((height, breadth), jnp.int32), pltpu.SemaphoreType.DMA((4,))],
        compiler_params=params,
        name="pack_rows",
    )(*(pltpu.with_memory_space_constraint(v, pltpu.HBM) for v in (x, speed_factor, land_sea_mask)))
    second = lax.ppermute(second, both, row_second)
    first = lax.ppermute(first, "lat", row_first)
    east, west = pl.pallas_call(
        pack_columns_kernel,
        out_shape=[columns] * 2,
        in_specs=[vmem] * 3,
        out_specs=[vmem] * 2,
        compiler_params=params,
        cost_estimate=pl.CostEstimate(flops=2_000_000_000, bytes_accessed=5_000_000, transcendentals=0),
        name="pack_columns",
    )(x, moving, sea)
    halves = pl.pallas_call(
        inside_kernel,
        out_shape=pltpu.VMEM((breadth // 128, (PLANES + 4) * height, 128), f32),
        in_specs=[smem] * 3 + [vmem] * 3,
        out_specs=vmem,
        compiler_params=params,
        cost_estimate=pl.CostEstimate(flops=4_000_000_000, bytes_accessed=5_000_000, transcendentals=0),
        name="advance_inside",
    )(courant, cos, sin, x, moving, sea)
    south, north, first, second = pl.pallas_call(
        functools.partial(corner_kernel, n_lat),
        out_shape=[row_halo] * 2 + [column_message] * 2,
        in_specs=[vmem] * 4,
        out_specs=[vmem] * 4,
        compiler_params=params,
        name="add_corners",
    )(first, second, east, west)
    second = lax.ppermute(second, "lon", column_second)
    first = lax.ppermute(first, "lon", column_first)

    cells = jnp.maximum(send_rows, 0).reshape(-1)
    slot = jnp.arange(slots, dtype=jnp.int32)
    spare = OUT_DEV + (slot // 16 * 8 + slot % 8) % SPARE
    targets = jnp.where(recv_rows < 0, spare, recv_rows).reshape(-1)
    slot_rows = devices * slots // 2
    slot_rows = devices * slots // 2
    table_shape = pltpu.VMEM((height * breadth, 128), f32)
    table, weight, edges = pl.pallas_call(
        profile_kernel,
        out_shape=[table_shape, shape(3 * (PLANES + 8), 128, kind=jnp.bfloat16), shape(2, 128, 256)],
        in_specs=[vmem] * 2,
        out_specs=[vmem] * 3,
        scratch_shapes=[pltpu.VMEM((128, 128), f32)],
        compiler_params=params,
        cost_estimate=pl.CostEstimate(flops=2_000_000_000, bytes_accessed=5_000_000, transcendentals=0),
        name="profiles_inside",
    )(halves, depth_kernel)
    propagated, picked, *_ = pl.pallas_call(
        finish_kernel,
        out_shape=[
            pltpu.HBM((PLANES * height, breadth), f32),
            pltpu.HBM((slot_rows, 128), jnp.bfloat16),
            pltpu.VMEM(halves.shape, f32),
            table_shape,
        ],
        in_specs=[smem, hbm] + [vmem] * 12,
        out_specs=[hbm, hbm, vmem, vmem],
        input_output_aliases={12: 2, 13: 3},
        scratch_shapes=[
            pltpu.VMEM((WINDOW // 2, 128), f32),
            pltpu.VMEM((slot_rows, 128), jnp.bfloat16),
            pltpu.SMEM((2 * WINDOW,), jnp.int32),
            pltpu.SemaphoreType.DMA((breadth // 128,)),
            pltpu.SemaphoreType.DMA((2,)),
            pltpu.SemaphoreType.DMA,
        ],
        compiler_params=params,
        name="finish_and_pick",
    )(courant, cells, moving, sea, weight, edges, south, north, first, second, lanes, subs, halves, table)

    picked = picked.reshape(devices, slots // 2, 128)
    received = lax.all_to_all(picked, both, split_axis=0, concat_axis=0, tiled=True)

    components = depth_kernel.shape[0]
    stokes = pl.pallas_call(
        add_kernel,
        out_shape=pltpu.HBM((components, OUT_DEV), f32),
        in_specs=[hbm, vmem],
        out_specs=hbm,
        scratch_shapes=[
            pltpu.VMEM((WINDOW // 2, 128), f32),
            pltpu.VMEM((components, OUT_DEV), f32),
            pltpu.SMEM((2 * WINDOW,), jnp.int32),
            pltpu.SemaphoreType.DMA((2,)),
            pltpu.SemaphoreType.DMA,
        ]
        + [pltpu.VMEM((OUT_DEV + SPARE, 128), f32)] * (2 * N_ACC),
        compiler_params=pltpu.CompilerParams(vmem_limit_bytes=ADD_VMEM_LIMIT),
        name="add_profiles",
    )(targets, received.reshape(slot_rows, 128))
    return propagated.reshape(DIRS, FREQ, height, breadth), stokes


def solution(mesh):
    placed = (
        P(None, None, "lat", "lon"),
        P("lat", "lon"),
        P("lat", "lon"),
        P(),
        P(),
        P(("lat", "lon"), None, None),
        P(("lat", "lon"), None, None),
    )
    return jax.shard_map(
        functools.partial(body, mesh.shape["lat"], mesh.shape["lon"]),
        mesh=mesh,
        in_specs=placed,
        out_specs=(P(None, None, "lat", "lon"), P(None, ("lat", "lon"))),
        check_vma=False,
    )
```

```python
import functools
import math

import jax
import jax.numpy as jnp
import numpy as np
from jax import lax
from jax.experimental import pallas as pl
from jax.experimental.pallas import tpu as pltpu
from jax.sharding import PartitionSpec as P

DIRS = 36
FREQ = 2
PLANES = DIRS * FREQ
HALF = PLANES // 2
QUAD = PLANES // 4
OUT_DEV = 4096
SPARE = 64
N_ACC = 4
ROWS = HALF + 12
WINDOW = 1024
VMEM_LIMIT = 16 * 1024 * 1024
ADD_VMEM_LIMIT = 32 * 1024 * 1024


def exchange_pairs(n_lat, n_lon):
    def flat(j, i):
        return j * n_lon + i % n_lon

    row_first = [(j, j ^ 1) for j in range(n_lat)]
    row_second = []
    for i in range(n_lon):
        row_second += [(flat(0, i), flat(0, i)), (flat(n_lat - 1, i), flat(n_lat - 1, n_lon - 1 - i))]
        for j in range(1, n_lat - 1, 2):
            row_second += [(flat(j, i), flat(j + 1, i)), (flat(j + 1, i), flat(j, i))]
    column_first = [(i, i ^ 1) for i in range(n_lon)]
    column_second = [(i, (i + 1 if i % 2 else i - 1) % n_lon) for i in range(n_lon)]
    return row_first, row_second, column_first, column_second


def pack_rows_kernel(x_hbm, speed_hbm, mask_hbm, first_ref, second_ref, mov_ref, sea_ref,
                     up_ref, down_ref, top_rows, bottom_rows, speed_ref, mask_ref, sems):
    height, breadth = speed_ref.shape
    copies = [
        pltpu.make_async_copy(source, target, sems.at[k])
        for k, (source, target) in enumerate((
            (speed_hbm, speed_ref),
            (mask_hbm, mask_ref),
            (x_hbm.at[pl.ds(0, HALF), pl.ds(height - 8, 8), :], top_rows),
            (x_hbm.at[pl.ds(HALF, HALF), pl.ds(0, 8), :], bottom_rows),
        ))
    ]
    for copy in copies:
        copy.start()
    even = lax.axis_index("lat") % 2 == 0
    for copy in copies:
        copy.wait()
    sea = mask_ref[...].astype(jnp.float32)
    moving = speed_ref[...] * sea
    mov_ref[...] = moving
    sea_ref[...] = sea
    for k in range(2):
        for q in range(HALF):
            up_ref[k, q : q + 1, :] = top_rows[q, 7 - k : 8 - k, :]
            down_ref[k, q : q + 1, :] = bottom_rows[q, k : k + 1, :]
        up_ref[k, HALF : HALF + 1, :] = moving[height - 1 - k : height - k, :]
        down_ref[k, HALF : HALF + 1, :] = moving[k : k + 1, :]
        up_ref[k, HALF + 1 : HALF + 2, :] = sea[height - 1 - k : height - k, :]
        down_ref[k, HALF + 1 : HALF + 2, :] = sea[k : k + 1, :]
        up_ref[k, HALF + 2 :, :] = jnp.zeros((ROWS - HALF - 2, breadth), jnp.float32)
        down_ref[k, HALF + 2 :, :] = jnp.zeros((ROWS - HALF - 2, breadth), jnp.float32)

    @pl.when(even)
    def _():
        first_ref[...] = up_ref[...].astype(jnp.bfloat16)
        second_ref[...] = down_ref[...].astype(jnp.bfloat16)

    @pl.when(jnp.logical_not(even))
    def _():
        first_ref[...] = down_ref[...].astype(jnp.bfloat16)
        second_ref[...] = up_ref[...].astype(jnp.bfloat16)


def pack_columns_kernel(x_ref, mov_ref, sea_ref, east_ref, west_ref):
    height, breadth = mov_ref.shape
    lane = lax.broadcasted_iota(jnp.int32, (height, 128), 1)
    east = jnp.zeros((height, 128), jnp.float32)
    west = jnp.zeros((height, 128), jnp.float32)
    for q in range(HALF + 2):
        mine = lane // 2 == q
        if q < HALF:
            p_e = q if q < QUAD else q + HALF
            edge_e, edge_w = x_ref[p_e, :, breadth - 128 :], x_ref[q + QUAD, :, :128]
        else:
            field = (mov_ref if q == HALF else sea_ref)[...]
            edge_e, edge_w = field[:, breadth - 128 :], field[:, :128]
        east = jnp.where(mine, pltpu.roll(edge_e, (2 * q + 2) % 128, axis=1), east)
        west = jnp.where(mine, pltpu.roll(edge_w, 2 * q, axis=1), west)
    east_ref[...] = east
    west_ref[...] = west


def corner_kernel(n_lat, second_ref, first_ref, east_ref, west_ref, south_ref, north_ref, out_first, out_second):
    height = east_ref.shape[0]
    breadth = first_ref.shape[2]
    lat = lax.axis_index("lat")
    even = lat % 2 == 0

    used = HALF + 4

    @pl.when(even)
    def _():
        north_ref[...] = first_ref[...].astype(jnp.float32)[:, :used]
        south_ref[...] = second_ref[...].astype(jnp.float32)[:, :used]

    @pl.when(jnp.logical_not(even))
    def _():
        south_ref[...] = first_ref[...].astype(jnp.float32)[:, :used]
        north_ref[...] = second_ref[...].astype(jnp.float32)[:, :used]

    @pl.when(lat == 0)
    def _():
        south_ref[...] = jnp.zeros_like(south_ref)

    @pl.when(lat == n_lat - 1)
    def _():
        flip_i = lax.broadcasted_iota(jnp.int32, (breadth, breadth), 0)
        flip_j = lax.broadcasted_iota(jnp.int32, (breadth, breadth), 1)
        flip = (flip_i + flip_j == breadth - 1).astype(jnp.bfloat16)
        both = jnp.concatenate([second_ref[0], second_ref[1]], axis=0)
        flipped = jnp.dot(both, flip, preferred_element_type=jnp.float32)
        north_ref[0] = flipped[:used]
        north_ref[1] = flipped[ROWS : ROWS + used]

    plane = lax.broadcasted_iota(jnp.int32, (HALF + 4, 128), 0)
    lane = lax.broadcasted_iota(jnp.int32, (HALF + 4, 128), 1)
    south = south_ref[0] * south_ref[0, HALF : HALF + 1, :]
    north = north_ref[0] * north_ref[0, HALF : HALF + 1, :]

    def to_lanes(column, low, high, place):
        mine = (plane >= low) & (plane < high) & (lane == place)
        return jnp.where(mine, column, 0.0)

    east_edge = to_lanes(south[:, breadth - 1 :], 0, QUAD, 2 * plane + 1)
    east_edge += to_lanes(north[:, breadth - 1 :], QUAD, HALF, 2 * plane + 1)
    west_edge = to_lanes(south[:, :1], QUAD, HALF, 2 * plane - HALF)
    west_edge += to_lanes(north[:, :1], 0, QUAD, 2 * plane + HALF)
    east_edge = jnp.broadcast_to(jnp.sum(east_edge, axis=0, keepdims=True), (8, 128))
    west_edge = jnp.broadcast_to(jnp.sum(west_edge, axis=0, keepdims=True), (8, 128))
    even_lon = lax.axis_index("lon") % 2 == 0
    out_first[:height] = jnp.where(even_lon, east_ref[...], west_ref[...])
    out_second[:height] = jnp.where(even_lon, west_ref[...], east_ref[...])
    out_first[height:] = jnp.where(even_lon, east_edge, west_edge)
    out_second[height:] = jnp.where(even_lon, west_edge, east_edge)


def for_windows(list_ref, window, sems, work):
    lines = WINDOW // 128
    count = list_ref.shape[0] // lines

    def fetch(i, w):
        source = list_ref.at[pl.ds(pl.multiple_of(i * lines, lines), lines), :]
        return pltpu.make_async_copy(source, window.at[pl.ds(w * lines, lines), :], sems.at[w])

    for w in range(2):
        fetch(w, w).start()

    @pl.loop(0, count // 2)
    def _(t):
        for w in range(2):
            i = 2 * t + w
            fetch(i, w).wait()
            work(lambda k, start=w * lines: window[start + k // 128, k % 128], i)

            @pl.when(i + 2 < count)
            def _():
                fetch(i + 2, w).start()


def inside_kernel(courant_ref, heading_ref, x_ref, mov_ref, sea_ref, halves):
    height, breadth = mov_ref.shape
    c0, c1 = courant_ref[0], courant_ref[1]
    moving = mov_ref[...]
    sea = sea_ref[...]
    lane = lax.broadcasted_iota(jnp.int32, (height, 128), 1)
    row = lax.broadcasted_iota(jnp.int32, (8, breadth), 0)
    for h in range(breadth // 128):
        halves[h, PLANES * height :, :] = jnp.zeros((4 * height, 128), jnp.float32)

    def quadrant(first, from_west, from_south):
        def upstream(flux):
            if from_west:
                moved = pltpu.roll(flux, 1, axis=1)
                side = jnp.concatenate([jnp.where(lane == 0, 0.0, moved[:, :128]), moved[:, 128:]], axis=1)
            else:
                moved = pltpu.roll(flux, breadth - 1, axis=1)
                edge = jnp.where(lane == 127, 0.0, moved[:, breadth - 128 :])
                side = jnp.concatenate([moved[:, : breadth - 128], edge], axis=1)
            if from_south:
                moved = pltpu.roll(flux, 1, axis=0)
                below = jnp.concatenate([jnp.where(row == 0, 0.0, moved[:8]), moved[8:]], axis=0)
            else:
                moved = pltpu.roll(flux, height - 1, axis=0)
                below = jnp.concatenate([moved[: height - 8], jnp.where(row == 7, 0.0, moved[height - 8 :])], axis=0)
            return side, below

        def step(t, carry):
            p = first + t
            courant = jnp.where(p % 2 == 1, c1, c0)
            cx = heading_ref[p] * courant
            cy = heading_ref[PLANES + p] * courant
            energy = x_ref[p]
            for _ in range(2):
                flux = moving * energy
                side, below = upstream(flux)
                div_x = cx * (flux - side) if from_west else cx * (side - flux)
                div_y = cy * (flux - below) if from_south else cy * (below - flux)
                energy = sea * ((energy - div_x) - div_y)
            start = pl.ds(pl.multiple_of(p * height, height), height)
            for h in range(breadth // 128):
                halves[h, start, :] = energy[:, h * 128 : (h + 1) * 128]
            return carry

        lax.fori_loop(0, QUAD, step, 0, unroll=6)

    quadrant(0, True, True)
    quadrant(QUAD, False, True)
    quadrant(2 * QUAD, False, False)
    quadrant(3 * QUAD, True, False)


def profile_rows(halves, weight, table, first_row, count, height, breadth):
    pad = jnp.zeros((8, 128), jnp.bfloat16)
    blocks = []
    for k in range(count):
        for h in range(breadth // 128):
            spectra = halves[h, pl.ds(first_row + k, PLANES, stride=height), :]
            high = spectra.astype(jnp.bfloat16)
            low = (spectra - high.astype(jnp.float32)).astype(jnp.bfloat16)
            blocks.append(jnp.concatenate([high, pad, low, pad, high, pad], axis=0))
    stacked = jnp.concatenate(blocks, axis=1)
    profile = lax.dot_general(stacked, weight, (((0,), (0,)), ((), ())), preferred_element_type=jnp.float32)
    start = first_row * breadth
    if not isinstance(start, int):
        start = pl.multiple_of(start, 128)
    table[pl.ds(start, count * breadth), :] = profile


def profile_kernel(halves, kernel_ref, table, weight_ref, edge_ref, wide_kernel):
    height, breadth = halves.shape[1] // (PLANES + 4), table.shape[0] // (halves.shape[1] // (PLANES + 4))
    pad = jnp.zeros((8, 128), jnp.bfloat16)
    wide_kernel[...] = jnp.zeros((128, 128), jnp.float32)
    wide_kernel[:64, :PLANES] = kernel_ref[...]
    wide_kernel[64:, :PLANES] = kernel_ref[...]
    turned = wide_kernel[...].T
    weight_high = turned[:PLANES].astype(jnp.bfloat16)
    weight_low = (turned[:PLANES] - weight_high.astype(jnp.float32)).astype(jnp.bfloat16)
    weight = jnp.concatenate([weight_high, pad, weight_high, pad, weight_low, pad], axis=0)
    weight_ref[...] = weight

    lane = lax.broadcasted_iota(jnp.int32, (128, 128), 0)
    plane = lax.broadcasted_iota(jnp.int32, (128, 128), 1)
    q = lane // 2
    used = lane < 2 * HALF
    for side, owner in ((0, jnp.where(q < QUAD, q, q + HALF)), (1, q + QUAD)):
        for k in range(2):
            chosen = used & (plane == owner) & (lane % 2 == (k if side == 0 else 1 - k))
            edge_ref[side, :, k * 128 : (k + 1) * 128] = jnp.dot(
                chosen.astype(jnp.float32), turned, precision=lax.Precision.HIGHEST, preferred_element_type=jnp.float32
            )
    group = 8

    @pl.loop(0, height // group)
    def _(r):
        profile_rows(halves, weight, table, r * group, group, height, breadth)


def finish_kernel(courant_ref, cells_ref, mov_ref, sea_ref, weight_ref, edge_ref, south_ref, north_ref, second_ref,
                  first_ref, lanes_ref, subs_ref, halves_in, table_in, out_ref, picked_ref, halves, table,
                  cells, lines, picks, window, out_sems, window_sems, pick_sem):
    cells[...] = jnp.maximum(cells_ref[...], 0)
    height, breadth = mov_ref.shape
    c0, c1 = courant_ref[0], courant_ref[1]
    even_lon = lax.axis_index("lon") % 2 == 0
    from_west = jnp.where(even_lon, second_ref[...], first_ref[...])
    from_east = jnp.where(even_lon, first_ref[...], second_ref[...])
    corner_w, corner_e = from_west[height : height + 1], from_east[height : height + 1]

    lane = lax.broadcasted_iota(jnp.int32, (height, 128), 1)
    row = lax.broadcasted_iota(jnp.int32, (height, 128), 0)
    odd = lane % 2 == 1

    def columns(e0, near, far, corner, cx, cy, sign):
        mov = jnp.where(odd, e0[:, 2 * HALF + 1 : 2 * HALF + 2], e0[:, 2 * HALF : 2 * HALF + 1])
        sea = e0[:, 2 * HALF + 2 + near : 2 * HALF + 3 + near]
        f0 = mov * e0
        f_far = pltpu.roll(f0, 1 if near > far else 127, axis=1)
        f_south = jnp.where(row == 0, corner, pltpu.roll(f0, 1, axis=0))
        f_north = jnp.where(row == height - 1, corner, pltpu.roll(f0, height - 1, axis=0))
        div_x = cx * (f0 - f_far) if sign > 0 else cx * (f_far - f0)
        div_y = jnp.where(lane < HALF, cy * (f0 - f_south), cy * (f_north - f0))
        return f0, mov * (sea * ((e0 - div_x) - div_y))

    lanes = lanes_ref[...]
    lane_courant = jnp.where(lanes[4:5] > 0.5, c1, c0)
    cx_w, cy_w, cx_e, cy_e = (lanes[k : k + 1] * lane_courant for k in range(4))
    west_flux0, west_flux1 = columns(from_west[:height], 1, 0, corner_w, cx_w, cy_w, 1)
    east_flux0, east_flux1 = columns(from_east[:height], 0, 1, corner_e, cx_e, cy_e, -1)

    wide = lax.broadcasted_iota(jnp.int32, (HALF + 4, breadth), 1)
    plane = lax.broadcasted_iota(jnp.int32, (HALF + 4, 1), 0)
    plane_l = lax.broadcasted_iota(jnp.int32, (HALF + 4, 128), 0)
    lane_l = lax.broadcasted_iota(jnp.int32, (HALF + 4, 128), 1)
    subs = subs_ref[...]
    sub_courant = jnp.where(plane % 2 == 1, c1, c0)

    def to_sublanes(corner, lane_of):
        return jnp.sum(jnp.where(lane_l == lane_of, corner, 0.0), axis=1, keepdims=True)

    def rows(near, far, first_west, west_corner, east_corner, cx, cy, sign):
        mov, sea = near[HALF : HALF + 1], near[HALF + 1 : HALF + 2]
        f0 = mov * near
        f_far = far[HALF : HALF + 1] * far
        f_west = jnp.where(wide == 0, west_corner, pltpu.roll(f0, 1, axis=1))
        f_east = jnp.where(wide == breadth - 1, east_corner, pltpu.roll(f0, breadth - 1, axis=1))
        from_west = (plane < QUAD) if first_west else (plane >= QUAD)
        div_x = jnp.where(from_west, cx * (f0 - f_west), cx * (f_east - f0))
        div_y = cy * (f0 - f_far) if sign > 0 else cy * (f_far - f0)
        return f0, mov * (sea * ((near - div_x) - div_y))

    sw = to_sublanes(corner_w, 2 * plane_l + 1)
    se = to_sublanes(corner_e, 2 * plane_l - HALF)
    ne = to_sublanes(corner_e, 2 * plane_l + HALF)
    nw = sw
    cx_s, cy_s, cx_n, cy_n = (subs[:, k : k + 1] * sub_courant for k in range(4))
    south_flux0, south_flux1 = rows(south_ref[0], south_ref[1], True, sw, se, cx_s, cy_s, 1)
    north_flux0, north_flux1 = rows(north_ref[0], north_ref[1], False, nw, ne, cx_n, cy_n, -1)

    def add_rows(first, near, next_row, flux0, flux1, cx, cy, first_west):
        sea0, sea1 = sea_ref[near : near + 1, :], sea_ref[next_row : next_row + 1, :]
        change = sea0 * (cy * flux0)
        flux = mov_ref[near : near + 1, :] * change
        west_flux = jnp.where(wide == 0, 0.0, pltpu.roll(flux, 1, axis=1))
        east_flux = jnp.where(wide == breadth - 1, 0.0, pltpu.roll(flux, breadth - 1, axis=1))
        from_west = (plane < QUAD) if first_west else (plane >= QUAD)
        div_x = jnp.where(from_west, cx * (flux - west_flux), cx * (east_flux - flux))
        near_change = sea0 * (((change - div_x) - cy * flux) + cy * flux1)
        next_change = sea1 * (cy * flux)
        for at, delta in ((near, near_change), (next_row, next_change)):
            for h in range(breadth // 128):
                place = pl.ds(first * height + at, HALF + 4, stride=height)
                halves[h, place, :] = halves[h, place, :] + delta[:, h * 128 : (h + 1) * 128]

    def add_columns(half, near, next_column, flux0, flux1, cx, cy, from_west):
        sea0, sea1 = sea_ref[:, near : near + 1], sea_ref[:, next_column : next_column + 1]
        change = sea0 * (cx * flux0)
        flux = mov_ref[:, near : near + 1] * change
        south_flux = jnp.where(row == 0, 0.0, pltpu.roll(flux, 1, axis=0))
        north_flux = jnp.where(row == height - 1, 0.0, pltpu.roll(flux, height - 1, axis=0))
        div_y = jnp.where(lane < HALF, cy * (flux - south_flux), cy * (north_flux - flux))
        near_change = sea0 * (((change - cx * flux) - div_y) + cx * flux1)
        next_change = sea1 * (cx * flux)
        if from_west:
            both = jnp.where(odd, next_change, pltpu.roll(near_change, 127, axis=1))
        else:
            both = jnp.where(odd, pltpu.roll(near_change, 1, axis=1), next_change)
        edge = lane < 2 if from_west else lane >= 126
        for q in range(HALF):
            p = q + QUAD if not from_west else (q if q < QUAD else q + HALF)
            turned = pltpu.roll(both, ((128 if from_west else 126) - 2 * q) % 128, axis=1)
            place = pl.ds(p * height, height)
            halves[half, place, :] = halves[half, place, :] + jnp.where(edge, turned, 0.0)
        return jnp.where(lane < 2 * HALF, both, 0.0)

    add_rows(0, 0, 1, south_flux0, south_flux1, cx_s, cy_s, True)
    add_rows(HALF, height - 1, height - 2, north_flux0, north_flux1, cx_n, -cy_n, False)
    change_w = add_columns(0, 0, 1, west_flux0, west_flux1, cx_w, cy_w, True)
    change_e = add_columns(breadth // 128 - 1, breadth - 1, breadth - 2, east_flux0, east_flux1, -cx_e, cy_e, False)
    whole = pl.ds(0, PLANES * height)
    writes = [
        pltpu.make_async_copy(halves.at[h, whole, :], out_ref.at[:, pl.ds(h * 128, 128)], out_sems.at[h])
        for h in range(breadth // 128)
    ]
    for write in writes:
        write.start()

    for change, columns_of, near, next_column in ((change_w, 0, 0, 1), (change_e, 1, breadth - 1, breadth - 2)):
        profile = jnp.dot(
            change, edge_ref[columns_of], precision=lax.Precision.HIGHEST, preferred_element_type=jnp.float32
        )
        for k, column in enumerate((near, next_column)):
            place = pl.ds(column, height, stride=breadth)
            table[place, :] = table[place, :] + profile[:, k * 128 : (k + 1) * 128]
    for first_row in (0, height - 2):
        profile_rows(halves, weight_ref[...], table, first_row, 2, height, breadth)

    first_half = lax.broadcasted_iota(jnp.int32, (1, 128), 1) < 64
    half = WINDOW // 2

    def pick(cell, i):
        for g in range(WINDOW // 16):
            for j in range(8):
                one, two = cell(16 * g + j), cell(16 * g + 8 + j)
                line = jnp.where(first_half, table[pl.ds(one, 1), :], table[pl.ds(two, 1), :])
                lines[8 * g + j : 8 * g + j + 1, :] = line
        here = pl.ds(pl.multiple_of(i * half, half), half)
        picks[here, :] = lines[...].astype(jnp.bfloat16)
        pltpu.make_async_copy(picks.at[here, :], picked_ref.at[here, :], pick_sem).start()

    for_windows(cells, window, window_sems, pick)
    pltpu.make_async_copy(picks, picked_ref, pick_sem).wait()
    for write in writes:
        write.wait()


def add_kernel(rows_ref, values_ref, out_ref, targets, lines, tile_sums, window, window_sems, out_sem, *sums):
    n_acc = len(sums) // 2
    tile = out_ref.shape[1]
    block = 512
    half = WINDOW // 2
    slot = lax.broadcasted_iota(jnp.int32, targets.shape, 1)
    spare = tile + (slot // 16 * 8 + slot % 8) % SPARE
    targets[...] = jnp.where(rows_ref[...] < 0, spare, rows_ref[...])

    @pl.loop(0, tile // block)
    def _(i):
        for total in sums:
            total[pl.ds(pl.multiple_of(i * block, block), block), :] = jnp.zeros((block, 128), jnp.float32)

    def add(row, i):
        lines[...] = values_ref[pl.ds(pl.multiple_of(i * half, half), half), :].astype(jnp.float32)
        for g in range(WINDOW // 16):
            for j in range(8):
                one, two = row(16 * g + j), row(16 * g + 8 + j)
                line = lines[8 * g + j : 8 * g + j + 1, :]
                left, right = sums[j % n_acc], sums[n_acc + j % n_acc]
                left[pl.ds(one, 1), :] = left[pl.ds(one, 1), :] + line
                right[pl.ds(two, 1), :] = right[pl.ds(two, 1), :] + line

    for_windows(targets, window, window_sems, add)
    first_half = lax.broadcasted_iota(jnp.int32, (block, 128), 1) < 64

    @pl.loop(0, tile // block)
    def _(i):
        here = pl.ds(pl.multiple_of(i * block, block), block)
        left, right = sums[0][here, :], sums[n_acc][here, :]
        for q in range(1, n_acc):
            left = left + sums[q][here, :]
            right = right + sums[n_acc + q][here, :]
        both = jnp.where(first_half, left, right).T
        tile_sums[:, here] = both[:64] + both[64:]
        pltpu.make_async_copy(tile_sums.at[:, here], out_ref.at[:, here], out_sem).start()

    pltpu.make_async_copy(tile_sums, out_ref, out_sem).wait()


def constant_tables():
    heading = (np.arange(DIRS) + 0.5) * (2.0 * math.pi / DIRS)
    cos = np.repeat(np.cos(heading), FREQ)
    sin = np.repeat(np.sin(heading), FREQ)
    lanes = np.zeros((8, 128))
    q = np.arange(HALF)
    from_west = np.where(q < QUAD, q, q + HALF)
    from_east = q + QUAD
    for column in range(2):
        lanes[0, 2 * q + column] = cos[from_west]
        lanes[1, 2 * q + column] = sin[from_west]
        lanes[2, 2 * q + column] = cos[from_east]
        lanes[3, 2 * q + column] = sin[from_east]
        lanes[4, 2 * q + column] = q % 2
    subs = np.zeros((HALF + 4, 128))
    subs[:HALF, 0], subs[:HALF, 1] = cos[:HALF], sin[:HALF]
    subs[:HALF, 2], subs[:HALF, 3] = cos[HALF:], sin[HALF:]
    return [t.astype(np.float32) for t in (np.concatenate([cos, sin]), lanes, subs)]


def body(n_lat, n_lon, spectrum, speed_factor, land_sea_mask, courant, depth_kernel, send_rows, recv_rows):
    height, breadth = speed_factor.shape
    devices, slots = send_rows.shape[1:]
    x = spectrum.reshape(PLANES, height, breadth)
    f32 = jnp.float32
    vmem = pl.BlockSpec(memory_space=pltpu.VMEM)
    smem = pl.BlockSpec(memory_space=pltpu.SMEM)
    hbm = pl.BlockSpec(memory_space=pltpu.HBM)
    params = pltpu.CompilerParams(vmem_limit_bytes=VMEM_LIMIT)

    both = ("lat", "lon")

    def shape(*dims, kind=f32):
        return jax.ShapeDtypeStruct(dims, kind)

    headings, lanes, subs = constant_tables()
    row_message = shape(2, ROWS, breadth, kind=jnp.bfloat16)
    row_halo = shape(2, HALF + 4, breadth)
    columns = shape(height, 128)
    column_message = shape(height + 8, 128)
    row_first, row_second, column_first, column_second = exchange_pairs(n_lat, n_lon)
    first, second, moving, sea = pl.pallas_call(
        pack_rows_kernel,
        out_shape=[row_message] * 2 + [shape(height, breadth)] * 2,
        in_specs=[hbm] * 3,
        out_specs=[vmem] * 4,
        scratch_shapes=[pltpu.VMEM((2, ROWS, breadth), f32)] * 2
        + [pltpu.VMEM((HALF, 8, breadth), f32)] * 2
        + [pltpu.VMEM((height, breadth), f32), pltpu.VMEM((height, breadth), jnp.int32), pltpu.SemaphoreType.DMA((4,))],
        compiler_params=params,
        name="pack_rows",
    )(*(pltpu.with_memory_space_constraint(v, pltpu.HBM) for v in (x, speed_factor, land_sea_mask)))
    second = lax.ppermute(second, both, row_second)
    first = lax.ppermute(first, "lat", row_first)
    east, west = pl.pallas_call(
        pack_columns_kernel,
        out_shape=[columns] * 2,
        in_specs=[vmem] * 3,
        out_specs=[vmem] * 2,
        compiler_params=params,
        cost_estimate=pl.CostEstimate(flops=2_000_000_000, bytes_accessed=5_000_000, transcendentals=0),
        name="pack_columns",
    )(x, moving, sea)
    halves = pl.pallas_call(
        inside_kernel,
        out_shape=pltpu.VMEM((breadth // 128, (PLANES + 4) * height, 128), f32),
        in_specs=[smem] * 2 + [vmem] * 3,
        out_specs=vmem,
        compiler_params=params,
        cost_estimate=pl.CostEstimate(flops=4_000_000_000, bytes_accessed=5_000_000, transcendentals=0),
        name="advance_inside",
    )(courant, headings, x, moving, sea)
    south, north, first, second = pl.pallas_call(
        functools.partial(corner_kernel, n_lat),
        out_shape=[row_halo] * 2 + [column_message] * 2,
        in_specs=[vmem] * 4,
        out_specs=[vmem] * 4,
        compiler_params=params,
        name="add_corners",
    )(second, first, east, west)
    second = lax.ppermute(second, "lon", column_second)
    first = lax.ppermute(first, "lon", column_first)

    lists = (devices * slots // 128, 128)
    slot_rows = devices * slots // 2
    slot_rows = devices * slots // 2
    table_shape = pltpu.VMEM((height * breadth, 128), f32)
    table, weight, edges = pl.pallas_call(
        profile_kernel,
        out_shape=[table_shape, shape(3 * (PLANES + 8), 128, kind=jnp.bfloat16), shape(2, 128, 256)],
        in_specs=[vmem] * 2,
        out_specs=[vmem] * 3,
        scratch_shapes=[pltpu.VMEM((128, 128), f32)],
        compiler_params=params,
        cost_estimate=pl.CostEstimate(flops=2_000_000_000, bytes_accessed=5_000_000, transcendentals=0),
        name="profiles_inside",
    )(halves, depth_kernel)
    propagated, picked, *_ = pl.pallas_call(
        finish_kernel,
        out_shape=[
            pltpu.HBM((PLANES * height, breadth), f32),
            pltpu.HBM((slot_rows, 128), jnp.bfloat16),
            pltpu.VMEM(halves.shape, f32),
            table_shape,
        ],
        in_specs=[smem] + [vmem] * 13,
        out_specs=[hbm, hbm, vmem, vmem],
        input_output_aliases={12: 2, 13: 3},
        scratch_shapes=[
            pltpu.VMEM(lists, jnp.int32),
            pltpu.VMEM((WINDOW // 2, 128), f32),
            pltpu.VMEM((slot_rows, 128), jnp.bfloat16),
            pltpu.SMEM((2 * WINDOW // 128, 128), jnp.int32),
            pltpu.SemaphoreType.DMA((breadth // 128,)),
            pltpu.SemaphoreType.DMA((2,)),
            pltpu.SemaphoreType.DMA,
        ],
        compiler_params=params,
        name="finish_and_pick",
    )(courant, send_rows.reshape(lists), moving, sea, weight, edges, south, north, second, first, lanes, subs, halves, table)

    picked = picked.reshape(devices, slots // 2, 128)
    received = lax.all_to_all(picked, both, split_axis=0, concat_axis=0, tiled=True)

    components = depth_kernel.shape[0]
    stokes = pl.pallas_call(
        add_kernel,
        out_shape=pltpu.HBM((components, OUT_DEV), f32),
        in_specs=[vmem] * 2,
        out_specs=hbm,
        scratch_shapes=[
            pltpu.VMEM(lists, jnp.int32),
            pltpu.VMEM((WINDOW // 2, 128), f32),
            pltpu.VMEM((components, OUT_DEV), f32),
            pltpu.SMEM((2 * WINDOW // 128, 128), jnp.int32),
            pltpu.SemaphoreType.DMA((2,)),
            pltpu.SemaphoreType.DMA,
        ]
        + [pltpu.VMEM((OUT_DEV + SPARE, 128), f32)] * (2 * N_ACC),
        compiler_params=pltpu.CompilerParams(vmem_limit_bytes=ADD_VMEM_LIMIT),
        name="add_profiles",
    )(recv_rows.reshape(lists), received.reshape(slot_rows, 128))
    return propagated.reshape(DIRS, FREQ, height, breadth), stokes


def solution(mesh):
    placed = (
        P(None, None, "lat", "lon"),
        P("lat", "lon"),
        P("lat", "lon"),
        P(),
        P(),
        P(("lat", "lon"), None, None),
        P(("lat", "lon"), None, None),
    )
    return jax.shard_map(
        functools.partial(body, mesh.shape["lat"], mesh.shape["lon"]),
        mesh=mesh,
        in_specs=placed,
        out_specs=(P(None, None, "lat", "lon"), P(None, ("lat", "lon"))),
        check_vma=False,
    )
```

```python
import functools
import math

import jax
import jax.numpy as jnp
import numpy as np
from jax import lax
from jax.experimental import pallas as pl
from jax.experimental.pallas import tpu as pltpu
from jax.sharding import PartitionSpec as P

DIRS = 36
FREQ = 2
PLANES = DIRS * FREQ
HALF = PLANES // 2
QUAD = PLANES // 4
OUT_DEV = 4096
SPARE = 64
N_ACC = 4
ROWS = HALF + 12
WINDOW = 1024
VMEM_LIMIT = 16 * 1024 * 1024
ADD_VMEM_LIMIT = 32 * 1024 * 1024


def exchange_pairs(n_lat, n_lon):
    def flat(j, i):
        return j * n_lon + i % n_lon

    row_first = [(j, j ^ 1) for j in range(n_lat)]
    row_second = []
    for i in range(n_lon):
        row_second += [(flat(0, i), flat(0, i)), (flat(n_lat - 1, i), flat(n_lat - 1, n_lon - 1 - i))]
        for j in range(1, n_lat - 1, 2):
            row_second += [(flat(j, i), flat(j + 1, i)), (flat(j + 1, i), flat(j, i))]
    column_first = [(i, i ^ 1) for i in range(n_lon)]
    column_second = [(i, (i + 1 if i % 2 else i - 1) % n_lon) for i in range(n_lon)]
    return row_first, row_second, column_first, column_second


def pack_rows_kernel(x_hbm, speed_hbm, mask_hbm, first_ref, second_ref, mov_ref, sea_ref,
                     up_ref, down_ref, top_rows, bottom_rows, speed_ref, mask_ref, sems):
    height, breadth = speed_ref.shape
    copies = [
        pltpu.make_async_copy(source, target, sems.at[k])
        for k, (source, target) in enumerate((
            (speed_hbm, speed_ref),
            (mask_hbm, mask_ref),
            (x_hbm.at[pl.ds(0, HALF), pl.ds(height - 8, 8), :], top_rows),
            (x_hbm.at[pl.ds(HALF, HALF), pl.ds(0, 8), :], bottom_rows),
        ))
    ]
    for copy in copies:
        copy.start()
    even = lax.axis_index("lat") % 2 == 0
    for copy in copies:
        copy.wait()
    sea = mask_ref[...].astype(jnp.float32)
    moving = speed_ref[...] * sea
    mov_ref[...] = moving
    sea_ref[...] = sea
    for k in range(2):
        for q in range(HALF):
            up_ref[k, q : q + 1, :] = top_rows[q, 7 - k : 8 - k, :]
            down_ref[k, q : q + 1, :] = bottom_rows[q, k : k + 1, :]
        up_ref[k, HALF : HALF + 1, :] = moving[height - 1 - k : height - k, :]
        down_ref[k, HALF : HALF + 1, :] = moving[k : k + 1, :]
        up_ref[k, HALF + 1 : HALF + 2, :] = sea[height - 1 - k : height - k, :]
        down_ref[k, HALF + 1 : HALF + 2, :] = sea[k : k + 1, :]
        up_ref[k, HALF + 2 :, :] = jnp.zeros((ROWS - HALF - 2, breadth), jnp.float32)
        down_ref[k, HALF + 2 :, :] = jnp.zeros((ROWS - HALF - 2, breadth), jnp.float32)

    @pl.when(even)
    def _():
        first_ref[...] = up_ref[...].astype(jnp.bfloat16)
        second_ref[...] = down_ref[...].astype(jnp.bfloat16)

    @pl.when(jnp.logical_not(even))
    def _():
        first_ref[...] = down_ref[...].astype(jnp.bfloat16)
        second_ref[...] = up_ref[...].astype(jnp.bfloat16)


def corner_kernel(n_lat, second_ref, first_ref, east_ref, west_ref, south_ref, north_ref, out_first, out_second):
    height = east_ref.shape[0]
    breadth = first_ref.shape[2]
    lat = lax.axis_index("lat")
    even = lat % 2 == 0

    used = HALF + 4

    @pl.when(even)
    def _():
        north_ref[...] = first_ref[...].astype(jnp.float32)[:, :used]
        south_ref[...] = second_ref[...].astype(jnp.float32)[:, :used]

    @pl.when(jnp.logical_not(even))
    def _():
        south_ref[...] = first_ref[...].astype(jnp.float32)[:, :used]
        north_ref[...] = second_ref[...].astype(jnp.float32)[:, :used]

    @pl.when(lat == 0)
    def _():
        south_ref[...] = jnp.zeros_like(south_ref)

    @pl.when(lat == n_lat - 1)
    def _():
        flip_i = lax.broadcasted_iota(jnp.int32, (breadth, breadth), 0)
        flip_j = lax.broadcasted_iota(jnp.int32, (breadth, breadth), 1)
        flip = (flip_i + flip_j == breadth - 1).astype(jnp.bfloat16)
        both = jnp.concatenate([second_ref[0], second_ref[1]], axis=0)
        flipped = jnp.dot(both, flip, preferred_element_type=jnp.float32)
        north_ref[0] = flipped[:used]
        north_ref[1] = flipped[ROWS : ROWS + used]

    plane = lax.broadcasted_iota(jnp.int32, (HALF + 4, 128), 0)
    lane = lax.broadcasted_iota(jnp.int32, (HALF + 4, 128), 1)
    south = south_ref[0] * south_ref[0, HALF : HALF + 1, :]
    north = north_ref[0] * north_ref[0, HALF : HALF + 1, :]

    def to_lanes(column, low, high, place):
        mine = (plane >= low) & (plane < high) & (lane == place)
        return jnp.where(mine, column, 0.0)

    east_edge = to_lanes(south[:, breadth - 1 :], 0, QUAD, 2 * plane + 1)
    east_edge += to_lanes(north[:, breadth - 1 :], QUAD, HALF, 2 * plane + 1)
    west_edge = to_lanes(south[:, :1], QUAD, HALF, 2 * plane - HALF)
    west_edge += to_lanes(north[:, :1], 0, QUAD, 2 * plane + HALF)
    east_edge = jnp.broadcast_to(jnp.sum(east_edge, axis=0, keepdims=True), (8, 128))
    west_edge = jnp.broadcast_to(jnp.sum(west_edge, axis=0, keepdims=True), (8, 128))
    even_lon = lax.axis_index("lon") % 2 == 0
    out_first[:height] = jnp.where(even_lon, east_ref[...], west_ref[...])
    out_second[:height] = jnp.where(even_lon, west_ref[...], east_ref[...])
    out_first[height:] = jnp.where(even_lon, east_edge, west_edge)
    out_second[height:] = jnp.where(even_lon, west_edge, east_edge)


def for_windows(list_ref, window, sems, work):
    lines = WINDOW // 128
    count = list_ref.shape[0] // lines

    def fetch(i, w):
        source = list_ref.at[pl.ds(pl.multiple_of(i * lines, lines), lines), :]
        return pltpu.make_async_copy(source, window.at[pl.ds(w * lines, lines), :], sems.at[w])

    for w in range(2):
        fetch(w, w).start()

    @pl.loop(0, count // 2)
    def _(t):
        for w in range(2):
            i = 2 * t + w
            fetch(i, w).wait()
            work(lambda k, start=w * lines: window[start + k // 128, k % 128], i)

            @pl.when(i + 2 < count)
            def _():
                fetch(i + 2, w).start()


def inside_kernel(courant_hbm, heading_hbm, x_hbm, mov_ref, sea_ref, halves, east_ref, west_ref,
                  x_ref, courant_ref, heading_ref, sems):
    height, breadth = mov_ref.shape
    small = [
        pltpu.make_async_copy(courant_hbm, courant_ref, sems.at[4]),
        pltpu.make_async_copy(heading_hbm, heading_ref, sems.at[5]),
    ]
    parts = [
        pltpu.make_async_copy(x_hbm.at[planes], x_ref.at[planes], sems.at[k])
        for k, planes in enumerate(pl.ds(k * QUAD, QUAD) for k in range(4))
    ]
    for copy in small + parts:
        copy.start()
    for copy in small:
        copy.wait()
    c0, c1 = courant_ref[0], courant_ref[1]
    moving = mov_ref[...]
    sea = sea_ref[...]
    lane = lax.broadcasted_iota(jnp.int32, (height, 128), 1)
    row = lax.broadcasted_iota(jnp.int32, (8, breadth), 0)
    for h in range(breadth // 128):
        halves[h, PLANES * height :, :] = jnp.zeros((4 * height, 128), jnp.float32)

    def quadrant(first, from_west, from_south):
        def upstream(flux):
            if from_west:
                moved = pltpu.roll(flux, 1, axis=1)
                side = jnp.concatenate([jnp.where(lane == 0, 0.0, moved[:, :128]), moved[:, 128:]], axis=1)
            else:
                moved = pltpu.roll(flux, breadth - 1, axis=1)
                edge = jnp.where(lane == 127, 0.0, moved[:, breadth - 128 :])
                side = jnp.concatenate([moved[:, : breadth - 128], edge], axis=1)
            if from_south:
                moved = pltpu.roll(flux, 1, axis=0)
                below = jnp.concatenate([jnp.where(row == 0, 0.0, moved[:8]), moved[8:]], axis=0)
            else:
                moved = pltpu.roll(flux, height - 1, axis=0)
                below = jnp.concatenate([moved[: height - 8], jnp.where(row == 7, 0.0, moved[height - 8 :])], axis=0)
            return side, below

        def step(t, carry):
            p = first + t
            courant = jnp.where(p % 2 == 1, c1, c0)
            cx = heading_ref[p] * courant
            cy = heading_ref[PLANES + p] * courant
            energy = x_ref[p]
            for _ in range(2):
                flux = moving * energy
                side, below = upstream(flux)
                div_x = cx * (flux - side) if from_west else cx * (side - flux)
                div_y = cy * (flux - below) if from_south else cy * (below - flux)
                energy = sea * ((energy - div_x) - div_y)
            start = pl.ds(pl.multiple_of(p * height, height), height)
            for h in range(breadth // 128):
                halves[h, start, :] = energy[:, h * 128 : (h + 1) * 128]
            return carry

        lax.fori_loop(0, QUAD, step, 0, unroll=6)

    for k, (from_west, from_south) in enumerate(((True, True), (False, True), (False, False), (True, False))):
        parts[k].wait()
        quadrant(k * QUAD, from_west, from_south)

    east = jnp.zeros((height, 128), jnp.float32)
    west = jnp.zeros((height, 128), jnp.float32)
    for q in range(HALF + 2):
        mine = lane // 2 == q
        if q < HALF:
            p_e = q if q < QUAD else q + HALF
            edge_e, edge_w = x_ref[p_e, :, breadth - 128 :], x_ref[q + QUAD, :, :128]
        else:
            field = moving if q == HALF else sea
            edge_e, edge_w = field[:, breadth - 128 :], field[:, :128]
        east = jnp.where(mine, pltpu.roll(edge_e, (2 * q + 2) % 128, axis=1), east)
        west = jnp.where(mine, pltpu.roll(edge_w, 2 * q, axis=1), west)
    east_ref[...] = east
    west_ref[...] = west


def profile_rows(halves, weight, table, first_row, count, height, breadth):
    pad = jnp.zeros((8, 128), jnp.bfloat16)
    blocks = []
    for k in range(count):
        for h in range(breadth // 128):
            spectra = halves[h, pl.ds(first_row + k, PLANES, stride=height), :]
            high = spectra.astype(jnp.bfloat16)
            low = (spectra - high.astype(jnp.float32)).astype(jnp.bfloat16)
            blocks.append(jnp.concatenate([high, pad, low, pad, high, pad], axis=0))
    stacked = jnp.concatenate(blocks, axis=1)
    profile = lax.dot_general(stacked, weight, (((0,), (0,)), ((), ())), preferred_element_type=jnp.float32)
    start = first_row * breadth
    if not isinstance(start, int):
        start = pl.multiple_of(start, 128)
    table[pl.ds(start, count * breadth), :] = profile


def profile_kernel(halves, kernel_ref, table, weight_ref, edge_ref, wide_kernel):
    height, breadth = halves.shape[1] // (PLANES + 4), table.shape[0] // (halves.shape[1] // (PLANES + 4))
    pad = jnp.zeros((8, 128), jnp.bfloat16)
    wide_kernel[...] = jnp.zeros((128, 128), jnp.float32)
    wide_kernel[:64, :PLANES] = kernel_ref[...]
    wide_kernel[64:, :PLANES] = kernel_ref[...]
    turned = wide_kernel[...].T
    weight_high = turned[:PLANES].astype(jnp.bfloat16)
    weight_low = (turned[:PLANES] - weight_high.astype(jnp.float32)).astype(jnp.bfloat16)
    weight = jnp.concatenate([weight_high, pad, weight_high, pad, weight_low, pad], axis=0)
    weight_ref[...] = weight

    lane = lax.broadcasted_iota(jnp.int32, (128, 128), 0)
    plane = lax.broadcasted_iota(jnp.int32, (128, 128), 1)
    q = lane // 2
    used = lane < 2 * HALF
    for side, owner in ((0, jnp.where(q < QUAD, q, q + HALF)), (1, q + QUAD)):
        for k in range(2):
            chosen = used & (plane == owner) & (lane % 2 == (k if side == 0 else 1 - k))
            edge_ref[side, :, k * 128 : (k + 1) * 128] = jnp.dot(
                chosen.astype(jnp.float32), turned, precision=lax.Precision.HIGHEST, preferred_element_type=jnp.float32
            )
    group = 8

    @pl.loop(0, height // group)
    def _(r):
        profile_rows(halves, weight, table, r * group, group, height, breadth)


def finish_kernel(courant_ref, cells_ref, mov_ref, sea_ref, weight_ref, edge_ref, south_ref, north_ref, second_ref,
                  first_ref, lanes_ref, subs_ref, halves_in, table_in, out_ref, picked_ref, halves, table,
                  cells, lines, picks, window, out_sems, window_sems, pick_sem):
    cells[...] = jnp.maximum(cells_ref[...], 0)
    height, breadth = mov_ref.shape
    c0, c1 = courant_ref[0], courant_ref[1]
    even_lon = lax.axis_index("lon") % 2 == 0
    from_west = jnp.where(even_lon, second_ref[...], first_ref[...])
    from_east = jnp.where(even_lon, first_ref[...], second_ref[...])
    corner_w, corner_e = from_west[height : height + 1], from_east[height : height + 1]

    lane = lax.broadcasted_iota(jnp.int32, (height, 128), 1)
    row = lax.broadcasted_iota(jnp.int32, (height, 128), 0)
    odd = lane % 2 == 1

    def columns(e0, near, far, corner, cx, cy, sign):
        mov = jnp.where(odd, e0[:, 2 * HALF + 1 : 2 * HALF + 2], e0[:, 2 * HALF : 2 * HALF + 1])
        sea = e0[:, 2 * HALF + 2 + near : 2 * HALF + 3 + near]
        f0 = mov * e0
        f_far = pltpu.roll(f0, 1 if near > far else 127, axis=1)
        f_south = jnp.where(row == 0, corner, pltpu.roll(f0, 1, axis=0))
        f_north = jnp.where(row == height - 1, corner, pltpu.roll(f0, height - 1, axis=0))
        div_x = cx * (f0 - f_far) if sign > 0 else cx * (f_far - f0)
        div_y = jnp.where(lane < HALF, cy * (f0 - f_south), cy * (f_north - f0))
        return f0, mov * (sea * ((e0 - div_x) - div_y))

    lanes = lanes_ref[...]
    lane_courant = jnp.where(lanes[4:5] > 0.5, c1, c0)
    cx_w, cy_w, cx_e, cy_e = (lanes[k : k + 1] * lane_courant for k in range(4))
    west_flux0, west_flux1 = columns(from_west[:height], 1, 0, corner_w, cx_w, cy_w, 1)
    east_flux0, east_flux1 = columns(from_east[:height], 0, 1, corner_e, cx_e, cy_e, -1)

    wide = lax.broadcasted_iota(jnp.int32, (HALF + 4, breadth), 1)
    plane = lax.broadcasted_iota(jnp.int32, (HALF + 4, 1), 0)
    plane_l = lax.broadcasted_iota(jnp.int32, (HALF + 4, 128), 0)
    lane_l = lax.broadcasted_iota(jnp.int32, (HALF + 4, 128), 1)
    subs = subs_ref[...]
    sub_courant = jnp.where(plane % 2 == 1, c1, c0)

    def to_sublanes(corner, lane_of):
        return jnp.sum(jnp.where(lane_l == lane_of, corner, 0.0), axis=1, keepdims=True)

    def rows(near, far, first_west, west_corner, east_corner, cx, cy, sign):
        mov, sea = near[HALF : HALF + 1], near[HALF + 1 : HALF + 2]
        f0 = mov * near
        f_far = far[HALF : HALF + 1] * far
        f_west = jnp.where(wide == 0, west_corner, pltpu.roll(f0, 1, axis=1))
        f_east = jnp.where(wide == breadth - 1, east_corner, pltpu.roll(f0, breadth - 1, axis=1))
        from_west = (plane < QUAD) if first_west else (plane >= QUAD)
        div_x = jnp.where(from_west, cx * (f0 - f_west), cx * (f_east - f0))
        div_y = cy * (f0 - f_far) if sign > 0 else cy * (f_far - f0)
        return f0, mov * (sea * ((near - div_x) - div_y))

    sw = to_sublanes(corner_w, 2 * plane_l + 1)
    se = to_sublanes(corner_e, 2 * plane_l - HALF)
    ne = to_sublanes(corner_e, 2 * plane_l + HALF)
    nw = sw
    cx_s, cy_s, cx_n, cy_n = (subs[:, k : k + 1] * sub_courant for k in range(4))
    south_flux0, south_flux1 = rows(south_ref[0], south_ref[1], True, sw, se, cx_s, cy_s, 1)
    north_flux0, north_flux1 = rows(north_ref[0], north_ref[1], False, nw, ne, cx_n, cy_n, -1)

    def add_rows(first, near, next_row, flux0, flux1, cx, cy, first_west):
        sea0, sea1 = sea_ref[near : near + 1, :], sea_ref[next_row : next_row + 1, :]
        change = sea0 * (cy * flux0)
        flux = mov_ref[near : near + 1, :] * change
        west_flux = jnp.where(wide == 0, 0.0, pltpu.roll(flux, 1, axis=1))
        east_flux = jnp.where(wide == breadth - 1, 0.0, pltpu.roll(flux, breadth - 1, axis=1))
        from_west = (plane < QUAD) if first_west else (plane >= QUAD)
        div_x = jnp.where(from_west, cx * (flux - west_flux), cx * (east_flux - flux))
        near_change = sea0 * (((change - div_x) - cy * flux) + cy * flux1)
        next_change = sea1 * (cy * flux)
        for at, delta in ((near, near_change), (next_row, next_change)):
            for h in range(breadth // 128):
                place = pl.ds(first * height + at, HALF + 4, stride=height)
                halves[h, place, :] = halves[h, place, :] + delta[:, h * 128 : (h + 1) * 128]

    def add_columns(half, near, next_column, flux0, flux1, cx, cy, from_west):
        sea0, sea1 = sea_ref[:, near : near + 1], sea_ref[:, next_column : next_column + 1]
        change = sea0 * (cx * flux0)
        flux = mov_ref[:, near : near + 1] * change
        south_flux = jnp.where(row == 0, 0.0, pltpu.roll(flux, 1, axis=0))
        north_flux = jnp.where(row == height - 1, 0.0, pltpu.roll(flux, height - 1, axis=0))
        div_y = jnp.where(lane < HALF, cy * (flux - south_flux), cy * (north_flux - flux))
        near_change = sea0 * (((change - cx * flux) - div_y) + cx * flux1)
        next_change = sea1 * (cx * flux)
        if from_west:
            both = jnp.where(odd, next_change, pltpu.roll(near_change, 127, axis=1))
        else:
            both = jnp.where(odd, pltpu.roll(near_change, 1, axis=1), next_change)
        edge = lane < 2 if from_west else lane >= 126
        for q in range(HALF):
            p = q + QUAD if not from_west else (q if q < QUAD else q + HALF)
            turned = pltpu.roll(both, ((128 if from_west else 126) - 2 * q) % 128, axis=1)
            place = pl.ds(p * height, height)
            halves[half, place, :] = halves[half, place, :] + jnp.where(edge, turned, 0.0)
        return jnp.where(lane < 2 * HALF, both, 0.0)

    add_rows(0, 0, 1, south_flux0, south_flux1, cx_s, cy_s, True)
    add_rows(HALF, height - 1, height - 2, north_flux0, north_flux1, cx_n, -cy_n, False)
    change_w = add_columns(0, 0, 1, west_flux0, west_flux1, cx_w, cy_w, True)
    change_e = add_columns(breadth // 128 - 1, breadth - 1, breadth - 2, east_flux0, east_flux1, -cx_e, cy_e, False)
    whole = pl.ds(0, PLANES * height)
    writes = [
        pltpu.make_async_copy(halves.at[h, whole, :], out_ref.at[:, pl.ds(h * 128, 128)], out_sems.at[h])
        for h in range(breadth // 128)
    ]
    for write in writes:
        write.start()

    for change, columns_of, near, next_column in ((change_w, 0, 0, 1), (change_e, 1, breadth - 1, breadth - 2)):
        profile = jnp.dot(
            change, edge_ref[columns_of], precision=lax.Precision.HIGHEST, preferred_element_type=jnp.float32
        )
        for k, column in enumerate((near, next_column)):
            place = pl.ds(column, height, stride=breadth)
            table[place, :] = table[place, :] + profile[:, k * 128 : (k + 1) * 128]
    for first_row in (0, height - 2):
        profile_rows(halves, weight_ref[...], table, first_row, 2, height, breadth)

    first_half = lax.broadcasted_iota(jnp.int32, (1, 128), 1) < 64
    half = WINDOW // 2

    def pick(cell, i):
        for g in range(WINDOW // 16):
            for j in range(8):
                one, two = cell(16 * g + j), cell(16 * g + 8 + j)
                line = jnp.where(first_half, table[pl.ds(one, 1), :], table[pl.ds(two, 1), :])
                lines[8 * g + j : 8 * g + j + 1, :] = line
        here = pl.ds(pl.multiple_of(i * half, half), half)
        picks[here, :] = lines[...].astype(jnp.bfloat16)
        pltpu.make_async_copy(picks.at[here, :], picked_ref.at[here, :], pick_sem).start()

    for_windows(cells, window, window_sems, pick)
    pltpu.make_async_copy(picks, picked_ref, pick_sem).wait()
    for write in writes:
        write.wait()


def add_kernel(rows_ref, values_ref, out_ref, targets, lines, tile_sums, window, window_sems, out_sem, *sums):
    n_acc = len(sums) // 2
    tile = out_ref.shape[1]
    block = 512
    half = WINDOW // 2
    slot = lax.broadcasted_iota(jnp.int32, targets.shape, 1)
    spare = tile + (slot // 16 * 8 + slot % 8) % SPARE
    targets[...] = jnp.where(rows_ref[...] < 0, spare, rows_ref[...])

    @pl.loop(0, tile // block)
    def _(i):
        for total in sums:
            total[pl.ds(pl.multiple_of(i * block, block), block), :] = jnp.zeros((block, 128), jnp.float32)

    def add(row, i):
        lines[...] = values_ref[pl.ds(pl.multiple_of(i * half, half), half), :].astype(jnp.float32)
        for g in range(WINDOW // 16):
            for j in range(8):
                one, two = row(16 * g + j), row(16 * g + 8 + j)
                line = lines[8 * g + j : 8 * g + j + 1, :]
                left, right = sums[j % n_acc], sums[n_acc + j % n_acc]
                left[pl.ds(one, 1), :] = left[pl.ds(one, 1), :] + line
                right[pl.ds(two, 1), :] = right[pl.ds(two, 1), :] + line

    for_windows(targets, window, window_sems, add)
    first_half = lax.broadcasted_iota(jnp.int32, (block, 128), 1) < 64

    @pl.loop(0, tile // block)
    def _(i):
        here = pl.ds(pl.multiple_of(i * block, block), block)
        left, right = sums[0][here, :], sums[n_acc][here, :]
        for q in range(1, n_acc):
            left = left + sums[q][here, :]
            right = right + sums[n_acc + q][here, :]
        both = jnp.where(first_half, left, right).T
        tile_sums[:, here] = both[:64] + both[64:]
        pltpu.make_async_copy(tile_sums.at[:, here], out_ref.at[:, here], out_sem).start()

    pltpu.make_async_copy(tile_sums, out_ref, out_sem).wait()


def constant_tables():
    heading = (np.arange(DIRS) + 0.5) * (2.0 * math.pi / DIRS)
    cos = np.repeat(np.cos(heading), FREQ)
    sin = np.repeat(np.sin(heading), FREQ)
    lanes = np.zeros((8, 128))
    q = np.arange(HALF)
    from_west = np.where(q < QUAD, q, q + HALF)
    from_east = q + QUAD
    for column in range(2):
        lanes[0, 2 * q + column] = cos[from_west]
        lanes[1, 2 * q + column] = sin[from_west]
        lanes[2, 2 * q + column] = cos[from_east]
        lanes[3, 2 * q + column] = sin[from_east]
        lanes[4, 2 * q + column] = q % 2
    subs = np.zeros((HALF + 4, 128))
    subs[:HALF, 0], subs[:HALF, 1] = cos[:HALF], sin[:HALF]
    subs[:HALF, 2], subs[:HALF, 3] = cos[HALF:], sin[HALF:]
    return [t.astype(np.float32) for t in (np.concatenate([cos, sin]), lanes, subs)]


def body(n_lat, n_lon, spectrum, speed_factor, land_sea_mask, courant, depth_kernel, send_rows, recv_rows):
    height, breadth = speed_factor.shape
    devices, slots = send_rows.shape[1:]
    x = spectrum.reshape(PLANES, height, breadth)
    f32 = jnp.float32
    vmem = pl.BlockSpec(memory_space=pltpu.VMEM)
    smem = pl.BlockSpec(memory_space=pltpu.SMEM)
    hbm = pl.BlockSpec(memory_space=pltpu.HBM)
    params = pltpu.CompilerParams(vmem_limit_bytes=VMEM_LIMIT)

    both = ("lat", "lon")

    def in_hbm(*arrays):
        return [pltpu.with_memory_space_constraint(array, pltpu.HBM) for array in arrays]

    def shape(*dims, kind=f32):
        return jax.ShapeDtypeStruct(dims, kind)

    headings, lanes, subs = constant_tables()
    row_message = shape(2, ROWS, breadth, kind=jnp.bfloat16)
    row_halo = shape(2, HALF + 4, breadth)
    columns = shape(height, 128)
    column_message = shape(height + 8, 128)
    row_first, row_second, column_first, column_second = exchange_pairs(n_lat, n_lon)
    first, second, moving, sea = pl.pallas_call(
        pack_rows_kernel,
        out_shape=[row_message] * 2 + [shape(height, breadth)] * 2,
        in_specs=[hbm] * 3,
        out_specs=[vmem] * 4,
        scratch_shapes=[pltpu.VMEM((2, ROWS, breadth), f32)] * 2
        + [pltpu.VMEM((HALF, 8, breadth), f32)] * 2
        + [pltpu.VMEM((height, breadth), f32), pltpu.VMEM((height, breadth), jnp.int32), pltpu.SemaphoreType.DMA((4,))],
        compiler_params=params,
        name="pack_rows",
    )(*in_hbm(x, speed_factor, land_sea_mask))
    second = lax.ppermute(second, both, row_second)
    first = lax.ppermute(first, "lat", row_first)
    halves, east, west = pl.pallas_call(
        inside_kernel,
        out_shape=[pltpu.VMEM((breadth // 128, (PLANES + 4) * height, 128), f32)] + [columns] * 2,
        in_specs=[hbm] * 3 + [vmem] * 2,
        out_specs=[vmem] * 3,
        scratch_shapes=[
            pltpu.VMEM((PLANES, height, breadth), f32),
            pltpu.SMEM(courant.shape, f32),
            pltpu.SMEM(headings.shape, f32),
            pltpu.SemaphoreType.DMA((6,)),
        ],
        compiler_params=params,
        cost_estimate=pl.CostEstimate(flops=4_000_000_000, bytes_accessed=5_000_000, transcendentals=0),
        name="advance_inside",
    )(*in_hbm(courant, headings, x), moving, sea)
    south, north, first, second = pl.pallas_call(
        functools.partial(corner_kernel, n_lat),
        out_shape=[row_halo] * 2 + [column_message] * 2,
        in_specs=[vmem] * 4,
        out_specs=[vmem] * 4,
        compiler_params=params,
        name="add_corners",
    )(second, first, east, west)
    second = lax.ppermute(second, "lon", column_second)
    first = lax.ppermute(first, "lon", column_first)

    lists = (devices * slots // 128, 128)
    slot_rows = devices * slots // 2
    slot_rows = devices * slots // 2
    table_shape = pltpu.VMEM((height * breadth, 128), f32)
    table, weight, edges = pl.pallas_call(
        profile_kernel,
        out_shape=[table_shape, shape(3 * (PLANES + 8), 128, kind=jnp.bfloat16), shape(2, 128, 256)],
        in_specs=[vmem] * 2,
        out_specs=[vmem] * 3,
        scratch_shapes=[pltpu.VMEM((128, 128), f32)],
        compiler_params=params,
        cost_estimate=pl.CostEstimate(flops=2_000_000_000, bytes_accessed=5_000_000, transcendentals=0),
        name="profiles_inside",
    )(halves, depth_kernel)
    propagated, picked, *_ = pl.pallas_call(
        finish_kernel,
        out_shape=[
            pltpu.HBM((PLANES * height, breadth), f32),
            pltpu.HBM((slot_rows, 128), jnp.bfloat16),
            pltpu.VMEM(halves.shape, f32),
            table_shape,
        ],
        in_specs=[smem] + [vmem] * 13,
        out_specs=[hbm, hbm, vmem, vmem],
        input_output_aliases={12: 2, 13: 3},
        scratch_shapes=[
            pltpu.VMEM(lists, jnp.int32),
            pltpu.VMEM((WINDOW // 2, 128), f32),
            pltpu.VMEM((slot_rows, 128), jnp.bfloat16),
            pltpu.SMEM((2 * WINDOW // 128, 128), jnp.int32),
            pltpu.SemaphoreType.DMA((breadth // 128,)),
            pltpu.SemaphoreType.DMA((2,)),
            pltpu.SemaphoreType.DMA,
        ],
        compiler_params=params,
        name="finish_and_pick",
    )(courant, send_rows.reshape(lists), moving, sea, weight, edges, south, north, second, first, lanes, subs, halves, table)

    picked = picked.reshape(devices, slots // 2, 128)
    received = lax.all_to_all(picked, both, split_axis=0, concat_axis=0, tiled=True)

    components = depth_kernel.shape[0]
    stokes = pl.pallas_call(
        add_kernel,
        out_shape=pltpu.HBM((components, OUT_DEV), f32),
        in_specs=[vmem] * 2,
        out_specs=hbm,
        scratch_shapes=[
            pltpu.VMEM(lists, jnp.int32),
            pltpu.VMEM((WINDOW // 2, 128), f32),
            pltpu.VMEM((components, OUT_DEV), f32),
            pltpu.SMEM((2 * WINDOW // 128, 128), jnp.int32),
            pltpu.SemaphoreType.DMA((2,)),
            pltpu.SemaphoreType.DMA,
        ]
        + [pltpu.VMEM((OUT_DEV + SPARE, 128), f32)] * (2 * N_ACC),
        compiler_params=pltpu.CompilerParams(vmem_limit_bytes=ADD_VMEM_LIMIT),
        name="add_profiles",
    )(recv_rows.reshape(lists), received.reshape(slot_rows, 128))
    return propagated.reshape(DIRS, FREQ, height, breadth), stokes


def solution(mesh):
    placed = (
        P(None, None, "lat", "lon"),
        P("lat", "lon"),
        P("lat", "lon"),
        P(),
        P(),
        P(("lat", "lon"), None, None),
        P(("lat", "lon"), None, None),
    )
    return jax.shard_map(
        functools.partial(body, mesh.shape["lat"], mesh.shape["lon"]),
        mesh=mesh,
        in_specs=placed,
        out_specs=(P(None, None, "lat", "lon"), P(None, ("lat", "lon"))),
        check_vma=False,
    )
```

```python
import functools
import math

import jax
import jax.numpy as jnp
import numpy as np
from jax import lax
from jax.experimental import pallas as pl
from jax.experimental.pallas import tpu as pltpu
from jax.sharding import PartitionSpec as P

DIRS = 36
FREQ = 2
PLANES = DIRS * FREQ
HALF = PLANES // 2
QUAD = PLANES // 4
OUT_DEV = 4096
SPARE = 64
N_ACC = 4
ROWS = HALF + 12
WINDOW = 1024
VMEM_LIMIT = 16 * 1024 * 1024
ADD_VMEM_LIMIT = 32 * 1024 * 1024


def exchange_pairs(n_lat, n_lon):
    def flat(j, i):
        return j * n_lon + i % n_lon

    row_first = [(j, j ^ 1) for j in range(n_lat)]
    row_second = []
    for i in range(n_lon):
        row_second += [(flat(0, i), flat(0, i)), (flat(n_lat - 1, i), flat(n_lat - 1, n_lon - 1 - i))]
        for j in range(1, n_lat - 1, 2):
            row_second += [(flat(j, i), flat(j + 1, i)), (flat(j + 1, i), flat(j, i))]
    column_first = [(i, i ^ 1) for i in range(n_lon)]
    column_second = [(i, (i + 1 if i % 2 else i - 1) % n_lon) for i in range(n_lon)]
    return row_first, row_second, column_first, column_second


def is_early():
    return lax.axis_index("lon") % 4 < 2


def pack_rows_kernel(courant_hbm, heading_hbm, x_hbm, speed_hbm, mask_hbm,
                     first_ref, second_ref, mov_ref, sea_ref, halves, east_ref, west_ref,
                     up_ref, down_ref, top_rows, bottom_rows, speed_ref, mask_ref, sems, *scratch):
    height, breadth = speed_ref.shape
    copies = [
        pltpu.make_async_copy(source, target, sems.at[k])
        for k, (source, target) in enumerate((
            (speed_hbm, speed_ref),
            (mask_hbm, mask_ref),
            (x_hbm.at[pl.ds(0, HALF), pl.ds(height - 8, 8), :], top_rows),
            (x_hbm.at[pl.ds(HALF, HALF), pl.ds(0, 8), :], bottom_rows),
        ))
    ]
    for copy in copies:
        copy.start()
    even = lax.axis_index("lat") % 2 == 0
    for copy in copies:
        copy.wait()
    sea = mask_ref[...].astype(jnp.float32)
    moving = speed_ref[...] * sea
    mov_ref[...] = moving
    sea_ref[...] = sea
    for k in range(2):
        for q in range(HALF):
            up_ref[k, q : q + 1, :] = top_rows[q, 7 - k : 8 - k, :]
            down_ref[k, q : q + 1, :] = bottom_rows[q, k : k + 1, :]
        up_ref[k, HALF : HALF + 1, :] = moving[height - 1 - k : height - k, :]
        down_ref[k, HALF : HALF + 1, :] = moving[k : k + 1, :]
        up_ref[k, HALF + 1 : HALF + 2, :] = sea[height - 1 - k : height - k, :]
        down_ref[k, HALF + 1 : HALF + 2, :] = sea[k : k + 1, :]
        up_ref[k, HALF + 2 :, :] = jnp.zeros((ROWS - HALF - 2, breadth), jnp.float32)
        down_ref[k, HALF + 2 :, :] = jnp.zeros((ROWS - HALF - 2, breadth), jnp.float32)

    @pl.when(even)
    def _():
        first_ref[...] = up_ref[...].astype(jnp.bfloat16)
        second_ref[...] = down_ref[...].astype(jnp.bfloat16)

    @pl.when(jnp.logical_not(even))
    def _():
        first_ref[...] = down_ref[...].astype(jnp.bfloat16)
        second_ref[...] = up_ref[...].astype(jnp.bfloat16)

    @pl.when(is_early())
    def _():
        advance_inside(courant_hbm, heading_hbm, x_hbm, mov_ref, sea_ref, halves, east_ref, west_ref, *scratch)


def corner_kernel(n_lat, second_ref, first_ref, east_ref, west_ref, halves, kernel_ref,
                  south_ref, north_ref, out_first, out_second, table, weight_ref, edge_ref, wide_kernel):
    height = east_ref.shape[0]
    breadth = first_ref.shape[2]
    lat = lax.axis_index("lat")
    even = lat % 2 == 0

    used = HALF + 4

    @pl.when(even)
    def _():
        north_ref[...] = first_ref[...].astype(jnp.float32)[:, :used]
        south_ref[...] = second_ref[...].astype(jnp.float32)[:, :used]

    @pl.when(jnp.logical_not(even))
    def _():
        south_ref[...] = first_ref[...].astype(jnp.float32)[:, :used]
        north_ref[...] = second_ref[...].astype(jnp.float32)[:, :used]

    @pl.when(lat == 0)
    def _():
        south_ref[...] = jnp.zeros_like(south_ref)

    @pl.when(lat == n_lat - 1)
    def _():
        flip_i = lax.broadcasted_iota(jnp.int32, (breadth, breadth), 0)
        flip_j = lax.broadcasted_iota(jnp.int32, (breadth, breadth), 1)
        flip = (flip_i + flip_j == breadth - 1).astype(jnp.bfloat16)
        both = jnp.concatenate([second_ref[0], second_ref[1]], axis=0)
        flipped = jnp.dot(both, flip, preferred_element_type=jnp.float32)
        north_ref[0] = flipped[:used]
        north_ref[1] = flipped[ROWS : ROWS + used]

    plane = lax.broadcasted_iota(jnp.int32, (HALF + 4, 128), 0)
    lane = lax.broadcasted_iota(jnp.int32, (HALF + 4, 128), 1)
    south = south_ref[0] * south_ref[0, HALF : HALF + 1, :]
    north = north_ref[0] * north_ref[0, HALF : HALF + 1, :]

    def to_lanes(column, low, high, place):
        mine = (plane >= low) & (plane < high) & (lane == place)
        return jnp.where(mine, column, 0.0)

    east_edge = to_lanes(south[:, breadth - 1 :], 0, QUAD, 2 * plane + 1)
    east_edge += to_lanes(north[:, breadth - 1 :], QUAD, HALF, 2 * plane + 1)
    west_edge = to_lanes(south[:, :1], QUAD, HALF, 2 * plane - HALF)
    west_edge += to_lanes(north[:, :1], 0, QUAD, 2 * plane + HALF)
    east_edge = jnp.broadcast_to(jnp.sum(east_edge, axis=0, keepdims=True), (8, 128))
    west_edge = jnp.broadcast_to(jnp.sum(west_edge, axis=0, keepdims=True), (8, 128))
    even_lon = lax.axis_index("lon") % 2 == 0
    out_first[:height] = jnp.where(even_lon, east_ref[...], west_ref[...])
    out_second[:height] = jnp.where(even_lon, west_ref[...], east_ref[...])
    out_first[height:] = jnp.where(even_lon, east_edge, west_edge)
    out_second[height:] = jnp.where(even_lon, west_edge, east_edge)

    @pl.when(is_early())
    def _():
        profiles_inside(halves, kernel_ref, table, weight_ref, edge_ref, wide_kernel)


def for_windows(list_ref, window, sems, work):
    lines = WINDOW // 128
    count = list_ref.shape[0] // lines

    def fetch(i, w):
        source = list_ref.at[pl.ds(pl.multiple_of(i * lines, lines), lines), :]
        return pltpu.make_async_copy(source, window.at[pl.ds(w * lines, lines), :], sems.at[w])

    for w in range(2):
        fetch(w, w).start()

    @pl.loop(0, count // 2)
    def _(t):
        for w in range(2):
            i = 2 * t + w
            fetch(i, w).wait()
            work(lambda k, start=w * lines: window[start + k // 128, k % 128], i)

            @pl.when(i + 2 < count)
            def _():
                fetch(i + 2, w).start()


def inside_kernel(courant_hbm, heading_hbm, x_hbm, mov_ref, sea_ref, _0, _1, _2, halves, east_ref, west_ref, *scratch):
    @pl.when(jnp.logical_not(is_early()))
    def _():
        advance_inside(courant_hbm, heading_hbm, x_hbm, mov_ref, sea_ref, halves, east_ref, west_ref, *scratch)


def advance_inside(courant_hbm, heading_hbm, x_hbm, mov_ref, sea_ref, halves, east_ref, west_ref,
                   x_ref, courant_ref, heading_ref, sems):
    height, breadth = mov_ref.shape
    small = [
        pltpu.make_async_copy(courant_hbm, courant_ref, sems.at[4]),
        pltpu.make_async_copy(heading_hbm, heading_ref, sems.at[5]),
    ]
    parts = [
        pltpu.make_async_copy(x_hbm.at[planes], x_ref.at[planes], sems.at[k])
        for k, planes in enumerate(pl.ds(k * QUAD, QUAD) for k in range(4))
    ]
    for copy in small + parts:
        copy.start()
    for copy in small:
        copy.wait()
    c0, c1 = courant_ref[0], courant_ref[1]
    moving = mov_ref[...]
    sea = sea_ref[...]
    lane = lax.broadcasted_iota(jnp.int32, (height, 128), 1)
    row = lax.broadcasted_iota(jnp.int32, (8, breadth), 0)
    for h in range(breadth // 128):
        halves[h, PLANES * height :, :] = jnp.zeros((4 * height, 128), jnp.float32)

    def quadrant(first, from_west, from_south):
        def upstream(flux):
            if from_west:
                moved = pltpu.roll(flux, 1, axis=1)
                side = jnp.concatenate([jnp.where(lane == 0, 0.0, moved[:, :128]), moved[:, 128:]], axis=1)
            else:
                moved = pltpu.roll(flux, breadth - 1, axis=1)
                edge = jnp.where(lane == 127, 0.0, moved[:, breadth - 128 :])
                side = jnp.concatenate([moved[:, : breadth - 128], edge], axis=1)
            if from_south:
                moved = pltpu.roll(flux, 1, axis=0)
                below = jnp.concatenate([jnp.where(row == 0, 0.0, moved[:8]), moved[8:]], axis=0)
            else:
                moved = pltpu.roll(flux, height - 1, axis=0)
                below = jnp.concatenate([moved[: height - 8], jnp.where(row == 7, 0.0, moved[height - 8 :])], axis=0)
            return side, below

        def step(t, carry):
            p = first + t
            courant = jnp.where(p % 2 == 1, c1, c0)
            cx = heading_ref[p] * courant
            cy = heading_ref[PLANES + p] * courant
            energy = x_ref[p]
            for _ in range(2):
                flux = moving * energy
                side, below = upstream(flux)
                div_x = cx * (flux - side) if from_west else cx * (side - flux)
                div_y = cy * (flux - below) if from_south else cy * (below - flux)
                energy = sea * ((energy - div_x) - div_y)
            start = pl.ds(pl.multiple_of(p * height, height), height)
            for h in range(breadth // 128):
                halves[h, start, :] = energy[:, h * 128 : (h + 1) * 128]
            return carry

        lax.fori_loop(0, QUAD, step, 0, unroll=6)

    for k, (from_west, from_south) in enumerate(((True, True), (False, True), (False, False), (True, False))):
        parts[k].wait()
        quadrant(k * QUAD, from_west, from_south)

    east = jnp.zeros((height, 128), jnp.float32)
    west = jnp.zeros((height, 128), jnp.float32)
    for q in range(HALF + 2):
        mine = lane // 2 == q
        if q < HALF:
            p_e = q if q < QUAD else q + HALF
            edge_e, edge_w = x_ref[p_e, :, breadth - 128 :], x_ref[q + QUAD, :, :128]
        else:
            field = moving if q == HALF else sea
            edge_e, edge_w = field[:, breadth - 128 :], field[:, :128]
        east = jnp.where(mine, pltpu.roll(edge_e, (2 * q + 2) % 128, axis=1), east)
        west = jnp.where(mine, pltpu.roll(edge_w, 2 * q, axis=1), west)
    east_ref[...] = east
    west_ref[...] = west


def profile_rows(halves, weight, table, first_row, count, height, breadth):
    pad = jnp.zeros((8, 128), jnp.bfloat16)
    blocks = []
    for k in range(count):
        for h in range(breadth // 128):
            spectra = halves[h, pl.ds(first_row + k, PLANES, stride=height), :]
            high = spectra.astype(jnp.bfloat16)
            low = (spectra - high.astype(jnp.float32)).astype(jnp.bfloat16)
            blocks.append(jnp.concatenate([high, pad, low, pad, high, pad], axis=0))
    stacked = jnp.concatenate(blocks, axis=1)
    profile = lax.dot_general(stacked, weight, (((0,), (0,)), ((), ())), preferred_element_type=jnp.float32)
    start = first_row * breadth
    if not isinstance(start, int):
        start = pl.multiple_of(start, 128)
    table[pl.ds(start, count * breadth), :] = profile


def profile_kernel(halves, kernel_ref, _0, _1, _2, table, weight_ref, edge_ref, wide_kernel):
    @pl.when(jnp.logical_not(is_early()))
    def _():
        profiles_inside(halves, kernel_ref, table, weight_ref, edge_ref, wide_kernel)


def profiles_inside(halves, kernel_ref, table, weight_ref, edge_ref, wide_kernel):
    height, breadth = halves.shape[1] // (PLANES + 4), table.shape[0] // (halves.shape[1] // (PLANES + 4))
    pad = jnp.zeros((8, 128), jnp.bfloat16)
    wide_kernel[...] = jnp.zeros((128, 128), jnp.float32)
    wide_kernel[:64, :PLANES] = kernel_ref[...]
    wide_kernel[64:, :PLANES] = kernel_ref[...]
    turned = wide_kernel[...].T
    weight_high = turned[:PLANES].astype(jnp.bfloat16)
    weight_low = (turned[:PLANES] - weight_high.astype(jnp.float32)).astype(jnp.bfloat16)
    weight = jnp.concatenate([weight_high, pad, weight_high, pad, weight_low, pad], axis=0)
    weight_ref[...] = weight

    lane = lax.broadcasted_iota(jnp.int32, (128, 128), 0)
    plane = lax.broadcasted_iota(jnp.int32, (128, 128), 1)
    q = lane // 2
    used = lane < 2 * HALF
    for side, owner in ((0, jnp.where(q < QUAD, q, q + HALF)), (1, q + QUAD)):
        for k in range(2):
            chosen = used & (plane == owner) & (lane % 2 == (k if side == 0 else 1 - k))
            edge_ref[side, :, k * 128 : (k + 1) * 128] = jnp.dot(
                chosen.astype(jnp.float32), turned, precision=lax.Precision.HIGHEST, preferred_element_type=jnp.float32
            )
    group = 8

    @pl.loop(0, height // group)
    def _(r):
        profile_rows(halves, weight, table, r * group, group, height, breadth)


def finish_kernel(courant_ref, cells_ref, mov_ref, sea_ref, weight_ref, edge_ref, south_ref, north_ref, second_ref,
                  first_ref, lanes_ref, subs_ref, halves_in, table_in, out_ref, picked_ref, halves, table,
                  cells, lines, picks, window, out_sems, window_sems, pick_sem):
    cells[...] = jnp.maximum(cells_ref[...], 0)
    height, breadth = mov_ref.shape
    c0, c1 = courant_ref[0], courant_ref[1]
    even_lon = lax.axis_index("lon") % 2 == 0
    from_west = jnp.where(even_lon, second_ref[...], first_ref[...])
    from_east = jnp.where(even_lon, first_ref[...], second_ref[...])
    corner_w, corner_e = from_west[height : height + 1], from_east[height : height + 1]

    lane = lax.broadcasted_iota(jnp.int32, (height, 128), 1)
    row = lax.broadcasted_iota(jnp.int32, (height, 128), 0)
    odd = lane % 2 == 1

    def columns(e0, near, far, corner, cx, cy, sign):
        mov = jnp.where(odd, e0[:, 2 * HALF + 1 : 2 * HALF + 2], e0[:, 2 * HALF : 2 * HALF + 1])
        sea = e0[:, 2 * HALF + 2 + near : 2 * HALF + 3 + near]
        f0 = mov * e0
        f_far = pltpu.roll(f0, 1 if near > far else 127, axis=1)
        f_south = jnp.where(row == 0, corner, pltpu.roll(f0, 1, axis=0))
        f_north = jnp.where(row == height - 1, corner, pltpu.roll(f0, height - 1, axis=0))
        div_x = cx * (f0 - f_far) if sign > 0 else cx * (f_far - f0)
        div_y = jnp.where(lane < HALF, cy * (f0 - f_south), cy * (f_north - f0))
        return f0, mov * (sea * ((e0 - div_x) - div_y))

    lanes = lanes_ref[...]
    lane_courant = jnp.where(lanes[4:5] > 0.5, c1, c0)
    cx_w, cy_w, cx_e, cy_e = (lanes[k : k + 1] * lane_courant for k in range(4))
    west_flux0, west_flux1 = columns(from_west[:height], 1, 0, corner_w, cx_w, cy_w, 1)
    east_flux0, east_flux1 = columns(from_east[:height], 0, 1, corner_e, cx_e, cy_e, -1)

    wide = lax.broadcasted_iota(jnp.int32, (HALF + 4, breadth), 1)
    plane = lax.broadcasted_iota(jnp.int32, (HALF + 4, 1), 0)
    plane_l = lax.broadcasted_iota(jnp.int32, (HALF + 4, 128), 0)
    lane_l = lax.broadcasted_iota(jnp.int32, (HALF + 4, 128), 1)
    subs = subs_ref[...]
    sub_courant = jnp.where(plane % 2 == 1, c1, c0)

    def to_sublanes(corner, lane_of):
        return jnp.sum(jnp.where(lane_l == lane_of, corner, 0.0), axis=1, keepdims=True)

    def rows(near, far, first_west, west_corner, east_corner, cx, cy, sign):
        mov, sea = near[HALF : HALF + 1], near[HALF + 1 : HALF + 2]
        f0 = mov * near
        f_far = far[HALF : HALF + 1] * far
        f_west = jnp.where(wide == 0, west_corner, pltpu.roll(f0, 1, axis=1))
        f_east = jnp.where(wide == breadth - 1, east_corner, pltpu.roll(f0, breadth - 1, axis=1))
        from_west = (plane < QUAD) if first_west else (plane >= QUAD)
        div_x = jnp.where(from_west, cx * (f0 - f_west), cx * (f_east - f0))
        div_y = cy * (f0 - f_far) if sign > 0 else cy * (f_far - f0)
        return f0, mov * (sea * ((near - div_x) - div_y))

    sw = to_sublanes(corner_w, 2 * plane_l + 1)
    se = to_sublanes(corner_e, 2 * plane_l - HALF)
    ne = to_sublanes(corner_e, 2 * plane_l + HALF)
    nw = sw
    cx_s, cy_s, cx_n, cy_n = (subs[:, k : k + 1] * sub_courant for k in range(4))
    south_flux0, south_flux1 = rows(south_ref[0], south_ref[1], True, sw, se, cx_s, cy_s, 1)
    north_flux0, north_flux1 = rows(north_ref[0], north_ref[1], False, nw, ne, cx_n, cy_n, -1)

    def add_rows(first, near, next_row, flux0, flux1, cx, cy, first_west):
        sea0, sea1 = sea_ref[near : near + 1, :], sea_ref[next_row : next_row + 1, :]
        change = sea0 * (cy * flux0)
        flux = mov_ref[near : near + 1, :] * change
        west_flux = jnp.where(wide == 0, 0.0, pltpu.roll(flux, 1, axis=1))
        east_flux = jnp.where(wide == breadth - 1, 0.0, pltpu.roll(flux, breadth - 1, axis=1))
        from_west = (plane < QUAD) if first_west else (plane >= QUAD)
        div_x = jnp.where(from_west, cx * (flux - west_flux), cx * (east_flux - flux))
        near_change = sea0 * (((change - div_x) - cy * flux) + cy * flux1)
        next_change = sea1 * (cy * flux)
        for at, delta in ((near, near_change), (next_row, next_change)):
            for h in range(breadth // 128):
                place = pl.ds(first * height + at, HALF + 4, stride=height)
                halves[h, place, :] = halves[h, place, :] + delta[:, h * 128 : (h + 1) * 128]

    def add_columns(half, near, next_column, flux0, flux1, cx, cy, from_west):
        sea0, sea1 = sea_ref[:, near : near + 1], sea_ref[:, next_column : next_column + 1]
        change = sea0 * (cx * flux0)
        flux = mov_ref[:, near : near + 1] * change
        south_flux = jnp.where(row == 0, 0.0, pltpu.roll(flux, 1, axis=0))
        north_flux = jnp.where(row == height - 1, 0.0, pltpu.roll(flux, height - 1, axis=0))
        div_y = jnp.where(lane < HALF, cy * (flux - south_flux), cy * (north_flux - flux))
        near_change = sea0 * (((change - cx * flux) - div_y) + cx * flux1)
        next_change = sea1 * (cx * flux)
        if from_west:
            both = jnp.where(odd, next_change, pltpu.roll(near_change, 127, axis=1))
        else:
            both = jnp.where(odd, pltpu.roll(near_change, 1, axis=1), next_change)
        edge = lane < 2 if from_west else lane >= 126
        for q in range(HALF):
            p = q + QUAD if not from_west else (q if q < QUAD else q + HALF)
            turned = pltpu.roll(both, ((128 if from_west else 126) - 2 * q) % 128, axis=1)
            place = pl.ds(p * height, height)
            halves[half, place, :] = halves[half, place, :] + jnp.where(edge, turned, 0.0)
        return jnp.where(lane < 2 * HALF, both, 0.0)

    add_rows(0, 0, 1, south_flux0, south_flux1, cx_s, cy_s, True)
    add_rows(HALF, height - 1, height - 2, north_flux0, north_flux1, cx_n, -cy_n, False)
    change_w = add_columns(0, 0, 1, west_flux0, west_flux1, cx_w, cy_w, True)
    change_e = add_columns(breadth // 128 - 1, breadth - 1, breadth - 2, east_flux0, east_flux1, -cx_e, cy_e, False)
    whole = pl.ds(0, PLANES * height)
    writes = [
        pltpu.make_async_copy(halves.at[h, whole, :], out_ref.at[:, pl.ds(h * 128, 128)], out_sems.at[h])
        for h in range(breadth // 128)
    ]
    for write in writes:
        write.start()

    for change, columns_of, near, next_column in ((change_w, 0, 0, 1), (change_e, 1, breadth - 1, breadth - 2)):
        profile = jnp.dot(
            change, edge_ref[columns_of], precision=lax.Precision.HIGHEST, preferred_element_type=jnp.float32
        )
        for k, column in enumerate((near, next_column)):
            place = pl.ds(column, height, stride=breadth)
            table[place, :] = table[place, :] + profile[:, k * 128 : (k + 1) * 128]
    for first_row in (0, height - 2):
        profile_rows(halves, weight_ref[...], table, first_row, 2, height, breadth)

    first_half = lax.broadcasted_iota(jnp.int32, (1, 128), 1) < 64
    half = WINDOW // 2

    def pick(cell, i):
        for g in range(WINDOW // 16):
            for j in range(8):
                one, two = cell(16 * g + j), cell(16 * g + 8 + j)
                line = jnp.where(first_half, table[pl.ds(one, 1), :], table[pl.ds(two, 1), :])
                lines[8 * g + j : 8 * g + j + 1, :] = line
        here = pl.ds(pl.multiple_of(i * half, half), half)
        picks[here, :] = lines[...].astype(jnp.bfloat16)
        pltpu.make_async_copy(picks.at[here, :], picked_ref.at[here, :], pick_sem).start()

    for_windows(cells, window, window_sems, pick)
    pltpu.make_async_copy(picks, picked_ref, pick_sem).wait()
    for write in writes:
        write.wait()


def add_kernel(rows_ref, values_ref, out_ref, targets, lines, tile_sums, window, window_sems, out_sem, *sums):
    n_acc = len(sums) // 2
    tile = out_ref.shape[1]
    block = 512
    half = WINDOW // 2
    slot = lax.broadcasted_iota(jnp.int32, targets.shape, 1)
    spare = tile + (slot // 16 * 8 + slot % 8) % SPARE
    targets[...] = jnp.where(rows_ref[...] < 0, spare, rows_ref[...])

    @pl.loop(0, tile // block)
    def _(i):
        for total in sums:
            total[pl.ds(pl.multiple_of(i * block, block), block), :] = jnp.zeros((block, 128), jnp.float32)

    def add(row, i):
        lines[...] = values_ref[pl.ds(pl.multiple_of(i * half, half), half), :].astype(jnp.float32)
        for g in range(WINDOW // 16):
            for j in range(8):
                one, two = row(16 * g + j), row(16 * g + 8 + j)
                line = lines[8 * g + j : 8 * g + j + 1, :]
                left, right = sums[j % n_acc], sums[n_acc + j % n_acc]
                left[pl.ds(one, 1), :] = left[pl.ds(one, 1), :] + line
                right[pl.ds(two, 1), :] = right[pl.ds(two, 1), :] + line

    for_windows(targets, window, window_sems, add)
    first_half = lax.broadcasted_iota(jnp.int32, (block, 128), 1) < 64

    @pl.loop(0, tile // block)
    def _(i):
        here = pl.ds(pl.multiple_of(i * block, block), block)
        left, right = sums[0][here, :], sums[n_acc][here, :]
        for q in range(1, n_acc):
            left = left + sums[q][here, :]
            right = right + sums[n_acc + q][here, :]
        both = jnp.where(first_half, left, right).T
        tile_sums[:, here] = both[:64] + both[64:]
        pltpu.make_async_copy(tile_sums.at[:, here], out_ref.at[:, here], out_sem).start()

    pltpu.make_async_copy(tile_sums, out_ref, out_sem).wait()


def constant_tables():
    heading = (np.arange(DIRS) + 0.5) * (2.0 * math.pi / DIRS)
    cos = np.repeat(np.cos(heading), FREQ)
    sin = np.repeat(np.sin(heading), FREQ)
    lanes = np.zeros((8, 128))
    q = np.arange(HALF)
    from_west = np.where(q < QUAD, q, q + HALF)
    from_east = q + QUAD
    for column in range(2):
        lanes[0, 2 * q + column] = cos[from_west]
        lanes[1, 2 * q + column] = sin[from_west]
        lanes[2, 2 * q + column] = cos[from_east]
        lanes[3, 2 * q + column] = sin[from_east]
        lanes[4, 2 * q + column] = q % 2
    subs = np.zeros((HALF + 4, 128))
    subs[:HALF, 0], subs[:HALF, 1] = cos[:HALF], sin[:HALF]
    subs[:HALF, 2], subs[:HALF, 3] = cos[HALF:], sin[HALF:]
    return [t.astype(np.float32) for t in (np.concatenate([cos, sin]), lanes, subs)]


def body(n_lat, n_lon, spectrum, speed_factor, land_sea_mask, courant, depth_kernel, send_rows, recv_rows):
    height, breadth = speed_factor.shape
    devices, slots = send_rows.shape[1:]
    x = spectrum.reshape(PLANES, height, breadth)
    f32 = jnp.float32
    vmem = pl.BlockSpec(memory_space=pltpu.VMEM)
    smem = pl.BlockSpec(memory_space=pltpu.SMEM)
    hbm = pl.BlockSpec(memory_space=pltpu.HBM)
    params = pltpu.CompilerParams(vmem_limit_bytes=VMEM_LIMIT)

    both = ("lat", "lon")

    def in_hbm(*arrays):
        return [pltpu.with_memory_space_constraint(array, pltpu.HBM) for array in arrays]

    def shape(*dims, kind=f32):
        return jax.ShapeDtypeStruct(dims, kind)

    headings, lanes, subs = constant_tables()
    row_message = shape(2, ROWS, breadth, kind=jnp.bfloat16)
    row_halo = shape(2, HALF + 4, breadth)
    columns = shape(height, 128)
    column_message = shape(height + 8, 128)
    row_first, row_second, column_first, column_second = exchange_pairs(n_lat, n_lon)
    inside_shapes = [
        pltpu.VMEM((breadth // 128, (PLANES + 4) * height, 128), f32),
        pltpu.VMEM(columns.shape, f32),
        pltpu.VMEM(columns.shape, f32),
    ]
    inside_scratch = [
        pltpu.VMEM((PLANES, height, breadth), f32),
        pltpu.SMEM(courant.shape, f32),
        pltpu.SMEM(headings.shape, f32),
        pltpu.SemaphoreType.DMA((6,)),
    ]
    first, second, moving, sea, *inside = pl.pallas_call(
        pack_rows_kernel,
        out_shape=[row_message] * 2 + [shape(height, breadth)] * 2 + inside_shapes,
        in_specs=[hbm] * 5,
        out_specs=[vmem] * 7,
        scratch_shapes=[pltpu.VMEM((2, ROWS, breadth), f32)] * 2
        + [pltpu.VMEM((HALF, 8, breadth), f32)] * 2
        + [pltpu.VMEM((height, breadth), f32), pltpu.VMEM((height, breadth), jnp.int32), pltpu.SemaphoreType.DMA((4,))]
        + inside_scratch,
        compiler_params=params,
        name="pack_rows",
    )(*in_hbm(courant, headings, x, speed_factor, land_sea_mask))
    second = lax.ppermute(second, both, row_second)
    first = lax.ppermute(first, "lat", row_first)
    halves, east, west = pl.pallas_call(
        inside_kernel,
        out_shape=inside_shapes,
        in_specs=[hbm] * 3 + [vmem] * 5,
        out_specs=[vmem] * 3,
        input_output_aliases={5: 0, 6: 1, 7: 2},
        scratch_shapes=inside_scratch,
        compiler_params=params,
        cost_estimate=pl.CostEstimate(flops=4_000_000_000, bytes_accessed=5_000_000, transcendentals=0),
        name="advance_inside",
    )(*in_hbm(courant, headings, x), moving, sea, *inside)
    profile_shapes = [
        pltpu.VMEM((height * breadth, 128), f32),
        pltpu.VMEM((3 * (PLANES + 8), 128), jnp.bfloat16),
        pltpu.VMEM((2, 128, 256), f32),
    ]
    south, north, first, second, *profiles = pl.pallas_call(
        functools.partial(corner_kernel, n_lat),
        out_shape=[row_halo] * 2 + [column_message] * 2 + profile_shapes,
        in_specs=[vmem] * 6,
        out_specs=[vmem] * 7,
        scratch_shapes=[pltpu.VMEM((128, 128), f32)],
        compiler_params=params,
        name="add_corners",
    )(second, first, east, west, halves, depth_kernel)
    second = lax.ppermute(second, "lon", column_second)
    first = lax.ppermute(first, "lon", column_first)

    lists = (devices * slots // 128, 128)
    slot_rows = devices * slots // 2
    slot_rows = devices * slots // 2
    table, weight, edges = pl.pallas_call(
        profile_kernel,
        out_shape=profile_shapes,
        in_specs=[vmem] * 5,
        out_specs=[vmem] * 3,
        input_output_aliases={2: 0, 3: 1, 4: 2},
        scratch_shapes=[pltpu.VMEM((128, 128), f32)],
        compiler_params=params,
        cost_estimate=pl.CostEstimate(flops=2_000_000_000, bytes_accessed=5_000_000, transcendentals=0),
        name="profiles_inside",
    )(halves, depth_kernel, *profiles)
    propagated, picked, *_ = pl.pallas_call(
        finish_kernel,
        out_shape=[
            pltpu.HBM((PLANES * height, breadth), f32),
            pltpu.HBM((slot_rows, 128), jnp.bfloat16),
            inside_shapes[0],
            profile_shapes[0],
        ],
        in_specs=[smem] + [vmem] * 13,
        out_specs=[hbm, hbm, vmem, vmem],
        input_output_aliases={12: 2, 13: 3},
        scratch_shapes=[
            pltpu.VMEM(lists, jnp.int32),
            pltpu.VMEM((WINDOW // 2, 128), f32),
            pltpu.VMEM((slot_rows, 128), jnp.bfloat16),
            pltpu.SMEM((2 * WINDOW // 128, 128), jnp.int32),
            pltpu.SemaphoreType.DMA((breadth // 128,)),
            pltpu.SemaphoreType.DMA((2,)),
            pltpu.SemaphoreType.DMA,
        ],
        compiler_params=params,
        name="finish_and_pick",
    )(courant, send_rows.reshape(lists), moving, sea, weight, edges, south, north, second, first, lanes, subs, halves, table)

    picked = picked.reshape(devices, slots // 2, 128)
    received = lax.all_to_all(picked, both, split_axis=0, concat_axis=0, tiled=True)

    components = depth_kernel.shape[0]
    stokes = pl.pallas_call(
        add_kernel,
        out_shape=pltpu.HBM((components, OUT_DEV), f32),
        in_specs=[vmem] * 2,
        out_specs=hbm,
        scratch_shapes=[
            pltpu.VMEM(lists, jnp.int32),
            pltpu.VMEM((WINDOW // 2, 128), f32),
            pltpu.VMEM((components, OUT_DEV), f32),
            pltpu.SMEM((2 * WINDOW // 128, 128), jnp.int32),
            pltpu.SemaphoreType.DMA((2,)),
            pltpu.SemaphoreType.DMA,
        ]
        + [pltpu.VMEM((OUT_DEV + SPARE, 128), f32)] * (2 * N_ACC),
        compiler_params=pltpu.CompilerParams(vmem_limit_bytes=ADD_VMEM_LIMIT),
        name="add_profiles",
    )(recv_rows.reshape(lists), received.reshape(slot_rows, 128))
    return propagated.reshape(DIRS, FREQ, height, breadth), stokes


def solution(mesh):
    placed = (
        P(None, None, "lat", "lon"),
        P("lat", "lon"),
        P("lat", "lon"),
        P(),
        P(),
        P(("lat", "lon"), None, None),
        P(("lat", "lon"), None, None),
    )
    return jax.shard_map(
        functools.partial(body, mesh.shape["lat"], mesh.shape["lon"]),
        mesh=mesh,
        in_specs=placed,
        out_specs=(P(None, None, "lat", "lon"), P(None, ("lat", "lon"))),
        check_vma=False,
    )
```

```python
import functools
import math

import jax
import jax.numpy as jnp
import numpy as np
from jax import lax
from jax.experimental import pallas as pl
from jax.experimental.pallas import tpu as pltpu
from jax.sharding import PartitionSpec as P

DIRS = 36
FREQ = 2
PLANES = DIRS * FREQ
HALF = PLANES // 2
QUAD = PLANES // 4
OUT_DEV = 4096
SPARE = 64
N_ACC = 4
ROWS = HALF + 12
WINDOW = 1024
VMEM_LIMIT = 16 * 1024 * 1024
ADD_VMEM_LIMIT = 32 * 1024 * 1024


def exchange_pairs(n_lat, n_lon):
    def flat(j, i):
        return j * n_lon + i % n_lon

    row_first = [(j, j ^ 1) for j in range(n_lat)]
    row_second = []
    for i in range(n_lon):
        row_second += [(flat(0, i), flat(0, i)), (flat(n_lat - 1, i), flat(n_lat - 1, n_lon - 1 - i))]
        for j in range(1, n_lat - 1, 2):
            row_second += [(flat(j, i), flat(j + 1, i)), (flat(j + 1, i), flat(j, i))]
    column_first = [(i, i ^ 1) for i in range(n_lon)]
    column_second = [(i, (i + 1 if i % 2 else i - 1) % n_lon) for i in range(n_lon)]
    return row_first, row_second, column_first, column_second


def is_early():
    return lax.axis_index("lon") % 4 == 0


def pack_rows_kernel(courant_hbm, heading_hbm, x_hbm, speed_hbm, mask_hbm,
                     first_ref, second_ref, mov_ref, sea_ref, halves, east_ref, west_ref,
                     up_ref, down_ref, top_rows, bottom_rows, speed_ref, mask_ref, sems, *scratch):
    height, breadth = speed_ref.shape
    copies = [
        pltpu.make_async_copy(source, target, sems.at[k])
        for k, (source, target) in enumerate((
            (speed_hbm, speed_ref),
            (mask_hbm, mask_ref),
            (x_hbm.at[pl.ds(0, HALF), pl.ds(height - 8, 8), :], top_rows),
            (x_hbm.at[pl.ds(HALF, HALF), pl.ds(0, 8), :], bottom_rows),
        ))
    ]
    for copy in copies:
        copy.start()
    even = lax.axis_index("lat") % 2 == 0
    for copy in copies:
        copy.wait()
    sea = mask_ref[...].astype(jnp.float32)
    moving = speed_ref[...] * sea
    mov_ref[...] = moving
    sea_ref[...] = sea
    for k in range(2):
        for q in range(HALF):
            up_ref[k, q : q + 1, :] = top_rows[q, 7 - k : 8 - k, :]
            down_ref[k, q : q + 1, :] = bottom_rows[q, k : k + 1, :]
        up_ref[k, HALF : HALF + 1, :] = moving[height - 1 - k : height - k, :]
        down_ref[k, HALF : HALF + 1, :] = moving[k : k + 1, :]
        up_ref[k, HALF + 1 : HALF + 2, :] = sea[height - 1 - k : height - k, :]
        down_ref[k, HALF + 1 : HALF + 2, :] = sea[k : k + 1, :]
        up_ref[k, HALF + 2 :, :] = jnp.zeros((ROWS - HALF - 2, breadth), jnp.float32)
        down_ref[k, HALF + 2 :, :] = jnp.zeros((ROWS - HALF - 2, breadth), jnp.float32)

    @pl.when(even)
    def _():
        first_ref[...] = up_ref[...].astype(jnp.bfloat16)
        second_ref[...] = down_ref[...].astype(jnp.bfloat16)

    @pl.when(jnp.logical_not(even))
    def _():
        first_ref[...] = down_ref[...].astype(jnp.bfloat16)
        second_ref[...] = up_ref[...].astype(jnp.bfloat16)

    @pl.when(is_early())
    def _():
        advance_inside(courant_hbm, heading_hbm, x_hbm, mov_ref, sea_ref, halves, east_ref, west_ref, *scratch)


def corner_kernel(n_lat, second_ref, first_ref, east_ref, west_ref, halves, kernel_ref,
                  south_ref, north_ref, out_first, out_second, table, weight_ref, edge_ref, wide_kernel):
    height = east_ref.shape[0]
    breadth = first_ref.shape[2]
    lat = lax.axis_index("lat")
    even = lat % 2 == 0

    used = HALF + 4

    @pl.when(even)
    def _():
        north_ref[...] = first_ref[...].astype(jnp.float32)[:, :used]
        south_ref[...] = second_ref[...].astype(jnp.float32)[:, :used]

    @pl.when(jnp.logical_not(even))
    def _():
        south_ref[...] = first_ref[...].astype(jnp.float32)[:, :used]
        north_ref[...] = second_ref[...].astype(jnp.float32)[:, :used]

    @pl.when(lat == 0)
    def _():
        south_ref[...] = jnp.zeros_like(south_ref)

    @pl.when(lat == n_lat - 1)
    def _():
        flip_i = lax.broadcasted_iota(jnp.int32, (breadth, breadth), 0)
        flip_j = lax.broadcasted_iota(jnp.int32, (breadth, breadth), 1)
        flip = (flip_i + flip_j == breadth - 1).astype(jnp.bfloat16)
        both = jnp.concatenate([second_ref[0], second_ref[1]], axis=0)
        flipped = jnp.dot(both, flip, preferred_element_type=jnp.float32)
        north_ref[0] = flipped[:used]
        north_ref[1] = flipped[ROWS : ROWS + used]

    plane = lax.broadcasted_iota(jnp.int32, (HALF + 4, 128), 0)
    lane = lax.broadcasted_iota(jnp.int32, (HALF + 4, 128), 1)
    south = south_ref[0] * south_ref[0, HALF : HALF + 1, :]
    north = north_ref[0] * north_ref[0, HALF : HALF + 1, :]

    def to_lanes(column, low, high, place):
        mine = (plane >= low) & (plane < high) & (lane == place)
        return jnp.where(mine, column, 0.0)

    east_edge = to_lanes(south[:, breadth - 1 :], 0, QUAD, 2 * plane + 1)
    east_edge += to_lanes(north[:, breadth - 1 :], QUAD, HALF, 2 * plane + 1)
    west_edge = to_lanes(south[:, :1], QUAD, HALF, 2 * plane - HALF)
    west_edge += to_lanes(north[:, :1], 0, QUAD, 2 * plane + HALF)
    east_edge = jnp.broadcast_to(jnp.sum(east_edge, axis=0, keepdims=True), (8, 128))
    west_edge = jnp.broadcast_to(jnp.sum(west_edge, axis=0, keepdims=True), (8, 128))
    even_lon = lax.axis_index("lon") % 2 == 0
    out_first[:height] = jnp.where(even_lon, east_ref[...], west_ref[...])
    out_second[:height] = jnp.where(even_lon, west_ref[...], east_ref[...])
    out_first[height:] = jnp.where(even_lon, east_edge, west_edge)
    out_second[height:] = jnp.where(even_lon, west_edge, east_edge)

    @pl.when(is_early())
    def _():
        profiles_inside(halves, kernel_ref, table, weight_ref, edge_ref, wide_kernel)


def for_windows(list_ref, window, sems, work):
    lines = WINDOW // 128
    count = list_ref.shape[0] // lines

    def fetch(i, w):
        source = list_ref.at[pl.ds(pl.multiple_of(i * lines, lines), lines), :]
        return pltpu.make_async_copy(source, window.at[pl.ds(w * lines, lines), :], sems.at[w])

    for w in range(2):
        fetch(w, w).start()

    @pl.loop(0, count // 2)
    def _(t):
        for w in range(2):
            i = 2 * t + w
            fetch(i, w).wait()
            work(lambda k, start=w * lines: window[start + k // 128, k % 128], i)

            @pl.when(i + 2 < count)
            def _():
                fetch(i + 2, w).start()


def inside_kernel(courant_hbm, heading_hbm, x_hbm, mov_ref, sea_ref, _0, _1, _2, halves, east_ref, west_ref, *scratch):
    @pl.when(jnp.logical_not(is_early()))
    def _():
        advance_inside(courant_hbm, heading_hbm, x_hbm, mov_ref, sea_ref, halves, east_ref, west_ref, *scratch)


def advance_inside(courant_hbm, heading_hbm, x_hbm, mov_ref, sea_ref, halves, east_ref, west_ref,
                   x_ref, courant_ref, heading_ref, sems):
    height, breadth = mov_ref.shape
    small = [
        pltpu.make_async_copy(courant_hbm, courant_ref, sems.at[4]),
        pltpu.make_async_copy(heading_hbm, heading_ref, sems.at[5]),
    ]
    parts = [
        pltpu.make_async_copy(x_hbm.at[planes], x_ref.at[planes], sems.at[k])
        for k, planes in enumerate(pl.ds(k * QUAD, QUAD) for k in range(4))
    ]
    for copy in small + parts:
        copy.start()
    for copy in small:
        copy.wait()
    c0, c1 = courant_ref[0], courant_ref[1]
    moving = mov_ref[...]
    sea = sea_ref[...]
    lane = lax.broadcasted_iota(jnp.int32, (height, 128), 1)
    row = lax.broadcasted_iota(jnp.int32, (8, breadth), 0)
    for h in range(breadth // 128):
        halves[h, PLANES * height :, :] = jnp.zeros((4 * height, 128), jnp.float32)

    def quadrant(first, from_west, from_south):
        def upstream(flux):
            if from_west:
                moved = pltpu.roll(flux, 1, axis=1)
                side = jnp.concatenate([jnp.where(lane == 0, 0.0, moved[:, :128]), moved[:, 128:]], axis=1)
            else:
                moved = pltpu.roll(flux, breadth - 1, axis=1)
                edge = jnp.where(lane == 127, 0.0, moved[:, breadth - 128 :])
                side = jnp.concatenate([moved[:, : breadth - 128], edge], axis=1)
            if from_south:
                moved = pltpu.roll(flux, 1, axis=0)
                below = jnp.concatenate([jnp.where(row == 0, 0.0, moved[:8]), moved[8:]], axis=0)
            else:
                moved = pltpu.roll(flux, height - 1, axis=0)
                below = jnp.concatenate([moved[: height - 8], jnp.where(row == 7, 0.0, moved[height - 8 :])], axis=0)
            return side, below

        def step(t, carry):
            p = first + t
            courant = jnp.where(p % 2 == 1, c1, c0)
            cx = heading_ref[p] * courant
            cy = heading_ref[PLANES + p] * courant
            energy = x_ref[p]
            for _ in range(2):
                flux = moving * energy
                side, below = upstream(flux)
                div_x = cx * (flux - side) if from_west else cx * (side - flux)
                div_y = cy * (flux - below) if from_south else cy * (below - flux)
                energy = sea * ((energy - div_x) - div_y)
            start = pl.ds(pl.multiple_of(p * height, height), height)
            for h in range(breadth // 128):
                halves[h, start, :] = energy[:, h * 128 : (h + 1) * 128]
            return carry

        lax.fori_loop(0, QUAD, step, 0, unroll=6)

    for k, (from_west, from_south) in enumerate(((True, True), (False, True), (False, False), (True, False))):
        parts[k].wait()
        quadrant(k * QUAD, from_west, from_south)

    east = jnp.zeros((height, 128), jnp.float32)
    west = jnp.zeros((height, 128), jnp.float32)
    for q in range(HALF + 2):
        mine = lane // 2 == q
        if q < HALF:
            p_e = q if q < QUAD else q + HALF
            edge_e, edge_w = x_ref[p_e, :, breadth - 128 :], x_ref[q + QUAD, :, :128]
        else:
            field = moving if q == HALF else sea
            edge_e, edge_w = field[:, breadth - 128 :], field[:, :128]
        east = jnp.where(mine, pltpu.roll(edge_e, (2 * q + 2) % 128, axis=1), east)
        west = jnp.where(mine, pltpu.roll(edge_w, 2 * q, axis=1), west)
    east_ref[...] = east
    west_ref[...] = west


def profile_rows(halves, weight, table, first_row, count, height, breadth):
    pad = jnp.zeros((8, 128), jnp.bfloat16)
    blocks = []
    for k in range(count):
        for h in range(breadth // 128):
            spectra = halves[h, pl.ds(first_row + k, PLANES, stride=height), :]
            high = spectra.astype(jnp.bfloat16)
            low = (spectra - high.astype(jnp.float32)).astype(jnp.bfloat16)
            blocks.append(jnp.concatenate([high, pad, low, pad, high, pad], axis=0))
    stacked = jnp.concatenate(blocks, axis=1)
    profile = lax.dot_general(stacked, weight, (((0,), (0,)), ((), ())), preferred_element_type=jnp.float32)
    start = first_row * breadth
    if not isinstance(start, int):
        start = pl.multiple_of(start, 128)
    table[pl.ds(start, count * breadth), :] = profile


def profile_kernel(halves, kernel_ref, _0, _1, _2, table, weight_ref, edge_ref, wide_kernel):
    @pl.when(jnp.logical_not(is_early()))
    def _():
        profiles_inside(halves, kernel_ref, table, weight_ref, edge_ref, wide_kernel)


def profiles_inside(halves, kernel_ref, table, weight_ref, edge_ref, wide_kernel):
    height, breadth = halves.shape[1] // (PLANES + 4), table.shape[0] // (halves.shape[1] // (PLANES + 4))
    pad = jnp.zeros((8, 128), jnp.bfloat16)
    wide_kernel[...] = jnp.zeros((128, 128), jnp.float32)
    wide_kernel[:64, :PLANES] = kernel_ref[...]
    wide_kernel[64:, :PLANES] = kernel_ref[...]
    turned = wide_kernel[...].T
    weight_high = turned[:PLANES].astype(jnp.bfloat16)
    weight_low = (turned[:PLANES] - weight_high.astype(jnp.float32)).astype(jnp.bfloat16)
    weight = jnp.concatenate([weight_high, pad, weight_high, pad, weight_low, pad], axis=0)
    weight_ref[...] = weight

    lane = lax.broadcasted_iota(jnp.int32, (128, 128), 0)
    plane = lax.broadcasted_iota(jnp.int32, (128, 128), 1)
    q = lane // 2
    used = lane < 2 * HALF
    for side, owner in ((0, jnp.where(q < QUAD, q, q + HALF)), (1, q + QUAD)):
        for k in range(2):
            chosen = used & (plane == owner) & (lane % 2 == (k if side == 0 else 1 - k))
            edge_ref[side, :, k * 128 : (k + 1) * 128] = jnp.dot(
                chosen.astype(jnp.float32), turned, precision=lax.Precision.HIGHEST, preferred_element_type=jnp.float32
            )
    group = 8

    @pl.loop(0, height // group)
    def _(r):
        profile_rows(halves, weight, table, r * group, group, height, breadth)


def finish_kernel(courant_ref, cells_ref, mov_ref, sea_ref, weight_ref, edge_ref, south_ref, north_ref, second_ref,
                  first_ref, lanes_ref, subs_ref, halves_in, table_in, out_ref, picked_ref, halves, table,
                  cells, lines, picks, window, out_sems, window_sems, pick_sem):
    cells[...] = jnp.maximum(cells_ref[...], 0)
    height, breadth = mov_ref.shape
    c0, c1 = courant_ref[0], courant_ref[1]
    even_lon = lax.axis_index("lon") % 2 == 0
    from_west = jnp.where(even_lon, second_ref[...], first_ref[...])
    from_east = jnp.where(even_lon, first_ref[...], second_ref[...])
    corner_w, corner_e = from_west[height : height + 1], from_east[height : height + 1]

    lane = lax.broadcasted_iota(jnp.int32, (height, 128), 1)
    row = lax.broadcasted_iota(jnp.int32, (height, 128), 0)
    odd = lane % 2 == 1

    def columns(e0, near, far, corner, cx, cy, sign):
        mov = jnp.where(odd, e0[:, 2 * HALF + 1 : 2 * HALF + 2], e0[:, 2 * HALF : 2 * HALF + 1])
        sea = e0[:, 2 * HALF + 2 + near : 2 * HALF + 3 + near]
        f0 = mov * e0
        f_far = pltpu.roll(f0, 1 if near > far else 127, axis=1)
        f_south = jnp.where(row == 0, corner, pltpu.roll(f0, 1, axis=0))
        f_north = jnp.where(row == height - 1, corner, pltpu.roll(f0, height - 1, axis=0))
        div_x = cx * (f0 - f_far) if sign > 0 else cx * (f_far - f0)
        div_y = jnp.where(lane < HALF, cy * (f0 - f_south), cy * (f_north - f0))
        return f0, mov * (sea * ((e0 - div_x) - div_y))

    lanes = lanes_ref[...]
    lane_courant = jnp.where(lanes[4:5] > 0.5, c1, c0)
    cx_w, cy_w, cx_e, cy_e = (lanes[k : k + 1] * lane_courant for k in range(4))
    west_flux0, west_flux1 = columns(from_west[:height], 1, 0, corner_w, cx_w, cy_w, 1)
    east_flux0, east_flux1 = columns(from_east[:height], 0, 1, corner_e, cx_e, cy_e, -1)

    wide = lax.broadcasted_iota(jnp.int32, (HALF + 4, breadth), 1)
    plane = lax.broadcasted_iota(jnp.int32, (HALF + 4, 1), 0)
    plane_l = lax.broadcasted_iota(jnp.int32, (HALF + 4, 128), 0)
    lane_l = lax.broadcasted_iota(jnp.int32, (HALF + 4, 128), 1)
    subs = subs_ref[...]
    sub_courant = jnp.where(plane % 2 == 1, c1, c0)

    def to_sublanes(corner, lane_of):
        return jnp.sum(jnp.where(lane_l == lane_of, corner, 0.0), axis=1, keepdims=True)

    def rows(near, far, first_west, west_corner, east_corner, cx, cy, sign):
        mov, sea = near[HALF : HALF + 1], near[HALF + 1 : HALF + 2]
        f0 = mov * near
        f_far = far[HALF : HALF + 1] * far
        f_west = jnp.where(wide == 0, west_corner, pltpu.roll(f0, 1, axis=1))
        f_east = jnp.where(wide == breadth - 1, east_corner, pltpu.roll(f0, breadth - 1, axis=1))
        from_west = (plane < QUAD) if first_west else (plane >= QUAD)
        div_x = jnp.where(from_west, cx * (f0 - f_west), cx * (f_east - f0))
        div_y = cy * (f0 - f_far) if sign > 0 else cy * (f_far - f0)
        return f0, mov * (sea * ((near - div_x) - div_y))

    sw = to_sublanes(corner_w, 2 * plane_l + 1)
    se = to_sublanes(corner_e, 2 * plane_l - HALF)
    ne = to_sublanes(corner_e, 2 * plane_l + HALF)
    nw = sw
    cx_s, cy_s, cx_n, cy_n = (subs[:, k : k + 1] * sub_courant for k in range(4))
    south_flux0, south_flux1 = rows(south_ref[0], south_ref[1], True, sw, se, cx_s, cy_s, 1)
    north_flux0, north_flux1 = rows(north_ref[0], north_ref[1], False, nw, ne, cx_n, cy_n, -1)

    def add_rows(first, near, next_row, flux0, flux1, cx, cy, first_west):
        sea0, sea1 = sea_ref[near : near + 1, :], sea_ref[next_row : next_row + 1, :]
        change = sea0 * (cy * flux0)
        flux = mov_ref[near : near + 1, :] * change
        west_flux = jnp.where(wide == 0, 0.0, pltpu.roll(flux, 1, axis=1))
        east_flux = jnp.where(wide == breadth - 1, 0.0, pltpu.roll(flux, breadth - 1, axis=1))
        from_west = (plane < QUAD) if first_west else (plane >= QUAD)
        div_x = jnp.where(from_west, cx * (flux - west_flux), cx * (east_flux - flux))
        near_change = sea0 * (((change - div_x) - cy * flux) + cy * flux1)
        next_change = sea1 * (cy * flux)
        for at, delta in ((near, near_change), (next_row, next_change)):
            for h in range(breadth // 128):
                place = pl.ds(first * height + at, HALF + 4, stride=height)
                halves[h, place, :] = halves[h, place, :] + delta[:, h * 128 : (h + 1) * 128]

    def add_columns(half, near, next_column, flux0, flux1, cx, cy, from_west):
        sea0, sea1 = sea_ref[:, near : near + 1], sea_ref[:, next_column : next_column + 1]
        change = sea0 * (cx * flux0)
        flux = mov_ref[:, near : near + 1] * change
        south_flux = jnp.where(row == 0, 0.0, pltpu.roll(flux, 1, axis=0))
        north_flux = jnp.where(row == height - 1, 0.0, pltpu.roll(flux, height - 1, axis=0))
        div_y = jnp.where(lane < HALF, cy * (flux - south_flux), cy * (north_flux - flux))
        near_change = sea0 * (((change - cx * flux) - div_y) + cx * flux1)
        next_change = sea1 * (cx * flux)
        if from_west:
            both = jnp.where(odd, next_change, pltpu.roll(near_change, 127, axis=1))
        else:
            both = jnp.where(odd, pltpu.roll(near_change, 1, axis=1), next_change)
        edge = lane < 2 if from_west else lane >= 126
        for q in range(HALF):
            p = q + QUAD if not from_west else (q if q < QUAD else q + HALF)
            turned = pltpu.roll(both, ((128 if from_west else 126) - 2 * q) % 128, axis=1)
            place = pl.ds(p * height, height)
            halves[half, place, :] = halves[half, place, :] + jnp.where(edge, turned, 0.0)
        return jnp.where(lane < 2 * HALF, both, 0.0)

    add_rows(0, 0, 1, south_flux0, south_flux1, cx_s, cy_s, True)
    add_rows(HALF, height - 1, height - 2, north_flux0, north_flux1, cx_n, -cy_n, False)
    change_w = add_columns(0, 0, 1, west_flux0, west_flux1, cx_w, cy_w, True)
    change_e = add_columns(breadth // 128 - 1, breadth - 1, breadth - 2, east_flux0, east_flux1, -cx_e, cy_e, False)
    whole = pl.ds(0, PLANES * height)
    writes = [
        pltpu.make_async_copy(halves.at[h, whole, :], out_ref.at[:, pl.ds(h * 128, 128)], out_sems.at[h])
        for h in range(breadth // 128)
    ]
    for write in writes:
        write.start()

    for change, columns_of, near, next_column in ((change_w, 0, 0, 1), (change_e, 1, breadth - 1, breadth - 2)):
        profile = jnp.dot(
            change, edge_ref[columns_of], precision=lax.Precision.HIGHEST, preferred_element_type=jnp.float32
        )
        for k, column in enumerate((near, next_column)):
            place = pl.ds(column, height, stride=breadth)
            table[place, :] = table[place, :] + profile[:, k * 128 : (k + 1) * 128]
    for first_row in (0, height - 2):
        profile_rows(halves, weight_ref[...], table, first_row, 2, height, breadth)

    first_half = lax.broadcasted_iota(jnp.int32, (1, 128), 1) < 64
    half = WINDOW // 2

    def pick(cell, i):
        for g in range(WINDOW // 16):
            for j in range(8):
                one, two = cell(16 * g + j), cell(16 * g + 8 + j)
                line = jnp.where(first_half, table[pl.ds(one, 1), :], table[pl.ds(two, 1), :])
                lines[8 * g + j : 8 * g + j + 1, :] = line
        here = pl.ds(pl.multiple_of(i * half, half), half)
        picks[here, :] = lines[...].astype(jnp.bfloat16)
        pltpu.make_async_copy(picks.at[here, :], picked_ref.at[here, :], pick_sem).start()

    for_windows(cells, window, window_sems, pick)
    pltpu.make_async_copy(picks, picked_ref, pick_sem).wait()
    for write in writes:
        write.wait()


def add_kernel(rows_ref, values_ref, out_ref, targets, lines, tile_sums, window, window_sems, out_sem, *sums):
    n_acc = len(sums) // 2
    tile = out_ref.shape[1]
    block = 512
    half = WINDOW // 2
    slot = lax.broadcasted_iota(jnp.int32, targets.shape, 1)
    spare = tile + (slot // 16 * 8 + slot % 8) % SPARE
    targets[...] = jnp.where(rows_ref[...] < 0, spare, rows_ref[...])

    @pl.loop(0, tile // block)
    def _(i):
        for total in sums:
            total[pl.ds(pl.multiple_of(i * block, block), block), :] = jnp.zeros((block, 128), jnp.float32)

    def add(row, i):
        lines[...] = values_ref[pl.ds(pl.multiple_of(i * half, half), half), :].astype(jnp.float32)
        for g in range(WINDOW // 16):
            for j in range(8):
                one, two = row(16 * g + j), row(16 * g + 8 + j)
                line = lines[8 * g + j : 8 * g + j + 1, :]
                left, right = sums[j % n_acc], sums[n_acc + j % n_acc]
                left[pl.ds(one, 1), :] = left[pl.ds(one, 1), :] + line
                right[pl.ds(two, 1), :] = right[pl.ds(two, 1), :] + line

    for_windows(targets, window, window_sems, add)
    first_half = lax.broadcasted_iota(jnp.int32, (block, 128), 1) < 64

    @pl.loop(0, tile // block)
    def _(i):
        here = pl.ds(pl.multiple_of(i * block, block), block)
        left, right = sums[0][here, :], sums[n_acc][here, :]
        for q in range(1, n_acc):
            left = left + sums[q][here, :]
            right = right + sums[n_acc + q][here, :]
        both = jnp.where(first_half, left, right).T
        tile_sums[:, here] = both[:64] + both[64:]
        pltpu.make_async_copy(tile_sums.at[:, here], out_ref.at[:, here], out_sem).start()

    pltpu.make_async_copy(tile_sums, out_ref, out_sem).wait()


def constant_tables():
    heading = (np.arange(DIRS) + 0.5) * (2.0 * math.pi / DIRS)
    cos = np.repeat(np.cos(heading), FREQ)
    sin = np.repeat(np.sin(heading), FREQ)
    lanes = np.zeros((8, 128))
    q = np.arange(HALF)
    from_west = np.where(q < QUAD, q, q + HALF)
    from_east = q + QUAD
    for column in range(2):
        lanes[0, 2 * q + column] = cos[from_west]
        lanes[1, 2 * q + column] = sin[from_west]
        lanes[2, 2 * q + column] = cos[from_east]
        lanes[3, 2 * q + column] = sin[from_east]
        lanes[4, 2 * q + column] = q % 2
    subs = np.zeros((HALF + 4, 128))
    subs[:HALF, 0], subs[:HALF, 1] = cos[:HALF], sin[:HALF]
    subs[:HALF, 2], subs[:HALF, 3] = cos[HALF:], sin[HALF:]
    return [t.astype(np.float32) for t in (np.concatenate([cos, sin]), lanes, subs)]


def body(n_lat, n_lon, spectrum, speed_factor, land_sea_mask, courant, depth_kernel, send_rows, recv_rows):
    height, breadth = speed_factor.shape
    devices, slots = send_rows.shape[1:]
    x = spectrum.reshape(PLANES, height, breadth)
    f32 = jnp.float32
    vmem = pl.BlockSpec(memory_space=pltpu.VMEM)
    smem = pl.BlockSpec(memory_space=pltpu.SMEM)
    hbm = pl.BlockSpec(memory_space=pltpu.HBM)
    params = pltpu.CompilerParams(vmem_limit_bytes=VMEM_LIMIT)

    both = ("lat", "lon")

    def in_hbm(*arrays):
        return [pltpu.with_memory_space_constraint(array, pltpu.HBM) for array in arrays]

    def shape(*dims, kind=f32):
        return jax.ShapeDtypeStruct(dims, kind)

    headings, lanes, subs = constant_tables()
    row_message = shape(2, ROWS, breadth, kind=jnp.bfloat16)
    row_halo = shape(2, HALF + 4, breadth)
    columns = shape(height, 128)
    column_message = shape(height + 8, 128)
    row_first, row_second, column_first, column_second = exchange_pairs(n_lat, n_lon)
    inside_shapes = [
        pltpu.VMEM((breadth // 128, (PLANES + 4) * height, 128), f32),
        pltpu.VMEM(columns.shape, f32),
        pltpu.VMEM(columns.shape, f32),
    ]
    inside_scratch = [
        pltpu.VMEM((PLANES, height, breadth), f32),
        pltpu.SMEM(courant.shape, f32),
        pltpu.SMEM(headings.shape, f32),
        pltpu.SemaphoreType.DMA((6,)),
    ]
    first, second, moving, sea, *inside = pl.pallas_call(
        pack_rows_kernel,
        out_shape=[row_message] * 2 + [shape(height, breadth)] * 2 + inside_shapes,
        in_specs=[hbm] * 5,
        out_specs=[vmem] * 7,
        scratch_shapes=[pltpu.VMEM((2, ROWS, breadth), f32)] * 2
        + [pltpu.VMEM((HALF, 8, breadth), f32)] * 2
        + [pltpu.VMEM((height, breadth), f32), pltpu.VMEM((height, breadth), jnp.int32), pltpu.SemaphoreType.DMA((4,))]
        + inside_scratch,
        compiler_params=params,
        name="pack_rows",
    )(*in_hbm(courant, headings, x, speed_factor, land_sea_mask))
    second = lax.ppermute(second, both, row_second)
    first = lax.ppermute(first, "lat", row_first)
    halves, east, west = pl.pallas_call(
        inside_kernel,
        out_shape=inside_shapes,
        in_specs=[hbm] * 3 + [vmem] * 5,
        out_specs=[vmem] * 3,
        input_output_aliases={5: 0, 6: 1, 7: 2},
        scratch_shapes=inside_scratch,
        compiler_params=params,
        cost_estimate=pl.CostEstimate(flops=4_000_000_000, bytes_accessed=5_000_000, transcendentals=0),
        name="advance_inside",
    )(*in_hbm(courant, headings, x), moving, sea, *inside)
    profile_shapes = [
        pltpu.VMEM((height * breadth, 128), f32),
        pltpu.VMEM((3 * (PLANES + 8), 128), jnp.bfloat16),
        pltpu.VMEM((2, 128, 256), f32),
    ]
    south, north, first, second, *profiles = pl.pallas_call(
        functools.partial(corner_kernel, n_lat),
        out_shape=[row_halo] * 2 + [column_message] * 2 + profile_shapes,
        in_specs=[vmem] * 6,
        out_specs=[vmem] * 7,
        scratch_shapes=[pltpu.VMEM((128, 128), f32)],
        compiler_params=params,
        name="add_corners",
    )(second, first, east, west, halves, depth_kernel)
    second = lax.ppermute(second, "lon", column_second)
    first = lax.ppermute(first, "lon", column_first)

    lists = (devices * slots // 128, 128)
    slot_rows = devices * slots // 2
    slot_rows = devices * slots // 2
    table, weight, edges = pl.pallas_call(
        profile_kernel,
        out_shape=profile_shapes,
        in_specs=[vmem] * 5,
        out_specs=[vmem] * 3,
        input_output_aliases={2: 0, 3: 1, 4: 2},
        scratch_shapes=[pltpu.VMEM((128, 128), f32)],
        compiler_params=params,
        cost_estimate=pl.CostEstimate(flops=2_000_000_000, bytes_accessed=5_000_000, transcendentals=0),
        name="profiles_inside",
    )(halves, depth_kernel, *profiles)
    propagated, picked, *_ = pl.pallas_call(
        finish_kernel,
        out_shape=[
            pltpu.HBM((PLANES * height, breadth), f32),
            pltpu.HBM((slot_rows, 128), jnp.bfloat16),
            inside_shapes[0],
            profile_shapes[0],
        ],
        in_specs=[smem] + [vmem] * 13,
        out_specs=[hbm, hbm, vmem, vmem],
        input_output_aliases={12: 2, 13: 3},
        scratch_shapes=[
            pltpu.VMEM(lists, jnp.int32),
            pltpu.VMEM((WINDOW // 2, 128), f32),
            pltpu.VMEM((slot_rows, 128), jnp.bfloat16),
            pltpu.SMEM((2 * WINDOW // 128, 128), jnp.int32),
            pltpu.SemaphoreType.DMA((breadth // 128,)),
            pltpu.SemaphoreType.DMA((2,)),
            pltpu.SemaphoreType.DMA,
        ],
        compiler_params=params,
        name="finish_and_pick",
    )(courant, send_rows.reshape(lists), moving, sea, weight, edges, south, north, second, first, lanes, subs, halves, table)

    picked = picked.reshape(devices, slots // 2, 128)
    received = lax.all_to_all(picked, both, split_axis=0, concat_axis=0, tiled=True)

    components = depth_kernel.shape[0]
    stokes = pl.pallas_call(
        add_kernel,
        out_shape=pltpu.HBM((components, OUT_DEV), f32),
        in_specs=[vmem] * 2,
        out_specs=hbm,
        scratch_shapes=[
            pltpu.VMEM(lists, jnp.int32),
            pltpu.VMEM((WINDOW // 2, 128), f32),
            pltpu.VMEM((components, OUT_DEV), f32),
            pltpu.SMEM((2 * WINDOW // 128, 128), jnp.int32),
            pltpu.SemaphoreType.DMA((2,)),
            pltpu.SemaphoreType.DMA,
        ]
        + [pltpu.VMEM((OUT_DEV + SPARE, 128), f32)] * (2 * N_ACC),
        compiler_params=pltpu.CompilerParams(vmem_limit_bytes=ADD_VMEM_LIMIT),
        name="add_profiles",
    )(recv_rows.reshape(lists), received.reshape(slot_rows, 128))
    return propagated.reshape(DIRS, FREQ, height, breadth), stokes


def solution(mesh):
    placed = (
        P(None, None, "lat", "lon"),
        P("lat", "lon"),
        P("lat", "lon"),
        P(),
        P(),
        P(("lat", "lon"), None, None),
        P(("lat", "lon"), None, None),
    )
    return jax.shard_map(
        functools.partial(body, mesh.shape["lat"], mesh.shape["lon"]),
        mesh=mesh,
        in_specs=placed,
        out_specs=(P(None, None, "lat", "lon"), P(None, ("lat", "lon"))),
        check_vma=False,
    )
```

```python
import functools
import math

import jax
import jax.numpy as jnp
import numpy as np
from jax import lax
from jax.experimental import pallas as pl
from jax.experimental.pallas import tpu as pltpu
from jax.sharding import PartitionSpec as P

DIRS = 36
FREQ = 2
PLANES = DIRS * FREQ
HALF = PLANES // 2
QUAD = PLANES // 4
OUT_DEV = 4096
SPARE = 64
N_ACC = 4
ROWS = HALF + 12
WINDOW = 1024
VMEM_LIMIT = 16 * 1024 * 1024
ADD_VMEM_LIMIT = 32 * 1024 * 1024


def exchange_pairs(n_lat, n_lon):
    def flat(j, i):
        return j * n_lon + i % n_lon

    row_first = [(j, j ^ 1) for j in range(n_lat)]
    row_second = []
    for i in range(n_lon):
        row_second += [(flat(0, i), flat(0, i)), (flat(n_lat - 1, i), flat(n_lat - 1, n_lon - 1 - i))]
        for j in range(1, n_lat - 1, 2):
            row_second += [(flat(j, i), flat(j + 1, i)), (flat(j + 1, i), flat(j, i))]
    column_first = [(i, i ^ 1) for i in range(n_lon)]
    column_second = [(i, (i + 1 if i % 2 else i - 1) % n_lon) for i in range(n_lon)]
    return row_first, row_second, column_first, column_second


def pack_rows_kernel(x_hbm, speed_hbm, mask_hbm, first_ref, second_ref, mov_ref, sea_ref,
                     up_ref, down_ref, top_rows, bottom_rows, speed_ref, mask_ref, sems):
    height, breadth = speed_ref.shape
    copies = [
        pltpu.make_async_copy(source, target, sems.at[k])
        for k, (source, target) in enumerate((
            (speed_hbm, speed_ref),
            (mask_hbm, mask_ref),
            (x_hbm.at[pl.ds(0, HALF), pl.ds(height - 8, 8), :], top_rows),
            (x_hbm.at[pl.ds(HALF, HALF), pl.ds(0, 8), :], bottom_rows),
        ))
    ]
    for copy in copies:
        copy.start()
    even = lax.axis_index("lat") % 2 == 0
    for copy in copies:
        copy.wait()
    sea = mask_ref[...].astype(jnp.float32)
    moving = speed_ref[...] * sea
    mov_ref[...] = moving
    sea_ref[...] = sea
    for k in range(2):
        for q in range(HALF):
            up_ref[k, q : q + 1, :] = top_rows[q, 7 - k : 8 - k, :]
            down_ref[k, q : q + 1, :] = bottom_rows[q, k : k + 1, :]
        up_ref[k, HALF : HALF + 1, :] = moving[height - 1 - k : height - k, :]
        down_ref[k, HALF : HALF + 1, :] = moving[k : k + 1, :]
        up_ref[k, HALF + 1 : HALF + 2, :] = sea[height - 1 - k : height - k, :]
        down_ref[k, HALF + 1 : HALF + 2, :] = sea[k : k + 1, :]
        up_ref[k, HALF + 2 :, :] = jnp.zeros((ROWS - HALF - 2, breadth), jnp.float32)
        down_ref[k, HALF + 2 :, :] = jnp.zeros((ROWS - HALF - 2, breadth), jnp.float32)

    @pl.when(even)
    def _():
        first_ref[...] = up_ref[...].astype(jnp.bfloat16)
        second_ref[...] = down_ref[...].astype(jnp.bfloat16)

    @pl.when(jnp.logical_not(even))
    def _():
        first_ref[...] = down_ref[...].astype(jnp.bfloat16)
        second_ref[...] = up_ref[...].astype(jnp.bfloat16)


def corner_kernel(n_lat, second_ref, first_ref, east_ref, west_ref, south_ref, north_ref, out_first, out_second):
    height = east_ref.shape[0]
    breadth = first_ref.shape[2]
    lat = lax.axis_index("lat")
    even = lat % 2 == 0

    used = HALF + 4

    @pl.when(even)
    def _():
        north_ref[...] = first_ref[...].astype(jnp.float32)[:, :used]
        south_ref[...] = second_ref[...].astype(jnp.float32)[:, :used]

    @pl.when(jnp.logical_not(even))
    def _():
        south_ref[...] = first_ref[...].astype(jnp.float32)[:, :used]
        north_ref[...] = second_ref[...].astype(jnp.float32)[:, :used]

    @pl.when(lat == 0)
    def _():
        south_ref[...] = jnp.zeros_like(south_ref)

    @pl.when(lat == n_lat - 1)
    def _():
        flip_i = lax.broadcasted_iota(jnp.int32, (breadth, breadth), 0)
        flip_j = lax.broadcasted_iota(jnp.int32, (breadth, breadth), 1)
        flip = (flip_i + flip_j == breadth - 1).astype(jnp.bfloat16)
        both = jnp.concatenate([second_ref[0], second_ref[1]], axis=0)
        flipped = jnp.dot(both, flip, preferred_element_type=jnp.float32)
        north_ref[0] = flipped[:used]
        north_ref[1] = flipped[ROWS : ROWS + used]

    plane = lax.broadcasted_iota(jnp.int32, (HALF + 4, 128), 0)
    lane = lax.broadcasted_iota(jnp.int32, (HALF + 4, 128), 1)
    south = south_ref[0] * south_ref[0, HALF : HALF + 1, :]
    north = north_ref[0] * north_ref[0, HALF : HALF + 1, :]

    def to_lanes(column, low, high, place):
        mine = (plane >= low) & (plane < high) & (lane == place)
        return jnp.where(mine, column, 0.0)

    east_edge = to_lanes(south[:, breadth - 1 :], 0, QUAD, 2 * plane + 1)
    east_edge += to_lanes(north[:, breadth - 1 :], QUAD, HALF, 2 * plane + 1)
    west_edge = to_lanes(south[:, :1], QUAD, HALF, 2 * plane - HALF)
    west_edge += to_lanes(north[:, :1], 0, QUAD, 2 * plane + HALF)
    east_edge = jnp.broadcast_to(jnp.sum(east_edge, axis=0, keepdims=True), (8, 128))
    west_edge = jnp.broadcast_to(jnp.sum(west_edge, axis=0, keepdims=True), (8, 128))
    even_lon = lax.axis_index("lon") % 2 == 0
    out_first[:height] = jnp.where(even_lon, east_ref[...], west_ref[...])
    out_second[:height] = jnp.where(even_lon, west_ref[...], east_ref[...])
    out_first[height:] = jnp.where(even_lon, east_edge, west_edge)
    out_second[height:] = jnp.where(even_lon, west_edge, east_edge)


def for_windows(list_ref, window, sems, work):
    lines = WINDOW // 128
    count = list_ref.shape[0] // lines

    def fetch(i, w):
        source = list_ref.at[pl.ds(pl.multiple_of(i * lines, lines), lines), :]
        return pltpu.make_async_copy(source, window.at[pl.ds(w * lines, lines), :], sems.at[w])

    for w in range(2):
        fetch(w, w).start()

    @pl.loop(0, count // 2)
    def _(t):
        for w in range(2):
            i = 2 * t + w
            fetch(i, w).wait()
            work(lambda k, start=w * lines: window[start + k // 128, k % 128], i)

            @pl.when(i + 2 < count)
            def _():
                fetch(i + 2, w).start()


def inside_kernel(courant_hbm, heading_hbm, x_hbm, mov_ref, sea_ref, halves, east_ref, west_ref,
                  x_ref, courant_ref, heading_ref, sems):
    height, breadth = mov_ref.shape
    small = [
        pltpu.make_async_copy(courant_hbm, courant_ref, sems.at[4]),
        pltpu.make_async_copy(heading_hbm, heading_ref, sems.at[5]),
    ]
    parts = [
        pltpu.make_async_copy(x_hbm.at[planes], x_ref.at[planes], sems.at[k])
        for k, planes in enumerate(pl.ds(k * QUAD, QUAD) for k in range(4))
    ]
    for copy in small + parts:
        copy.start()
    for copy in small:
        copy.wait()
    c0, c1 = courant_ref[0], courant_ref[1]
    moving = mov_ref[...]
    sea = sea_ref[...]
    lane = lax.broadcasted_iota(jnp.int32, (height, 128), 1)
    row = lax.broadcasted_iota(jnp.int32, (8, breadth), 0)
    for h in range(breadth // 128):
        halves[h, PLANES * height :, :] = jnp.zeros((4 * height, 128), jnp.float32)

    def quadrant(first, from_west, from_south):
        def upstream(flux):
            if from_west:
                moved = pltpu.roll(flux, 1, axis=1)
                side = jnp.concatenate([jnp.where(lane == 0, 0.0, moved[:, :128]), moved[:, 128:]], axis=1)
            else:
                moved = pltpu.roll(flux, breadth - 1, axis=1)
                edge = jnp.where(lane == 127, 0.0, moved[:, breadth - 128 :])
                side = jnp.concatenate([moved[:, : breadth - 128], edge], axis=1)
            if from_south:
                moved = pltpu.roll(flux, 1, axis=0)
                below = jnp.concatenate([jnp.where(row == 0, 0.0, moved[:8]), moved[8:]], axis=0)
            else:
                moved = pltpu.roll(flux, height - 1, axis=0)
                below = jnp.concatenate([moved[: height - 8], jnp.where(row == 7, 0.0, moved[height - 8 :])], axis=0)
            return side, below

        def step(t, carry):
            p = first + t
            courant = jnp.where(p % 2 == 1, c1, c0)
            cx = heading_ref[p] * courant
            cy = heading_ref[PLANES + p] * courant
            energy = x_ref[p]
            for _ in range(2):
                flux = moving * energy
                side, below = upstream(flux)
                div_x = cx * (flux - side) if from_west else cx * (side - flux)
                div_y = cy * (flux - below) if from_south else cy * (below - flux)
                energy = sea * ((energy - div_x) - div_y)
            start = pl.ds(pl.multiple_of(p * height, height), height)
            for h in range(breadth // 128):
                halves[h, start, :] = energy[:, h * 128 : (h + 1) * 128]
            return carry

        lax.fori_loop(0, QUAD, step, 0, unroll=6)

    for k, (from_west, from_south) in enumerate(((True, True), (False, True), (False, False), (True, False))):
        parts[k].wait()
        quadrant(k * QUAD, from_west, from_south)

    east = jnp.zeros((height, 128), jnp.float32)
    west = jnp.zeros((height, 128), jnp.float32)
    for q in range(HALF + 2):
        mine = lane // 2 == q
        if q < HALF:
            p_e = q if q < QUAD else q + HALF
            edge_e, edge_w = x_ref[p_e, :, breadth - 128 :], x_ref[q + QUAD, :, :128]
        else:
            field = moving if q == HALF else sea
            edge_e, edge_w = field[:, breadth - 128 :], field[:, :128]
        east = jnp.where(mine, pltpu.roll(edge_e, (2 * q + 2) % 128, axis=1), east)
        west = jnp.where(mine, pltpu.roll(edge_w, 2 * q, axis=1), west)
    east_ref[...] = east
    west_ref[...] = west


def profile_rows(halves, weight, table, first_row, count, height, breadth):
    pad = jnp.zeros((8, 128), jnp.bfloat16)
    blocks = []
    for k in range(count):
        for h in range(breadth // 128):
            spectra = halves[h, pl.ds(first_row + k, PLANES, stride=height), :]
            high = spectra.astype(jnp.bfloat16)
            low = (spectra - high.astype(jnp.float32)).astype(jnp.bfloat16)
            blocks.append(jnp.concatenate([high, pad, low, pad, high, pad], axis=0))
    stacked = jnp.concatenate(blocks, axis=1)
    profile = lax.dot_general(stacked, weight, (((0,), (0,)), ((), ())), preferred_element_type=jnp.float32)
    start = first_row * breadth
    if not isinstance(start, int):
        start = pl.multiple_of(start, 128)
    table[pl.ds(start, count * breadth), :] = profile


def profile_kernel(courant_ref, kernel_ref, mov_ref, sea_ref, south_ref, north_ref, subs_ref, halves_in,
                   halves, table, edge_ref, wide_kernel):
    height, breadth = mov_ref.shape
    wide = lax.broadcasted_iota(jnp.int32, (HALF + 4, breadth), 1)
    plane = lax.broadcasted_iota(jnp.int32, (HALF + 4, 1), 0)
    subs = subs_ref[...]
    sub_courant = jnp.where(plane % 2 == 1, courant_ref[1], courant_ref[0])

    def x_change(flux, cx, west_first):
        west_flux = jnp.where(wide == 0, 0.0, pltpu.roll(flux, 1, axis=1))
        east_flux = jnp.where(wide == breadth - 1, 0.0, pltpu.roll(flux, breadth - 1, axis=1))
        from_west = (plane < QUAD) if west_first else (plane >= QUAD)
        return jnp.where(from_west, cx * (flux - west_flux), cx * (east_flux - flux))

    def add_rows(first, halo, near, next_row, cx, cy, west_first):
        rim, far = halo[0], halo[1]
        rim_mov, rim_sea = rim[HALF : HALF + 1], rim[HALF + 1 : HALF + 2]
        flux0 = rim_mov * rim
        div_y = cy * (flux0 - far[HALF : HALF + 1] * far)
        flux1 = rim_mov * (rim_sea * ((rim - x_change(flux0, cx, west_first)) - div_y))
        sea0, sea1 = sea_ref[near : near + 1, :], sea_ref[next_row : next_row + 1, :]
        change = sea0 * (cy * flux0)
        flux = mov_ref[near : near + 1, :] * change
        near_change = sea0 * (((change - x_change(flux, cx, west_first)) - cy * flux) + cy * flux1)
        next_change = sea1 * (cy * flux)
        for at, delta in ((near, near_change), (next_row, next_change)):
            for h in range(breadth // 128):
                place = pl.ds(first * height + at, HALF + 4, stride=height)
                halves[h, place, :] = halves[h, place, :] + delta[:, h * 128 : (h + 1) * 128]

    cx_s, cy_s, cx_n, cy_n = (subs[:, k : k + 1] * sub_courant for k in range(4))
    add_rows(0, south_ref, 0, 1, cx_s, cy_s, True)
    add_rows(HALF, north_ref, height - 1, height - 2, cx_n, -cy_n, False)

    pad = jnp.zeros((8, 128), jnp.bfloat16)
    wide_kernel[...] = jnp.zeros((128, 128), jnp.float32)
    wide_kernel[:64, :PLANES] = kernel_ref[...]
    wide_kernel[64:, :PLANES] = kernel_ref[...]
    turned = wide_kernel[...].T
    weight_high = turned[:PLANES].astype(jnp.bfloat16)
    weight_low = (turned[:PLANES] - weight_high.astype(jnp.float32)).astype(jnp.bfloat16)
    weight = jnp.concatenate([weight_high, pad, weight_high, pad, weight_low, pad], axis=0)

    wide_kernel[...] = turned
    edge_ref[...] = jnp.zeros_like(edge_ref)
    for q in range(HALF):
        for side, p in ((0, q if q < QUAD else q + HALF), (1, q + QUAD)):
            for k in range(2):
                lane = 2 * q + (k if side == 0 else 1 - k)
                edge_ref[side, lane : lane + 1, k * 128 : (k + 1) * 128] = wide_kernel[p : p + 1, :]
    group = 8

    @pl.loop(0, height // group)
    def _(r):
        profile_rows(halves, weight, table, r * group, group, height, breadth)


def finish_kernel(courant_ref, cells_ref, mov_ref, sea_ref, edge_ref, south_ref, north_ref, second_ref, first_ref,
                  lanes_ref, halves_in, table_in, out_ref, picked_ref, halves, table,
                  cells, lines, picks, window, out_sems, window_sems, pick_sem):
    cells[...] = jnp.maximum(cells_ref[...], 0)
    height, breadth = mov_ref.shape
    even_lon = lax.axis_index("lon") % 2 == 0
    from_west = jnp.where(even_lon, second_ref[...], first_ref[...])
    from_east = jnp.where(even_lon, first_ref[...], second_ref[...])
    lane = lax.broadcasted_iota(jnp.int32, (height, 128), 1)
    row = lax.broadcasted_iota(jnp.int32, (height, 128), 0)
    odd = lane % 2 == 1
    southern = lane < HALF
    lanes = lanes_ref[...]
    lane_courant = jnp.where(lanes[4:5] > 0.5, courant_ref[1], courant_ref[0])

    def y_change(flux, cy, rim):
        south_flux = jnp.where(row == 0, rim, pltpu.roll(flux, 1, axis=0))
        north_flux = jnp.where(row == height - 1, rim, pltpu.roll(flux, height - 1, axis=0))
        return jnp.where(southern, cy * (flux - south_flux), cy * (north_flux - flux))

    def add_columns(half, message, near, next_column, cx, cy, west):
        outer, corner = message[:height], message[height : height + 1]
        outer_mov = jnp.where(odd, outer[:, 2 * HALF + 1 : 2 * HALF + 2], outer[:, 2 * HALF : 2 * HALF + 1])
        sea_lane = 2 * HALF + (3 if west else 2)
        flux0 = outer_mov * outer
        far = pltpu.roll(flux0, 1 if west else 127, axis=1)
        energy = (outer - cx * (flux0 - far)) - y_change(flux0, cy, corner)
        flux1 = outer_mov * (outer[:, sea_lane : sea_lane + 1] * energy)
        at_column = slice(near, near + 1)
        rim = jnp.where(
            southern[:1],
            south_ref[0, HALF : HALF + 1, at_column] * south_ref[0, HALF + 1 : HALF + 2, at_column],
            north_ref[0, HALF : HALF + 1, at_column] * north_ref[0, HALF + 1 : HALF + 2, at_column],
        ) * (cx * corner)
        sea0, sea1 = sea_ref[:, at_column], sea_ref[:, next_column : next_column + 1]
        change = sea0 * (cx * flux0)
        flux = mov_ref[:, at_column] * change
        near_change = sea0 * (((change - cx * flux) - y_change(flux, cy, rim)) + cx * flux1)
        next_change = sea1 * (cx * flux)
        if west:
            both = jnp.where(odd, next_change, pltpu.roll(near_change, 127, axis=1))
        else:
            both = jnp.where(odd, pltpu.roll(near_change, 1, axis=1), next_change)
        edge = lane < 2 if west else lane >= 126
        for q in range(HALF):
            p = q + QUAD if not west else (q if q < QUAD else q + HALF)
            turned = pltpu.roll(both, ((128 if west else 126) - 2 * q) % 128, axis=1)
            place = pl.ds(p * height, height)
            halves[half, place, :] = halves[half, place, :] + jnp.where(edge, turned, 0.0)
        both = jnp.where(lane < 2 * HALF, both, 0.0)
        profile = jnp.dot(
            both, edge_ref[0 if west else 1], precision=lax.Precision.HIGHEST, preferred_element_type=jnp.float32
        )
        for k, column in enumerate((near, next_column)):
            place = pl.ds(column, height, stride=breadth)
            table[place, :] = table[place, :] + profile[:, k * 128 : (k + 1) * 128]

    cx_w, cy_w, cx_e, cy_e = (lanes[k : k + 1] * lane_courant for k in range(4))
    add_columns(0, from_west, 0, 1, cx_w, cy_w, True)
    add_columns(breadth // 128 - 1, from_east, breadth - 1, breadth - 2, -cx_e, cy_e, False)
    whole = pl.ds(0, PLANES * height)
    writes = [
        pltpu.make_async_copy(halves.at[h, whole, :], out_ref.at[:, pl.ds(h * 128, 128)], out_sems.at[h])
        for h in range(breadth // 128)
    ]
    for write in writes:
        write.start()

    first_half = lax.broadcasted_iota(jnp.int32, (1, 128), 1) < 64
    half = WINDOW // 2

    def pick(cell, i):
        start = pl.multiple_of(i * half, half)
        for g in range(WINDOW // 32):
            for j in range(16):
                slot = 32 * g + 16 * (j // 8) + j % 8
                one, two = cell(slot), cell(slot + 8)
                line = jnp.where(first_half, table[pl.ds(one, 1), :], table[pl.ds(two, 1), :])
                lines[16 * g + j : 16 * g + j + 1, :] = line
            picks[pl.ds(start + 16 * g, 16), :] = lines[16 * g : 16 * g + 16, :].astype(jnp.bfloat16)
        here = pl.ds(start, half)
        pltpu.make_async_copy(picks.at[here, :], picked_ref.at[here, :], pick_sem).start()

    for_windows(cells, window, window_sems, pick)
    pltpu.make_async_copy(picks, picked_ref, pick_sem).wait()
    for write in writes:
        write.wait()


def add_kernel(rows_ref, values_ref, out_ref, targets, lines, tile_sums, window, window_sems, out_sem, *sums):
    n_acc = len(sums) // 2
    tile = out_ref.shape[1]
    block = 512
    half = WINDOW // 2
    slot = lax.broadcasted_iota(jnp.int32, targets.shape, 1)
    spare = tile + (slot // 16 * 8 + slot % 8) % SPARE
    targets[...] = jnp.where(rows_ref[...] < 0, spare, rows_ref[...])

    @pl.loop(0, tile // block)
    def _(i):
        for total in sums:
            total[pl.ds(pl.multiple_of(i * block, block), block), :] = jnp.zeros((block, 128), jnp.float32)

    def add(row, i):
        start = pl.multiple_of(i * half, half)
        for g in range(WINDOW // 32):
            lines[16 * g : 16 * g + 16, :] = values_ref[pl.ds(start + 16 * g, 16), :].astype(jnp.float32)
            for j in range(16):
                slot = 32 * g + 16 * (j // 8) + j % 8
                one, two = row(slot), row(slot + 8)
                line = lines[16 * g + j : 16 * g + j + 1, :]
                left, right = sums[j % n_acc], sums[n_acc + j % n_acc]
                left[pl.ds(one, 1), :] = left[pl.ds(one, 1), :] + line
                right[pl.ds(two, 1), :] = right[pl.ds(two, 1), :] + line

    for_windows(targets, window, window_sems, add)
    first_half = lax.broadcasted_iota(jnp.int32, (block, 128), 1) < 64

    @pl.loop(0, tile // block)
    def _(i):
        here = pl.ds(pl.multiple_of(i * block, block), block)
        left, right = sums[0][here, :], sums[n_acc][here, :]
        for q in range(1, n_acc):
            left = left + sums[q][here, :]
            right = right + sums[n_acc + q][here, :]
        both = jnp.where(first_half, left, right).T
        tile_sums[:, here] = both[:64] + both[64:]
        pltpu.make_async_copy(tile_sums.at[:, here], out_ref.at[:, here], out_sem).start()

    pltpu.make_async_copy(tile_sums, out_ref, out_sem).wait()


def constant_tables():
    heading = (np.arange(DIRS) + 0.5) * (2.0 * math.pi / DIRS)
    cos = np.repeat(np.cos(heading), FREQ)
    sin = np.repeat(np.sin(heading), FREQ)
    lanes = np.zeros((8, 128))
    q = np.arange(HALF)
    from_west = np.where(q < QUAD, q, q + HALF)
    from_east = q + QUAD
    for column in range(2):
        lanes[0, 2 * q + column] = cos[from_west]
        lanes[1, 2 * q + column] = sin[from_west]
        lanes[2, 2 * q + column] = cos[from_east]
        lanes[3, 2 * q + column] = sin[from_east]
        lanes[4, 2 * q + column] = q % 2
    subs = np.zeros((HALF + 4, 128))
    subs[:HALF, 0], subs[:HALF, 1] = cos[:HALF], sin[:HALF]
    subs[:HALF, 2], subs[:HALF, 3] = cos[HALF:], sin[HALF:]
    return [t.astype(np.float32) for t in (np.concatenate([cos, sin]), lanes, subs)]


def body(n_lat, n_lon, spectrum, speed_factor, land_sea_mask, courant, depth_kernel, send_rows, recv_rows):
    height, breadth = speed_factor.shape
    devices, slots = send_rows.shape[1:]
    x = spectrum.reshape(PLANES, height, breadth)
    f32 = jnp.float32
    vmem = pl.BlockSpec(memory_space=pltpu.VMEM)
    smem = pl.BlockSpec(memory_space=pltpu.SMEM)
    hbm = pl.BlockSpec(memory_space=pltpu.HBM)
    params = pltpu.CompilerParams(vmem_limit_bytes=VMEM_LIMIT)

    both = ("lat", "lon")

    def in_hbm(*arrays):
        return [pltpu.with_memory_space_constraint(array, pltpu.HBM) for array in arrays]

    def shape(*dims, kind=f32):
        return jax.ShapeDtypeStruct(dims, kind)

    headings, lanes, subs = constant_tables()
    row_message = shape(2, ROWS, breadth, kind=jnp.bfloat16)
    row_halo = shape(2, HALF + 4, breadth)
    columns = shape(height, 128)
    column_message = shape(height + 8, 128)
    row_first, row_second, column_first, column_second = exchange_pairs(n_lat, n_lon)
    first, second, moving, sea = pl.pallas_call(
        pack_rows_kernel,
        out_shape=[row_message] * 2 + [shape(height, breadth)] * 2,
        in_specs=[hbm] * 3,
        out_specs=[vmem] * 4,
        scratch_shapes=[pltpu.VMEM((2, ROWS, breadth), f32)] * 2
        + [pltpu.VMEM((HALF, 8, breadth), f32)] * 2
        + [pltpu.VMEM((height, breadth), f32), pltpu.VMEM((height, breadth), jnp.int32), pltpu.SemaphoreType.DMA((4,))],
        compiler_params=params,
        name="pack_rows",
    )(*in_hbm(x, speed_factor, land_sea_mask))
    second = lax.ppermute(second, both, row_second)
    first = lax.ppermute(first, "lat", row_first)
    halves, east, west = pl.pallas_call(
        inside_kernel,
        out_shape=[pltpu.VMEM((breadth // 128, (PLANES + 4) * height, 128), f32)] + [columns] * 2,
        in_specs=[hbm] * 3 + [vmem] * 2,
        out_specs=[vmem] * 3,
        scratch_shapes=[
            pltpu.VMEM((PLANES, height, breadth), f32),
            pltpu.SMEM(courant.shape, f32),
            pltpu.SMEM(headings.shape, f32),
            pltpu.SemaphoreType.DMA((6,)),
        ],
        compiler_params=params,
        cost_estimate=pl.CostEstimate(flops=4_000_000_000, bytes_accessed=5_000_000, transcendentals=0),
        name="advance_inside",
    )(*in_hbm(courant, headings, x), moving, sea)
    south, north, first, second = pl.pallas_call(
        functools.partial(corner_kernel, n_lat),
        out_shape=[row_halo] * 2 + [column_message] * 2,
        in_specs=[vmem] * 4,
        out_specs=[vmem] * 4,
        compiler_params=params,
        name="add_corners",
    )(second, first, east, west)
    second = lax.ppermute(second, "lon", column_second)
    first = lax.ppermute(first, "lon", column_first)

    lists = (devices * slots // 128, 128)
    slot_rows = devices * slots // 2
    slot_rows = devices * slots // 2
    halves_shape = pltpu.VMEM(halves.shape, f32)
    table_shape = pltpu.VMEM((height * breadth, 128), f32)
    halves, table, edges = pl.pallas_call(
        profile_kernel,
        out_shape=[halves_shape, table_shape, shape(2, 128, 256)],
        in_specs=[smem] + [vmem] * 7,
        out_specs=[vmem] * 3,
        input_output_aliases={7: 0},
        scratch_shapes=[pltpu.VMEM((128, 128), f32)],
        compiler_params=params,
        cost_estimate=pl.CostEstimate(flops=2_000_000_000, bytes_accessed=5_000_000, transcendentals=0),
        name="profiles_inside",
    )(courant, depth_kernel, moving, sea, south, north, subs, halves)
    propagated, picked, *_ = pl.pallas_call(
        finish_kernel,
        out_shape=[
            pltpu.HBM((PLANES * height, breadth), f32),
            pltpu.HBM((slot_rows, 128), jnp.bfloat16),
            halves_shape,
            table_shape,
        ],
        in_specs=[smem] + [vmem] * 11,
        out_specs=[hbm, hbm, vmem, vmem],
        input_output_aliases={10: 2, 11: 3},
        scratch_shapes=[
            pltpu.VMEM(lists, jnp.int32),
            pltpu.VMEM((WINDOW // 2, 128), f32),
            pltpu.VMEM((slot_rows, 128), jnp.bfloat16),
            pltpu.SMEM((2 * WINDOW // 128, 128), jnp.int32),
            pltpu.SemaphoreType.DMA((breadth // 128,)),
            pltpu.SemaphoreType.DMA((2,)),
            pltpu.SemaphoreType.DMA,
        ],
        compiler_params=params,
        name="finish_and_pick",
    )(courant, send_rows.reshape(lists), moving, sea, edges, south, north, second, first, lanes, halves, table)

    picked = picked.reshape(devices, slots // 2, 128)
    received = lax.all_to_all(picked, both, split_axis=0, concat_axis=0, tiled=True)

    components = depth_kernel.shape[0]
    stokes = pl.pallas_call(
        add_kernel,
        out_shape=pltpu.HBM((components, OUT_DEV), f32),
        in_specs=[vmem] * 2,
        out_specs=hbm,
        scratch_shapes=[
            pltpu.VMEM(lists, jnp.int32),
            pltpu.VMEM((WINDOW // 2, 128), f32),
            pltpu.VMEM((components, OUT_DEV), f32),
            pltpu.SMEM((2 * WINDOW // 128, 128), jnp.int32),
            pltpu.SemaphoreType.DMA((2,)),
            pltpu.SemaphoreType.DMA,
        ]
        + [pltpu.VMEM((OUT_DEV + SPARE, 128), f32)] * (2 * N_ACC),
        compiler_params=pltpu.CompilerParams(vmem_limit_bytes=ADD_VMEM_LIMIT),
        name="add_profiles",
    )(recv_rows.reshape(lists), received.reshape(slot_rows, 128))
    return propagated.reshape(DIRS, FREQ, height, breadth), stokes


def solution(mesh):
    placed = (
        P(None, None, "lat", "lon"),
        P("lat", "lon"),
        P("lat", "lon"),
        P(),
        P(),
        P(("lat", "lon"), None, None),
        P(("lat", "lon"), None, None),
    )
    return jax.shard_map(
        functools.partial(body, mesh.shape["lat"], mesh.shape["lon"]),
        mesh=mesh,
        in_specs=placed,
        out_specs=(P(None, None, "lat", "lon"), P(None, ("lat", "lon"))),
        check_vma=False,
    )
```

```python
import functools
import math

import jax
import jax.numpy as jnp
import numpy as np
from jax import lax
from jax.experimental import pallas as pl
from jax.experimental.pallas import tpu as pltpu
from jax.sharding import PartitionSpec as P

DIRS = 36
FREQ = 2
PLANES = DIRS * FREQ
HALF = PLANES // 2
QUAD = PLANES // 4
OUT_DEV = 4096
SPARE = 64
N_ACC = 5
ROWS = HALF + 12
WINDOW = 1024
VMEM_LIMIT = 16 * 1024 * 1024
ADD_VMEM_LIMIT = 32 * 1024 * 1024


def exchange_pairs(n_lat, n_lon):
    def flat(j, i):
        return j * n_lon + i % n_lon

    row_first = [(j, j ^ 1) for j in range(n_lat)]
    row_second = []
    for i in range(n_lon):
        row_second += [(flat(0, i), flat(0, i)), (flat(n_lat - 1, i), flat(n_lat - 1, n_lon - 1 - i))]
        for j in range(1, n_lat - 1, 2):
            row_second += [(flat(j, i), flat(j + 1, i)), (flat(j + 1, i), flat(j, i))]
    column_first = [(i, i ^ 1) for i in range(n_lon)]
    column_second = [(i, (i + 1 if i % 2 else i - 1) % n_lon) for i in range(n_lon)]
    return row_first, row_second, column_first, column_second


def pack_rows_kernel(x_hbm, speed_hbm, mask_hbm, first_ref, second_ref, mov_ref, sea_ref,
                     up_ref, down_ref, top_rows, bottom_rows, speed_ref, mask_ref, sems):
    height, breadth = speed_ref.shape
    copies = [
        pltpu.make_async_copy(source, target, sems.at[k])
        for k, (source, target) in enumerate((
            (speed_hbm, speed_ref),
            (mask_hbm, mask_ref),
            (x_hbm.at[pl.ds(0, HALF), pl.ds(height - 8, 8), :], top_rows),
            (x_hbm.at[pl.ds(HALF, HALF), pl.ds(0, 8), :], bottom_rows),
        ))
    ]
    for copy in copies:
        copy.start()
    even = lax.axis_index("lat") % 2 == 0
    for copy in copies:
        copy.wait()
    sea = mask_ref[...].astype(jnp.float32)
    moving = speed_ref[...] * sea
    mov_ref[...] = moving
    sea_ref[...] = sea
    for k in range(2):
        for q in range(HALF):
            up_ref[k, q : q + 1, :] = top_rows[q, 7 - k : 8 - k, :]
            down_ref[k, q : q + 1, :] = bottom_rows[q, k : k + 1, :]
        up_ref[k, HALF : HALF + 1, :] = moving[height - 1 - k : height - k, :]
        down_ref[k, HALF : HALF + 1, :] = moving[k : k + 1, :]
        up_ref[k, HALF + 1 : HALF + 2, :] = sea[height - 1 - k : height - k, :]
        down_ref[k, HALF + 1 : HALF + 2, :] = sea[k : k + 1, :]
        up_ref[k, HALF + 2 :, :] = jnp.zeros((ROWS - HALF - 2, breadth), jnp.float32)
        down_ref[k, HALF + 2 :, :] = jnp.zeros((ROWS - HALF - 2, breadth), jnp.float32)

    @pl.when(even)
    def _():
        first_ref[...] = up_ref[...].astype(jnp.bfloat16)
        second_ref[...] = down_ref[...].astype(jnp.bfloat16)

    @pl.when(jnp.logical_not(even))
    def _():
        first_ref[...] = down_ref[...].astype(jnp.bfloat16)
        second_ref[...] = up_ref[...].astype(jnp.bfloat16)


def corner_kernel(n_lat, second_ref, first_ref, east_ref, west_ref, south_ref, north_ref, out_first, out_second):
    height = east_ref.shape[0]
    breadth = first_ref.shape[2]
    lat = lax.axis_index("lat")
    even = lat % 2 == 0

    used = HALF + 4

    @pl.when(even)
    def _():
        north_ref[...] = first_ref[...].astype(jnp.float32)[:, :used]
        south_ref[...] = second_ref[...].astype(jnp.float32)[:, :used]

    @pl.when(jnp.logical_not(even))
    def _():
        south_ref[...] = first_ref[...].astype(jnp.float32)[:, :used]
        north_ref[...] = second_ref[...].astype(jnp.float32)[:, :used]

    @pl.when(lat == 0)
    def _():
        south_ref[...] = jnp.zeros_like(south_ref)

    @pl.when(lat == n_lat - 1)
    def _():
        flip_i = lax.broadcasted_iota(jnp.int32, (breadth, breadth), 0)
        flip_j = lax.broadcasted_iota(jnp.int32, (breadth, breadth), 1)
        flip = (flip_i + flip_j == breadth - 1).astype(jnp.bfloat16)
        both = jnp.concatenate([second_ref[0], second_ref[1]], axis=0)
        flipped = jnp.dot(both, flip, preferred_element_type=jnp.float32)
        north_ref[0] = flipped[:used]
        north_ref[1] = flipped[ROWS : ROWS + used]

    plane = lax.broadcasted_iota(jnp.int32, (HALF + 4, 128), 0)
    lane = lax.broadcasted_iota(jnp.int32, (HALF + 4, 128), 1)
    south = south_ref[0] * south_ref[0, HALF : HALF + 1, :]
    north = north_ref[0] * north_ref[0, HALF : HALF + 1, :]

    def to_lanes(column, low, high, place):
        mine = (plane >= low) & (plane < high) & (lane == place)
        return jnp.where(mine, column, 0.0)

    east_edge = to_lanes(south[:, breadth - 1 :], 0, QUAD, 2 * plane + 1)
    east_edge += to_lanes(north[:, breadth - 1 :], QUAD, HALF, 2 * plane + 1)
    west_edge = to_lanes(south[:, :1], QUAD, HALF, 2 * plane - HALF)
    west_edge += to_lanes(north[:, :1], 0, QUAD, 2 * plane + HALF)
    east_edge = jnp.broadcast_to(jnp.sum(east_edge, axis=0, keepdims=True), (8, 128))
    west_edge = jnp.broadcast_to(jnp.sum(west_edge, axis=0, keepdims=True), (8, 128))
    even_lon = lax.axis_index("lon") % 2 == 0
    out_first[:height] = jnp.where(even_lon, east_ref[...], west_ref[...])
    out_second[:height] = jnp.where(even_lon, west_ref[...], east_ref[...])
    out_first[height:] = jnp.where(even_lon, east_edge, west_edge)
    out_second[height:] = jnp.where(even_lon, west_edge, east_edge)


def for_windows(list_ref, window, sems, work):
    lines = WINDOW // 128
    count = list_ref.shape[0] // lines

    def fetch(i, w):
        source = list_ref.at[pl.ds(pl.multiple_of(i * lines, lines), lines), :]
        return pltpu.make_async_copy(source, window.at[pl.ds(w * lines, lines), :], sems.at[w])

    for w in range(2):
        fetch(w, w).start()

    @pl.loop(0, count // 2)
    def _(t):
        for w in range(2):
            i = 2 * t + w
            fetch(i, w).wait()
            work(lambda k, start=w * lines: window[start + k // 128, k % 128], i)

            @pl.when(i + 2 < count)
            def _():
                fetch(i + 2, w).start()


def inside_kernel(courant_hbm, heading_hbm, x_hbm, mov_ref, sea_ref, halves, east_ref, west_ref,
                  x_ref, courant_ref, heading_ref, sems):
    height, breadth = mov_ref.shape
    small = [
        pltpu.make_async_copy(courant_hbm, courant_ref, sems.at[4]),
        pltpu.make_async_copy(heading_hbm, heading_ref, sems.at[5]),
    ]
    parts = [
        pltpu.make_async_copy(x_hbm.at[planes], x_ref.at[planes], sems.at[k])
        for k, planes in enumerate(pl.ds(k * QUAD, QUAD) for k in range(4))
    ]
    for copy in small + parts:
        copy.start()
    for copy in small:
        copy.wait()
    c0, c1 = courant_ref[0], courant_ref[1]
    moving = mov_ref[...]
    sea = sea_ref[...]
    lane = lax.broadcasted_iota(jnp.int32, (height, 128), 1)
    row = lax.broadcasted_iota(jnp.int32, (8, breadth), 0)
    for h in range(breadth // 128):
        halves[h, PLANES * height :, :] = jnp.zeros((4 * height, 128), jnp.float32)

    def quadrant(first, from_west, from_south):
        def upstream(flux):
            if from_west:
                moved = pltpu.roll(flux, 1, axis=1)
                side = jnp.concatenate([jnp.where(lane == 0, 0.0, moved[:, :128]), moved[:, 128:]], axis=1)
            else:
                moved = pltpu.roll(flux, breadth - 1, axis=1)
                edge = jnp.where(lane == 127, 0.0, moved[:, breadth - 128 :])
                side = jnp.concatenate([moved[:, : breadth - 128], edge], axis=1)
            if from_south:
                moved = pltpu.roll(flux, 1, axis=0)
                below = jnp.concatenate([jnp.where(row == 0, 0.0, moved[:8]), moved[8:]], axis=0)
            else:
                moved = pltpu.roll(flux, height - 1, axis=0)
                below = jnp.concatenate([moved[: height - 8], jnp.where(row == 7, 0.0, moved[height - 8 :])], axis=0)
            return side, below

        def step(t, carry):
            p = first + t
            courant = jnp.where(p % 2 == 1, c1, c0)
            cx = heading_ref[p] * courant
            cy = heading_ref[PLANES + p] * courant
            energy = x_ref[p]
            for _ in range(2):
                flux = moving * energy
                side, below = upstream(flux)
                div_x = cx * (flux - side) if from_west else cx * (side - flux)
                div_y = cy * (flux - below) if from_south else cy * (below - flux)
                energy = sea * ((energy - div_x) - div_y)
            start = pl.ds(pl.multiple_of(p * height, height), height)
            for h in range(breadth // 128):
                halves[h, start, :] = energy[:, h * 128 : (h + 1) * 128]
            return carry

        lax.fori_loop(0, QUAD, step, 0, unroll=6)

    for k, (from_west, from_south) in enumerate(((True, True), (False, True), (False, False), (True, False))):
        parts[k].wait()
        quadrant(k * QUAD, from_west, from_south)

    east = jnp.zeros((height, 128), jnp.float32)
    west = jnp.zeros((height, 128), jnp.float32)
    for q in range(HALF + 2):
        mine = lane // 2 == q
        if q < HALF:
            p_e = q if q < QUAD else q + HALF
            edge_e, edge_w = x_ref[p_e, :, breadth - 128 :], x_ref[q + QUAD, :, :128]
        else:
            field = moving if q == HALF else sea
            edge_e, edge_w = field[:, breadth - 128 :], field[:, :128]
        east = jnp.where(mine, pltpu.roll(edge_e, (2 * q + 2) % 128, axis=1), east)
        west = jnp.where(mine, pltpu.roll(edge_w, 2 * q, axis=1), west)
    east_ref[...] = east
    west_ref[...] = west


def profile_rows(halves, weight, table, first_row, count, height, breadth):
    pad = jnp.zeros((8, 128), jnp.bfloat16)
    blocks = []
    for k in range(count):
        for h in range(breadth // 128):
            spectra = halves[h, pl.ds(first_row + k, PLANES, stride=height), :]
            high = spectra.astype(jnp.bfloat16)
            low = (spectra - high.astype(jnp.float32)).astype(jnp.bfloat16)
            blocks.append(jnp.concatenate([high, pad, low, pad, high, pad], axis=0))
    stacked = jnp.concatenate(blocks, axis=1)
    profile = lax.dot_general(stacked, weight, (((0,), (0,)), ((), ())), preferred_element_type=jnp.float32)
    start = first_row * breadth
    if not isinstance(start, int):
        start = pl.multiple_of(start, 128)
    table[pl.ds(start, count * breadth), :] = profile


def profile_kernel(courant_ref, kernel_ref, mov_ref, sea_ref, south_ref, north_ref, subs_ref, halves_in,
                   halves, table, edge_ref, wide_kernel):
    height, breadth = mov_ref.shape
    wide = lax.broadcasted_iota(jnp.int32, (HALF + 4, breadth), 1)
    plane = lax.broadcasted_iota(jnp.int32, (HALF + 4, 1), 0)
    subs = subs_ref[...]
    sub_courant = jnp.where(plane % 2 == 1, courant_ref[1], courant_ref[0])

    def x_change(flux, cx, west_first):
        west_flux = jnp.where(wide == 0, 0.0, pltpu.roll(flux, 1, axis=1))
        east_flux = jnp.where(wide == breadth - 1, 0.0, pltpu.roll(flux, breadth - 1, axis=1))
        from_west = (plane < QUAD) if west_first else (plane >= QUAD)
        return jnp.where(from_west, cx * (flux - west_flux), cx * (east_flux - flux))

    def add_rows(first, halo, near, next_row, cx, cy, west_first):
        rim, far = halo[0], halo[1]
        rim_mov, rim_sea = rim[HALF : HALF + 1], rim[HALF + 1 : HALF + 2]
        flux0 = rim_mov * rim
        div_y = cy * (flux0 - far[HALF : HALF + 1] * far)
        flux1 = rim_mov * (rim_sea * ((rim - x_change(flux0, cx, west_first)) - div_y))
        sea0, sea1 = sea_ref[near : near + 1, :], sea_ref[next_row : next_row + 1, :]
        change = sea0 * (cy * flux0)
        flux = mov_ref[near : near + 1, :] * change
        near_change = sea0 * (((change - x_change(flux, cx, west_first)) - cy * flux) + cy * flux1)
        next_change = sea1 * (cy * flux)
        for at, delta in ((near, near_change), (next_row, next_change)):
            for h in range(breadth // 128):
                place = pl.ds(first * height + at, HALF + 4, stride=height)
                halves[h, place, :] = halves[h, place, :] + delta[:, h * 128 : (h + 1) * 128]

    cx_s, cy_s, cx_n, cy_n = (subs[:, k : k + 1] * sub_courant for k in range(4))
    add_rows(0, south_ref, 0, 1, cx_s, cy_s, True)
    add_rows(HALF, north_ref, height - 1, height - 2, cx_n, -cy_n, False)

    pad = jnp.zeros((8, 128), jnp.bfloat16)
    wide_kernel[...] = jnp.zeros((128, 128), jnp.float32)
    wide_kernel[:64, :PLANES] = kernel_ref[...]
    wide_kernel[64:, :PLANES] = kernel_ref[...]
    turned = wide_kernel[...].T
    weight_high = turned[:PLANES].astype(jnp.bfloat16)
    weight_low = (turned[:PLANES] - weight_high.astype(jnp.float32)).astype(jnp.bfloat16)
    weight = jnp.concatenate([weight_high, pad, weight_high, pad, weight_low, pad], axis=0)

    wide_kernel[...] = turned
    edge_ref[...] = jnp.zeros_like(edge_ref)
    for q in range(HALF):
        for side, p in ((0, q if q < QUAD else q + HALF), (1, q + QUAD)):
            for k in range(2):
                lane = 2 * q + (k if side == 0 else 1 - k)
                edge_ref[side, lane : lane + 1, k * 128 : (k + 1) * 128] = wide_kernel[p : p + 1, :]
    group = 8

    @pl.loop(0, height // group)
    def _(r):
        profile_rows(halves, weight, table, r * group, group, height, breadth)


def finish_kernel(courant_ref, cells_ref, mov_ref, sea_ref, edge_ref, south_ref, north_ref, second_ref, first_ref,
                  lanes_ref, halves_in, table_in, out_ref, picked_ref, halves, table,
                  cells, lines, picks, window, out_sems, window_sems, pick_sem):
    cells[...] = jnp.maximum(cells_ref[...], 0)
    height, breadth = mov_ref.shape
    even_lon = lax.axis_index("lon") % 2 == 0
    from_west = jnp.where(even_lon, second_ref[...], first_ref[...])
    from_east = jnp.where(even_lon, first_ref[...], second_ref[...])
    lane = lax.broadcasted_iota(jnp.int32, (height, 128), 1)
    row = lax.broadcasted_iota(jnp.int32, (height, 128), 0)
    odd = lane % 2 == 1
    southern = lane < HALF
    lanes = lanes_ref[...]
    lane_courant = jnp.where(lanes[4:5] > 0.5, courant_ref[1], courant_ref[0])

    def y_change(flux, cy, rim):
        south_flux = jnp.where(row == 0, rim, pltpu.roll(flux, 1, axis=0))
        north_flux = jnp.where(row == height - 1, rim, pltpu.roll(flux, height - 1, axis=0))
        return jnp.where(southern, cy * (flux - south_flux), cy * (north_flux - flux))

    def add_columns(half, message, near, next_column, cx, cy, west):
        outer, corner = message[:height], message[height : height + 1]
        outer_mov = jnp.where(odd, outer[:, 2 * HALF + 1 : 2 * HALF + 2], outer[:, 2 * HALF : 2 * HALF + 1])
        sea_lane = 2 * HALF + (3 if west else 2)
        flux0 = outer_mov * outer
        far = pltpu.roll(flux0, 1 if west else 127, axis=1)
        energy = (outer - cx * (flux0 - far)) - y_change(flux0, cy, corner)
        flux1 = outer_mov * (outer[:, sea_lane : sea_lane + 1] * energy)
        at_column = slice(near, near + 1)
        rim = jnp.where(
            southern[:1],
            south_ref[0, HALF : HALF + 1, at_column] * south_ref[0, HALF + 1 : HALF + 2, at_column],
            north_ref[0, HALF : HALF + 1, at_column] * north_ref[0, HALF + 1 : HALF + 2, at_column],
        ) * (cx * corner)
        sea0, sea1 = sea_ref[:, at_column], sea_ref[:, next_column : next_column + 1]
        change = sea0 * (cx * flux0)
        flux = mov_ref[:, at_column] * change
        near_change = sea0 * (((change - cx * flux) - y_change(flux, cy, rim)) + cx * flux1)
        next_change = sea1 * (cx * flux)
        if west:
            both = jnp.where(odd, next_change, pltpu.roll(near_change, 127, axis=1))
        else:
            both = jnp.where(odd, pltpu.roll(near_change, 1, axis=1), next_change)
        edge = lane < 2 if west else lane >= 126
        for q in range(HALF):
            p = q + QUAD if not west else (q if q < QUAD else q + HALF)
            turned = pltpu.roll(both, ((128 if west else 126) - 2 * q) % 128, axis=1)
            place = pl.ds(p * height, height)
            halves[half, place, :] = halves[half, place, :] + jnp.where(edge, turned, 0.0)
        both = jnp.where(lane < 2 * HALF, both, 0.0)
        profile = jnp.dot(
            both, edge_ref[0 if west else 1], precision=lax.Precision.HIGHEST, preferred_element_type=jnp.float32
        )
        for k, column in enumerate((near, next_column)):
            place = pl.ds(column, height, stride=breadth)
            table[place, :] = table[place, :] + profile[:, k * 128 : (k + 1) * 128]

    cx_w, cy_w, cx_e, cy_e = (lanes[k : k + 1] * lane_courant for k in range(4))
    add_columns(0, from_west, 0, 1, cx_w, cy_w, True)
    add_columns(breadth // 128 - 1, from_east, breadth - 1, breadth - 2, -cx_e, cy_e, False)
    whole = pl.ds(0, PLANES * height)
    writes = [
        pltpu.make_async_copy(halves.at[h, whole, :], out_ref.at[:, pl.ds(h * 128, 128)], out_sems.at[h])
        for h in range(breadth // 128)
    ]
    for write in writes:
        write.start()

    first_half = lax.broadcasted_iota(jnp.int32, (1, 128), 1) < 64
    half = WINDOW // 2

    def pick(cell, i):
        for k in range(half):
            slot = 16 * (k // 8) + k % 8
            one, two = cell(slot), cell(slot + 8)
            line = jnp.where(first_half, table[pl.ds(one, 1), :], table[pl.ds(two, 1), :])
            lines[k : k + 1, :] = line
        here = pl.ds(pl.multiple_of(i * half, half), half)
        picks[here, :] = lines[...].astype(jnp.bfloat16)
        pltpu.make_async_copy(picks.at[here, :], picked_ref.at[here, :], pick_sem).start()

    for_windows(cells, window, window_sems, pick)
    pltpu.make_async_copy(picks, picked_ref, pick_sem).wait()
    for write in writes:
        write.wait()


def add_kernel(rows_ref, values_ref, out_ref, targets, lines, tile_sums, window, window_sems, out_sem, *sums):
    n_acc = len(sums) // 2
    tile = out_ref.shape[1]
    block = 512
    half = WINDOW // 2
    slot = lax.broadcasted_iota(jnp.int32, targets.shape, 1)
    spare = tile + (slot // 16 * 8 + slot % 8) % SPARE
    targets[...] = jnp.where(rows_ref[...] < 0, spare, rows_ref[...])

    @pl.loop(0, tile // block)
    def _(i):
        for total in sums:
            total[pl.ds(pl.multiple_of(i * block, block), block), :] = jnp.zeros((block, 128), jnp.float32)

    def add(row, i):
        lines[...] = values_ref[pl.ds(pl.multiple_of(i * half, half), half), :].astype(jnp.float32)
        for k in range(half):
            slot = 16 * (k // 8) + k % 8
            one, two = row(slot), row(slot + 8)
            line = lines[k : k + 1, :]
            left, right = sums[k % n_acc], sums[n_acc + k % n_acc]
            left[pl.ds(one, 1), :] = left[pl.ds(one, 1), :] + line
            right[pl.ds(two, 1), :] = right[pl.ds(two, 1), :] + line

    for_windows(targets, window, window_sems, add)
    first_half = lax.broadcasted_iota(jnp.int32, (block, 128), 1) < 64

    @pl.loop(0, tile // block, unroll=4)
    def _(i):
        here = pl.ds(pl.multiple_of(i * block, block), block)
        left, right = sums[0][here, :], sums[n_acc][here, :]
        for q in range(1, n_acc):
            left = left + sums[q][here, :]
            right = right + sums[n_acc + q][here, :]
        both = jnp.where(first_half, left, right).T
        tile_sums[:, here] = both[:64] + both[64:]
        pltpu.make_async_copy(tile_sums.at[:, here], out_ref.at[:, here], out_sem).start()

    pltpu.make_async_copy(tile_sums, out_ref, out_sem).wait()


def constant_tables():
    heading = (np.arange(DIRS) + 0.5) * (2.0 * math.pi / DIRS)
    cos = np.repeat(np.cos(heading), FREQ)
    sin = np.repeat(np.sin(heading), FREQ)
    lanes = np.zeros((8, 128))
    q = np.arange(HALF)
    from_west = np.where(q < QUAD, q, q + HALF)
    from_east = q + QUAD
    for column in range(2):
        lanes[0, 2 * q + column] = cos[from_west]
        lanes[1, 2 * q + column] = sin[from_west]
        lanes[2, 2 * q + column] = cos[from_east]
        lanes[3, 2 * q + column] = sin[from_east]
        lanes[4, 2 * q + column] = q % 2
    subs = np.zeros((HALF + 4, 128))
    subs[:HALF, 0], subs[:HALF, 1] = cos[:HALF], sin[:HALF]
    subs[:HALF, 2], subs[:HALF, 3] = cos[HALF:], sin[HALF:]
    return [t.astype(np.float32) for t in (np.concatenate([cos, sin]), lanes, subs)]


def body(n_lat, n_lon, spectrum, speed_factor, land_sea_mask, courant, depth_kernel, send_rows, recv_rows):
    height, breadth = speed_factor.shape
    devices, slots = send_rows.shape[1:]
    x = spectrum.reshape(PLANES, height, breadth)
    f32 = jnp.float32
    vmem = pl.BlockSpec(memory_space=pltpu.VMEM)
    smem = pl.BlockSpec(memory_space=pltpu.SMEM)
    hbm = pl.BlockSpec(memory_space=pltpu.HBM)
    params = pltpu.CompilerParams(vmem_limit_bytes=VMEM_LIMIT)

    both = ("lat", "lon")

    def in_hbm(*arrays):
        return [pltpu.with_memory_space_constraint(array, pltpu.HBM) for array in arrays]

    def shape(*dims, kind=f32):
        return jax.ShapeDtypeStruct(dims, kind)

    headings, lanes, subs = constant_tables()
    row_message = shape(2, ROWS, breadth, kind=jnp.bfloat16)
    row_halo = shape(2, HALF + 4, breadth)
    columns = shape(height, 128)
    column_message = shape(height + 8, 128)
    row_first, row_second, column_first, column_second = exchange_pairs(n_lat, n_lon)
    first, second, moving, sea = pl.pallas_call(
        pack_rows_kernel,
        out_shape=[row_message] * 2 + [shape(height, breadth)] * 2,
        in_specs=[hbm] * 3,
        out_specs=[vmem] * 4,
        scratch_shapes=[pltpu.VMEM((2, ROWS, breadth), f32)] * 2
        + [pltpu.VMEM((HALF, 8, breadth), f32)] * 2
        + [pltpu.VMEM((height, breadth), f32), pltpu.VMEM((height, breadth), jnp.int32), pltpu.SemaphoreType.DMA((4,))],
        compiler_params=params,
        name="pack_rows",
    )(*in_hbm(x, speed_factor, land_sea_mask))
    second = lax.ppermute(second, both, row_second)
    first = lax.ppermute(first, "lat", row_first)
    halves, east, west = pl.pallas_call(
        inside_kernel,
        out_shape=[pltpu.VMEM((breadth // 128, (PLANES + 4) * height, 128), f32)] + [columns] * 2,
        in_specs=[hbm] * 3 + [vmem] * 2,
        out_specs=[vmem] * 3,
        scratch_shapes=[
            pltpu.VMEM((PLANES, height, breadth), f32),
            pltpu.SMEM(courant.shape, f32),
            pltpu.SMEM(headings.shape, f32),
            pltpu.SemaphoreType.DMA((6,)),
        ],
        compiler_params=params,
        cost_estimate=pl.CostEstimate(flops=4_000_000_000, bytes_accessed=5_000_000, transcendentals=0),
        name="advance_inside",
    )(*in_hbm(courant, headings, x), moving, sea)
    south, north, first, second = pl.pallas_call(
        functools.partial(corner_kernel, n_lat),
        out_shape=[row_halo] * 2 + [column_message] * 2,
        in_specs=[vmem] * 4,
        out_specs=[vmem] * 4,
        compiler_params=params,
        name="add_corners",
    )(second, first, east, west)
    second = lax.ppermute(second, "lon", column_second)
    first = lax.ppermute(first, "lon", column_first)

    lists = (devices * slots // 128, 128)
    slot_rows = devices * slots // 2
    slot_rows = devices * slots // 2
    halves_shape = pltpu.VMEM(halves.shape, f32)
    table_shape = pltpu.VMEM((height * breadth, 128), f32)
    halves, table, edges = pl.pallas_call(
        profile_kernel,
        out_shape=[halves_shape, table_shape, shape(2, 128, 256)],
        in_specs=[smem] + [vmem] * 7,
        out_specs=[vmem] * 3,
        input_output_aliases={7: 0},
        scratch_shapes=[pltpu.VMEM((128, 128), f32)],
        compiler_params=params,
        cost_estimate=pl.CostEstimate(flops=2_000_000_000, bytes_accessed=5_000_000, transcendentals=0),
        name="profiles_inside",
    )(courant, depth_kernel, moving, sea, south, north, subs, halves)
    propagated, picked, *_ = pl.pallas_call(
        finish_kernel,
        out_shape=[
            pltpu.HBM((PLANES * height, breadth), f32),
            pltpu.HBM((slot_rows, 128), jnp.bfloat16),
            halves_shape,
            table_shape,
        ],
        in_specs=[smem] + [vmem] * 11,
        out_specs=[hbm, hbm, vmem, vmem],
        input_output_aliases={10: 2, 11: 3},
        scratch_shapes=[
            pltpu.VMEM(lists, jnp.int32),
            pltpu.VMEM((WINDOW // 2, 128), f32),
            pltpu.VMEM((slot_rows, 128), jnp.bfloat16),
            pltpu.SMEM((2 * WINDOW // 128, 128), jnp.int32),
            pltpu.SemaphoreType.DMA((breadth // 128,)),
            pltpu.SemaphoreType.DMA((2,)),
            pltpu.SemaphoreType.DMA,
        ],
        compiler_params=params,
        name="finish_and_pick",
    )(courant, send_rows.reshape(lists), moving, sea, edges, south, north, second, first, lanes, halves, table)

    picked = picked.reshape(devices, slots // 2, 128)
    received = lax.all_to_all(picked, both, split_axis=0, concat_axis=0, tiled=True)

    components = depth_kernel.shape[0]
    stokes = pl.pallas_call(
        add_kernel,
        out_shape=pltpu.HBM((components, OUT_DEV), f32),
        in_specs=[vmem] * 2,
        out_specs=hbm,
        scratch_shapes=[
            pltpu.VMEM(lists, jnp.int32),
            pltpu.VMEM((WINDOW // 2, 128), f32),
            pltpu.VMEM((components, OUT_DEV), f32),
            pltpu.SMEM((2 * WINDOW // 128, 128), jnp.int32),
            pltpu.SemaphoreType.DMA((2,)),
            pltpu.SemaphoreType.DMA,
        ]
        + [pltpu.VMEM((OUT_DEV + SPARE, 128), f32)] * (2 * N_ACC),
        compiler_params=pltpu.CompilerParams(vmem_limit_bytes=ADD_VMEM_LIMIT),
        name="add_profiles",
    )(recv_rows.reshape(lists), received.reshape(slot_rows, 128))
    return propagated.reshape(DIRS, FREQ, height, breadth), stokes


def solution(mesh):
    placed = (
        P(None, None, "lat", "lon"),
        P("lat", "lon"),
        P("lat", "lon"),
        P(),
        P(),
        P(("lat", "lon"), None, None),
        P(("lat", "lon"), None, None),
    )
    return jax.shard_map(
        functools.partial(body, mesh.shape["lat"], mesh.shape["lon"]),
        mesh=mesh,
        in_specs=placed,
        out_specs=(P(None, None, "lat", "lon"), P(None, ("lat", "lon"))),
        check_vma=False,
    )
```

```python
import functools
import math

import jax
import jax.numpy as jnp
import numpy as np
from jax import lax
from jax.experimental import pallas as pl
from jax.experimental.pallas import tpu as pltpu
from jax.sharding import PartitionSpec as P

DIRS = 36
FREQ = 2
PLANES = DIRS * FREQ
HALF = PLANES // 2
QUAD = PLANES // 4
OUT_DEV = 4096
SPARE = 64
N_ACC = 5
ROWS = HALF + 12
WINDOW = 1024
VMEM_LIMIT = 16 * 1024 * 1024
ADD_VMEM_LIMIT = 32 * 1024 * 1024


def exchange_pairs(n_lat, n_lon):
    def flat(j, i):
        return j * n_lon + i % n_lon

    row_first = [(j, j ^ 1) for j in range(n_lat)]
    row_second = []
    for i in range(n_lon):
        row_second += [(flat(0, i), flat(0, i)), (flat(n_lat - 1, i), flat(n_lat - 1, n_lon - 1 - i))]
        for j in range(1, n_lat - 1, 2):
            row_second += [(flat(j, i), flat(j + 1, i)), (flat(j + 1, i), flat(j, i))]
    column_first = [(i, i ^ 1) for i in range(n_lon)]
    column_second = [(i, (i + 1 if i % 2 else i - 1) % n_lon) for i in range(n_lon)]
    return row_first, row_second, column_first, column_second


def pack_rows_kernel(x_hbm, speed_hbm, mask_hbm, first_ref, second_ref, mov_ref, sea_ref,
                     up_ref, down_ref, top_rows, bottom_rows, speed_ref, mask_ref, sems):
    height, breadth = speed_ref.shape
    copies = [
        pltpu.make_async_copy(source, target, sems.at[k])
        for k, (source, target) in enumerate((
            (speed_hbm, speed_ref),
            (mask_hbm, mask_ref),
            (x_hbm.at[pl.ds(0, HALF), pl.ds(height - 8, 8), :], top_rows),
            (x_hbm.at[pl.ds(HALF, HALF), pl.ds(0, 8), :], bottom_rows),
        ))
    ]
    for copy in copies:
        copy.start()
    even = lax.axis_index("lat") % 2 == 0
    for copy in copies:
        copy.wait()
    sea = mask_ref[...].astype(jnp.float32)
    moving = speed_ref[...] * sea
    mov_ref[...] = moving
    sea_ref[...] = sea
    for k in range(2):
        for q in range(HALF):
            up_ref[k, q : q + 1, :] = top_rows[q, 7 - k : 8 - k, :]
            down_ref[k, q : q + 1, :] = bottom_rows[q, k : k + 1, :]
        up_ref[k, HALF : HALF + 1, :] = moving[height - 1 - k : height - k, :]
        down_ref[k, HALF : HALF + 1, :] = moving[k : k + 1, :]
        up_ref[k, HALF + 1 : HALF + 2, :] = sea[height - 1 - k : height - k, :]
        down_ref[k, HALF + 1 : HALF + 2, :] = sea[k : k + 1, :]
        up_ref[k, HALF + 2 :, :] = jnp.zeros((ROWS - HALF - 2, breadth), jnp.float32)
        down_ref[k, HALF + 2 :, :] = jnp.zeros((ROWS - HALF - 2, breadth), jnp.float32)

    @pl.when(even)
    def _():
        first_ref[...] = up_ref[...].astype(jnp.bfloat16)
        second_ref[...] = down_ref[...].astype(jnp.bfloat16)

    @pl.when(jnp.logical_not(even))
    def _():
        first_ref[...] = down_ref[...].astype(jnp.bfloat16)
        second_ref[...] = up_ref[...].astype(jnp.bfloat16)


def corner_kernel(n_lat, second_ref, first_ref, east_ref, west_ref, south_ref, north_ref, out_first, out_second):
    height = east_ref.shape[0]
    breadth = first_ref.shape[2]
    lat = lax.axis_index("lat")
    even = lat % 2 == 0

    used = HALF + 4

    @pl.when(even)
    def _():
        north_ref[...] = first_ref[...].astype(jnp.float32)[:, :used]
        south_ref[...] = second_ref[...].astype(jnp.float32)[:, :used]

    @pl.when(jnp.logical_not(even))
    def _():
        south_ref[...] = first_ref[...].astype(jnp.float32)[:, :used]
        north_ref[...] = second_ref[...].astype(jnp.float32)[:, :used]

    @pl.when(lat == 0)
    def _():
        south_ref[...] = jnp.zeros_like(south_ref)

    @pl.when(lat == n_lat - 1)
    def _():
        flip_i = lax.broadcasted_iota(jnp.int32, (breadth, breadth), 0)
        flip_j = lax.broadcasted_iota(jnp.int32, (breadth, breadth), 1)
        flip = (flip_i + flip_j == breadth - 1).astype(jnp.bfloat16)
        both = jnp.concatenate([second_ref[0], second_ref[1]], axis=0)
        flipped = jnp.dot(both, flip, preferred_element_type=jnp.float32)
        north_ref[0] = flipped[:used]
        north_ref[1] = flipped[ROWS : ROWS + used]

    plane = lax.broadcasted_iota(jnp.int32, (HALF + 4, 128), 0)
    lane = lax.broadcasted_iota(jnp.int32, (HALF + 4, 128), 1)
    south = south_ref[0] * south_ref[0, HALF : HALF + 1, :]
    north = north_ref[0] * north_ref[0, HALF : HALF + 1, :]

    def to_lanes(column, low, high, place):
        mine = (plane >= low) & (plane < high) & (lane == place)
        return jnp.where(mine, column, 0.0)

    east_edge = to_lanes(south[:, breadth - 1 :], 0, QUAD, 2 * plane + 1)
    east_edge += to_lanes(north[:, breadth - 1 :], QUAD, HALF, 2 * plane + 1)
    west_edge = to_lanes(south[:, :1], QUAD, HALF, 2 * plane - HALF)
    west_edge += to_lanes(north[:, :1], 0, QUAD, 2 * plane + HALF)
    east_edge = jnp.broadcast_to(jnp.sum(east_edge, axis=0, keepdims=True), (8, 128))
    west_edge = jnp.broadcast_to(jnp.sum(west_edge, axis=0, keepdims=True), (8, 128))
    even_lon = lax.axis_index("lon") % 2 == 0
    out_first[:height] = jnp.where(even_lon, east_ref[...], west_ref[...])
    out_second[:height] = jnp.where(even_lon, west_ref[...], east_ref[...])
    out_first[height:] = jnp.where(even_lon, east_edge, west_edge)
    out_second[height:] = jnp.where(even_lon, west_edge, east_edge)


def for_windows(list_ref, window, sems, work):
    lines = WINDOW // 128
    count = list_ref.shape[0] // lines

    def fetch(i, w):
        source = list_ref.at[pl.ds(pl.multiple_of(i * lines, lines), lines), :]
        return pltpu.make_async_copy(source, window.at[pl.ds(w * lines, lines), :], sems.at[w])

    for w in range(2):
        fetch(w, w).start()

    @pl.loop(0, count // 2)
    def _(t):
        for w in range(2):
            i = 2 * t + w
            fetch(i, w).wait()
            work(lambda k, start=w * lines: window[start + k // 128, k % 128], i)

            @pl.when(i + 2 < count)
            def _():
                fetch(i + 2, w).start()


def inside_kernel(courant_hbm, heading_hbm, x_hbm, mov_ref, sea_ref, halves, east_ref, west_ref,
                  x_ref, courant_ref, heading_ref, sems):
    height, breadth = mov_ref.shape
    small = [
        pltpu.make_async_copy(courant_hbm, courant_ref, sems.at[5]),
        pltpu.make_async_copy(heading_hbm, heading_ref, sems.at[6]),
    ]
    cuts = (0, 6, QUAD, HALF, 3 * QUAD, PLANES)
    parts = [
        pltpu.make_async_copy(x_hbm.at[pl.ds(low, high - low)], x_ref.at[pl.ds(low, high - low)], sems.at[k])
        for k, (low, high) in enumerate(zip(cuts, cuts[1:]))
    ]
    for copy in small + parts:
        copy.start()
    for copy in small:
        copy.wait()
    c0, c1 = courant_ref[0], courant_ref[1]
    moving = mov_ref[...]
    sea = sea_ref[...]
    lane = lax.broadcasted_iota(jnp.int32, (height, 128), 1)
    row = lax.broadcasted_iota(jnp.int32, (8, breadth), 0)
    for h in range(breadth // 128):
        halves[h, PLANES * height :, :] = jnp.zeros((4 * height, 128), jnp.float32)

    def quadrant(first, count, from_west, from_south):
        def upstream(flux):
            turned = [pltpu.roll(flux[:, k : k + 128], 1 if from_west else 127, axis=1) for k in range(0, breadth, 128)]
            if from_west:
                sides = [jnp.where(lane == 0, turned[k - 1] if k else 0.0, turned[k]) for k in range(len(turned))]
            else:
                sides = [
                    jnp.where(lane == 127, turned[k + 1] if k + 1 < len(turned) else 0.0, turned[k])
                    for k in range(len(turned))
                ]
            moved = [pltpu.roll(flux[k : k + 8], 1 if from_south else 7, axis=0) for k in range(0, height, 8)]
            if from_south:
                below = [jnp.where(row == 0, moved[k - 1] if k else 0.0, moved[k]) for k in range(len(moved))]
            else:
                below = [
                    jnp.where(row == 7, moved[k + 1] if k + 1 < len(moved) else 0.0, moved[k])
                    for k in range(len(moved))
                ]
            return jnp.concatenate(sides, axis=1), jnp.concatenate(below, axis=0)

        def step(t, carry):
            p = first + t
            courant = jnp.where(p % 2 == 1, c1, c0)
            cx = heading_ref[p] * courant
            cy = heading_ref[PLANES + p] * courant
            energy = x_ref[p]
            for _ in range(2):
                flux = moving * energy
                side, below = upstream(flux)
                div_x = cx * (flux - side) if from_west else cx * (side - flux)
                div_y = cy * (flux - below) if from_south else cy * (below - flux)
                energy = sea * ((energy - div_x) - div_y)
            start = pl.ds(pl.multiple_of(p * height, height), height)
            for h in range(breadth // 128):
                halves[h, start, :] = energy[:, h * 128 : (h + 1) * 128]
            return carry

        lax.fori_loop(0, count, step, 0, unroll=6)

    for copy, low, high in zip(parts, cuts, cuts[1:]):
        copy.wait()
        quadrant(low, high - low, low // QUAD in (0, 3), low < HALF)

    east = jnp.zeros((height, 128), jnp.float32)
    west = jnp.zeros((height, 128), jnp.float32)
    for q in range(HALF + 2):
        mine = lane // 2 == q
        if q < HALF:
            p_e = q if q < QUAD else q + HALF
            edge_e, edge_w = x_ref[p_e, :, breadth - 128 :], x_ref[q + QUAD, :, :128]
        else:
            field = moving if q == HALF else sea
            edge_e, edge_w = field[:, breadth - 128 :], field[:, :128]
        east = jnp.where(mine, pltpu.roll(edge_e, (2 * q + 2) % 128, axis=1), east)
        west = jnp.where(mine, pltpu.roll(edge_w, 2 * q, axis=1), west)
    east_ref[...] = east
    west_ref[...] = west


def profile_rows(halves, weight, table, first_row, count, height, breadth):
    pad = jnp.zeros((8, 128), jnp.bfloat16)
    blocks = []
    for k in range(count):
        for h in range(breadth // 128):
            spectra = halves[h, pl.ds(first_row + k, PLANES, stride=height), :]
            high = spectra.astype(jnp.bfloat16)
            low = (spectra - high.astype(jnp.float32)).astype(jnp.bfloat16)
            blocks.append(jnp.concatenate([high, pad, low, pad, high, pad], axis=0))
    stacked = jnp.concatenate(blocks, axis=1)
    profile = lax.dot_general(stacked, weight, (((0,), (0,)), ((), ())), preferred_element_type=jnp.float32)
    start = first_row * breadth
    if not isinstance(start, int):
        start = pl.multiple_of(start, 128)
    table[pl.ds(start, count * breadth), :] = profile


def profile_kernel(courant_ref, kernel_ref, mov_ref, sea_ref, south_ref, north_ref, subs_ref, halves_in,
                   halves, table, edge_ref, wide_kernel):
    height, breadth = mov_ref.shape
    wide = lax.broadcasted_iota(jnp.int32, (HALF + 4, breadth), 1)
    plane = lax.broadcasted_iota(jnp.int32, (HALF + 4, 1), 0)
    subs = subs_ref[...]
    sub_courant = jnp.where(plane % 2 == 1, courant_ref[1], courant_ref[0])

    def x_change(flux, cx, west_first):
        west_flux = jnp.where(wide == 0, 0.0, pltpu.roll(flux, 1, axis=1))
        east_flux = jnp.where(wide == breadth - 1, 0.0, pltpu.roll(flux, breadth - 1, axis=1))
        from_west = (plane < QUAD) if west_first else (plane >= QUAD)
        return jnp.where(from_west, cx * (flux - west_flux), cx * (east_flux - flux))

    def add_rows(first, halo, near, next_row, cx, cy, west_first):
        rim, far = halo[0], halo[1]
        rim_mov, rim_sea = rim[HALF : HALF + 1], rim[HALF + 1 : HALF + 2]
        flux0 = rim_mov * rim
        div_y = cy * (flux0 - far[HALF : HALF + 1] * far)
        flux1 = rim_mov * (rim_sea * ((rim - x_change(flux0, cx, west_first)) - div_y))
        sea0, sea1 = sea_ref[near : near + 1, :], sea_ref[next_row : next_row + 1, :]
        change = sea0 * (cy * flux0)
        flux = mov_ref[near : near + 1, :] * change
        near_change = sea0 * (((change - x_change(flux, cx, west_first)) - cy * flux) + cy * flux1)
        next_change = sea1 * (cy * flux)
        for at, delta in ((near, near_change), (next_row, next_change)):
            for h in range(breadth // 128):
                place = pl.ds(first * height + at, HALF + 4, stride=height)
                halves[h, place, :] = halves[h, place, :] + delta[:, h * 128 : (h + 1) * 128]

    cx_s, cy_s, cx_n, cy_n = (subs[:, k : k + 1] * sub_courant for k in range(4))
    add_rows(0, south_ref, 0, 1, cx_s, cy_s, True)
    add_rows(HALF, north_ref, height - 1, height - 2, cx_n, -cy_n, False)

    pad = jnp.zeros((8, 128), jnp.bfloat16)
    wide_kernel[...] = jnp.zeros((128, 128), jnp.float32)
    wide_kernel[:64, :PLANES] = kernel_ref[...]
    wide_kernel[64:, :PLANES] = kernel_ref[...]
    turned = wide_kernel[...].T
    weight_high = turned[:PLANES].astype(jnp.bfloat16)
    weight_low = (turned[:PLANES] - weight_high.astype(jnp.float32)).astype(jnp.bfloat16)
    weight = jnp.concatenate([weight_high, pad, weight_high, pad, weight_low, pad], axis=0)

    wide_kernel[...] = turned
    edge_ref[...] = jnp.zeros_like(edge_ref)
    for q in range(HALF):
        for side, p in ((0, q if q < QUAD else q + HALF), (1, q + QUAD)):
            for k in range(2):
                lane = 2 * q + (k if side == 0 else 1 - k)
                edge_ref[side, lane : lane + 1, k * 128 : (k + 1) * 128] = wide_kernel[p : p + 1, :]

    profile_rows(halves, weight, table, 0, height, height, breadth)
    table[height * breadth :, :] = jnp.zeros((8, 128), jnp.float32)


def finish_kernel(courant_ref, cells_ref, mov_ref, sea_ref, edge_ref, south_ref, north_ref, second_ref, first_ref,
                  lanes_ref, halves_in, table_in, out_ref, picked_ref, halves, table,
                  cells, lines, picks, window, out_sems, window_sems, pick_sem):
    height, breadth = mov_ref.shape
    cells[...] = jnp.where(cells_ref[...] < 0, height * breadth, cells_ref[...])
    even_lon = lax.axis_index("lon") % 2 == 0
    from_west = jnp.where(even_lon, second_ref[...], first_ref[...])
    from_east = jnp.where(even_lon, first_ref[...], second_ref[...])
    lane = lax.broadcasted_iota(jnp.int32, (height, 128), 1)
    row = lax.broadcasted_iota(jnp.int32, (height, 128), 0)
    odd = lane % 2 == 1
    southern = lane < HALF
    lanes = lanes_ref[...]
    lane_courant = jnp.where(lanes[4:5] > 0.5, courant_ref[1], courant_ref[0])

    def y_change(flux, cy, rim):
        south_flux = jnp.where(row == 0, rim, pltpu.roll(flux, 1, axis=0))
        north_flux = jnp.where(row == height - 1, rim, pltpu.roll(flux, height - 1, axis=0))
        return jnp.where(southern, cy * (flux - south_flux), cy * (north_flux - flux))

    def add_columns(half, message, near, next_column, cx, cy, west):
        outer, corner = message[:height], message[height : height + 1]
        outer_mov = jnp.where(odd, outer[:, 2 * HALF + 1 : 2 * HALF + 2], outer[:, 2 * HALF : 2 * HALF + 1])
        sea_lane = 2 * HALF + (3 if west else 2)
        flux0 = outer_mov * outer
        far = pltpu.roll(flux0, 1 if west else 127, axis=1)
        energy = (outer - cx * (flux0 - far)) - y_change(flux0, cy, corner)
        flux1 = outer_mov * (outer[:, sea_lane : sea_lane + 1] * energy)
        at_column = slice(near, near + 1)
        rim = jnp.where(
            southern[:1],
            south_ref[0, HALF : HALF + 1, at_column] * south_ref[0, HALF + 1 : HALF + 2, at_column],
            north_ref[0, HALF : HALF + 1, at_column] * north_ref[0, HALF + 1 : HALF + 2, at_column],
        ) * (cx * corner)
        sea0, sea1 = sea_ref[:, at_column], sea_ref[:, next_column : next_column + 1]
        change = sea0 * (cx * flux0)
        flux = mov_ref[:, at_column] * change
        near_change = sea0 * (((change - cx * flux) - y_change(flux, cy, rim)) + cx * flux1)
        next_change = sea1 * (cx * flux)
        if west:
            both = jnp.where(odd, next_change, pltpu.roll(near_change, 127, axis=1))
        else:
            both = jnp.where(odd, pltpu.roll(near_change, 1, axis=1), next_change)
        edge = lane < 2 if west else lane >= 126
        for q in range(HALF):
            p = q + QUAD if not west else (q if q < QUAD else q + HALF)
            turned = pltpu.roll(both, ((128 if west else 126) - 2 * q) % 128, axis=1)
            place = pl.ds(p * height, height)
            halves[half, place, :] = halves[half, place, :] + jnp.where(edge, turned, 0.0)
        both = jnp.where(lane < 2 * HALF, both, 0.0)
        profile = jnp.dot(
            both, edge_ref[0 if west else 1], precision=lax.Precision.HIGHEST, preferred_element_type=jnp.float32
        )
        for k, column in enumerate((near, next_column)):
            place = pl.ds(column, height, stride=breadth)
            table[place, :] = table[place, :] + profile[:, k * 128 : (k + 1) * 128]

    cx_w, cy_w, cx_e, cy_e = (lanes[k : k + 1] * lane_courant for k in range(4))
    add_columns(0, from_west, 0, 1, cx_w, cy_w, True)
    add_columns(breadth // 128 - 1, from_east, breadth - 1, breadth - 2, -cx_e, cy_e, False)
    whole = pl.ds(0, PLANES * height)
    writes = [
        pltpu.make_async_copy(halves.at[h, whole, :], out_ref.at[:, pl.ds(h * 128, 128)], out_sems.at[h])
        for h in range(breadth // 128)
    ]
    for write in writes:
        write.start()

    first_half = lax.broadcasted_iota(jnp.int32, (1, 128), 1) < 64
    half = WINDOW // 2

    def pick(cell, i):
        def read(first, count):
            for k in range(first, first + count):
                slot = 16 * (k // 8) + k % 8
                one, two = cell(slot), cell(slot + 8)
                lines[k : k + 1, :] = jnp.where(first_half, table[pl.ds(one, 1), :], table[pl.ds(two, 1), :])

        for first in range(0, half, 64):
            read(first, 32)

            @pl.when(cell(2 * first + 64) < height * breadth)
            def _():
                read(first + 32, 32)

        here = pl.ds(pl.multiple_of(i * half, half), half)
        picks[here, :] = lines[...].astype(jnp.bfloat16)
        pltpu.make_async_copy(picks.at[here, :], picked_ref.at[here, :], pick_sem).start()

    lines[...] = jnp.zeros_like(lines)
    for_windows(cells, window, window_sems, pick)
    pltpu.make_async_copy(picks, picked_ref, pick_sem).wait()
    for write in writes:
        write.wait()


def add_kernel(rows_ref, values_ref, out_ref, targets, lines, tile_sums, window, window_sems, out_sem, *sums):
    n_acc = len(sums) // 2
    tile = out_ref.shape[1]
    block = 512
    half = WINDOW // 2
    slot = lax.broadcasted_iota(jnp.int32, targets.shape, 1)
    spare = tile + (slot // 16 * 8 + slot % 8) % SPARE
    targets[...] = jnp.where(rows_ref[...] < 0, spare, rows_ref[...])

    @pl.loop(0, tile // block)
    def _(i):
        for total in sums:
            total[pl.ds(pl.multiple_of(i * block, block), block), :] = jnp.zeros((block, 128), jnp.float32)

    def add(row, i):
        lines[...] = values_ref[pl.ds(pl.multiple_of(i * half, half), half), :].astype(jnp.float32)
        for k in range(half):
            slot = 16 * (k // 8) + k % 8
            one, two = row(slot), row(slot + 8)
            line = lines[k : k + 1, :]
            left, right = sums[k % n_acc], sums[n_acc + k % n_acc]
            left[pl.ds(one, 1), :] = left[pl.ds(one, 1), :] + line
            right[pl.ds(two, 1), :] = right[pl.ds(two, 1), :] + line

    for_windows(targets, window, window_sems, add)
    first_half = lax.broadcasted_iota(jnp.int32, (block, 128), 1) < 64

    @pl.loop(0, tile // block, unroll=4)
    def _(i):
        here = pl.ds(pl.multiple_of(i * block, block), block)
        left, right = sums[0][here, :], sums[n_acc][here, :]
        for q in range(1, n_acc):
            left = left + sums[q][here, :]
            right = right + sums[n_acc + q][here, :]
        both = jnp.where(first_half, left, right).T
        tile_sums[:, here] = both[:64] + both[64:]
        pltpu.make_async_copy(tile_sums.at[:, here], out_ref.at[:, here], out_sem).start()

    pltpu.make_async_copy(tile_sums, out_ref, out_sem).wait()


def constant_tables():
    heading = (np.arange(DIRS) + 0.5) * (2.0 * math.pi / DIRS)
    cos = np.repeat(np.cos(heading), FREQ)
    sin = np.repeat(np.sin(heading), FREQ)
    lanes = np.zeros((8, 128))
    q = np.arange(HALF)
    from_west = np.where(q < QUAD, q, q + HALF)
    from_east = q + QUAD
    for column in range(2):
        lanes[0, 2 * q + column] = cos[from_west]
        lanes[1, 2 * q + column] = sin[from_west]
        lanes[2, 2 * q + column] = cos[from_east]
        lanes[3, 2 * q + column] = sin[from_east]
        lanes[4, 2 * q + column] = q % 2
    subs = np.zeros((HALF + 4, 128))
    subs[:HALF, 0], subs[:HALF, 1] = cos[:HALF], sin[:HALF]
    subs[:HALF, 2], subs[:HALF, 3] = cos[HALF:], sin[HALF:]
    return [t.astype(np.float32) for t in (np.concatenate([cos, sin]), lanes, subs)]


def body(n_lat, n_lon, spectrum, speed_factor, land_sea_mask, courant, depth_kernel, send_rows, recv_rows):
    height, breadth = speed_factor.shape
    devices, slots = send_rows.shape[1:]
    x = spectrum.reshape(PLANES, height, breadth)
    f32 = jnp.float32
    vmem = pl.BlockSpec(memory_space=pltpu.VMEM)
    smem = pl.BlockSpec(memory_space=pltpu.SMEM)
    hbm = pl.BlockSpec(memory_space=pltpu.HBM)
    params = pltpu.CompilerParams(vmem_limit_bytes=VMEM_LIMIT)

    both = ("lat", "lon")

    def in_hbm(*arrays):
        return [pltpu.with_memory_space_constraint(array, pltpu.HBM) for array in arrays]

    def shape(*dims, kind=f32):
        return jax.ShapeDtypeStruct(dims, kind)

    headings, lanes, subs = constant_tables()
    row_message = shape(2, ROWS, breadth, kind=jnp.bfloat16)
    row_halo = shape(2, HALF + 4, breadth)
    columns = shape(height, 128)
    column_message = shape(height + 8, 128)
    row_first, row_second, column_first, column_second = exchange_pairs(n_lat, n_lon)
    first, second, moving, sea = pl.pallas_call(
        pack_rows_kernel,
        out_shape=[row_message] * 2 + [shape(height, breadth)] * 2,
        in_specs=[hbm] * 3,
        out_specs=[vmem] * 4,
        scratch_shapes=[pltpu.VMEM((2, ROWS, breadth), f32)] * 2
        + [pltpu.VMEM((HALF, 8, breadth), f32)] * 2
        + [pltpu.VMEM((height, breadth), f32), pltpu.VMEM((height, breadth), jnp.int32), pltpu.SemaphoreType.DMA((4,))],
        compiler_params=params,
        name="pack_rows",
    )(*in_hbm(x, speed_factor, land_sea_mask))
    second = lax.ppermute(second, both, row_second)
    first = lax.ppermute(first, "lat", row_first)
    halves, east, west = pl.pallas_call(
        inside_kernel,
        out_shape=[pltpu.VMEM((breadth // 128, (PLANES + 4) * height, 128), f32)] + [columns] * 2,
        in_specs=[hbm] * 3 + [vmem] * 2,
        out_specs=[vmem] * 3,
        scratch_shapes=[
            pltpu.VMEM((PLANES, height, breadth), f32),
            pltpu.SMEM(courant.shape, f32),
            pltpu.SMEM(headings.shape, f32),
            pltpu.SemaphoreType.DMA((7,)),
        ],
        compiler_params=params,
        cost_estimate=pl.CostEstimate(flops=4_000_000_000, bytes_accessed=5_000_000, transcendentals=0),
        name="advance_inside",
    )(*in_hbm(courant, headings, x), moving, sea)
    south, north, first, second = pl.pallas_call(
        functools.partial(corner_kernel, n_lat),
        out_shape=[row_halo] * 2 + [column_message] * 2,
        in_specs=[vmem] * 4,
        out_specs=[vmem] * 4,
        compiler_params=params,
        name="add_corners",
    )(second, first, east, west)
    second = lax.ppermute(second, "lon", column_second)
    first = lax.ppermute(first, "lon", column_first)

    lists = (devices * slots // 128, 128)
    slot_rows = devices * slots // 2
    slot_rows = devices * slots // 2
    halves_shape = pltpu.VMEM(halves.shape, f32)
    table_shape = pltpu.VMEM((height * breadth + 8, 128), f32)
    halves, table, edges = pl.pallas_call(
        profile_kernel,
        out_shape=[halves_shape, table_shape, shape(2, 128, 256)],
        in_specs=[smem] + [vmem] * 7,
        out_specs=[vmem] * 3,
        input_output_aliases={7: 0},
        scratch_shapes=[pltpu.VMEM((128, 128), f32)],
        compiler_params=params,
        cost_estimate=pl.CostEstimate(flops=2_000_000_000, bytes_accessed=5_000_000, transcendentals=0),
        name="profiles_inside",
    )(courant, depth_kernel, moving, sea, south, north, subs, halves)
    propagated, picked, *_ = pl.pallas_call(
        finish_kernel,
        out_shape=[
            pltpu.HBM((PLANES * height, breadth), f32),
            pltpu.HBM((slot_rows, 128), jnp.bfloat16),
            halves_shape,
            table_shape,
        ],
        in_specs=[smem] + [vmem] * 11,
        out_specs=[hbm, hbm, vmem, vmem],
        input_output_aliases={10: 2, 11: 3},
        scratch_shapes=[
            pltpu.VMEM(lists, jnp.int32),
            pltpu.VMEM((WINDOW // 2, 128), f32),
            pltpu.VMEM((slot_rows, 128), jnp.bfloat16),
            pltpu.SMEM((2 * WINDOW // 128, 128), jnp.int32),
            pltpu.SemaphoreType.DMA((breadth // 128,)),
            pltpu.SemaphoreType.DMA((2,)),
            pltpu.SemaphoreType.DMA,
        ],
        compiler_params=params,
        name="finish_and_pick",
    )(courant, send_rows.reshape(lists), moving, sea, edges, south, north, second, first, lanes, halves, table)

    picked = picked.reshape(devices, slots // 2, 128)
    received = lax.all_to_all(picked, both, split_axis=0, concat_axis=0, tiled=True)

    components = depth_kernel.shape[0]
    stokes = pl.pallas_call(
        add_kernel,
        out_shape=pltpu.HBM((components, OUT_DEV), f32),
        in_specs=[vmem] * 2,
        out_specs=hbm,
        scratch_shapes=[
            pltpu.VMEM(lists, jnp.int32),
            pltpu.VMEM((WINDOW // 2, 128), f32),
            pltpu.VMEM((components, OUT_DEV), f32),
            pltpu.SMEM((2 * WINDOW // 128, 128), jnp.int32),
            pltpu.SemaphoreType.DMA((2,)),
            pltpu.SemaphoreType.DMA,
        ]
        + [pltpu.VMEM((OUT_DEV + SPARE, 128), f32)] * (2 * N_ACC),
        compiler_params=pltpu.CompilerParams(vmem_limit_bytes=ADD_VMEM_LIMIT),
        name="add_profiles",
    )(recv_rows.reshape(lists), received.reshape(slot_rows, 128))
    return propagated.reshape(DIRS, FREQ, height, breadth), stokes


def solution(mesh):
    placed = (
        P(None, None, "lat", "lon"),
        P("lat", "lon"),
        P("lat", "lon"),
        P(),
        P(),
        P(("lat", "lon"), None, None),
        P(("lat", "lon"), None, None),
    )
    return jax.shard_map(
        functools.partial(body, mesh.shape["lat"], mesh.shape["lon"]),
        mesh=mesh,
        in_specs=placed,
        out_specs=(P(None, None, "lat", "lon"), P(None, ("lat", "lon"))),
        check_vma=False,
    )
```

```python
import functools
import math

import jax
import jax.numpy as jnp
import numpy as np
from jax import lax
from jax.experimental import pallas as pl
from jax.experimental.pallas import tpu as pltpu
from jax.sharding import PartitionSpec as P

DIRS = 36
FREQ = 2
PLANES = DIRS * FREQ
HALF = PLANES // 2
QUAD = PLANES // 4
OUT_DEV = 4096
SPARE = 64
N_ACC = 5
ROWS = HALF + 12
WINDOW = 1024
VMEM_LIMIT = 16 * 1024 * 1024
ADD_VMEM_LIMIT = 32 * 1024 * 1024


def exchange_pairs(n_lat, n_lon):
    def flat(j, i):
        return j * n_lon + i % n_lon

    row_first = [(j, j ^ 1) for j in range(n_lat)]
    row_second = []
    for i in range(n_lon):
        row_second += [(flat(0, i), flat(0, i)), (flat(n_lat - 1, i), flat(n_lat - 1, n_lon - 1 - i))]
        for j in range(1, n_lat - 1, 2):
            row_second += [(flat(j, i), flat(j + 1, i)), (flat(j + 1, i), flat(j, i))]
    column_first = [(i, i ^ 1) for i in range(n_lon)]
    column_second = [(i, (i + 1 if i % 2 else i - 1) % n_lon) for i in range(n_lon)]
    return row_first, row_second, column_first, column_second


def pack_rows_kernel(x_hbm, speed_hbm, mask_hbm, first_ref, second_ref, mov_ref, sea_ref,
                     up_ref, down_ref, top_rows, bottom_rows, speed_ref, mask_ref, sems):
    height, breadth = speed_ref.shape
    copies = [
        pltpu.make_async_copy(source, target, sems.at[k])
        for k, (source, target) in enumerate((
            (speed_hbm, speed_ref),
            (mask_hbm, mask_ref),
            (x_hbm.at[pl.ds(0, HALF), pl.ds(height - 2, 2), :], top_rows.at[:, pl.ds(6, 2), :]),
            (x_hbm.at[pl.ds(HALF, HALF), pl.ds(0, 2), :], bottom_rows.at[:, pl.ds(0, 2), :]),
        ))
    ]
    for copy in copies:
        copy.start()
    even = lax.axis_index("lat") % 2 == 0
    for copy in copies:
        copy.wait()
    sea = mask_ref[...].astype(jnp.float32)
    moving = speed_ref[...] * sea
    mov_ref[...] = moving
    sea_ref[...] = sea
    for k in range(2):
        up_ref[k, :HALF, :] = top_rows[:, 7 - k, :]
        down_ref[k, :HALF, :] = bottom_rows[:, k, :]
        up_ref[k, HALF : HALF + 1, :] = moving[height - 1 - k : height - k, :]
        down_ref[k, HALF : HALF + 1, :] = moving[k : k + 1, :]
        up_ref[k, HALF + 1 : HALF + 2, :] = sea[height - 1 - k : height - k, :]
        down_ref[k, HALF + 1 : HALF + 2, :] = sea[k : k + 1, :]
        up_ref[k, HALF + 2 :, :] = jnp.zeros((ROWS - HALF - 2, breadth), jnp.float32)
        down_ref[k, HALF + 2 :, :] = jnp.zeros((ROWS - HALF - 2, breadth), jnp.float32)

    @pl.when(even)
    def _():
        first_ref[...] = up_ref[...].astype(jnp.bfloat16)
        second_ref[...] = down_ref[...].astype(jnp.bfloat16)

    @pl.when(jnp.logical_not(even))
    def _():
        first_ref[...] = down_ref[...].astype(jnp.bfloat16)
        second_ref[...] = up_ref[...].astype(jnp.bfloat16)


def corner_kernel(n_lat, second_ref, first_ref, east_ref, west_ref, south_ref, north_ref, out_first, out_second):
    height = east_ref.shape[0]
    breadth = first_ref.shape[2]
    lat = lax.axis_index("lat")
    even = lat % 2 == 0

    used = HALF + 4

    @pl.when(even)
    def _():
        north_ref[...] = first_ref[...].astype(jnp.float32)[:, :used]
        south_ref[...] = second_ref[...].astype(jnp.float32)[:, :used]

    @pl.when(jnp.logical_not(even))
    def _():
        south_ref[...] = first_ref[...].astype(jnp.float32)[:, :used]
        north_ref[...] = second_ref[...].astype(jnp.float32)[:, :used]

    @pl.when(lat == 0)
    def _():
        south_ref[...] = jnp.zeros_like(south_ref)

    @pl.when(lat == n_lat - 1)
    def _():
        flip_i = lax.broadcasted_iota(jnp.int32, (breadth, breadth), 0)
        flip_j = lax.broadcasted_iota(jnp.int32, (breadth, breadth), 1)
        flip = (flip_i + flip_j == breadth - 1).astype(jnp.bfloat16)
        both = jnp.concatenate([second_ref[0], second_ref[1]], axis=0)
        flipped = jnp.dot(both, flip, preferred_element_type=jnp.float32)
        north_ref[0] = flipped[:used]
        north_ref[1] = flipped[ROWS : ROWS + used]

    plane = lax.broadcasted_iota(jnp.int32, (HALF + 4, 128), 0)
    lane = lax.broadcasted_iota(jnp.int32, (HALF + 4, 128), 1)
    south = south_ref[0] * south_ref[0, HALF : HALF + 1, :]
    north = north_ref[0] * north_ref[0, HALF : HALF + 1, :]

    def to_lanes(column, low, high, place):
        mine = (plane >= low) & (plane < high) & (lane == place)
        return jnp.where(mine, column, 0.0)

    east_edge = to_lanes(south[:, breadth - 1 :], 0, QUAD, 2 * plane + 1)
    east_edge += to_lanes(north[:, breadth - 1 :], QUAD, HALF, 2 * plane + 1)
    west_edge = to_lanes(south[:, :1], QUAD, HALF, 2 * plane - HALF)
    west_edge += to_lanes(north[:, :1], 0, QUAD, 2 * plane + HALF)
    east_edge = jnp.broadcast_to(jnp.sum(east_edge, axis=0, keepdims=True), (8, 128))
    west_edge = jnp.broadcast_to(jnp.sum(west_edge, axis=0, keepdims=True), (8, 128))
    even_lon = lax.axis_index("lon") % 2 == 0
    out_first[:height] = jnp.where(even_lon, east_ref[...], west_ref[...])
    out_second[:height] = jnp.where(even_lon, west_ref[...], east_ref[...])
    out_first[height:] = jnp.where(even_lon, east_edge, west_edge)
    out_second[height:] = jnp.where(even_lon, west_edge, east_edge)


def fetch_window(list_ref, window, sems, i, w):
    lines = WINDOW // 128
    source = list_ref.at[pl.ds(pl.multiple_of(i * lines, lines), lines), :]
    return pltpu.make_async_copy(source, window.at[pl.ds(w * lines, lines), :], sems.at[w])


def start_windows(list_ref, window, sems):
    for w in range(2):
        fetch_window(list_ref, window, sems, w, w).start()


def for_windows(list_ref, window, sems, work):
    lines = WINDOW // 128
    count = list_ref.shape[0] // lines

    @pl.loop(0, count // 2)
    def _(t):
        for w in range(2):
            i = 2 * t + w
            fetch_window(list_ref, window, sems, i, w).wait()
            work(lambda k, start=w * lines: window[start + k // 128, k % 128], i)

            @pl.when(i + 2 < count)
            def _():
                fetch_window(list_ref, window, sems, i + 2, w).start()


def inside_kernel(courant_hbm, heading_hbm, x_hbm, mov_ref, sea_ref, halves, east_ref, west_ref,
                  x_ref, courant_ref, heading_ref, sems):
    height, breadth = mov_ref.shape
    small = [
        pltpu.make_async_copy(courant_hbm, courant_ref, sems.at[5]),
        pltpu.make_async_copy(heading_hbm, heading_ref, sems.at[6]),
    ]
    cuts = (0, 6, QUAD, HALF, 3 * QUAD, PLANES)
    parts = [
        pltpu.make_async_copy(x_hbm.at[pl.ds(low, high - low)], x_ref.at[pl.ds(low, high - low)], sems.at[k])
        for k, (low, high) in enumerate(zip(cuts, cuts[1:]))
    ]
    for copy in small + parts:
        copy.start()
    for copy in small:
        copy.wait()
    c0, c1 = courant_ref[0], courant_ref[1]
    moving = mov_ref[...]
    sea = sea_ref[...]
    lane = lax.broadcasted_iota(jnp.int32, (height, 128), 1)
    row = lax.broadcasted_iota(jnp.int32, (8, breadth), 0)
    for h in range(breadth // 128):
        halves[h, PLANES * height :, :] = jnp.zeros((4 * height, 128), jnp.float32)

    def quadrant(first, count, from_west, from_south):
        def upstream(flux):
            turned = [pltpu.roll(flux[:, k : k + 128], 1 if from_west else 127, axis=1) for k in range(0, breadth, 128)]
            if from_west:
                sides = [jnp.where(lane == 0, turned[k - 1] if k else 0.0, turned[k]) for k in range(len(turned))]
            else:
                sides = [
                    jnp.where(lane == 127, turned[k + 1] if k + 1 < len(turned) else 0.0, turned[k])
                    for k in range(len(turned))
                ]
            moved = [pltpu.roll(flux[k : k + 8], 1 if from_south else 7, axis=0) for k in range(0, height, 8)]
            if from_south:
                below = [jnp.where(row == 0, moved[k - 1] if k else 0.0, moved[k]) for k in range(len(moved))]
            else:
                below = [
                    jnp.where(row == 7, moved[k + 1] if k + 1 < len(moved) else 0.0, moved[k])
                    for k in range(len(moved))
                ]
            return jnp.concatenate(sides, axis=1), jnp.concatenate(below, axis=0)

        def step(t, carry):
            p = first + t
            courant = jnp.where(p % 2 == 1, c1, c0)
            cx = heading_ref[p] * courant
            cy = heading_ref[PLANES + p] * courant
            energy = x_ref[p]
            for _ in range(2):
                flux = moving * energy
                side, below = upstream(flux)
                div_x = cx * (flux - side) if from_west else cx * (side - flux)
                div_y = cy * (flux - below) if from_south else cy * (below - flux)
                energy = sea * ((energy - div_x) - div_y)
            start = pl.ds(pl.multiple_of(p * height, height), height)
            for h in range(breadth // 128):
                halves[h, start, :] = energy[:, h * 128 : (h + 1) * 128]
            return carry

        lax.fori_loop(0, count, step, 0, unroll=9 if count % 9 == 0 else 6)

    for copy, low, high in zip(parts, cuts, cuts[1:]):
        copy.wait()
        quadrant(low, high - low, low // QUAD in (0, 3), low < HALF)

    east = jnp.zeros((height, 128), jnp.float32)
    west = jnp.zeros((height, 128), jnp.float32)
    for q in range(HALF + 2):
        mine = lane // 2 == q
        if q < HALF:
            p_e = q if q < QUAD else q + HALF
            edge_e, edge_w = x_ref[p_e, :, breadth - 128 :], x_ref[q + QUAD, :, :128]
        else:
            field = moving if q == HALF else sea
            edge_e, edge_w = field[:, breadth - 128 :], field[:, :128]
        east = jnp.where(mine, pltpu.roll(edge_e, (2 * q + 2) % 128, axis=1), east)
        west = jnp.where(mine, pltpu.roll(edge_w, 2 * q, axis=1), west)
    east_ref[...] = east
    west_ref[...] = west


def profile_rows(halves, weight, table, first_row, count, height, breadth):
    pad = jnp.zeros((8, 128), jnp.bfloat16)
    blocks = []
    for k in range(count):
        for h in range(breadth // 128):
            spectra = halves[h, pl.ds(first_row + k, PLANES, stride=height), :]
            high = spectra.astype(jnp.bfloat16)
            low = (spectra - high.astype(jnp.float32)).astype(jnp.bfloat16)
            blocks.append(jnp.concatenate([high, pad, low, pad, high, pad], axis=0))
    stacked = jnp.concatenate(blocks, axis=1)
    profile = lax.dot_general(stacked, weight, (((0,), (0,)), ((), ())), preferred_element_type=jnp.float32)
    start = first_row * breadth
    if not isinstance(start, int):
        start = pl.multiple_of(start, 128)
    table[pl.ds(start, count * breadth), :] = profile


def profile_kernel(courant_ref, kernel_ref, mov_ref, sea_ref, south_ref, north_ref, subs_ref, halves_in,
                   halves, table, edge_ref, wide_kernel):
    height, breadth = mov_ref.shape
    wide = lax.broadcasted_iota(jnp.int32, (HALF + 4, breadth), 1)
    plane = lax.broadcasted_iota(jnp.int32, (HALF + 4, 1), 0)
    subs = subs_ref[...]
    sub_courant = jnp.where(plane % 2 == 1, courant_ref[1], courant_ref[0])

    def x_change(flux, cx, west_first):
        west_flux = jnp.where(wide == 0, 0.0, pltpu.roll(flux, 1, axis=1))
        east_flux = jnp.where(wide == breadth - 1, 0.0, pltpu.roll(flux, breadth - 1, axis=1))
        from_west = (plane < QUAD) if west_first else (plane >= QUAD)
        return jnp.where(from_west, cx * (flux - west_flux), cx * (east_flux - flux))

    def add_rows(first, halo, near, next_row, cx, cy, west_first):
        rim, far = halo[0], halo[1]
        rim_mov, rim_sea = rim[HALF : HALF + 1], rim[HALF + 1 : HALF + 2]
        flux0 = rim_mov * rim
        div_y = cy * (flux0 - far[HALF : HALF + 1] * far)
        flux1 = rim_mov * (rim_sea * ((rim - x_change(flux0, cx, west_first)) - div_y))
        sea0, sea1 = sea_ref[near : near + 1, :], sea_ref[next_row : next_row + 1, :]
        change = sea0 * (cy * flux0)
        flux = mov_ref[near : near + 1, :] * change
        near_change = sea0 * (((change - x_change(flux, cx, west_first)) - cy * flux) + cy * flux1)
        next_change = sea1 * (cy * flux)
        for at, delta in ((near, near_change), (next_row, next_change)):
            for h in range(breadth // 128):
                place = pl.ds(first * height + at, HALF + 4, stride=height)
                halves[h, place, :] = halves[h, place, :] + delta[:, h * 128 : (h + 1) * 128]

    cx_s, cy_s, cx_n, cy_n = (subs[:, k : k + 1] * sub_courant for k in range(4))
    add_rows(0, south_ref, 0, 1, cx_s, cy_s, True)
    add_rows(HALF, north_ref, height - 1, height - 2, cx_n, -cy_n, False)

    pad = jnp.zeros((8, 128), jnp.bfloat16)
    wide_kernel[...] = jnp.zeros((128, 128), jnp.float32)
    wide_kernel[:64, :PLANES] = kernel_ref[...]
    wide_kernel[64:, :PLANES] = kernel_ref[...]
    turned = wide_kernel[...].T
    weight_high = turned[:PLANES].astype(jnp.bfloat16)
    weight_low = (turned[:PLANES] - weight_high.astype(jnp.float32)).astype(jnp.bfloat16)
    weight = jnp.concatenate([weight_high, pad, weight_high, pad, weight_low, pad], axis=0)

    wide_kernel[...] = turned
    edge_ref[...] = jnp.zeros_like(edge_ref)
    for q in range(HALF):
        for side, p in ((0, q if q < QUAD else q + HALF), (1, q + QUAD)):
            for k in range(2):
                lane = 2 * q + (k if side == 0 else 1 - k)
                edge_ref[side, lane : lane + 1, k * 128 : (k + 1) * 128] = wide_kernel[p : p + 1, :]

    profile_rows(halves, weight, table, 0, height, height, breadth)
    table[height * breadth :, :] = jnp.zeros((8, 128), jnp.float32)


def finish_kernel(courant_ref, cells_ref, mov_ref, sea_ref, edge_ref, south_ref, north_ref, second_ref, first_ref,
                  lanes_ref, halves_in, table_in, out_ref, picked_ref, halves, table,
                  cells, lines, picks, window, out_sems, window_sems, pick_sem):
    height, breadth = mov_ref.shape
    cells[...] = jnp.where(cells_ref[...] < 0, height * breadth, cells_ref[...])
    start_windows(cells, window, window_sems)
    even_lon = lax.axis_index("lon") % 2 == 0
    from_west = jnp.where(even_lon, second_ref[...], first_ref[...])
    from_east = jnp.where(even_lon, first_ref[...], second_ref[...])
    lane = lax.broadcasted_iota(jnp.int32, (height, 128), 1)
    row = lax.broadcasted_iota(jnp.int32, (height, 128), 0)
    odd = lane % 2 == 1
    southern = lane < HALF
    lanes = lanes_ref[...]
    lane_courant = jnp.where(lanes[4:5] > 0.5, courant_ref[1], courant_ref[0])

    def y_change(flux, cy, rim):
        south_flux = jnp.where(row == 0, rim, pltpu.roll(flux, 1, axis=0))
        north_flux = jnp.where(row == height - 1, rim, pltpu.roll(flux, height - 1, axis=0))
        return jnp.where(southern, cy * (flux - south_flux), cy * (north_flux - flux))

    def add_columns(half, message, near, next_column, cx, cy, west):
        outer, corner = message[:height], message[height : height + 1]
        outer_mov = jnp.where(odd, outer[:, 2 * HALF + 1 : 2 * HALF + 2], outer[:, 2 * HALF : 2 * HALF + 1])
        sea_lane = 2 * HALF + (3 if west else 2)
        flux0 = outer_mov * outer
        far = pltpu.roll(flux0, 1 if west else 127, axis=1)
        energy = (outer - cx * (flux0 - far)) - y_change(flux0, cy, corner)
        flux1 = outer_mov * (outer[:, sea_lane : sea_lane + 1] * energy)
        at_column = slice(near, near + 1)
        rim = jnp.where(
            southern[:1],
            south_ref[0, HALF : HALF + 1, at_column] * south_ref[0, HALF + 1 : HALF + 2, at_column],
            north_ref[0, HALF : HALF + 1, at_column] * north_ref[0, HALF + 1 : HALF + 2, at_column],
        ) * (cx * corner)
        sea0, sea1 = sea_ref[:, at_column], sea_ref[:, next_column : next_column + 1]
        change = sea0 * (cx * flux0)
        flux = mov_ref[:, at_column] * change
        near_change = sea0 * (((change - cx * flux) - y_change(flux, cy, rim)) + cx * flux1)
        next_change = sea1 * (cx * flux)
        if west:
            both = jnp.where(odd, next_change, pltpu.roll(near_change, 127, axis=1))
        else:
            both = jnp.where(odd, pltpu.roll(near_change, 1, axis=1), next_change)
        edge = lane < 2 if west else lane >= 126
        for q in range(HALF):
            p = q + QUAD if not west else (q if q < QUAD else q + HALF)
            turned = pltpu.roll(both, ((128 if west else 126) - 2 * q) % 128, axis=1)
            place = pl.ds(p * height, height)
            halves[half, place, :] = halves[half, place, :] + jnp.where(edge, turned, 0.0)
        both = jnp.where(lane < 2 * HALF, both, 0.0)
        profile = jnp.dot(
            both, edge_ref[0 if west else 1], precision=lax.Precision.HIGHEST, preferred_element_type=jnp.float32
        )
        for k, column in enumerate((near, next_column)):
            place = pl.ds(column, height, stride=breadth)
            table[place, :] = table[place, :] + profile[:, k * 128 : (k + 1) * 128]

    cx_w, cy_w, cx_e, cy_e = (lanes[k : k + 1] * lane_courant for k in range(4))
    add_columns(0, from_west, 0, 1, cx_w, cy_w, True)
    add_columns(breadth // 128 - 1, from_east, breadth - 1, breadth - 2, -cx_e, cy_e, False)
    whole = pl.ds(0, PLANES * height)
    writes = [
        pltpu.make_async_copy(halves.at[h, whole, :], out_ref.at[:, pl.ds(h * 128, 128)], out_sems.at[h])
        for h in range(breadth // 128)
    ]
    for write in writes:
        write.start()

    first_half = lax.broadcasted_iota(jnp.int32, (1, 128), 1) < 64
    half = WINDOW // 2

    def pick(cell, i):
        def read(first, count):
            for k in range(first, first + count):
                slot = 16 * (k // 8) + k % 8
                one, two = cell(slot), cell(slot + 8)
                lines[k : k + 1, :] = jnp.where(first_half, table[pl.ds(one, 1), :], table[pl.ds(two, 1), :])

        for first in range(0, half, 64):
            read(first, 32)

        for first in range(0, half, 64):

            @pl.when(cell(2 * first + 64) < height * breadth)
            def _():
                read(first + 32, 32)

        here = pl.ds(pl.multiple_of(i * half, half), half)
        picks[here, :] = lines[...].astype(jnp.bfloat16)
        pltpu.make_async_copy(picks.at[here, :], picked_ref.at[here, :], pick_sem).start()

    lines[...] = jnp.zeros_like(lines)
    for_windows(cells, window, window_sems, pick)
    pltpu.make_async_copy(picks, picked_ref, pick_sem).wait()
    for write in writes:
        write.wait()


def add_kernel(rows_ref, values_ref, out_ref, targets, lines, tile_sums, window, window_sems, out_sem, *sums):
    n_acc = len(sums) // 2
    tile = out_ref.shape[1]
    block = 512
    half = WINDOW // 2
    slot = lax.broadcasted_iota(jnp.int32, targets.shape, 1)
    spare = tile + (slot // 16 * 8 + slot % 8) % SPARE
    targets[...] = jnp.where(rows_ref[...] < 0, spare, rows_ref[...])
    start_windows(targets, window, window_sems)

    @pl.loop(0, tile // block, unroll=2)
    def _(i):
        for total in sums:
            total[pl.ds(pl.multiple_of(i * block, block), block), :] = jnp.zeros((block, 128), jnp.float32)

    def add(row, i):
        lines[...] = values_ref[pl.ds(pl.multiple_of(i * half, half), half), :].astype(jnp.float32)
        for k in range(half):
            slot = 16 * (k // 8) + k % 8
            one, two = row(slot), row(slot + 8)
            line = lines[k : k + 1, :]
            left, right = sums[k % n_acc], sums[n_acc + k % n_acc]
            left[pl.ds(one, 1), :] = left[pl.ds(one, 1), :] + line
            right[pl.ds(two, 1), :] = right[pl.ds(two, 1), :] + line

    for_windows(targets, window, window_sems, add)
    first_half = lax.broadcasted_iota(jnp.int32, (block, 128), 1) < 64

    @pl.loop(0, tile // block, unroll=8)
    def _(i):
        here = pl.ds(pl.multiple_of(i * block, block), block)
        left, right = sums[0][here, :], sums[n_acc][here, :]
        for q in range(1, n_acc):
            left = left + sums[q][here, :]
            right = right + sums[n_acc + q][here, :]
        both = jnp.where(first_half, left, right).T
        tile_sums[:, here] = both[:64] + both[64:]
        pltpu.make_async_copy(tile_sums.at[:, here], out_ref.at[:, here], out_sem).start()

    pltpu.make_async_copy(tile_sums, out_ref, out_sem).wait()


def constant_tables():
    heading = (np.arange(DIRS) + 0.5) * (2.0 * math.pi / DIRS)
    cos = np.repeat(np.cos(heading), FREQ)
    sin = np.repeat(np.sin(heading), FREQ)
    lanes = np.zeros((8, 128))
    q = np.arange(HALF)
    from_west = np.where(q < QUAD, q, q + HALF)
    from_east = q + QUAD
    for column in range(2):
        lanes[0, 2 * q + column] = cos[from_west]
        lanes[1, 2 * q + column] = sin[from_west]
        lanes[2, 2 * q + column] = cos[from_east]
        lanes[3, 2 * q + column] = sin[from_east]
        lanes[4, 2 * q + column] = q % 2
    subs = np.zeros((HALF + 4, 128))
    subs[:HALF, 0], subs[:HALF, 1] = cos[:HALF], sin[:HALF]
    subs[:HALF, 2], subs[:HALF, 3] = cos[HALF:], sin[HALF:]
    return [t.astype(np.float32) for t in (np.concatenate([cos, sin]), lanes, subs)]


def body(n_lat, n_lon, spectrum, speed_factor, land_sea_mask, courant, depth_kernel, send_rows, recv_rows):
    height, breadth = speed_factor.shape
    devices, slots = send_rows.shape[1:]
    x = spectrum.reshape(PLANES, height, breadth)
    f32 = jnp.float32
    vmem = pl.BlockSpec(memory_space=pltpu.VMEM)
    smem = pl.BlockSpec(memory_space=pltpu.SMEM)
    hbm = pl.BlockSpec(memory_space=pltpu.HBM)
    params = pltpu.CompilerParams(vmem_limit_bytes=VMEM_LIMIT)

    both = ("lat", "lon")

    def in_hbm(*arrays):
        return [pltpu.with_memory_space_constraint(array, pltpu.HBM) for array in arrays]

    def shape(*dims, kind=f32):
        return jax.ShapeDtypeStruct(dims, kind)

    headings, lanes, subs = constant_tables()
    row_message = shape(2, ROWS, breadth, kind=jnp.bfloat16)
    row_halo = shape(2, HALF + 4, breadth)
    columns = shape(height, 128)
    column_message = shape(height + 8, 128)
    row_first, row_second, column_first, column_second = exchange_pairs(n_lat, n_lon)
    first, second, moving, sea = pl.pallas_call(
        pack_rows_kernel,
        out_shape=[row_message] * 2 + [shape(height, breadth)] * 2,
        in_specs=[hbm] * 3,
        out_specs=[vmem] * 4,
        scratch_shapes=[pltpu.VMEM((2, ROWS, breadth), f32)] * 2
        + [pltpu.VMEM((HALF, 8, breadth), f32)] * 2
        + [pltpu.VMEM((height, breadth), f32), pltpu.VMEM((height, breadth), jnp.int32), pltpu.SemaphoreType.DMA((4,))],
        compiler_params=params,
        name="pack_rows",
    )(*in_hbm(x, speed_factor, land_sea_mask))
    second = lax.ppermute(second, both, row_second)
    first = lax.ppermute(first, "lat", row_first)
    halves, east, west = pl.pallas_call(
        inside_kernel,
        out_shape=[pltpu.VMEM((breadth // 128, (PLANES + 4) * height, 128), f32)] + [columns] * 2,
        in_specs=[hbm] * 3 + [vmem] * 2,
        out_specs=[vmem] * 3,
        scratch_shapes=[
            pltpu.VMEM((PLANES, height, breadth), f32),
            pltpu.SMEM(courant.shape, f32),
            pltpu.SMEM(headings.shape, f32),
            pltpu.SemaphoreType.DMA((7,)),
        ],
        compiler_params=params,
        cost_estimate=pl.CostEstimate(flops=4_000_000_000, bytes_accessed=5_000_000, transcendentals=0),
        name="advance_inside",
    )(*in_hbm(courant, headings, x), moving, sea)
    south, north, first, second = pl.pallas_call(
        functools.partial(corner_kernel, n_lat),
        out_shape=[row_halo] * 2 + [column_message] * 2,
        in_specs=[vmem] * 4,
        out_specs=[vmem] * 4,
        compiler_params=params,
        name="add_corners",
    )(second, first, east, west)
    second = lax.ppermute(second, "lon", column_second)
    first = lax.ppermute(first, "lon", column_first)

    lists = (devices * slots // 128, 128)
    slot_rows = devices * slots // 2
    slot_rows = devices * slots // 2
    halves_shape = pltpu.VMEM(halves.shape, f32)
    table_shape = pltpu.VMEM((height * breadth + 8, 128), f32)
    halves, table, edges = pl.pallas_call(
        profile_kernel,
        out_shape=[halves_shape, table_shape, shape(2, 128, 256)],
        in_specs=[smem] + [vmem] * 7,
        out_specs=[vmem] * 3,
        input_output_aliases={7: 0},
        scratch_shapes=[pltpu.VMEM((128, 128), f32)],
        compiler_params=params,
        cost_estimate=pl.CostEstimate(flops=2_000_000_000, bytes_accessed=5_000_000, transcendentals=0),
        name="profiles_inside",
    )(courant, depth_kernel, moving, sea, south, north, subs, halves)
    propagated, picked, *_ = pl.pallas_call(
        finish_kernel,
        out_shape=[
            pltpu.HBM((PLANES * height, breadth), f32),
            pltpu.HBM((slot_rows, 128), jnp.bfloat16),
            halves_shape,
            table_shape,
        ],
        in_specs=[smem] + [vmem] * 11,
        out_specs=[hbm, hbm, vmem, vmem],
        input_output_aliases={10: 2, 11: 3},
        scratch_shapes=[
            pltpu.VMEM(lists, jnp.int32),
            pltpu.VMEM((WINDOW // 2, 128), f32),
            pltpu.VMEM((slot_rows, 128), jnp.bfloat16),
            pltpu.SMEM((2 * WINDOW // 128, 128), jnp.int32),
            pltpu.SemaphoreType.DMA((breadth // 128,)),
            pltpu.SemaphoreType.DMA((2,)),
            pltpu.SemaphoreType.DMA,
        ],
        compiler_params=params,
        name="finish_and_pick",
    )(courant, send_rows.reshape(lists), moving, sea, edges, south, north, second, first, lanes, halves, table)

    picked = picked.reshape(devices, slots // 2, 128)
    received = lax.all_to_all(picked, both, split_axis=0, concat_axis=0, tiled=True)

    components = depth_kernel.shape[0]
    stokes = pl.pallas_call(
        add_kernel,
        out_shape=pltpu.HBM((components, OUT_DEV), f32),
        in_specs=[vmem] * 2,
        out_specs=hbm,
        scratch_shapes=[
            pltpu.VMEM(lists, jnp.int32),
            pltpu.VMEM((WINDOW // 2, 128), f32),
            pltpu.VMEM((components, OUT_DEV), f32),
            pltpu.SMEM((2 * WINDOW // 128, 128), jnp.int32),
            pltpu.SemaphoreType.DMA((2,)),
            pltpu.SemaphoreType.DMA,
        ]
        + [pltpu.VMEM((OUT_DEV + SPARE, 128), f32)] * (2 * N_ACC),
        compiler_params=pltpu.CompilerParams(vmem_limit_bytes=ADD_VMEM_LIMIT),
        name="add_profiles",
    )(recv_rows.reshape(lists), received.reshape(slot_rows, 128))
    return propagated.reshape(DIRS, FREQ, height, breadth), stokes


def solution(mesh):
    placed = (
        P(None, None, "lat", "lon"),
        P("lat", "lon"),
        P("lat", "lon"),
        P(),
        P(),
        P(("lat", "lon"), None, None),
        P(("lat", "lon"), None, None),
    )
    return jax.shard_map(
        functools.partial(body, mesh.shape["lat"], mesh.shape["lon"]),
        mesh=mesh,
        in_specs=placed,
        out_specs=(P(None, None, "lat", "lon"), P(None, ("lat", "lon"))),
        check_vma=False,
    )
```

```python
import functools
import math

import jax
import jax.numpy as jnp
import numpy as np
from jax import lax
from jax.experimental import pallas as pl
from jax.experimental.pallas import tpu as pltpu
from jax.sharding import PartitionSpec as P

DIRS = 36
FREQ = 2
PLANES = DIRS * FREQ
HALF = PLANES // 2
QUAD = PLANES // 4
OUT_DEV = 4096
SPARE = 64
N_ACC = 5
ROWS = HALF + 12
WINDOW = 1024
VMEM_LIMIT = 16 * 1024 * 1024
ADD_VMEM_LIMIT = 32 * 1024 * 1024


def exchange_pairs(n_lat, n_lon):
    def flat(j, i):
        return j * n_lon + i % n_lon

    row_first = [(j, j ^ 1) for j in range(n_lat)]
    row_second = []
    for i in range(n_lon):
        row_second += [(flat(0, i), flat(0, i)), (flat(n_lat - 1, i), flat(n_lat - 1, n_lon - 1 - i))]
        for j in range(1, n_lat - 1, 2):
            row_second += [(flat(j, i), flat(j + 1, i)), (flat(j + 1, i), flat(j, i))]
    column_first = [(i, i ^ 1) for i in range(n_lon)]
    column_second = [(i, (i + 1 if i % 2 else i - 1) % n_lon) for i in range(n_lon)]
    return row_first, row_second, column_first, column_second


def pack_rows_kernel(x_hbm, speed_hbm, mask_hbm, first_ref, second_ref, mov_ref, sea_ref,
                     up_ref, down_ref, top_rows, bottom_rows, speed_ref, mask_ref, sems):
    height, breadth = speed_ref.shape
    copies = [
        pltpu.make_async_copy(source, target, sems.at[k])
        for k, (source, target) in enumerate((
            (speed_hbm, speed_ref),
            (mask_hbm, mask_ref),
            (x_hbm.at[pl.ds(0, HALF), pl.ds(height - 2, 2), :], top_rows.at[:, pl.ds(6, 2), :]),
            (x_hbm.at[pl.ds(HALF, HALF), pl.ds(0, 2), :], bottom_rows.at[:, pl.ds(0, 2), :]),
        ))
    ]
    for copy in copies:
        copy.start()
    even = lax.axis_index("lat") % 2 == 0
    for copy in copies:
        copy.wait()
    sea = mask_ref[...].astype(jnp.float32)
    moving = speed_ref[...] * sea
    mov_ref[...] = moving
    sea_ref[...] = sea
    for k in range(2):
        up_ref[k, :HALF, :] = top_rows[:, 7 - k, :]
        down_ref[k, :HALF, :] = bottom_rows[:, k, :]
        up_ref[k, HALF : HALF + 1, :] = moving[height - 1 - k : height - k, :]
        down_ref[k, HALF : HALF + 1, :] = moving[k : k + 1, :]
        up_ref[k, HALF + 1 : HALF + 2, :] = sea[height - 1 - k : height - k, :]
        down_ref[k, HALF + 1 : HALF + 2, :] = sea[k : k + 1, :]
        up_ref[k, HALF + 2 :, :] = jnp.zeros((ROWS - HALF - 2, breadth), jnp.float32)
        down_ref[k, HALF + 2 :, :] = jnp.zeros((ROWS - HALF - 2, breadth), jnp.float32)

    @pl.when(even)
    def _():
        first_ref[...] = up_ref[...].astype(jnp.bfloat16)
        second_ref[...] = down_ref[...].astype(jnp.bfloat16)

    @pl.when(jnp.logical_not(even))
    def _():
        first_ref[...] = down_ref[...].astype(jnp.bfloat16)
        second_ref[...] = up_ref[...].astype(jnp.bfloat16)


def corner_kernel(n_lat, second_ref, first_ref, east_ref, west_ref, south_ref, north_ref, out_first, out_second):
    height = east_ref.shape[0]
    breadth = first_ref.shape[2]
    lat = lax.axis_index("lat")
    even = lat % 2 == 0

    used = HALF + 4

    @pl.when(even)
    def _():
        north_ref[...] = first_ref[...].astype(jnp.float32)[:, :used]
        south_ref[...] = second_ref[...].astype(jnp.float32)[:, :used]

    @pl.when(jnp.logical_not(even))
    def _():
        south_ref[...] = first_ref[...].astype(jnp.float32)[:, :used]
        north_ref[...] = second_ref[...].astype(jnp.float32)[:, :used]

    @pl.when(lat == 0)
    def _():
        south_ref[...] = jnp.zeros_like(south_ref)

    @pl.when(lat == n_lat - 1)
    def _():
        flip_i = lax.broadcasted_iota(jnp.int32, (breadth, breadth), 0)
        flip_j = lax.broadcasted_iota(jnp.int32, (breadth, breadth), 1)
        flip = (flip_i + flip_j == breadth - 1).astype(jnp.bfloat16)
        both = jnp.concatenate([second_ref[0], second_ref[1]], axis=0)
        flipped = jnp.dot(both, flip, preferred_element_type=jnp.float32)
        north_ref[0] = flipped[:used]
        north_ref[1] = flipped[ROWS : ROWS + used]

    plane = lax.broadcasted_iota(jnp.int32, (HALF + 4, 128), 0)
    lane = lax.broadcasted_iota(jnp.int32, (HALF + 4, 128), 1)
    south = south_ref[0] * south_ref[0, HALF : HALF + 1, :]
    north = north_ref[0] * north_ref[0, HALF : HALF + 1, :]

    def to_lanes(column, low, high, place):
        mine = (plane >= low) & (plane < high) & (lane == place)
        return jnp.where(mine, column, 0.0)

    east_edge = to_lanes(south[:, breadth - 1 :], 0, QUAD, 2 * plane + 1)
    east_edge += to_lanes(north[:, breadth - 1 :], QUAD, HALF, 2 * plane + 1)
    west_edge = to_lanes(south[:, :1], QUAD, HALF, 2 * plane - HALF)
    west_edge += to_lanes(north[:, :1], 0, QUAD, 2 * plane + HALF)
    east_edge = jnp.broadcast_to(jnp.sum(east_edge, axis=0, keepdims=True), (8, 128))
    west_edge = jnp.broadcast_to(jnp.sum(west_edge, axis=0, keepdims=True), (8, 128))
    even_lon = lax.axis_index("lon") % 2 == 0
    out_first[:height] = jnp.where(even_lon, east_ref[...], west_ref[...])
    out_second[:height] = jnp.where(even_lon, west_ref[...], east_ref[...])
    out_first[height:] = jnp.where(even_lon, east_edge, west_edge)
    out_second[height:] = jnp.where(even_lon, west_edge, east_edge)


def fetch_window(list_ref, window, sems, i, w):
    lines = WINDOW // 128
    source = list_ref.at[pl.ds(pl.multiple_of(i * lines, lines), lines), :]
    return pltpu.make_async_copy(source, window.at[pl.ds(w * lines, lines), :], sems.at[w])


def start_windows(list_ref, window, sems):
    for w in range(2):
        fetch_window(list_ref, window, sems, w, w).start()


def for_windows(list_ref, window, sems, work):
    lines = WINDOW // 128
    count = list_ref.shape[0] // lines

    @pl.loop(0, count // 2)
    def _(t):
        for w in range(2):
            i = 2 * t + w
            fetch_window(list_ref, window, sems, i, w).wait()
            work(lambda k, start=w * lines: window[start + k // 128, k % 128], i)

            @pl.when(i + 2 < count)
            def _():
                fetch_window(list_ref, window, sems, i + 2, w).start()


def inside_kernel(courant_hbm, heading_hbm, x_hbm, mov_ref, sea_ref, halves, east_ref, west_ref,
                  x_ref, courant_ref, heading_ref, sems):
    height, breadth = mov_ref.shape
    small = [
        pltpu.make_async_copy(courant_hbm, courant_ref, sems.at[5]),
        pltpu.make_async_copy(heading_hbm, heading_ref, sems.at[6]),
    ]
    cuts = (0, 6, QUAD, HALF, 3 * QUAD, PLANES)
    parts = [
        pltpu.make_async_copy(x_hbm.at[pl.ds(low, high - low)], x_ref.at[pl.ds(low, high - low)], sems.at[k])
        for k, (low, high) in enumerate(zip(cuts, cuts[1:]))
    ]
    for copy in small + parts:
        copy.start()
    for copy in small:
        copy.wait()
    c0, c1 = courant_ref[0], courant_ref[1]
    moving = mov_ref[...]
    sea = sea_ref[...]
    lane = lax.broadcasted_iota(jnp.int32, (height, 128), 1)
    row = lax.broadcasted_iota(jnp.int32, (8, breadth), 0)
    for h in range(breadth // 128):
        halves[h, PLANES * height :, :] = jnp.zeros((4 * height, 128), jnp.float32)

    def quadrant(first, count, from_west, from_south):
        def upstream(flux):
            turned = [pltpu.roll(flux[:, k : k + 128], 1 if from_west else 127, axis=1) for k in range(0, breadth, 128)]
            if from_west:
                sides = [jnp.where(lane == 0, turned[k - 1] if k else 0.0, turned[k]) for k in range(len(turned))]
            else:
                sides = [
                    jnp.where(lane == 127, turned[k + 1] if k + 1 < len(turned) else 0.0, turned[k])
                    for k in range(len(turned))
                ]
            moved = [pltpu.roll(flux[k : k + 8], 1 if from_south else 7, axis=0) for k in range(0, height, 8)]
            if from_south:
                below = [jnp.where(row == 0, moved[k - 1] if k else 0.0, moved[k]) for k in range(len(moved))]
            else:
                below = [
                    jnp.where(row == 7, moved[k + 1] if k + 1 < len(moved) else 0.0, moved[k])
                    for k in range(len(moved))
                ]
            return jnp.concatenate(sides, axis=1), jnp.concatenate(below, axis=0)

        def step(t, carry):
            p = first + t
            courant = jnp.where(p % 2 == 1, c1, c0)
            cx = heading_ref[p] * courant
            cy = heading_ref[PLANES + p] * courant
            energy = x_ref[p]
            for _ in range(2):
                flux = moving * energy
                side, below = upstream(flux)
                div_x = cx * (flux - side) if from_west else cx * (side - flux)
                div_y = cy * (flux - below) if from_south else cy * (below - flux)
                energy = sea * ((energy - div_x) - div_y)
            start = pl.ds(pl.multiple_of(p * height, height), height)
            for h in range(breadth // 128):
                halves[h, start, :] = energy[:, h * 128 : (h + 1) * 128]
            return carry

        lax.fori_loop(0, count, step, 0, unroll=9 if count % 9 == 0 else 6)

    for copy, low, high in zip(parts, cuts, cuts[1:]):
        copy.wait()
        quadrant(low, high - low, low // QUAD in (0, 3), low < HALF)

    east = jnp.zeros((height, 128), jnp.float32)
    west = jnp.zeros((height, 128), jnp.float32)
    for q in range(HALF + 2):
        mine = lane // 2 == q
        if q < HALF:
            p_e = q if q < QUAD else q + HALF
            edge_e, edge_w = x_ref[p_e, :, breadth - 128 :], x_ref[q + QUAD, :, :128]
        else:
            field = moving if q == HALF else sea
            edge_e, edge_w = field[:, breadth - 128 :], field[:, :128]
        east = jnp.where(mine, pltpu.roll(edge_e, (2 * q + 2) % 128, axis=1), east)
        west = jnp.where(mine, pltpu.roll(edge_w, 2 * q, axis=1), west)
    east_ref[...] = east
    west_ref[...] = west


def profile_rows(halves, weight, table, first_row, count, height, breadth):
    pad = jnp.zeros((8, 128), jnp.bfloat16)
    blocks = []
    for k in range(count):
        for h in range(breadth // 128):
            spectra = halves[h, pl.ds(first_row + k, PLANES, stride=height), :]
            high = spectra.astype(jnp.bfloat16)
            low = (spectra - high.astype(jnp.float32)).astype(jnp.bfloat16)
            blocks.append(jnp.concatenate([high, pad, low, pad, high, pad], axis=0))
    stacked = jnp.concatenate(blocks, axis=1)
    profile = lax.dot_general(stacked, weight, (((0,), (0,)), ((), ())), preferred_element_type=jnp.float32)
    start = first_row * breadth
    if not isinstance(start, int):
        start = pl.multiple_of(start, 128)
    table[pl.ds(start, count * breadth), :] = profile


def profile_kernel(courant_ref, kernel_ref, mov_ref, sea_ref, south_ref, north_ref, subs_ref, halves_in,
                   halves, table, edge_ref, wide_kernel):
    height, breadth = mov_ref.shape
    wide = lax.broadcasted_iota(jnp.int32, (HALF + 4, breadth), 1)
    plane = lax.broadcasted_iota(jnp.int32, (HALF + 4, 1), 0)
    subs = subs_ref[...]
    sub_courant = jnp.where(plane % 2 == 1, courant_ref[1], courant_ref[0])

    def x_change(flux, cx, west_first):
        west_flux = jnp.where(wide == 0, 0.0, pltpu.roll(flux, 1, axis=1))
        east_flux = jnp.where(wide == breadth - 1, 0.0, pltpu.roll(flux, breadth - 1, axis=1))
        from_west = (plane < QUAD) if west_first else (plane >= QUAD)
        return jnp.where(from_west, cx * (flux - west_flux), cx * (east_flux - flux))

    def add_rows(first, halo, near, next_row, cx, cy, west_first):
        rim, far = halo[0], halo[1]
        rim_mov, rim_sea = rim[HALF : HALF + 1], rim[HALF + 1 : HALF + 2]
        flux0 = rim_mov * rim
        div_y = cy * (flux0 - far[HALF : HALF + 1] * far)
        flux1 = rim_mov * (rim_sea * ((rim - x_change(flux0, cx, west_first)) - div_y))
        sea0, sea1 = sea_ref[near : near + 1, :], sea_ref[next_row : next_row + 1, :]
        change = sea0 * (cy * flux0)
        flux = mov_ref[near : near + 1, :] * change
        near_change = sea0 * (((change - x_change(flux, cx, west_first)) - cy * flux) + cy * flux1)
        next_change = sea1 * (cy * flux)
        for at, delta in ((near, near_change), (next_row, next_change)):
            for h in range(breadth // 128):
                place = pl.ds(first * height + at, HALF + 4, stride=height)
                halves[h, place, :] = halves[h, place, :] + delta[:, h * 128 : (h + 1) * 128]

    cx_s, cy_s, cx_n, cy_n = (subs[:, k : k + 1] * sub_courant for k in range(4))
    add_rows(0, south_ref, 0, 1, cx_s, cy_s, True)
    add_rows(HALF, north_ref, height - 1, height - 2, cx_n, -cy_n, False)

    pad = jnp.zeros((8, 128), jnp.bfloat16)
    wide_kernel[...] = jnp.zeros((128, 128), jnp.float32)
    wide_kernel[:64, :PLANES] = kernel_ref[...]
    wide_kernel[64:, :PLANES] = kernel_ref[...]
    turned = wide_kernel[...].T
    weight_high = turned[:PLANES].astype(jnp.bfloat16)
    weight_low = (turned[:PLANES] - weight_high.astype(jnp.float32)).astype(jnp.bfloat16)
    weight = jnp.concatenate([weight_high, pad, weight_high, pad, weight_low, pad], axis=0)

    wide_kernel[...] = turned
    edge_ref[...] = jnp.zeros_like(edge_ref)
    for q in range(HALF):
        for side, p in ((0, q if q < QUAD else q + HALF), (1, q + QUAD)):
            for k in range(2):
                lane = 2 * q + (k if side == 0 else 1 - k)
                edge_ref[side, lane : lane + 1, k * 128 : (k + 1) * 128] = wide_kernel[p : p + 1, :]

    profile_rows(halves, weight, table, 0, height, height, breadth)
    table[height * breadth :, :] = jnp.zeros((8, 128), jnp.float32)


def finish_kernel(courant_ref, cells_ref, mov_ref, sea_ref, edge_ref, south_ref, north_ref, second_ref, first_ref,
                  lanes_ref, halves_in, table_in, out_ref, picked_ref, halves, table,
                  cells, lines, picks, window, out_sems, window_sems, pick_sem):
    height, breadth = mov_ref.shape
    cells[...] = jnp.where(cells_ref[...] < 0, height * breadth, cells_ref[...])
    start_windows(cells, window, window_sems)
    even_lon = lax.axis_index("lon") % 2 == 0
    from_west = jnp.where(even_lon, second_ref[...], first_ref[...])
    from_east = jnp.where(even_lon, first_ref[...], second_ref[...])
    lane = lax.broadcasted_iota(jnp.int32, (height, 128), 1)
    row = lax.broadcasted_iota(jnp.int32, (height, 128), 0)
    odd = lane % 2 == 1
    southern = lane < HALF
    lanes = lanes_ref[...]
    lane_courant = jnp.where(lanes[4:5] > 0.5, courant_ref[1], courant_ref[0])

    def y_change(flux, cy, rim):
        south_flux = jnp.where(row == 0, rim, pltpu.roll(flux, 1, axis=0))
        north_flux = jnp.where(row == height - 1, rim, pltpu.roll(flux, height - 1, axis=0))
        return jnp.where(southern, cy * (flux - south_flux), cy * (north_flux - flux))

    def add_columns(half, message, near, next_column, cx, cy, west):
        outer, corner = message[:height], message[height : height + 1]
        outer_mov = jnp.where(odd, outer[:, 2 * HALF + 1 : 2 * HALF + 2], outer[:, 2 * HALF : 2 * HALF + 1])
        sea_lane = 2 * HALF + (3 if west else 2)
        flux0 = outer_mov * outer
        far = pltpu.roll(flux0, 1 if west else 127, axis=1)
        energy = (outer - cx * (flux0 - far)) - y_change(flux0, cy, corner)
        flux1 = outer_mov * (outer[:, sea_lane : sea_lane + 1] * energy)
        at_column = slice(near, near + 1)
        rim = jnp.where(
            southern[:1],
            south_ref[0, HALF : HALF + 1, at_column] * south_ref[0, HALF + 1 : HALF + 2, at_column],
            north_ref[0, HALF : HALF + 1, at_column] * north_ref[0, HALF + 1 : HALF + 2, at_column],
        ) * (cx * corner)
        sea0, sea1 = sea_ref[:, at_column], sea_ref[:, next_column : next_column + 1]
        change = sea0 * (cx * flux0)
        flux = mov_ref[:, at_column] * change
        near_change = sea0 * (((change - cx * flux) - y_change(flux, cy, rim)) + cx * flux1)
        next_change = sea1 * (cx * flux)
        if west:
            both = jnp.where(odd, next_change, pltpu.roll(near_change, 127, axis=1))
        else:
            both = jnp.where(odd, pltpu.roll(near_change, 1, axis=1), next_change)
        edge = lane < 2 if west else lane >= 126
        for q in range(HALF):
            p = q + QUAD if not west else (q if q < QUAD else q + HALF)
            turned = pltpu.roll(both, ((128 if west else 126) - 2 * q) % 128, axis=1)
            place = pl.ds(p * height, height)
            halves[half, place, :] = halves[half, place, :] + jnp.where(edge, turned, 0.0)
        both = jnp.where(lane < 2 * HALF, both, 0.0)
        profile = jnp.dot(
            both, edge_ref[0 if west else 1], precision=lax.Precision.HIGHEST, preferred_element_type=jnp.float32
        )
        for k, column in enumerate((near, next_column)):
            place = pl.ds(column, height, stride=breadth)
            table[place, :] = table[place, :] + profile[:, k * 128 : (k + 1) * 128]

    cx_w, cy_w, cx_e, cy_e = (lanes[k : k + 1] * lane_courant for k in range(4))
    add_columns(0, from_west, 0, 1, cx_w, cy_w, True)
    add_columns(breadth // 128 - 1, from_east, breadth - 1, breadth - 2, -cx_e, cy_e, False)
    whole = pl.ds(0, PLANES * height)
    writes = [
        pltpu.make_async_copy(halves.at[h, whole, :], out_ref.at[:, pl.ds(h * 128, 128)], out_sems.at[h])
        for h in range(breadth // 128)
    ]
    for write in writes:
        write.start()

    first_half = lax.broadcasted_iota(jnp.int32, (1, 128), 1) < 64
    half = WINDOW // 2

    def pick(cell, i):
        def read(first, count):
            for k in range(first, first + count):
                slot = 16 * (k // 8) + k % 8
                one, two = cell(slot), cell(slot + 8)
                lines[k : k + 1, :] = jnp.where(first_half, table[pl.ds(one, 1), :], table[pl.ds(two, 1), :])

        for first in range(0, half, 64):
            read(first, 32)

            @pl.when(cell(2 * first + 64) < height * breadth)
            def _():
                read(first + 32, 32)

        here = pl.ds(pl.multiple_of(i * half, half), half)
        picks[here, :] = lines[...].astype(jnp.bfloat16)
        pltpu.make_async_copy(picks.at[here, :], picked_ref.at[here, :], pick_sem).start()

    lines[...] = jnp.zeros_like(lines)
    for_windows(cells, window, window_sems, pick)
    pltpu.make_async_copy(picks, picked_ref, pick_sem).wait()
    for write in writes:
        write.wait()


def add_kernel(rows_ref, values_ref, out_ref, targets, lines, tile_sums, window, window_sems, out_sem, *sums):
    n_acc = len(sums) // 2
    tile = out_ref.shape[1]
    block = 512
    half = WINDOW // 2
    slot = lax.broadcasted_iota(jnp.int32, targets.shape, 1)
    spare = tile + (slot // 16 * 8 + slot % 8) % SPARE
    targets[...] = jnp.where(rows_ref[...] < 0, spare, rows_ref[...])
    start_windows(targets, window, window_sems)

    @pl.loop(0, tile // block, unroll=2)
    def _(i):
        for total in sums:
            total[pl.ds(pl.multiple_of(i * block, block), block), :] = jnp.zeros((block, 128), jnp.float32)

    def add(row, i):
        lines[...] = values_ref[pl.ds(pl.multiple_of(i * half, half), half), :].astype(jnp.float32)
        for k in range(half):
            slot = 16 * (k // 8) + k % 8
            one, two = row(slot), row(slot + 8)
            line = lines[k : k + 1, :]
            left, right = sums[k % n_acc], sums[n_acc + k % n_acc]
            left[pl.ds(one, 1), :] = left[pl.ds(one, 1), :] + line
            right[pl.ds(two, 1), :] = right[pl.ds(two, 1), :] + line

    for_windows(targets, window, window_sems, add)
    first_half = lax.broadcasted_iota(jnp.int32, (block, 128), 1) < 64

    @pl.loop(0, tile // block, unroll=8)
    def _(i):
        here = pl.ds(pl.multiple_of(i * block, block), block)
        left, right = sums[0][here, :], sums[n_acc][here, :]
        for q in range(1, n_acc):
            left = left + sums[q][here, :]
            right = right + sums[n_acc + q][here, :]
        both = jnp.where(first_half, left, right).T
        tile_sums[:, here] = both[:64] + both[64:]
        pltpu.make_async_copy(tile_sums.at[:, here], out_ref.at[:, here], out_sem).start()

    pltpu.make_async_copy(tile_sums, out_ref, out_sem).wait()


def constant_tables():
    heading = (np.arange(DIRS) + 0.5) * (2.0 * math.pi / DIRS)
    cos = np.repeat(np.cos(heading), FREQ)
    sin = np.repeat(np.sin(heading), FREQ)
    lanes = np.zeros((8, 128))
    q = np.arange(HALF)
    from_west = np.where(q < QUAD, q, q + HALF)
    from_east = q + QUAD
    for column in range(2):
        lanes[0, 2 * q + column] = cos[from_west]
        lanes[1, 2 * q + column] = sin[from_west]
        lanes[2, 2 * q + column] = cos[from_east]
        lanes[3, 2 * q + column] = sin[from_east]
        lanes[4, 2 * q + column] = q % 2
    subs = np.zeros((HALF + 4, 128))
    subs[:HALF, 0], subs[:HALF, 1] = cos[:HALF], sin[:HALF]
    subs[:HALF, 2], subs[:HALF, 3] = cos[HALF:], sin[HALF:]
    return [t.astype(np.float32) for t in (np.concatenate([cos, sin]), lanes, subs)]


def body(n_lat, n_lon, spectrum, speed_factor, land_sea_mask, courant, depth_kernel, send_rows, recv_rows):
    height, breadth = speed_factor.shape
    devices, slots = send_rows.shape[1:]
    x = spectrum.reshape(PLANES, height, breadth)
    f32 = jnp.float32
    vmem = pl.BlockSpec(memory_space=pltpu.VMEM)
    smem = pl.BlockSpec(memory_space=pltpu.SMEM)
    hbm = pl.BlockSpec(memory_space=pltpu.HBM)
    params = pltpu.CompilerParams(vmem_limit_bytes=VMEM_LIMIT)

    both = ("lat", "lon")

    def in_hbm(*arrays):
        return [pltpu.with_memory_space_constraint(array, pltpu.HBM) for array in arrays]

    def shape(*dims, kind=f32):
        return jax.ShapeDtypeStruct(dims, kind)

    headings, lanes, subs = constant_tables()
    row_message = shape(2, ROWS, breadth, kind=jnp.bfloat16)
    row_halo = shape(2, HALF + 4, breadth)
    columns = shape(height, 128)
    column_message = shape(height + 8, 128)
    row_first, row_second, column_first, column_second = exchange_pairs(n_lat, n_lon)
    first, second, moving, sea = pl.pallas_call(
        pack_rows_kernel,
        out_shape=[row_message] * 2 + [shape(height, breadth)] * 2,
        in_specs=[hbm] * 3,
        out_specs=[vmem] * 4,
        scratch_shapes=[pltpu.VMEM((2, ROWS, breadth), f32)] * 2
        + [pltpu.VMEM((HALF, 8, breadth), f32)] * 2
        + [pltpu.VMEM((height, breadth), f32), pltpu.VMEM((height, breadth), jnp.int32), pltpu.SemaphoreType.DMA((4,))],
        compiler_params=params,
        name="pack_rows",
    )(*in_hbm(x, speed_factor, land_sea_mask))
    second = lax.ppermute(second, both, row_second)
    first = lax.ppermute(first, "lat", row_first)
    halves, east, west = pl.pallas_call(
        inside_kernel,
        out_shape=[pltpu.VMEM((breadth // 128, (PLANES + 4) * height, 128), f32)] + [columns] * 2,
        in_specs=[hbm] * 3 + [vmem] * 2,
        out_specs=[vmem] * 3,
        scratch_shapes=[
            pltpu.VMEM((PLANES, height, breadth), f32),
            pltpu.SMEM(courant.shape, f32),
            pltpu.SMEM(headings.shape, f32),
            pltpu.SemaphoreType.DMA((7,)),
        ],
        compiler_params=params,
        cost_estimate=pl.CostEstimate(flops=4_000_000_000, bytes_accessed=5_000_000, transcendentals=0),
        name="advance_inside",
    )(*in_hbm(courant, headings, x), moving, sea)
    south, north, first, second = pl.pallas_call(
        functools.partial(corner_kernel, n_lat),
        out_shape=[row_halo] * 2 + [column_message] * 2,
        in_specs=[vmem] * 4,
        out_specs=[vmem] * 4,
        compiler_params=params,
        name="add_corners",
    )(second, first, east, west)
    second = lax.ppermute(second, "lon", column_second)
    first = lax.ppermute(first, "lon", column_first)

    lists = (devices * slots // 128, 128)
    slot_rows = devices * slots // 2
    slot_rows = devices * slots // 2
    halves_shape = pltpu.VMEM(halves.shape, f32)
    table_shape = pltpu.VMEM((height * breadth + 8, 128), f32)
    halves, table, edges = pl.pallas_call(
        profile_kernel,
        out_shape=[halves_shape, table_shape, shape(2, 128, 256)],
        in_specs=[smem] + [vmem] * 7,
        out_specs=[vmem] * 3,
        input_output_aliases={7: 0},
        scratch_shapes=[pltpu.VMEM((128, 128), f32)],
        compiler_params=params,
        cost_estimate=pl.CostEstimate(flops=2_000_000_000, bytes_accessed=5_000_000, transcendentals=0),
        name="profiles_inside",
    )(courant, depth_kernel, moving, sea, south, north, subs, halves)
    propagated, picked, *_ = pl.pallas_call(
        finish_kernel,
        out_shape=[
            pltpu.HBM((PLANES * height, breadth), f32),
            pltpu.HBM((slot_rows, 128), jnp.bfloat16),
            halves_shape,
            table_shape,
        ],
        in_specs=[smem] + [vmem] * 11,
        out_specs=[hbm, hbm, vmem, vmem],
        input_output_aliases={10: 2, 11: 3},
        scratch_shapes=[
            pltpu.VMEM(lists, jnp.int32),
            pltpu.VMEM((WINDOW // 2, 128), f32),
            pltpu.VMEM((slot_rows, 128), jnp.bfloat16),
            pltpu.SMEM((2 * WINDOW // 128, 128), jnp.int32),
            pltpu.SemaphoreType.DMA((breadth // 128,)),
            pltpu.SemaphoreType.DMA((2,)),
            pltpu.SemaphoreType.DMA,
        ],
        compiler_params=params,
        name="finish_and_pick",
    )(courant, send_rows.reshape(lists), moving, sea, edges, south, north, second, first, lanes, halves, table)

    picked = picked.reshape(devices, slots // 2, 128)
    received = lax.all_to_all(picked, both, split_axis=0, concat_axis=0, tiled=True)

    components = depth_kernel.shape[0]
    stokes = pl.pallas_call(
        add_kernel,
        out_shape=pltpu.HBM((components, OUT_DEV), f32),
        in_specs=[vmem] * 2,
        out_specs=hbm,
        scratch_shapes=[
            pltpu.VMEM(lists, jnp.int32),
            pltpu.VMEM((WINDOW // 2, 128), f32),
            pltpu.VMEM((components, OUT_DEV), f32),
            pltpu.SMEM((2 * WINDOW // 128, 128), jnp.int32),
            pltpu.SemaphoreType.DMA((2,)),
            pltpu.SemaphoreType.DMA,
        ]
        + [pltpu.VMEM((OUT_DEV + SPARE, 128), f32)] * (2 * N_ACC),
        compiler_params=pltpu.CompilerParams(vmem_limit_bytes=ADD_VMEM_LIMIT),
        name="add_profiles",
    )(recv_rows.reshape(lists), received.reshape(slot_rows, 128))
    return propagated.reshape(DIRS, FREQ, height, breadth), stokes


def solution(mesh):
    placed = (
        P(None, None, "lat", "lon"),
        P("lat", "lon"),
        P("lat", "lon"),
        P(),
        P(),
        P(("lat", "lon"), None, None),
        P(("lat", "lon"), None, None),
    )
    return jax.shard_map(
        functools.partial(body, mesh.shape["lat"], mesh.shape["lon"]),
        mesh=mesh,
        in_specs=placed,
        out_specs=(P(None, None, "lat", "lon"), P(None, ("lat", "lon"))),
        check_vma=False,
    )
```

```python
import functools
import math

import jax
import jax.numpy as jnp
import numpy as np
from jax import lax
from jax.experimental import pallas as pl
from jax.experimental.pallas import tpu as pltpu
from jax.sharding import PartitionSpec as P

DIRS = 36
FREQ = 2
PLANES = DIRS * FREQ
HALF = PLANES // 2
QUAD = PLANES // 4
OUT_DEV = 4096
SPARE = 64
N_ACC = 5
ROWS = HALF + 12
WINDOW = 1024
VMEM_LIMIT = 16 * 1024 * 1024
ADD_VMEM_LIMIT = 32 * 1024 * 1024


def exchange_pairs(n_lat, n_lon):
    def flat(j, i):
        return j * n_lon + i % n_lon

    row_first = [(j, j ^ 1) for j in range(n_lat)]
    row_second = []
    for i in range(n_lon):
        row_second += [(flat(0, i), flat(0, i)), (flat(n_lat - 1, i), flat(n_lat - 1, n_lon - 1 - i))]
        for j in range(1, n_lat - 1, 2):
            row_second += [(flat(j, i), flat(j + 1, i)), (flat(j + 1, i), flat(j, i))]
    column_first = [(i, i ^ 1) for i in range(n_lon)]
    column_second = [(i, (i + 1 if i % 2 else i - 1) % n_lon) for i in range(n_lon)]
    return row_first, row_second, column_first, column_second


def pack_rows_kernel(x_hbm, speed_hbm, mask_hbm, first_ref, second_ref, mov_ref, sea_ref,
                     up_ref, down_ref, top_rows, bottom_rows, speed_ref, mask_ref, sems):
    height, breadth = speed_ref.shape
    copies = [
        pltpu.make_async_copy(source, target, sems.at[k])
        for k, (source, target) in enumerate((
            (speed_hbm, speed_ref),
            (mask_hbm, mask_ref),
            (x_hbm.at[pl.ds(0, HALF), pl.ds(height - 2, 2), :], top_rows.at[:, pl.ds(6, 2), :]),
            (x_hbm.at[pl.ds(HALF, HALF), pl.ds(0, 2), :], bottom_rows.at[:, pl.ds(0, 2), :]),
        ))
    ]
    for copy in copies:
        copy.start()
    even = lax.axis_index("lat") % 2 == 0
    for copy in copies:
        copy.wait()
    sea = mask_ref[...].astype(jnp.float32)
    moving = speed_ref[...] * sea
    mov_ref[...] = moving
    sea_ref[...] = sea
    for k in range(2):
        up_ref[k, :HALF, :] = top_rows[:, 7 - k, :]
        down_ref[k, :HALF, :] = bottom_rows[:, k, :]
        up_ref[k, HALF : HALF + 1, :] = moving[height - 1 - k : height - k, :]
        down_ref[k, HALF : HALF + 1, :] = moving[k : k + 1, :]
        up_ref[k, HALF + 1 : HALF + 2, :] = sea[height - 1 - k : height - k, :]
        down_ref[k, HALF + 1 : HALF + 2, :] = sea[k : k + 1, :]
        up_ref[k, HALF + 2 :, :] = jnp.zeros((ROWS - HALF - 2, breadth), jnp.float32)
        down_ref[k, HALF + 2 :, :] = jnp.zeros((ROWS - HALF - 2, breadth), jnp.float32)

    @pl.when(even)
    def _():
        first_ref[...] = up_ref[...].astype(jnp.bfloat16)
        second_ref[...] = down_ref[...].astype(jnp.bfloat16)

    @pl.when(jnp.logical_not(even))
    def _():
        first_ref[...] = down_ref[...].astype(jnp.bfloat16)
        second_ref[...] = up_ref[...].astype(jnp.bfloat16)


def corner_kernel(n_lat, second_ref, first_ref, east_ref, west_ref, south_ref, north_ref, out_first, out_second):
    height = east_ref.shape[0]
    breadth = first_ref.shape[2]
    lat = lax.axis_index("lat")
    even = lat % 2 == 0

    used = HALF + 4

    @pl.when(even)
    def _():
        north_ref[...] = first_ref[...].astype(jnp.float32)[:, :used]
        south_ref[...] = second_ref[...].astype(jnp.float32)[:, :used]

    @pl.when(jnp.logical_not(even))
    def _():
        south_ref[...] = first_ref[...].astype(jnp.float32)[:, :used]
        north_ref[...] = second_ref[...].astype(jnp.float32)[:, :used]

    @pl.when(lat == 0)
    def _():
        south_ref[...] = jnp.zeros_like(south_ref)

    @pl.when(lat == n_lat - 1)
    def _():
        flip_i = lax.broadcasted_iota(jnp.int32, (breadth, breadth), 0)
        flip_j = lax.broadcasted_iota(jnp.int32, (breadth, breadth), 1)
        flip = (flip_i + flip_j == breadth - 1).astype(jnp.bfloat16)
        both = jnp.concatenate([second_ref[0], second_ref[1]], axis=0)
        flipped = jnp.dot(both, flip, preferred_element_type=jnp.float32)
        north_ref[0] = flipped[:used]
        north_ref[1] = flipped[ROWS : ROWS + used]

    plane = lax.broadcasted_iota(jnp.int32, (HALF + 4, 128), 0)
    lane = lax.broadcasted_iota(jnp.int32, (HALF + 4, 128), 1)
    south = south_ref[0] * south_ref[0, HALF : HALF + 1, :]
    north = north_ref[0] * north_ref[0, HALF : HALF + 1, :]

    def to_lanes(column, low, high, place):
        mine = (plane >= low) & (plane < high) & (lane == place)
        return jnp.where(mine, column, 0.0)

    east_edge = to_lanes(south[:, breadth - 1 :], 0, QUAD, 2 * plane + 1)
    east_edge += to_lanes(north[:, breadth - 1 :], QUAD, HALF, 2 * plane + 1)
    west_edge = to_lanes(south[:, :1], QUAD, HALF, 2 * plane - HALF)
    west_edge += to_lanes(north[:, :1], 0, QUAD, 2 * plane + HALF)
    east_edge = jnp.broadcast_to(jnp.sum(east_edge, axis=0, keepdims=True), (8, 128))
    west_edge = jnp.broadcast_to(jnp.sum(west_edge, axis=0, keepdims=True), (8, 128))
    even_lon = lax.axis_index("lon") % 2 == 0
    out_first[:height] = jnp.where(even_lon, east_ref[...], west_ref[...])
    out_second[:height] = jnp.where(even_lon, west_ref[...], east_ref[...])
    out_first[height:] = jnp.where(even_lon, east_edge, west_edge)
    out_second[height:] = jnp.where(even_lon, west_edge, east_edge)


def fetch_window(list_ref, window, sems, i, w):
    lines = WINDOW // 128
    source = list_ref.at[pl.ds(pl.multiple_of(i * lines, lines), lines), :]
    return pltpu.make_async_copy(source, window.at[pl.ds(w * lines, lines), :], sems.at[w])


def start_windows(list_ref, window, sems):
    for w in range(2):
        fetch_window(list_ref, window, sems, w, w).start()


def for_windows(list_ref, window, sems, work):
    lines = WINDOW // 128
    count = list_ref.shape[0] // lines

    @pl.loop(0, count // 2)
    def _(t):
        for w in range(2):
            i = 2 * t + w
            fetch_window(list_ref, window, sems, i, w).wait()
            work(lambda k, start=w * lines: window[start + k // 128, k % 128], i)

            @pl.when(i + 2 < count)
            def _():
                fetch_window(list_ref, window, sems, i + 2, w).start()


def inside_kernel(courant_hbm, heading_hbm, x_hbm, mov_ref, sea_ref, halves, east_ref, west_ref,
                  x_ref, courant_ref, heading_ref, sems):
    height, breadth = mov_ref.shape
    small = [
        pltpu.make_async_copy(courant_hbm, courant_ref, sems.at[5]),
        pltpu.make_async_copy(heading_hbm, heading_ref, sems.at[6]),
    ]
    cuts = (0, 6, QUAD, HALF, 3 * QUAD, PLANES)
    parts = [
        pltpu.make_async_copy(x_hbm.at[pl.ds(low, high - low)], x_ref.at[pl.ds(low, high - low)], sems.at[k])
        for k, (low, high) in enumerate(zip(cuts, cuts[1:]))
    ]
    for copy in small + parts:
        copy.start()
    for copy in small:
        copy.wait()
    c0, c1 = courant_ref[0], courant_ref[1]
    moving = mov_ref[...]
    sea = sea_ref[...]
    lane = lax.broadcasted_iota(jnp.int32, (height, 128), 1)
    row = lax.broadcasted_iota(jnp.int32, (8, breadth), 0)
    for h in range(breadth // 128):
        halves[h, PLANES * height :, :] = jnp.zeros((5 * height, 128), jnp.float32)

    def quadrant(first, count, from_west, from_south):
        def upstream(flux):
            turned = [pltpu.roll(flux[:, k : k + 128], 1 if from_west else 127, axis=1) for k in range(0, breadth, 128)]
            if from_west:
                sides = [jnp.where(lane == 0, turned[k - 1] if k else 0.0, turned[k]) for k in range(len(turned))]
            else:
                sides = [
                    jnp.where(lane == 127, turned[k + 1] if k + 1 < len(turned) else 0.0, turned[k])
                    for k in range(len(turned))
                ]
            moved = [pltpu.roll(flux[k : k + 8], 1 if from_south else 7, axis=0) for k in range(0, height, 8)]
            if from_south:
                below = [jnp.where(row == 0, moved[k - 1] if k else 0.0, moved[k]) for k in range(len(moved))]
            else:
                below = [
                    jnp.where(row == 7, moved[k + 1] if k + 1 < len(moved) else 0.0, moved[k])
                    for k in range(len(moved))
                ]
            return jnp.concatenate(sides, axis=1), jnp.concatenate(below, axis=0)

        def step(t, carry):
            p = first + t
            courant = jnp.where(p % 2 == 1, c1, c0)
            cx = heading_ref[p] * courant
            cy = heading_ref[PLANES + p] * courant
            energy = x_ref[p]
            for _ in range(2):
                flux = moving * energy
                side, below = upstream(flux)
                div_x = cx * (flux - side) if from_west else cx * (side - flux)
                div_y = cy * (flux - below) if from_south else cy * (below - flux)
                energy = sea * ((energy - div_x) - div_y)
            start = pl.ds(pl.multiple_of(p * height, height), height)
            for h in range(breadth // 128):
                halves[h, start, :] = energy[:, h * 128 : (h + 1) * 128]
            return carry

        lax.fori_loop(0, count, step, 0, unroll=9 if count % 9 == 0 else 6)

    for copy, low, high in zip(parts, cuts, cuts[1:]):
        copy.wait()
        quadrant(low, high - low, low // QUAD in (0, 3), low < HALF)

    east = jnp.zeros((height, 128), jnp.float32)
    west = jnp.zeros((height, 128), jnp.float32)
    for q in range(HALF + 2):
        mine = lane // 2 == q
        if q < HALF:
            p_e = q if q < QUAD else q + HALF
            edge_e, edge_w = x_ref[p_e, :, breadth - 128 :], x_ref[q + QUAD, :, :128]
        else:
            field = moving if q == HALF else sea
            edge_e, edge_w = field[:, breadth - 128 :], field[:, :128]
        east = jnp.where(mine, pltpu.roll(edge_e, (2 * q + 2) % 128, axis=1), east)
        west = jnp.where(mine, pltpu.roll(edge_w, 2 * q, axis=1), west)
    east_ref[...] = east
    west_ref[...] = west


def profile_rows(halves, weight, table, first_row, count, height, breadth):
    pad = jnp.zeros((8, 128), jnp.bfloat16)
    blocks = []
    for k in range(count):
        for h in range(breadth // 128):
            spectra = halves[h, pl.ds(first_row + k, PLANES, stride=height), :]
            high = spectra.astype(jnp.bfloat16)
            low = (spectra - high.astype(jnp.float32)).astype(jnp.bfloat16)
            blocks.append(jnp.concatenate([high, pad, low, pad, high, pad], axis=0))
    stacked = jnp.concatenate(blocks, axis=1)
    profile = lax.dot_general(stacked, weight, (((0,), (0,)), ((), ())), preferred_element_type=jnp.float32)
    start = first_row * breadth
    if not isinstance(start, int):
        start = pl.multiple_of(start, 128)
    table[pl.ds(start, count * breadth), :] = profile


def profile_kernel(courant_ref, kernel_ref, mov_ref, sea_ref, south_ref, north_ref, subs_ref, halves_in,
                   halves, table, edge_ref, wide_kernel):
    height, breadth = mov_ref.shape
    wide = lax.broadcasted_iota(jnp.int32, (HALF + 4, breadth), 1)
    plane = lax.broadcasted_iota(jnp.int32, (HALF + 4, 1), 0)
    subs = subs_ref[...]
    sub_courant = jnp.where(plane % 2 == 1, courant_ref[1], courant_ref[0])

    def x_change(flux, cx, west_first):
        west_flux = jnp.where(wide == 0, 0.0, pltpu.roll(flux, 1, axis=1))
        east_flux = jnp.where(wide == breadth - 1, 0.0, pltpu.roll(flux, breadth - 1, axis=1))
        from_west = (plane < QUAD) if west_first else (plane >= QUAD)
        return jnp.where(from_west, cx * (flux - west_flux), cx * (east_flux - flux))

    def add_rows(first, halo, near, next_row, cx, cy, west_first):
        rim, far = halo[0], halo[1]
        rim_mov, rim_sea = rim[HALF : HALF + 1], rim[HALF + 1 : HALF + 2]
        flux0 = rim_mov * rim
        div_y = cy * (flux0 - far[HALF : HALF + 1] * far)
        flux1 = rim_mov * (rim_sea * ((rim - x_change(flux0, cx, west_first)) - div_y))
        sea0, sea1 = sea_ref[near : near + 1, :], sea_ref[next_row : next_row + 1, :]
        change = sea0 * (cy * flux0)
        flux = mov_ref[near : near + 1, :] * change
        near_change = sea0 * (((change - x_change(flux, cx, west_first)) - cy * flux) + cy * flux1)
        next_change = sea1 * (cy * flux)
        for at, delta in ((near, near_change), (next_row, next_change)):
            for h in range(breadth // 128):
                place = pl.ds(first * height + at, HALF + 4, stride=height)
                halves[h, place, :] = halves[h, place, :] + delta[:, h * 128 : (h + 1) * 128]

    cx_s, cy_s, cx_n, cy_n = (subs[:, k : k + 1] * sub_courant for k in range(4))
    add_rows(0, south_ref, 0, 1, cx_s, cy_s, True)
    add_rows(HALF, north_ref, height - 1, height - 2, cx_n, -cy_n, False)

    pad = jnp.zeros((8, 128), jnp.bfloat16)
    wide_kernel[...] = jnp.zeros((128, 128), jnp.float32)
    wide_kernel[:64, :PLANES] = kernel_ref[...]
    wide_kernel[64:, :PLANES] = kernel_ref[...]
    turned = wide_kernel[...].T
    weight_high = turned[:PLANES].astype(jnp.bfloat16)
    weight_low = (turned[:PLANES] - weight_high.astype(jnp.float32)).astype(jnp.bfloat16)
    weight = jnp.concatenate([weight_high, pad, weight_high, pad, weight_low, pad], axis=0)

    wide_kernel[...] = turned
    edge_ref[...] = jnp.zeros_like(edge_ref)
    for q in range(HALF):
        for side, p in ((0, q if q < QUAD else q + HALF), (1, q + QUAD)):
            for k in range(2):
                lane = 2 * q + (k if side == 0 else 1 - k)
                edge_ref[side, lane : lane + 1, k * 128 : (k + 1) * 128] = wide_kernel[p : p + 1, :]

    profile_rows(halves, weight, table, 0, height, height, breadth)
    table[height * breadth :, :] = jnp.zeros((breadth, 128), jnp.float32)


def finish_kernel(courant_ref, cells_ref, mov_ref, sea_ref, edge_ref, south_ref, north_ref, second_ref, first_ref,
                  lanes_ref, halves_in, table_in, out_ref, picked_ref, halves, table,
                  cells, lines, picks, window, out_sems, window_sems, pick_sem):
    height, breadth = mov_ref.shape
    cells[...] = jnp.where(cells_ref[...] < 0, height * breadth, cells_ref[...])
    start_windows(cells, window, window_sems)
    even_lon = lax.axis_index("lon") % 2 == 0
    from_west = jnp.where(even_lon, second_ref[...], first_ref[...])
    from_east = jnp.where(even_lon, first_ref[...], second_ref[...])
    lane = lax.broadcasted_iota(jnp.int32, (height, 128), 1)
    row = lax.broadcasted_iota(jnp.int32, (height, 128), 0)
    odd = lane % 2 == 1
    southern = lane < HALF
    lanes = lanes_ref[...]
    lane_courant = jnp.where(lanes[4:5] > 0.5, courant_ref[1], courant_ref[0])

    def y_change(flux, cy, rim):
        south_flux = jnp.where(row == 0, rim, pltpu.roll(flux, 1, axis=0))
        north_flux = jnp.where(row == height - 1, rim, pltpu.roll(flux, height - 1, axis=0))
        return jnp.where(southern, cy * (flux - south_flux), cy * (north_flux - flux))

    def add_columns(half, message, near, next_column, cx, cy, west):
        outer, corner = message[:height], message[height : height + 1]
        outer_mov = jnp.where(odd, outer[:, 2 * HALF + 1 : 2 * HALF + 2], outer[:, 2 * HALF : 2 * HALF + 1])
        sea_lane = 2 * HALF + (3 if west else 2)
        flux0 = outer_mov * outer
        far = pltpu.roll(flux0, 1 if west else 127, axis=1)
        energy = (outer - cx * (flux0 - far)) - y_change(flux0, cy, corner)
        flux1 = outer_mov * (outer[:, sea_lane : sea_lane + 1] * energy)
        at_column = slice(near, near + 1)
        rim = jnp.where(
            southern[:1],
            south_ref[0, HALF : HALF + 1, at_column] * south_ref[0, HALF + 1 : HALF + 2, at_column],
            north_ref[0, HALF : HALF + 1, at_column] * north_ref[0, HALF + 1 : HALF + 2, at_column],
        ) * (cx * corner)
        sea0, sea1 = sea_ref[:, at_column], sea_ref[:, next_column : next_column + 1]
        change = sea0 * (cx * flux0)
        flux = mov_ref[:, at_column] * change
        near_change = sea0 * (((change - cx * flux) - y_change(flux, cy, rim)) + cx * flux1)
        next_change = sea1 * (cx * flux)
        if west:
            both = jnp.where(odd, next_change, pltpu.roll(near_change, 127, axis=1))
        else:
            both = jnp.where(odd, pltpu.roll(near_change, 1, axis=1), next_change)
        edge = lane < 2 if west else lane >= 126
        for q in range(HALF):
            p = q + QUAD if not west else (q if q < QUAD else q + HALF)
            turned = pltpu.roll(both, ((128 if west else 126) - 2 * q) % 128, axis=1)
            place = pl.ds(p * height, height)
            halves[half, place, :] = halves[half, place, :] + jnp.where(edge, turned, 0.0)
        both = jnp.where(lane < 2 * HALF, both, 0.0)
        profile = jnp.dot(
            both, edge_ref[0 if west else 1], precision=lax.Precision.HIGHEST, preferred_element_type=jnp.float32
        )
        for k, column in enumerate((near, next_column)):
            place = pl.ds(column, height, stride=breadth)
            table[place, :] = table[place, :] + profile[:, k * 128 : (k + 1) * 128]

    cx_w, cy_w, cx_e, cy_e = (lanes[k : k + 1] * lane_courant for k in range(4))
    add_columns(0, from_west, 0, 1, cx_w, cy_w, True)
    add_columns(breadth // 128 - 1, from_east, breadth - 1, breadth - 2, -cx_e, cy_e, False)
    whole = pl.ds(0, PLANES * height)
    writes = [
        pltpu.make_async_copy(halves.at[h, whole, :], out_ref.at[:, pl.ds(h * 128, 128)], out_sems.at[h])
        for h in range(breadth // 128)
    ]
    for write in writes:
        write.start()

    first_half = lax.broadcasted_iota(jnp.int32, (1, 128), 1) < 64
    half = WINDOW // 2

    def pick(cell, i):
        def read(first, count):
            for k in range(first, first + count):
                slot = 16 * (k // 8) + k % 8
                one, two = cell(slot), cell(slot + 8)
                lines[k : k + 1, :] = jnp.where(first_half, table[pl.ds(one, 1), :], table[pl.ds(two, 1), :])

        for first in range(0, half, 64):
            read(first, 32)

            @pl.when(cell(2 * first + 64) < height * breadth)
            def _():
                read(first + 32, 32)

        here = pl.ds(pl.multiple_of(i * half, half), half)
        picks[here, :] = lines[...].astype(jnp.bfloat16)
        pltpu.make_async_copy(picks.at[here, :], picked_ref.at[here, :], pick_sem).start()

    lines[...] = jnp.zeros_like(lines)
    for_windows(cells, window, window_sems, pick)
    pltpu.make_async_copy(picks, picked_ref, pick_sem).wait()
    for write in writes:
        write.wait()


def add_kernel(rows_ref, values_ref, out_ref, targets, lines, tile_sums, window, window_sems, out_sem, *sums):
    n_acc = len(sums) // 2
    tile = out_ref.shape[1]
    block = 512
    half = WINDOW // 2
    slot = lax.broadcasted_iota(jnp.int32, targets.shape, 1)
    spare = tile + (slot // 16 * 8 + slot % 8) % SPARE
    targets[...] = jnp.where(rows_ref[...] < 0, spare, rows_ref[...])
    start_windows(targets, window, window_sems)

    @pl.loop(0, tile // block, unroll=2)
    def _(i):
        for total in sums:
            total[pl.ds(pl.multiple_of(i * block, block), block), :] = jnp.zeros((block, 128), jnp.float32)

    def add(row, i):
        lines[...] = values_ref[pl.ds(pl.multiple_of(i * half, half), half), :].astype(jnp.float32)
        for k in range(half):
            slot = 16 * (k // 8) + k % 8
            one, two = row(slot), row(slot + 8)
            line = lines[k : k + 1, :]
            left, right = sums[k % n_acc], sums[n_acc + k % n_acc]
            left[pl.ds(one, 1), :] = left[pl.ds(one, 1), :] + line
            right[pl.ds(two, 1), :] = right[pl.ds(two, 1), :] + line

    for_windows(targets, window, window_sems, add)
    first_half = lax.broadcasted_iota(jnp.int32, (block, 128), 1) < 64

    @pl.loop(0, tile // block, unroll=8)
    def _(i):
        here = pl.ds(pl.multiple_of(i * block, block), block)
        left, right = sums[0][here, :], sums[n_acc][here, :]
        for q in range(1, n_acc):
            left = left + sums[q][here, :]
            right = right + sums[n_acc + q][here, :]
        both = jnp.where(first_half, left, right).T
        tile_sums[:, here] = both[:64] + both[64:]
        pltpu.make_async_copy(tile_sums.at[:, here], out_ref.at[:, here], out_sem).start()

    pltpu.make_async_copy(tile_sums, out_ref, out_sem).wait()


def constant_tables():
    heading = (np.arange(DIRS) + 0.5) * (2.0 * math.pi / DIRS)
    cos = np.repeat(np.cos(heading), FREQ)
    sin = np.repeat(np.sin(heading), FREQ)
    lanes = np.zeros((8, 128))
    q = np.arange(HALF)
    from_west = np.where(q < QUAD, q, q + HALF)
    from_east = q + QUAD
    for column in range(2):
        lanes[0, 2 * q + column] = cos[from_west]
        lanes[1, 2 * q + column] = sin[from_west]
        lanes[2, 2 * q + column] = cos[from_east]
        lanes[3, 2 * q + column] = sin[from_east]
        lanes[4, 2 * q + column] = q % 2
    subs = np.zeros((HALF + 4, 128))
    subs[:HALF, 0], subs[:HALF, 1] = cos[:HALF], sin[:HALF]
    subs[:HALF, 2], subs[:HALF, 3] = cos[HALF:], sin[HALF:]
    return [t.astype(np.float32) for t in (np.concatenate([cos, sin]), lanes, subs)]


def body(n_lat, n_lon, spectrum, speed_factor, land_sea_mask, courant, depth_kernel, send_rows, recv_rows):
    height, breadth = speed_factor.shape
    devices, slots = send_rows.shape[1:]
    x = spectrum.reshape(PLANES, height, breadth)
    f32 = jnp.float32
    vmem = pl.BlockSpec(memory_space=pltpu.VMEM)
    smem = pl.BlockSpec(memory_space=pltpu.SMEM)
    hbm = pl.BlockSpec(memory_space=pltpu.HBM)
    params = pltpu.CompilerParams(vmem_limit_bytes=VMEM_LIMIT)

    both = ("lat", "lon")

    def in_hbm(*arrays):
        return [pltpu.with_memory_space_constraint(array, pltpu.HBM) for array in arrays]

    def shape(*dims, kind=f32):
        return jax.ShapeDtypeStruct(dims, kind)

    headings, lanes, subs = constant_tables()
    row_message = shape(2, ROWS, breadth, kind=jnp.bfloat16)
    row_halo = shape(2, HALF + 4, breadth)
    columns = shape(height, 128)
    column_message = shape(height + 8, 128)
    row_first, row_second, column_first, column_second = exchange_pairs(n_lat, n_lon)
    first, second, moving, sea = pl.pallas_call(
        pack_rows_kernel,
        out_shape=[row_message] * 2 + [shape(height, breadth)] * 2,
        in_specs=[hbm] * 3,
        out_specs=[vmem] * 4,
        scratch_shapes=[pltpu.VMEM((2, ROWS, breadth), f32)] * 2
        + [pltpu.VMEM((HALF, 8, breadth), f32)] * 2
        + [pltpu.VMEM((height, breadth), f32), pltpu.VMEM((height, breadth), jnp.int32), pltpu.SemaphoreType.DMA((4,))],
        compiler_params=params,
        name="pack_rows",
    )(*in_hbm(x, speed_factor, land_sea_mask))
    second = lax.ppermute(second, both, row_second)
    first = lax.ppermute(first, "lat", row_first)
    halves, east, west = pl.pallas_call(
        inside_kernel,
        out_shape=[pltpu.VMEM((breadth // 128, (PLANES + 5) * height, 128), f32)] + [columns] * 2,
        in_specs=[hbm] * 3 + [vmem] * 2,
        out_specs=[vmem] * 3,
        scratch_shapes=[
            pltpu.VMEM((PLANES, height, breadth), f32),
            pltpu.SMEM(courant.shape, f32),
            pltpu.SMEM(headings.shape, f32),
            pltpu.SemaphoreType.DMA((7,)),
        ],
        compiler_params=params,
        cost_estimate=pl.CostEstimate(flops=4_000_000_000, bytes_accessed=5_000_000, transcendentals=0),
        name="advance_inside",
    )(*in_hbm(courant, headings, x), moving, sea)
    south, north, first, second = pl.pallas_call(
        functools.partial(corner_kernel, n_lat),
        out_shape=[row_halo] * 2 + [column_message] * 2,
        in_specs=[vmem] * 4,
        out_specs=[vmem] * 4,
        compiler_params=params,
        name="add_corners",
    )(second, first, east, west)
    second = lax.ppermute(second, "lon", column_second)
    first = lax.ppermute(first, "lon", column_first)

    lists = (devices * slots // 128, 128)
    slot_rows = devices * slots // 2
    slot_rows = devices * slots // 2
    halves_shape = pltpu.VMEM(halves.shape, f32)
    table_shape = pltpu.VMEM((height * breadth + breadth, 128), f32)
    halves, table, edges = pl.pallas_call(
        profile_kernel,
        out_shape=[halves_shape, table_shape, shape(2, 128, 256)],
        in_specs=[smem] + [vmem] * 7,
        out_specs=[vmem] * 3,
        input_output_aliases={7: 0},
        scratch_shapes=[pltpu.VMEM((128, 128), f32)],
        compiler_params=params,
        cost_estimate=pl.CostEstimate(flops=2_000_000_000, bytes_accessed=5_000_000, transcendentals=0),
        name="profiles_inside",
    )(courant, depth_kernel, moving, sea, south, north, subs, halves)
    propagated, picked, *_ = pl.pallas_call(
        finish_kernel,
        out_shape=[
            pltpu.HBM((PLANES * height, breadth), f32),
            pltpu.HBM((slot_rows, 128), jnp.bfloat16),
            halves_shape,
            table_shape,
        ],
        in_specs=[smem] + [vmem] * 11,
        out_specs=[hbm, hbm, vmem, vmem],
        input_output_aliases={10: 2, 11: 3},
        scratch_shapes=[
            pltpu.VMEM(lists, jnp.int32),
            pltpu.VMEM((WINDOW // 2, 128), f32),
            pltpu.VMEM((slot_rows, 128), jnp.bfloat16),
            pltpu.SMEM((2 * WINDOW // 128, 128), jnp.int32),
            pltpu.SemaphoreType.DMA((breadth // 128,)),
            pltpu.SemaphoreType.DMA((2,)),
            pltpu.SemaphoreType.DMA,
        ],
        compiler_params=params,
        name="finish_and_pick",
    )(courant, send_rows.reshape(lists), moving, sea, edges, south, north, second, first, lanes, halves, table)

    picked = picked.reshape(devices, slots // 2, 128)
    received = lax.all_to_all(picked, both, split_axis=0, concat_axis=0, tiled=True)

    components = depth_kernel.shape[0]
    stokes = pl.pallas_call(
        add_kernel,
        out_shape=pltpu.HBM((components, OUT_DEV), f32),
        in_specs=[vmem] * 2,
        out_specs=hbm,
        scratch_shapes=[
            pltpu.VMEM(lists, jnp.int32),
            pltpu.VMEM((WINDOW // 2, 128), f32),
            pltpu.VMEM((components, OUT_DEV), f32),
            pltpu.SMEM((2 * WINDOW // 128, 128), jnp.int32),
            pltpu.SemaphoreType.DMA((2,)),
            pltpu.SemaphoreType.DMA,
        ]
        + [pltpu.VMEM((OUT_DEV + SPARE + 8, 128), f32)] * (2 * N_ACC),
        compiler_params=pltpu.CompilerParams(vmem_limit_bytes=ADD_VMEM_LIMIT),
        name="add_profiles",
    )(recv_rows.reshape(lists), received.reshape(slot_rows, 128))
    return propagated.reshape(DIRS, FREQ, height, breadth), stokes


def solution(mesh):
    placed = (
        P(None, None, "lat", "lon"),
        P("lat", "lon"),
        P("lat", "lon"),
        P(),
        P(),
        P(("lat", "lon"), None, None),
        P(("lat", "lon"), None, None),
    )
    return jax.shard_map(
        functools.partial(body, mesh.shape["lat"], mesh.shape["lon"]),
        mesh=mesh,
        in_specs=placed,
        out_specs=(P(None, None, "lat", "lon"), P(None, ("lat", "lon"))),
        check_vma=False,
    )
```
